32 devices in a mesh: dp: 4 (over y, x), heads: 4 (over z), tensor: 2 (over core).
Axes of the slice: x: 2, y: 2, z: 4, core: 2. Of those that a mesh axis runs over, the one named last changes fastest.
Arguments:
- tokens: bfloat16 [6144, 2048], P('dp', ('heads', 'tensor')), may hold values from -6 to 6
- cotangent: bfloat16 [6144, 2048], P('dp', ('heads', 'tensor')), may hold values from -6 to 6
- lengths: int32 [12], replicated, may hold values from 1 to 1024, as said below
- dealing: int32 [12], replicated, may hold values from 0 to 11, as said below
- w_query: float32 [2048, 2048], P('dp', ('heads', 'tensor')), may hold values from -0.125 to 0.125
- w_key: float32 [2048, 2048], P('dp', ('heads', 'tensor')), may hold values from -0.125 to 0.125
- w_value: float32 [2048, 4096], P('dp', ('heads', 'tensor')), may hold values from -0.125 to 0.125
- w_swish: float32 [2048, 4096], P('dp', ('heads', 'tensor')), may hold values from -0.125 to 0.125
- w_out: float32 [4096, 2048], P(('heads', 'tensor'), 'dp'), may hold values from -0.1875 to 0.1875
- w_gate: float32 [2048, 4096], P('dp', ('heads', 'tensor')), may hold values from -0.125 to 0.125
- w_up: float32 [2048, 4096], P('dp', ('heads', 'tensor')), may hold values from -0.125 to 0.125
- w_down: float32 [4096, 2048], P(('heads', 'tensor'), 'dp'), may hold values from -0.1875 to 0.1875
- gain_attn: float32 [2048], P('dp'), may hold values from 0.25 to 1.75
- gain_mlp: float32 [2048], P('dp'), may hold values from 0.25 to 1.75
Outputs:
- mixed: bfloat16 [6144, 2048], P('dp', ('heads', 'tensor'))
- grad_tokens: bfloat16 [6144, 2048], P('dp', ('heads', 'tensor'))
- grad_query: float32 [2048, 2048], P('dp', ('heads', 'tensor'))
- grad_key: float32 [2048, 2048], P('dp', ('heads', 'tensor'))
- grad_value: float32 [2048, 4096], P('dp', ('heads', 'tensor'))
- grad_swish: float32 [2048, 4096], P('dp', ('heads', 'tensor'))
- grad_out: float32 [4096, 2048], P(('heads', 'tensor'), 'dp')
- grad_gate: float32 [2048, 4096], P('dp', ('heads', 'tensor'))
- grad_up: float32 [2048, 4096], P('dp', ('heads', 'tensor'))
- grad_down: float32 [4096, 2048], P(('heads', 'tensor'), 'dp')
- grad_gain_attn: float32 [2048], P('dp')
- grad_gain_mlp: float32 [2048], P('dp')
The draws below stay inside these ranges and needn't reach their ends.
Inputs may be any that keep to these rules, and one draw needn't show every extreme that they name: For each g, the 3 sequences named by dealing[g * 3] to dealing[(g + 1) * 3 - 1] have lengths that sum to 1536, and exactly one of them has length 1024. `dealing`: A permutation of the sequences.
All inputs are finite; a program needn't handle non-finite values.
Results may differ from the reference program's by a relative error of at most 0.02.
The reference program's roundings to bfloat16 on the way count: a program that leaves them out, or rounds other values in their place, can miss the bound.
Values may be sent and summed in bfloat16 or wider, within the bound.
A program may use at most 256 MiB of HBM per device.

```python
from functools import partial
import jax
import jax.numpy as jnp
from jax import lax

D = 2048
HEADS = 8
QK_DIM = 256
V_DIM = 512
FF = 4096
TOK_DEV = 1536
SEQ_DEV = 3
SEQ_MAX = 1024
SEQS = 12
TOKENS = 6144
N_DP = 4


def deal_draw(key):
    groups = SEQS // SEQ_DEV
    group_keys = jax.random.split(jax.random.fold_in(key, 11), groups)
    remain = TOK_DEV - SEQ_MAX

    def one_group(group_key):
        first_key, second_key = jax.random.split(group_key)
        split_at = jax.random.randint(first_key, (), 1, remain, dtype=jnp.int32)
        base = jnp.stack([jnp.int32(SEQ_MAX), split_at, jnp.int32(remain) - split_at]).astype(jnp.int32)
        return base[jax.random.permutation(second_key, SEQ_DEV)]
    dealt = jax.vmap(one_group)(group_keys).reshape(-1)
    ordering = jax.random.permutation(jax.random.fold_in(key, 12), SEQS).astype(jnp.int32)
    length_table = jnp.zeros((SEQS,), jnp.int32).at[ordering].set(dealt)
    return (length_table, ordering)


def draw_lengths(key, part):
    return deal_draw(key)[0]


def draw_dealing(key, part):
    return deal_draw(key)[1]


def block_scale(own_key, shape, shards, least, top_value):
    def one(axis_at, parts):
        heights = jax.random.uniform(jax.random.fold_in(jax.random.fold_in(own_key, 6), axis_at), (parts,), jnp.float32, least / len(shards), top_value / len(shards))
        return jnp.repeat(jnp.exp(heights), shape[axis_at] // parts).reshape((-1,) + (1,) * (len(shape) - axis_at - 1))

    gain = one(*shards[0])
    for cut in shards[1:]:
        gain = gain * one(*cut)
    return gain


def centred(key, shape, spread, reach, shards=(), kind=jnp.bfloat16):
    entries = jax.random.normal(key, shape, jnp.float32) * spread
    if len(shards) > 0:
        entries = block_scale(key, shape, shards, -0.22, 0.18) * entries
    return jnp.clip(entries, min=-reach, max=reach).astype(kind)


def setup_inputs(seed: int = 0) -> dict:
    seeds = jax.random.split(jax.random.key(seed), 15)
    return {
        "tokens": centred(seeds[0], (TOKENS, D), 1.0, 6.0, ((0, 4), (1, 8))),
        "cotangent": centred(seeds[1], (TOKENS, D), 1.0, 6.0, ((0, 4), (1, 8))),
        "lengths": draw_lengths(jax.random.fold_in(seeds[14], 71), 0),
        "dealing": draw_dealing(jax.random.fold_in(seeds[14], 71), 0),
        "w_query": centred(seeds[4], (D, HEADS * QK_DIM), D ** -0.5, 0.125, ((0, 4), (1, 8)), jnp.float32),
        "w_key": centred(seeds[5], (D, HEADS * QK_DIM), D ** -0.5, 0.125, ((0, 4), (1, 8)), jnp.float32),
        "w_value": centred(seeds[6], (D, HEADS * V_DIM), D ** -0.5, 0.125, ((0, 4), (1, 8)), jnp.float32),
        "w_swish": centred(seeds[7], (D, HEADS * V_DIM), D ** -0.5, 0.125, ((0, 4), (1, 8)), jnp.float32),
        "w_out": centred(seeds[8], (HEADS * V_DIM, D), (HEADS * V_DIM // 4) ** -0.5, 0.1875, ((0, 8), (1, 4)), jnp.float32),
        "w_gate": centred(seeds[9], (D, FF), D ** -0.5, 0.125, ((0, 4), (1, 8)), jnp.float32),
        "w_up": centred(seeds[10], (D, FF), D ** -0.5, 0.125, ((0, 4), (1, 8)), jnp.float32),
        "w_down": centred(seeds[11], (FF, D), (FF // 4) ** -0.5, 0.1875, ((0, 8), (1, 4)), jnp.float32),
        "gain_attn": jnp.clip(1.0 + 0.15 * jax.random.normal(seeds[12], (D,), jnp.float32), 0.25, 1.75),
        "gain_mlp": jnp.clip(1.0 + 0.15 * jax.random.normal(seeds[13], (D,), jnp.float32), 0.25, 1.75),
    }


GROUP_EPS = 1.0

@jax.custom_vjp
def low(v):
    return lax.optimization_barrier(v.astype(jnp.bfloat16)).astype(jnp.float32)

@jax.custom_vjp
def low_back(v):
    return v

def low_keep(v):
    return (low(v), None)

def low_pass(kept, grad):
    return (grad,)

def back_keep(v):
    return (v, None)

def back_low(kept, grad):
    return (low(grad),)
low.defvjp(low_keep, low_pass)
low_back.defvjp(back_keep, back_low)

def matmul(left, right):
    return jnp.dot(left, right, precision=lax.Precision.HIGHEST, preferred_element_type=jnp.float32)

def layer_norm(values, epsilon):
    center = values - lax.optimization_barrier(jnp.mean(values, -1, keepdims=True))
    return center * lax.rsqrt(lax.optimization_barrier(jnp.mean(center * center, -1, keepdims=True)) + epsilon)

def deal_rows(lengths, dealing):
    starts = (jnp.cumsum(lengths) - lengths).astype(jnp.int32)
    dealt_len = jnp.take(lengths, dealing).reshape(N_DP, SEQ_DEV)
    dealt_start = (jnp.cumsum(dealt_len, 1) - dealt_len).astype(jnp.int32)
    home_start = jnp.take(starts, dealing).reshape(N_DP, SEQ_DEV).astype(jnp.int32)
    rows = jnp.arange(TOK_DEV, dtype=jnp.int32)
    seq_ids = (lax.optimization_barrier(jnp.sum((rows[None, :, None] >= dealt_start[:, None, :]).astype(jnp.int32), -1)) - 1).astype(jnp.int32)
    source = (jnp.take_along_axis(home_start - dealt_start, seq_ids, 1) + rows[None, :]).astype(jnp.int32)
    return (source, seq_ids)

def retain_head(inputs, seq_ids):
    query, keys, values, log_decay = inputs
    every = jnp.arange(query.shape[0], dtype=jnp.int32)
    distance = every[:, None] - every[None, :]
    valid = (distance >= 0) & (seq_ids[:, None] == seq_ids[None, :])
    decay = jnp.where(valid, jnp.exp(jnp.maximum(distance, 0).astype(jnp.float32) * log_decay), 0.0) * QK_DIM ** (-0.5)
    score = low_back(matmul(query, keys.T))
    weight = low(score * decay)
    return low_back(matmul(weight, values))

def layer(params, inputs, seq_ids):
    query_w, key_w, value_w, swish_w, out_w, gate_w, up_w, down_w, gain_one, gain_two = [low(item) for item in params]
    rows_here = inputs.shape[0]
    normed_in = low(layer_norm(inputs, 1e-05) * gain_one)
    query = low_back(low(matmul(normed_in, query_w)))
    keys = low_back(low(matmul(normed_in, key_w)))
    values = low_back(low(matmul(normed_in, value_w)))
    swish_in = low_back(matmul(normed_in, swish_w))
    head_query = query.reshape(rows_here, HEADS, QK_DIM).transpose(1, 0, 2)
    head_keys = keys.reshape(rows_here, HEADS, QK_DIM).transpose(1, 0, 2)
    head_values = values.reshape(rows_here, HEADS, V_DIM).transpose(1, 0, 2)
    log_decays = jnp.log1p(-jnp.exp2(-5.0 - jnp.arange(HEADS).astype(jnp.float32)))
    retained = lax.map(jax.checkpoint(partial(retain_head, seq_ids=seq_ids)), (head_query, head_keys, head_values, log_decays))
    normed = layer_norm(retained, GROUP_EPS).transpose(1, 0, 2).reshape(rows_here, HEADS * V_DIM)
    mixed_in = low(jax.nn.silu(swish_in) * normed)
    resid = inputs + low_back(matmul(mixed_in, out_w))
    normed_mid = low(layer_norm(resid, 1e-05) * gain_two)
    gate = low_back(matmul(normed_mid, gate_w))
    up_proj = low_back(matmul(normed_mid, up_w))
    hidden = low(jax.nn.gelu(gate) * up_proj)
    return resid + matmul(hidden, down_w)

def reference(tokens, cotangent, lengths, dealing, w_query, w_key, w_value, w_swish, w_out, w_gate, w_up, w_down, gain_attn, gain_mlp):
    sources, seq_rows = deal_rows(lengths, dealing)
    params = (w_query, w_key, w_value, w_swish, w_out, w_gate, w_up, w_down, gain_attn, gain_mlp)
    inputs_all = tokens.astype(jnp.float32)
    upstream_all = cotangent.astype(jnp.float32)

    def group_step(totals, items):
        source, seq_ids = items
        inputs = jnp.take(inputs_all, source, axis=0)
        upstream = jnp.take(upstream_all, source, axis=0)
        outputs, pullback = jax.vjp(partial(layer, seq_ids=seq_ids), params, inputs)
        param_grads, input_grads = pullback(upstream)
        totals = tuple((total + grad for total, grad in zip(totals, param_grads)))
        return (totals, (outputs.astype(jnp.bfloat16), input_grads.astype(jnp.bfloat16)))
    initial = tuple((jnp.zeros(item.shape, jnp.float32) for item in params))
    totals, (outputs, input_grads) = lax.scan(group_step, initial, (sources, seq_rows))
    flat = sources.reshape(-1)
    mixed = jnp.zeros(tokens.shape, jnp.bfloat16).at[flat].set(outputs.reshape(-1, tokens.shape[1]))
    grad_tokens = jnp.zeros(tokens.shape, jnp.bfloat16).at[flat].set(input_grads.reshape(-1, tokens.shape[1]))
    return (mixed, grad_tokens, totals[0], totals[1], totals[2], totals[3], totals[4], totals[5], totals[6], totals[7], totals[8], totals[9])
```

```python
import functools

import jax
import jax.numpy as jnp
from jax import lax
from jax.experimental import pallas as pl
from jax.experimental.pallas import tpu as pltpu
from jax.sharding import PartitionSpec as P

QK_DIM = 256
SEQ_DEV = 3
QBLOCK = 512
PIECE = 32
AXES = ("dp", "heads", "tensor")
TP = ("heads", "tensor")
SWAP_AXES = (0, 0, 0, 0, 1)
MESH = pl.DeviceIdType.MESH


EPSILON = 1e-05
GROUP_EPS = 1.0


def layer_norm(values, epsilon):
    center = values - jnp.mean(values, -1, keepdims=True)
    scale = lax.rsqrt(jnp.mean(center * center, -1, keepdims=True) + epsilon)
    return (center * scale, scale)


def norm_back(grad, normed, scale):
    return scale * (
        grad
        - jnp.mean(grad, -1, keepdims=True)
        - normed * jnp.mean(grad * normed, -1, keepdims=True)
    )


def product(left, right):
    return jnp.dot(left, right, preferred_element_type=jnp.float32)


def inner_rows(left, right):
    return lax.dot_general(
        left, right, (((1,), (1,)), ((), ())), preferred_element_type=jnp.float32
    )


def inner_cols(left, right):
    return lax.dot_general(
        left, right, (((0,), (0,)), ((), ())), preferred_element_type=jnp.float32
    )


def lowered(value):
    return value.astype(jnp.bfloat16)


def around(axes):
    return tuple(lax.axis_index(name) for name in axes)


def wide(value):
    return value.astype(jnp.float32)


def within(number, count):
    return (number >= 0) & (number < count)


def greet(others):
    barrier = pltpu.get_barrier_semaphore()
    for other in others:
        pl.semaphore_signal(barrier, inc=1, device_id=other, device_id_type=MESH)
    pl.semaphore_wait(barrier, len(others))


def plane_peers(at, sizes):
    group, level, core = at
    return [(lax.rem(group + k, sizes[0]), level, core) for k in range(1, sizes[0])]


def column_peers(at, sizes):
    group, level, core = at
    return [(group, lax.rem(level + k, sizes[1]), core) for k in range(1, sizes[1])] + [
        (group, level, 1 - core)
    ]


class Spread:
    def __init__(self, at, sizes, items, sems):
        self.at, self.count, self.items = at, sizes[0], items
        self.local, self.sent, self.got = sems

    @staticmethod
    def scratch(items, sizes):
        return [
            pltpu.SemaphoreType.DMA((items,)),
            pltpu.SemaphoreType.DMA((items, sizes[0] - 1)),
            pltpu.SemaphoreType.DMA((items, sizes[0] - 1)),
        ]

    def place(self, number, owner):
        source, target, axis = self.items[number]
        size = source.shape[axis]
        span = pl.ds(pl.multiple_of(owner * size, size), size)
        return target.at[span] if axis == 0 else target.at[:, span]

    def own(self, number):
        return pltpu.make_async_copy(
            self.items[number][0], self.place(number, self.at[0]), self.local.at[number]
        )

    def away(self, number, k):
        return pltpu.make_async_remote_copy(
            src_ref=self.items[number][0],
            dst_ref=self.place(number, self.at[0]),
            send_sem=self.sent.at[number, k - 1],
            recv_sem=self.got.at[number, k - 1],
            device_id=(lax.rem(self.at[0] + k, self.count),) + self.at[1:],
            device_id_type=MESH,
        )

    def landed(self, number, k):
        owner = lax.rem(self.at[0] + self.count - k, self.count)
        return pltpu.make_async_remote_copy(
            src_ref=self.items[number][0],
            dst_ref=self.place(number, owner),
            send_sem=self.sent.at[number, k - 1],
            recv_sem=self.got.at[number, k - 1],
            device_id=(owner,) + self.at[1:],
            device_id_type=MESH,
        )

    def start(self, number):
        self.own(number).start()
        for k in range(1, self.count):
            self.away(number, k).start()

    def wait(self, number):
        self.own(number).wait()
        for k in range(1, self.count):
            self.landed(number, k).wait_recv()

    def drain(self, number):
        for k in range(1, self.count):
            self.away(number, k).wait_send()


class Gather:
    def __init__(self, at, sizes, count, full, sems):
        self.at, self.levels, self.count, self.full = at, sizes[1], count, full
        self.sent_up, self.got_up, self.sent_down, self.got_down, self.sent_core, self.got_core = sems

    @staticmethod
    def scratch(count, sizes, piece):
        levels = sizes[1]
        dma = pltpu.SemaphoreType.DMA
        return [pltpu.VMEM((count, levels, 2) + piece, jnp.bfloat16)] + [
            dma((levels - 1, count)) for _ in range(4)
        ] + [dma((2 * levels - 1, count)) for _ in range(2)]

    def copy(self, ref, sent, got, target):
        return pltpu.make_async_remote_copy(
            src_ref=ref, dst_ref=ref, send_sem=sent, recv_sem=got, device_id=target, device_id_type=MESH
        )

    def up(self, k, hop, origin, sem):
        group, level, core = self.at
        target = (group, lax.rem(level + 1, self.levels), core)
        return self.copy(self.full.at[k, origin, core], self.sent_up.at[sem, k], self.got_up.at[sem, k], target)

    def down(self, k, hop, origin, sem):
        group, level, core = self.at
        target = (group, lax.rem(level + self.levels - 1, self.levels), core)
        return self.copy(
            self.full.at[k, origin, core], self.sent_down.at[sem, k], self.got_down.at[sem, k], target
        )

    def across(self, k, origin, side, sem):
        group, level, core = self.at
        return self.copy(
            self.full.at[k, origin, side], self.sent_core.at[sem, k], self.got_core.at[sem, k], (group, level, 1 - core)
        )

    def start(self, k):
        group, level, core = self.at

        @pl.when(level < self.levels - 1)
        def _():
            self.up(k, 0, level, 0).start()

        @pl.when(level > 0)
        def _():
            self.down(k, 0, level, 0).start()

        self.across(k, level, core, 0).start()

    def hop(self, k, hop):
        group, level, core = self.at
        last = self.levels - 1

        @pl.when(level >= hop)
        def _():
            origin = level - hop
            self.up(k, hop, origin, hop - 1).wait_recv()
            if hop < last:

                @pl.when(level < last)
                def _():
                    self.up(k, hop, origin, hop).start()

            self.across(k, origin, core, hop).start()

        @pl.when(level + hop <= last)
        def _():
            origin = level + hop
            self.down(k, hop, origin, hop - 1).wait_recv()
            if hop < last:

                @pl.when(level > 0)
                def _():
                    self.down(k, hop, origin, hop).start()

            self.across(k, origin, core, last + hop).start()

    def ready(self, k):
        group, level, core = self.at
        last = self.levels - 1
        self.across(k, level, 1 - core, 0).wait_recv()
        for hop in range(1, self.levels):

            @pl.when(level >= hop)
            def _():
                self.across(k, level - hop, 1 - core, hop).wait_recv()

            @pl.when(level + hop <= last)
            def _():
                self.across(k, level + hop, 1 - core, last + hop).wait_recv()

    def drain(self):
        group, level, core = self.at
        last = self.levels - 1

        def one(k, _):
            self.across(k, level, core, 0).wait_send()
            for hop in range(self.levels):
                if hop < last:

                    @pl.when((level >= hop) & (level < last))
                    def _():
                        self.up(k, hop, level - hop, hop).wait_send()

                    @pl.when((level + hop <= last) & (level > 0))
                    def _():
                        self.down(k, hop, level + hop, hop).wait_send()

                if hop > 0:

                    @pl.when(level >= hop)
                    def _():
                        self.across(k, level - hop, core, hop).wait_send()

                    @pl.when(level + hop <= last)
                    def _():
                        self.across(k, level + hop, core, last + hop).wait_send()

            return 0

        lax.fori_loop(0, self.count, one, 0)


class Scatter:
    def __init__(self, at, sizes, count, part, cross, from_below, from_above, total, sems):
        self.at, self.levels, self.count = at, sizes[1], count
        self.part, self.cross, self.from_below, self.from_above, self.total = (
            part,
            cross,
            from_below,
            from_above,
            total,
        )
        self.sent_core, self.got_core, self.sent_up, self.got_up, self.sent_down, self.got_down = sems

    @staticmethod
    def scratch(count, sizes, piece):
        levels = sizes[1]
        dma = pltpu.SemaphoreType.DMA
        return (
            [pltpu.VMEM((count, levels, 2) + piece, jnp.bfloat16)]
            + [pltpu.VMEM((count, levels) + piece, jnp.bfloat16) for _ in range(3)]
            + [pltpu.VMEM(piece, jnp.float32)]
            + [dma((count,)) for _ in range(2)]
            + [dma((levels, count)) for _ in range(4)]
        )

    def across(self, k):
        group, level, core = self.at
        return pltpu.make_async_remote_copy(
            src_ref=self.part.at[k, :, 1 - core],
            dst_ref=self.cross.at[k],
            send_sem=self.sent_core.at[k],
            recv_sem=self.got_core.at[k],
            device_id=(group, level, 1 - core),
            device_id_type=MESH,
        )

    def up(self, k, owner):
        group, level, core = self.at
        return pltpu.make_async_remote_copy(
            src_ref=self.cross.at[k, owner],
            dst_ref=self.from_below.at[k, owner],
            send_sem=self.sent_up.at[owner, k],
            recv_sem=self.got_up.at[owner, k],
            device_id=(group, lax.rem(level + 1, self.levels), core),
            device_id_type=MESH,
        )

    def down(self, k, owner):
        group, level, core = self.at
        return pltpu.make_async_remote_copy(
            src_ref=self.cross.at[k, owner],
            dst_ref=self.from_above.at[k, owner],
            send_sem=self.sent_down.at[owner, k],
            recv_sem=self.got_down.at[owner, k],
            device_id=(group, lax.rem(level + self.levels - 1, self.levels), core),
            device_id_type=MESH,
        )

    def start(self, k):
        self.across(k).start()

    def join(self, k):
        core = self.at[2]
        self.across(k).wait_recv()
        for owner in range(self.levels):
            self.cross[k, owner] = lowered(wide(self.part[k, owner, core]) + wide(self.cross[k, owner]))

    def step_up(self, k):
        level = self.at[1]
        for owner in range(self.levels - 1, 0, -1):

            @pl.when(level < owner)
            def _():
                @pl.when(level > 0)
                def _():
                    self.up(k, owner).wait_recv()
                    self.cross[k, owner] = lowered(wide(self.cross[k, owner]) + wide(self.from_below[k, owner]))

                self.up(k, owner).start()

    def step_down(self, k):
        level = self.at[1]
        for owner in range(self.levels - 1):

            @pl.when(level > owner)
            def _():
                @pl.when(level < self.levels - 1)
                def _():
                    self.down(k, owner).wait_recv()
                    self.cross[k, owner] = lowered(wide(self.cross[k, owner]) + wide(self.from_above[k, owner]))

                self.down(k, owner).start()

    def steps(self, wave):
        level = self.at[1]
        above = wave - level
        below = wave - (self.levels - 1 - level)

        @pl.when(within(above, self.count))
        def _():
            self.step_up(above)

        @pl.when(within(below, self.count))
        def _():
            self.step_down(below)

    def finish(self, k):
        level = self.at[1]
        self.total[...] = wide(self.cross[k, level])

        @pl.when(level > 0)
        def _():
            self.up(k, level).wait_recv()
            self.total[...] += wide(self.from_below[k, level])

        @pl.when(level < self.levels - 1)
        def _():
            self.down(k, level).wait_recv()
            self.total[...] += wide(self.from_above[k, level])

    def drain(self):
        level = self.at[1]

        def one(k, _):
            self.across(k).wait_send()
            for owner in range(self.levels):

                @pl.when(level < owner)
                def _():
                    self.up(k, owner).wait_send()

                @pl.when(level > owner)
                def _():
                    self.down(k, owner).wait_send()

            return 0

        lax.fori_loop(0, self.count, one, 0)


def in_order(count, step):
    def body(number, carry):
        step(number)
        return carry

    lax.fori_loop(0, count, body, 0)


def span(number, size):
    return pl.ds(pl.multiple_of(number * size, size), size)


class Swap:
    def __init__(self, at, sizes, items, sems):
        self.at, self.count, self.items = at, sizes[0], items
        self.local, self.sent, self.got = sems

    scratch = Spread.scratch

    def block(self, number, owner):
        source, target, axis = self.items[number]
        size = source.shape[axis] // self.count
        window = pl.ds(pl.multiple_of(owner * size, size), size)
        return source.at[window] if axis == 0 else source.at[:, window]

    def own(self, number):
        return pltpu.make_async_copy(
            self.block(number, self.at[0]), self.items[number][1].at[0], self.local.at[number]
        )

    def away(self, number, k):
        peer = lax.rem(self.at[0] + k, self.count)
        return pltpu.make_async_remote_copy(
            src_ref=self.block(number, peer),
            dst_ref=self.items[number][1].at[k],
            send_sem=self.sent.at[number, k - 1],
            recv_sem=self.got.at[number, k - 1],
            device_id=(peer,) + self.at[1:],
            device_id_type=MESH,
        )

    def start(self, number):
        self.own(number).start()
        for k in range(1, self.count):
            self.away(number, k).start()

    def wait(self, number):
        self.own(number).wait()
        for k in range(1, self.count):
            self.away(number, k).wait()


def matmul(left, right):
    return jnp.dot(left, right, preferred_element_type=jnp.float32)


def open_kernel(sizes, shards, gain, *refs):
    x_part, gain, *refs = (shards, gain) + refs
    sources, refs = refs[:5], refs[5:]
    normed_out, query_out, key_out, value_out, swish_out, *refs = refs
    weight_outs, refs = refs[:5], refs[5:]
    rows_out, unit_out, scale_out, *refs = refs
    full, *refs = refs
    gather_sems, refs = refs[:6], refs[6:]
    spread_sems, refs = refs[:3], refs[3:]
    weights, refs = refs[:4], refs[4:]
    normed, query, keys, values, swish, load_sem, out_sem, weight_sem, normed_sem = refs
    at = around(AXES)
    group, level, core = at
    place = 2 * level + core
    count, levels, _, chunk, width = full.shape
    ranks = 2 * levels
    load = pltpu.make_async_copy(x_part, full.at[:, level, core], load_sem)
    load.start()
    greet(plane_peers(at, sizes) + column_peers(at, sizes))
    items = [(s, t, 0) for s, t in zip(sources[:4], weights)] + [(sources[4], weight_outs[4], 1)]
    spread = Spread(at, sizes, items, spread_sems)
    gather = Gather(at, sizes, count, full, gather_sems)
    load.wait()
    gather.start(0)
    for number in range(5):
        spread.start(number)
    piece = chunk // ranks

    def norm(k):
        def block(number, carry):
            rows = span(number, 16)
            value = jnp.concatenate(
                [wide(full[k, q, c, rows, :]) for q in range(levels) for c in range(2)], axis=1
            )
            unit, scale = layer_norm(value, EPSILON)
            where = pl.ds(pl.multiple_of(k * chunk + number * 16, 16), 16)
            normed[where, :] = lowered(unit * gain[...])
            mine = wide(full[k, level, core, rows, :])
            mean = jnp.mean(value, -1, keepdims=True)
            unit_out[where, :] = (mine - mean) * scale
            scale_out[where, :] = jnp.broadcast_to(scale, (16, 128))
            return carry

        lax.fori_loop(0, chunk // 16, block, 0)
        mine = span(place, piece)
        rows_out[span(k, piece), :] = jnp.concatenate(
            [full[k, q, c, mine, :] for q in range(levels) for c in range(2)], axis=1
        )
        pltpu.make_async_copy(
            normed.at[span(k, chunk)], normed_out.at[span(k, chunk)], normed_sem.at[k]
        ).start()

    def wave(number):
        @pl.when(number + 1 < count)
        def _():
            gather.start(number + 1)

        for hop in range(1, levels):

            @pl.when(within(number - hop, count))
            def _():
                gather.hop(number - hop, hop)

        @pl.when(within(number - levels, count))
        def _():
            gather.ready(number - levels)
            norm(number - levels)

    in_order(count + levels, wave)
    outs = [(query, query_out), (keys, key_out), (values, value_out), (swish, swish_out)]
    for number, (held, out) in enumerate(outs):
        spread.wait(number)
        pltpu.make_async_copy(weights[number], weight_outs[number], weight_sem.at[number]).start()

        def rows(k):
            where = span(k, chunk)
            held[where, :] = matmul(normed[where, :], weights[number][...]).astype(held.dtype)

        in_order(count, rows)
        pltpu.make_async_copy(held, out, out_sem.at[number]).start()
    spread.wait(4)
    for number, (held, out) in enumerate(outs):
        pltpu.make_async_copy(held, out, out_sem.at[number]).wait()
        pltpu.make_async_copy(weights[number], weight_outs[number], weight_sem.at[number]).wait()
    for number in range(5):
        spread.drain(number)
    gather.drain()

    def stored(k):
        pltpu.make_async_copy(
            normed.at[span(k, chunk)], normed_out.at[span(k, chunk)], normed_sem.at[k]
        ).wait()

    in_order(count, stored)


def middle_kernel(sizes, mixed_in, out_w, x_rows, gain, gate_src, up_src, down_src, dy_src, *refs):
    normed_out, gate_out, up_out, hidden_out, resid_out, gate_w_out, up_w_out, down_w_out, dy_out, *refs = refs
    scatter_refs, refs = refs[:11], refs[11:]
    full, *refs = refs
    gather_sems, refs = refs[:6], refs[6:]
    spread_sems, refs = refs[:3], refs[3:]
    gate_w, up_w, gate, up, store_sem, weight_sem = refs
    at = around(AXES)
    group, level, core = at
    count, levels, _, piece, width = full.shape
    chunk = 2 * levels * piece
    greet(plane_peers(at, sizes) + column_peers(at, sizes))
    spread = Spread(
        at,
        sizes,
        [(gate_src, gate_w, 0), (up_src, up_w, 0), (down_src, down_w_out, 1), (dy_src, dy_out, 0)],
        spread_sems,
    )
    for number in range(4):
        spread.start(number)
    part = scatter_refs[0]
    scatter = Scatter(at, sizes, count, *scatter_refs[:5], scatter_refs[5:])
    gather = Gather(at, sizes, count, full, gather_sems)
    tile = 512

    def stores(k):
        where = span(k, chunk)
        copies = [
            pltpu.make_async_copy(held.at[where], out.at[where], store_sem.at[number, k])
            for number, (held, out) in enumerate(((gate, gate_out), (up, up_out)))
        ]
        for q in range(levels):
            for c in range(2):
                rows = pl.ds(pl.multiple_of(k * chunk + (2 * q + c) * piece, piece), piece)
                copies.append(
                    pltpu.make_async_copy(full.at[k, q, c], normed_out.at[rows], store_sem.at[2 + 2 * q + c, k])
                )
        return copies

    def first(k):
        rows = mixed_in[span(k, chunk), :]
        for column in range(0, width, tile):
            value = matmul(rows, out_w[:, column : column + tile])
            part[k, :, :, :, column : column + tile] = lowered(value).reshape(levels, 2, piece, tile)
        scatter.start(k)

    def norm(k):
        scatter.finish(k)
        rows = span(k, piece)

        def block(number, carry):
            sub = span(number, 16)
            where = pl.ds(pl.multiple_of(k * piece + number * 16, 16), 16)
            resid = wide(x_rows[where, :]) + scatter.total[sub, :]
            resid_out[where, :] = resid
            unit, _ = layer_norm(resid, EPSILON)
            full[k, level, core, sub, :] = lowered(unit * gain[...])
            return carry

        lax.fori_loop(0, piece // 16, block, 0)
        gather.start(k)

    def last(k):
        gather.ready(k)
        rows = full[k].reshape(chunk, width)
        where = span(k, chunk)
        gate[where, :] = matmul(rows, gate_w[...])
        up[where, :] = matmul(rows, up_w[...])
        for copy in stores(k):
            copy.start()
        hidden_out[where, :] = lowered(jax.nn.gelu(gate[where, :]) * up[where, :])

    lag = levels - 1

    def wave(number):
        @pl.when(number < count)
        def _():
            first(number)

        for hop in range(1, levels):

            @pl.when(within(number - lag - hop, count))
            def _():
                gather.hop(number - lag - hop, hop)

        @pl.when(number == 2 * lag + 1)
        def _():
            spread.wait(0)
            spread.wait(1)
            pltpu.make_async_copy(gate_w, gate_w_out, weight_sem.at[0]).start()
            pltpu.make_async_copy(up_w, up_w_out, weight_sem.at[1]).start()

        @pl.when(within(number - 2 * lag - 1, count))
        def _():
            last(number - 2 * lag - 1)

        @pl.when(number < count)
        def _():
            scatter.join(number)

        scatter.steps(number)

        @pl.when(within(number - lag, count))
        def _():
            norm(number - lag)

    in_order(count + 2 * lag + 1, wave)
    spread.wait(2)
    spread.wait(3)
    pltpu.make_async_copy(gate_w, gate_w_out, weight_sem.at[0]).wait()
    pltpu.make_async_copy(up_w, up_w_out, weight_sem.at[1]).wait()
    for number in range(4):
        spread.drain(number)
    scatter.drain()
    gather.drain()

    def stored(k):
        for copy in stores(k):
            copy.wait()

    in_order(count, stored)


def feed_kernel(sizes, dy_part, hidden, gate, up, down_w, resid, *refs):
    mixed_out, dy_out, gate_grad, up_grad, dy_rows, *refs = refs
    scatter_refs, refs = refs[:11], refs[11:]
    full, *refs = refs
    gather_sems, refs = refs[:6], refs[6:]
    tile_acc, load_sem, store_sem = refs
    at = around(AXES)
    group, level, core = at
    place = 2 * level + core
    count, levels, _, chunk, width = full.shape
    ranks = 2 * levels
    piece = chunk // ranks
    load = pltpu.make_async_copy(dy_part, full.at[:, level, core], load_sem)
    load.start()
    greet(column_peers(at, sizes))
    part = scatter_refs[0]
    scatter = Scatter(at, sizes, count, *scatter_refs[:5], scatter_refs[5:])
    gather = Gather(at, sizes, count, full, gather_sems)
    load.wait()
    gather.start(0)

    def stores(k):
        return [
            pltpu.make_async_copy(
                full.at[k, q, c],
                dy_out.at[span(k, chunk), (2 * q + c) * width : (2 * q + c + 1) * width],
                store_sem.at[2 * q + c, k],
            )
            for q in range(levels)
            for c in range(2)
        ]

    def first(k):
        rows = hidden[span(k, chunk), :]
        mine = span(place, piece)
        for rank in range(ranks):
            columns = slice(rank * width, (rank + 1) * width)
            tile_acc[...] = matmul(rows, down_w[:, columns])
            tile_acc[mine, :] += resid[span(k, piece), columns]
            part[k, rank // 2, rank % 2] = lowered(tile_acc[...])
        scatter.start(k)

    def last(k):
        gather.ready(k)
        for copy in stores(k):
            copy.start()
        where = span(k, chunk)
        rows = jnp.concatenate([full[k, q, c] for q in range(levels) for c in range(2)], axis=1)
        back = inner_rows(rows, down_w[...])
        mine = span(place, piece)
        dy_rows[span(k, piece), :] = jnp.concatenate(
            [full[k, q, c, mine, :] for q in range(levels) for c in range(2)], axis=1
        )
        g, u = gate[where, :], up[where, :]
        root = 0.7978845608028654
        bend = jnp.tanh(root * (g + 0.044715 * g * g * g))
        curve = 0.5 * (1.0 + bend)
        slope = curve + 0.5 * g * (1.0 - bend * bend) * root * (1.0 + 0.134145 * g * g)
        gate_grad[where, :] = lowered(back * u * slope)
        up_grad[where, :] = lowered(back * g * curve)

    lag = levels - 1

    def wave(number):
        @pl.when(number + 1 < count)
        def _():
            gather.start(number + 1)

        @pl.when(number < count)
        def _():
            first(number)

        for hop in range(1, levels):

            @pl.when(within(number - hop, count))
            def _():
                gather.hop(number - hop, hop)

        @pl.when(number < count)
        def _():
            scatter.join(number)

        scatter.steps(number)

        @pl.when(within(number - lag, count))
        def _():
            scatter.finish(number - lag)
            mixed_out[span(number - lag, chunk), :] = lowered(scatter.total[...])

        @pl.when(within(number - levels, count))
        def _():
            last(number - levels)

    in_order(count + levels, wave)
    scatter.drain()
    gather.drain()

    def stored(k):
        for copy in stores(k):
            copy.wait()

    in_order(count, stored)


def back_kernel(sizes, gate_grad, up_grad, gate_w, up_w, resid, dy_rows, gain, out_w, retained, swish, *refs):
    sources, refs = refs[:4], refs[4:]
    branch_out, swish_grad, retained_grad, gain_out, *refs = refs
    targets, refs = refs[:4], refs[4:]
    scatter_refs, refs = refs[:11], refs[11:]
    full, *refs = refs
    gather_sems, refs = refs[:6], refs[6:]
    spread_sems, refs = refs[:3], refs[3:]
    swap_sems, refs = refs[:3], refs[3:]
    (store_sem,) = refs
    at = around(AXES)
    group, level, core = at
    count, levels, _, piece, width = full.shape
    chunk = 2 * levels * piece
    greet(plane_peers(at, sizes) + column_peers(at, sizes))
    spread = Spread(at, sizes, [(sources[0], targets[0], 0)], spread_sems)
    swap = Swap(at, sizes, list(zip(sources[1:], targets[1:], (1, 0, 0))), swap_sems)
    spread.start(0)
    for number in range(3):
        swap.start(number)
    part = scatter_refs[0]
    scatter = Scatter(at, sizes, count, *scatter_refs[:5], scatter_refs[5:])
    gather = Gather(at, sizes, count, full, gather_sems)
    gain_out[...] = jnp.zeros(gain_out.shape, jnp.float32)
    tile = 512

    def stores(k):
        copies = []
        for q in range(levels):
            for c in range(2):
                rows = pl.ds(pl.multiple_of(k * chunk + (2 * q + c) * piece, piece), piece)
                copies.append(
                    pltpu.make_async_copy(full.at[k, q, c], branch_out.at[rows], store_sem.at[2 * q + c, k])
                )
        return copies

    def first(k):
        where = span(k, chunk)
        for column in range(0, width, tile):
            columns = slice(column, column + tile)
            value = inner_rows(gate_grad[where, :], gate_w[columns, :])
            value += inner_rows(up_grad[where, :], up_w[columns, :])
            part[k, :, :, :, columns] = lowered(value).reshape(levels, 2, piece, tile)
        scatter.start(k)

    def norm(k):
        scatter.finish(k)

        def block(number, carry):
            sub = span(number, 16)
            where = pl.ds(pl.multiple_of(k * piece + number * 16, 16), 16)
            unit, scale = layer_norm(resid[where, :], EPSILON)
            delta = scatter.total[sub, :]
            outer = delta * unit
            gain_out[...] += outer[:8] + outer[8:]
            value = wide(dy_rows[where, :]) + norm_back(delta * gain[...], unit, scale)
            full[k, level, core, sub, :] = lowered(value)
            return carry

        lax.fori_loop(0, piece // 16, block, 0)
        gather.start(k)

    def last(k):
        gather.ready(k)
        for copy in stores(k):
            copy.start()
        rows = full[k].reshape(chunk, width)
        where = span(k, chunk)
        delta = inner_rows(rows, out_w[...])
        normed, scale = layer_norm(retained[where, :], GROUP_EPS)
        value = swish[where, :]
        gated = jax.nn.sigmoid(value)
        swish_grad[where, :] = lowered(delta * normed * gated * (1.0 + value * (1.0 - gated)))
        retained_grad[where, :] = lowered(norm_back(delta * value * gated, normed, scale))

    lag = levels - 1

    def wave(number):
        @pl.when(number < count)
        def _():
            first(number)

        for hop in range(1, levels):

            @pl.when(within(number - lag - hop, count))
            def _():
                gather.hop(number - lag - hop, hop)

        @pl.when(within(number - 2 * lag - 1, count))
        def _():
            last(number - 2 * lag - 1)

        @pl.when(number < count)
        def _():
            scatter.join(number)

        scatter.steps(number)

        @pl.when(within(number - lag, count))
        def _():
            norm(number - lag)

    in_order(count + 2 * lag + 1, wave)
    spread.wait(0)
    for number in range(3):
        swap.wait(number)
    spread.drain(0)
    scatter.drain()
    gather.drain()

    def stored(k):
        for copy in stores(k):
            copy.wait()

    in_order(count, stored)


def close_kernel(sizes, gain, normed_in, *refs):
    deltas, refs = refs[:4], refs[4:]
    weights, refs = refs[:4], refs[4:]
    number_of = len(SWAP_AXES)
    sources, refs = refs[:number_of], refs[number_of:]
    delta_out, sums_out, *refs = refs
    targets, refs = refs[:number_of], refs[number_of:]
    scatter_refs, refs = refs[:11], refs[11:]
    swap_sems, refs = refs[:3], refs[3:]
    sums, sums_sent, sums_got = refs
    at = around(AXES)
    group, level, core = at
    place = 2 * level + core
    part = scatter_refs[0]
    count, levels, _, chunk, width = part.shape
    ranks = 2 * levels
    greet(plane_peers(at, sizes) + column_all(at, sizes))
    swap = Swap(at, sizes, [(s, t, a) for s, t, a in zip(sources, targets, SWAP_AXES)], swap_sems)
    for number in range(number_of):
        swap.start(number)
    scatter = Scatter(at, sizes, count, *scatter_refs[:5], scatter_refs[5:])

    def first(k):
        where = span(k, chunk)
        rows = [d[where, :] for d in deltas]
        one = jnp.zeros((chunk, width), jnp.float32)
        two = jnp.zeros((chunk, width), jnp.float32)
        for rank in range(ranks):
            columns = slice(rank * width, (rank + 1) * width)
            value = inner_rows(rows[0], weights[0][columns, :])
            for row, weight in zip(rows[1:], weights[1:]):
                value += inner_rows(row, weight[columns, :])
            part[k, rank // 2, rank % 2] = lowered(value)
            one += value * gain[:, columns]
            two += value * wide(normed_in[where, columns])
        scatter.start(k)
        ones = jnp.ones((8, width), jnp.float32)
        flat = [
            lax.dot_general(
                ones,
                item,
                (((1,), (1,)), ((), ())),
                precision=lax.Precision.HIGHEST,
                preferred_element_type=jnp.float32,
            )
            for item in (one, two)
        ]
        line = lax.broadcasted_iota(jnp.int32, (8, chunk), 0)
        sums[place, k] = jnp.where(line == 0, flat[0], flat[1])

    def sums_copy(k):
        peer = lax.rem(place + k, ranks)
        return pltpu.make_async_remote_copy(
            src_ref=sums.at[place],
            dst_ref=sums.at[place],
            send_sem=sums_sent.at[k - 1],
            recv_sem=sums_got.at[k - 1],
            device_id=(group, peer // 2, lax.rem(peer, 2)),
            device_id_type=MESH,
        )

    def sums_landed(k):
        peer = lax.rem(place + ranks - k, ranks)
        return pltpu.make_async_remote_copy(
            src_ref=sums.at[peer],
            dst_ref=sums.at[peer],
            send_sem=sums_sent.at[k - 1],
            recv_sem=sums_got.at[k - 1],
            device_id=(group, peer // 2, lax.rem(peer, 2)),
            device_id_type=MESH,
        )

    lag = levels - 1

    def wave(number):
        @pl.when(number < count)
        def _():
            first(number)
            scatter.join(number)

        scatter.steps(number)

        @pl.when(number == count - 1)
        def _():
            for k in range(1, ranks):
                sums_copy(k).start()

        @pl.when(within(number - lag, count))
        def _():
            scatter.finish(number - lag)
            delta_out[span(number - lag, chunk), :] = scatter.total[...]

    in_order(count + lag, wave)
    for k in range(1, ranks):
        sums_landed(k).wait_recv()
    sums_out[...] = jnp.sum(sums[...], 0)
    for k in range(1, ranks):
        sums_copy(k).wait_send()
    for number in range(number_of):
        swap.wait(number)
    scatter.drain()


def spread_kernel(sizes, number_of, axes, *refs):
    sources, refs = refs[:number_of], refs[number_of:]
    targets, sems = refs[:number_of], refs[number_of:]
    at = around(AXES)
    greet(plane_peers(at, sizes))
    spread = Spread(at, sizes, list(zip(sources, targets, axes)), sems)
    for number in range(number_of):
        spread.start(number)
    for number in range(number_of):
        spread.wait(number)
    for number in range(number_of):
        spread.drain(number)


def column_all(at, sizes):
    group, level, core = at
    return column_peers(at, sizes) + [
        (group, lax.rem(level + k, sizes[1]), 1 - core) for k in range(1, sizes[1])
    ]


def struct(shape, kind=jnp.bfloat16):
    return jax.ShapeDtypeStruct(shape, kind)


VMEM = pltpu.VMEM
DMA = pltpu.SemaphoreType.DMA


def kernel_call(body, number, ins, outs, scratch):
    places = {True: pl.BlockSpec(memory_space=pltpu.VMEM), False: pl.BlockSpec(memory_space=pl.ANY)}
    return pl.pallas_call(
        body,
        out_shape=[shape for _, shape in outs],
        in_specs=[places[inside] for inside, _ in ins],
        out_specs=[places[inside] for inside, _ in outs],
        scratch_shapes=scratch,
        compiler_params=pltpu.CompilerParams(
            collective_id=number, has_side_effects=True, vmem_limit_bytes=60 * 2**20
        ),
    )(*[array for _, array in ins])


def spread_shape(shard, axis, sizes):
    shape = list(shard.shape)
    shape[axis] *= sizes[0]
    return struct(tuple(shape), shard.dtype)


def swap_shape(whole, axis, sizes):
    shape = list(whole.shape)
    shape[axis] //= sizes[0]
    return struct((sizes[0],) + tuple(shape), whole.dtype)


def spread_call(number, shards, axes, sizes):
    count = len(shards)
    return kernel_call(
        functools.partial(spread_kernel, sizes, count, axes),
        number,
        [(False, s) for s in shards],
        [(False, spread_shape(s, a, sizes)) for s, a in zip(shards, axes)],
        Spread.scratch(count, sizes),
    )


def pick_rows(targets, carry, pieces):
    count = pieces[0].shape[0]
    inside = ((targets >= 0) & (targets < count))[:, None]
    position = jnp.clip(targets, 0, count - 1)
    return tuple(
        (
            jnp.where(inside, jnp.take(piece, position, axis=0), held)
            for piece, held in zip(pieces, carry)
        )
    )


def decay_block(start, seq_ids, log_decay, block, factor):
    every = jnp.arange(seq_ids.shape[0], dtype=jnp.int32)
    near = start + jnp.arange(block, dtype=jnp.int32)
    distance = near[:, None] - every[None, :]
    own = lax.dynamic_slice_in_dim(seq_ids, start, block)
    valid = (distance >= 0) & (own[:, None] == seq_ids[None, :])
    return (
        jnp.where(valid, jnp.exp(jnp.maximum(distance, 0).astype(jnp.float32) * log_decay), 0.0)
        * factor
    )


def shards(
    tokens,
    cotangent,
    lengths,
    dealing,
    w_query,
    w_key,
    w_value,
    w_swish,
    w_out,
    w_gate,
    w_up,
    w_down,
    gain_attn,
    gain_mlp,
):
    group = lax.axis_index("dp")
    place = lax.axis_index(("heads", "tensor"))
    rows_dev = tokens.shape[0]
    slice_width = tokens.shape[1]
    seq_count = lengths.shape[0]
    ident = jnp.arange(seq_count, dtype=jnp.int32)
    starts = jnp.cumsum(lengths) - lengths
    picked = lax.dynamic_slice_in_dim(dealing, group * SEQ_DEV, SEQ_DEV)
    match = picked[:, None] == ident[None, :]
    dealt_len = jnp.sum(jnp.where(match, lengths[None, :], 0), 1)
    home_start = jnp.sum(jnp.where(match, starts[None, :], 0), 1)
    dealt_start = jnp.cumsum(dealt_len) - dealt_len
    rows = jnp.arange(rows_dev, dtype=jnp.int32)
    seq_ids = jnp.sum((rows[:, None] >= dealt_start[None, :]).astype(jnp.int32), 1) - 1
    member = seq_ids[:, None] == jnp.arange(SEQ_DEV, dtype=jnp.int32)[None, :]
    source = jnp.sum(jnp.where(member, (home_start - dealt_start)[None, :], 0), 1) + rows
    sizes = (lax.axis_size("dp"), lax.axis_size("heads"))
    ranks = sizes[1] * lax.axis_size("tensor")
    chunk = ranks * PIECE
    chunks = rows_dev // chunk
    width = slice_width * ranks
    query_s, key_s, value_s, swish_s, out_s, gate_s, up_s, down_s = (
        lowered(w) for w in (w_query, w_key, w_value, w_swish, w_out, w_gate, w_up, w_down)
    )
    gain_rows = jnp.pad(jnp.stack([gain_attn, gain_mlp]), ((0, 6), (0, 0)))
    x_all, gains_all = spread_call(0, (tokens, gain_rows), (0, 0), sizes)
    gains_all = wide(lowered(gains_all.reshape(sizes[0], 8, -1)))
    wide_one = gains_all[:, 0].reshape(1, width)
    wide_two = gains_all[:, 1].reshape(1, width)
    empty = jnp.zeros(tokens.shape, jnp.bfloat16)
    (x_part,) = pick_rows(source, (empty,), (x_all,))
    qk_dim, v_dim = w_query.shape[1], w_value.shape[1]
    own = rows_dev // ranks
    first_shards = (query_s, key_s, value_s, swish_s, out_s)
    first_axes = (0, 0, 0, 0, 1)
    full_shapes = [spread_shape(s, a, sizes) for s, a in zip(first_shards, first_axes)]
    (
        normed_in,
        query,
        keys,
        values,
        swish_in,
        query_w,
        key_w,
        value_w,
        swish_w,
        out_w,
        x_rows,
        unit_share,
        scale_one,
    ) = kernel_call(
        functools.partial(open_kernel, sizes),
        1,
        [(False, x_part.reshape(chunks, chunk, slice_width)), (True, wide_one)]
        + [(False, s) for s in first_shards],
        [
            (False, struct((rows_dev, width))),
            (False, struct((rows_dev, qk_dim))),
            (False, struct((rows_dev, qk_dim))),
            (False, struct((rows_dev, v_dim))),
            (False, struct((rows_dev, v_dim), jnp.float32)),
        ]
        + [(False, s) for s in full_shapes]
        + [
            (True, struct((own, width))),
            (True, struct((rows_dev, slice_width), jnp.float32)),
            (True, struct((rows_dev, 128), jnp.float32)),
        ],
        Gather.scratch(chunks, sizes, (chunk, slice_width))
        + Spread.scratch(5, sizes)
        + [VMEM(s.shape, s.dtype) for s in full_shapes[:4]]
        + [
            VMEM((rows_dev, width), jnp.bfloat16),
            VMEM((rows_dev, qk_dim), jnp.bfloat16),
            VMEM((rows_dev, qk_dim), jnp.bfloat16),
            VMEM((rows_dev, v_dim), jnp.bfloat16),
            VMEM((rows_dev, v_dim), jnp.float32),
            DMA,
            DMA((4,)),
            DMA((4,)),
            DMA((chunks,)),
        ],
    )
    log_decay = jnp.log1p(-jnp.exp2(-5.0 - place.astype(jnp.float32)))
    score_factor = QK_DIM ** (-0.5)
    blocks = rows_dev // QBLOCK

    def forward_block(number):
        start = number * QBLOCK
        decay = decay_block(start, seq_ids, log_decay, QBLOCK, score_factor)
        weight = (inner_rows(lax.dynamic_slice_in_dim(query, start, QBLOCK), keys) * decay).astype(
            jnp.bfloat16
        )
        return product(weight, values)

    retained = lax.map(forward_block, jnp.arange(blocks, dtype=jnp.int32)).reshape(
        rows_dev, values.shape[1]
    )
    normed, _ = layer_norm(retained, GROUP_EPS)
    mixed_in = (swish_in * jax.nn.sigmoid(swish_in) * normed).astype(jnp.bfloat16)
    ff_dim = w_gate.shape[1]
    middle_shards = (gate_s, up_s, down_s, cotangent)
    middle_axes = (0, 0, 1, 0)
    middle_shapes = [spread_shape(s, a, sizes) for s, a in zip(middle_shards, middle_axes)]
    normed_mid, gate, up_proj, hidden, resid, gate_w, up_w, down_w, dy_all = kernel_call(
        functools.partial(middle_kernel, sizes),
        2,
        [(True, mixed_in), (True, out_w), (True, x_rows), (True, wide_two)]
        + [(False, s) for s in middle_shards],
        [
            (False, struct((rows_dev, width))),
            (False, struct((rows_dev, ff_dim), jnp.float32)),
            (False, struct((rows_dev, ff_dim), jnp.float32)),
            (True, struct((rows_dev, ff_dim))),
            (True, struct((own, width), jnp.float32)),
        ]
        + [(False, s) for s in middle_shapes],
        Scatter.scratch(chunks, sizes, (PIECE, width))
        + Gather.scratch(chunks, sizes, (PIECE, width))
        + Spread.scratch(4, sizes)
        + [
            VMEM(middle_shapes[0].shape, jnp.bfloat16),
            VMEM(middle_shapes[1].shape, jnp.bfloat16),
            VMEM((rows_dev, ff_dim), jnp.float32),
            VMEM((rows_dev, ff_dim), jnp.float32),
            DMA((2 + ranks, chunks)),
            DMA((2,)),
        ],
    )
    (dy_part,) = pick_rows(source, (empty,), (dy_all,))
    mixed_share, dy_full, delta_gate, delta_up, dy_rows = kernel_call(
        functools.partial(feed_kernel, sizes),
        3,
        [
            (False, dy_part.reshape(chunks, chunk, slice_width)),
            (True, hidden),
            (True, gate),
            (True, up_proj),
            (True, down_w),
            (True, resid),
        ],
        [
            (True, struct((rows_dev, slice_width))),
            (False, struct((rows_dev, width))),
            (True, struct((rows_dev, ff_dim))),
            (True, struct((rows_dev, ff_dim))),
            (True, struct((own, width))),
        ],
        Scatter.scratch(chunks, sizes, (chunk, slice_width))
        + Gather.scratch(chunks, sizes, (chunk, slice_width))
        + [VMEM((chunk, slice_width), jnp.float32), DMA, DMA((ranks, chunks))],
    )
    grad_down = lowered(inner_cols(hidden, dy_full))
    grad_gate = lowered(inner_cols(normed_mid, delta_gate))
    grad_up = lowered(inner_cols(normed_mid, delta_up))
    back_swaps = ((grad_down, 1), (grad_gate, 0), (grad_up, 0))
    delta_branch, delta_swish, delta_retained, gain_two_part, mixed_all, *ff_grads = kernel_call(
        functools.partial(back_kernel, sizes),
        4,
        [
            (True, delta_gate),
            (True, delta_up),
            (True, gate_w),
            (True, up_w),
            (True, resid),
            (True, dy_rows),
            (True, wide_two),
            (True, out_w),
            (True, retained),
            (True, swish_in),
            (False, mixed_share),
        ]
        + [(False, g) for g, _ in back_swaps],
        [
            (False, struct((rows_dev, width))),
            (True, struct((rows_dev, v_dim))),
            (True, struct((rows_dev, v_dim))),
            (True, struct((8, width), jnp.float32)),
            (False, spread_shape(mixed_share, 0, sizes)),
        ]
        + [(False, swap_shape(g, a, sizes)) for g, a in back_swaps],
        Scatter.scratch(chunks, sizes, (PIECE, width))
        + Gather.scratch(chunks, sizes, (PIECE, width))
        + Spread.scratch(1, sizes)
        + Swap.scratch(3, sizes)
        + [DMA((ranks, chunks))],
    )
    grad_out = lowered(inner_cols(mixed_in, delta_branch))

    def backward_block(carry, number):
        delta_keys, delta_values = carry
        start = number * QBLOCK
        decay = decay_block(start, seq_ids, log_decay, QBLOCK, score_factor)
        query_block = lax.dynamic_slice_in_dim(query, start, QBLOCK)
        grad_block = lax.dynamic_slice_in_dim(delta_retained, start, QBLOCK)
        weight = (inner_rows(query_block, keys) * decay).astype(jnp.bfloat16)
        delta_score = (inner_rows(grad_block, values) * decay).astype(jnp.bfloat16)
        delta_keys = delta_keys + inner_cols(delta_score, query_block)
        delta_values = delta_values + inner_cols(weight, grad_block)
        return ((delta_keys, delta_values), product(delta_score, keys))

    start_carry = (jnp.zeros(keys.shape, jnp.float32), jnp.zeros(values.shape, jnp.float32))
    (delta_keys, delta_values), delta_query = lax.scan(
        backward_block, start_carry, jnp.arange(blocks, dtype=jnp.int32)
    )
    delta_query = delta_query.reshape(rows_dev, query.shape[1]).astype(jnp.bfloat16)
    delta_keys = delta_keys.astype(jnp.bfloat16)
    delta_values = delta_values.astype(jnp.bfloat16)
    grad_query = lowered(inner_cols(normed_in, delta_query))
    grad_key = lowered(inner_cols(normed_in, delta_keys))
    grad_value = lowered(inner_cols(normed_in, delta_values))
    grad_swish = lowered(inner_cols(normed_in, delta_swish))
    close_swaps = tuple(zip((grad_query, grad_key, grad_value, grad_swish, grad_out), SWAP_AXES))
    delta_in, sums, *attn_grads = kernel_call(
        functools.partial(close_kernel, sizes),
        5,
        [(True, wide_one), (True, normed_in)]
        + [(True, d) for d in (delta_query, delta_keys, delta_values, delta_swish)]
        + [(True, w) for w in (query_w, key_w, value_w, swish_w)]
        + [(False, g) for g, _ in close_swaps],
        [
            (True, struct((rows_dev, slice_width), jnp.float32)),
            (True, struct((chunks, 8, chunk), jnp.float32)),
        ]
        + [(False, swap_shape(g, a, sizes)) for g, a in close_swaps],
        Scatter.scratch(chunks, sizes, (chunk, slice_width))
        + Swap.scratch(len(SWAP_AXES), sizes)
        + [VMEM((ranks, chunks, 8, chunk), jnp.float32), DMA((ranks - 1,)), DMA((ranks - 1,))],
    )
    col_start = place * slice_width
    mean_one = sums[:, 0].reshape(rows_dev, 1) / width
    mean_two = sums[:, 1].reshape(rows_dev, 1) / width
    gain_share = lax.dynamic_slice_in_dim(wide_one, col_start, slice_width, 1)
    resid_share = wide(lax.dynamic_slice_in_dim(delta_branch, col_start, slice_width, 1))
    grad_share = lowered(
        resid_share + scale_one[:, :1] * (delta_in * gain_share - mean_one - unit_share * mean_two)
    )
    gain_one_part = lax.dynamic_update_slice_in_dim(
        jnp.zeros((width,), jnp.float32), jnp.sum(delta_in * unit_share, 0), col_start, 0
    )
    gains = lax.psum(jnp.stack([gain_one_part, jnp.sum(gain_two_part, 0)]), AXES)
    gain_width = gain_attn.shape[0]
    gains = lax.dynamic_slice_in_dim(gains, group * gain_width, gain_width, 1)
    (grad_all,) = spread_call(6, (grad_share,), (0,), sizes)
    grads = [jnp.sum(wide(g), 0) for g in attn_grads + ff_grads[1:] + ff_grads[:1]]
    slot_match = dealing[:, None] == ident[None, :]
    slot_len = jnp.sum(jnp.where(slot_match, lengths[None, :], 0), 1)
    slot_home = jnp.sum(jnp.where(slot_match, starts[None, :], 0), 1)
    per_group = slot_len.reshape(-1, SEQ_DEV)
    slot_start = (jnp.cumsum(per_group, 1) - per_group).reshape(-1)
    slot_base = ident // SEQ_DEV * rows_dev + slot_start - slot_home
    owner_base = jnp.sum(jnp.where(dealing[None, :] == ident[:, None], slot_base[None, :], 0), 1)
    global_rows = group * rows_dev + rows
    seq_of = jnp.sum((global_rows[:, None] >= starts[None, :]).astype(jnp.int32), 1) - 1
    targets = (
        jnp.sum(jnp.where(seq_of[:, None] == ident[None, :], owner_base[None, :], 0), 1)
        + global_rows
    )
    mixed_rows, grad_rows = pick_rows(targets, (empty, empty), (mixed_all, grad_all))
    return (
        mixed_rows,
        grad_rows,
        grads[0],
        grads[1],
        grads[2],
        grads[3],
        grads[4],
        grads[5],
        grads[6],
        grads[7],
        gains[0],
        gains[1],
    )


def solution(mesh):
    in_specs = (
        P("dp", ("heads", "tensor")),
        P("dp", ("heads", "tensor")),
        P(),
        P(),
        P("dp", ("heads", "tensor")),
        P("dp", ("heads", "tensor")),
        P("dp", ("heads", "tensor")),
        P("dp", ("heads", "tensor")),
        P(("heads", "tensor"), "dp"),
        P("dp", ("heads", "tensor")),
        P("dp", ("heads", "tensor")),
        P(("heads", "tensor"), "dp"),
        P("dp"),
        P("dp"),
    )
    out_specs = (
        P("dp", ("heads", "tensor")),
        P("dp", ("heads", "tensor")),
        P("dp", ("heads", "tensor")),
        P("dp", ("heads", "tensor")),
        P("dp", ("heads", "tensor")),
        P("dp", ("heads", "tensor")),
        P(("heads", "tensor"), "dp"),
        P("dp", ("heads", "tensor")),
        P("dp", ("heads", "tensor")),
        P(("heads", "tensor"), "dp"),
        P("dp"),
        P("dp"),
    )
    return jax.shard_map(shards, mesh=mesh, in_specs=in_specs, out_specs=out_specs, check_vma=False)
```

```python
import functools

import jax
import jax.numpy as jnp
from jax import lax
from jax.experimental import pallas as pl
from jax.experimental.pallas import tpu as pltpu
from jax.sharding import PartitionSpec as P

QK_DIM = 256
SEQ_DEV = 3
PIECE = 32
AXES = ("dp", "heads", "tensor")
SWAP_AXES = (0, 0, 0, 0, 1)
MESH = pl.DeviceIdType.MESH


EPSILON = 1e-05
GROUP_EPS = 1.0


def layer_norm(values, epsilon):
    center = values - jnp.mean(values, -1, keepdims=True)
    scale = lax.rsqrt(jnp.mean(center * center, -1, keepdims=True) + epsilon)
    return (center * scale, scale)


def norm_back(grad, normed, scale):
    return scale * (
        grad
        - jnp.mean(grad, -1, keepdims=True)
        - normed * jnp.mean(grad * normed, -1, keepdims=True)
    )


def product(left, right):
    return jnp.dot(left, right, preferred_element_type=jnp.float32)


def inner_rows(left, right):
    return lax.dot_general(
        left, right, (((1,), (1,)), ((), ())), preferred_element_type=jnp.float32
    )


def inner_cols(left, right):
    return lax.dot_general(
        left, right, (((0,), (0,)), ((), ())), preferred_element_type=jnp.float32
    )


def lowered(value):
    return value.astype(jnp.bfloat16)


def around(axes):
    return tuple(lax.axis_index(name) for name in axes)


def wide(value):
    return value.astype(jnp.float32)


def within(number, count):
    return (number >= 0) & (number < count)


def greet(others):
    barrier = pltpu.get_barrier_semaphore()
    for other in others:
        pl.semaphore_signal(barrier, inc=1, device_id=other, device_id_type=MESH)
    pl.semaphore_wait(barrier, len(others))


def plane_peers(at, sizes):
    group, level, core = at
    return [(lax.rem(group + k, sizes[0]), level, core) for k in range(1, sizes[0])]


def column_peers(at, sizes):
    group, level, core = at
    return [(group, lax.rem(level + k, sizes[1]), core) for k in range(1, sizes[1])] + [
        (group, level, 1 - core)
    ]


class Spread:
    def __init__(self, at, sizes, items, sems):
        self.at, self.count, self.items = at, sizes[0], items
        self.local, self.sent, self.got = sems

    @staticmethod
    def scratch(items, sizes):
        return [
            pltpu.SemaphoreType.DMA((items,)),
            pltpu.SemaphoreType.DMA((items, sizes[0] - 1)),
            pltpu.SemaphoreType.DMA((items, sizes[0] - 1)),
        ]

    def place(self, number, owner):
        source, target, axis = self.items[number]
        size = source.shape[axis]
        span = pl.ds(pl.multiple_of(owner * size, size), size)
        return target.at[span] if axis == 0 else target.at[:, span]

    def own(self, number):
        return pltpu.make_async_copy(
            self.items[number][0], self.place(number, self.at[0]), self.local.at[number]
        )

    def away(self, number, k):
        return pltpu.make_async_remote_copy(
            src_ref=self.items[number][0],
            dst_ref=self.place(number, self.at[0]),
            send_sem=self.sent.at[number, k - 1],
            recv_sem=self.got.at[number, k - 1],
            device_id=(lax.rem(self.at[0] + k, self.count),) + self.at[1:],
            device_id_type=MESH,
        )

    def landed(self, number, k):
        owner = lax.rem(self.at[0] + self.count - k, self.count)
        return pltpu.make_async_remote_copy(
            src_ref=self.items[number][0],
            dst_ref=self.place(number, owner),
            send_sem=self.sent.at[number, k - 1],
            recv_sem=self.got.at[number, k - 1],
            device_id=(owner,) + self.at[1:],
            device_id_type=MESH,
        )

    def start(self, number):
        self.own(number).start()
        for k in range(1, self.count):
            self.away(number, k).start()

    def wait(self, number):
        self.own(number).wait()
        for k in range(1, self.count):
            self.landed(number, k).wait_recv()

    def drain(self, number):
        for k in range(1, self.count):
            self.away(number, k).wait_send()


class Gather:
    def __init__(self, at, sizes, count, full, sems):
        self.at, self.levels, self.count, self.full = at, sizes[1], count, full
        self.sent_up, self.got_up, self.sent_down, self.got_down, self.sent_core, self.got_core = sems

    @staticmethod
    def scratch(count, sizes, piece):
        levels = sizes[1]
        dma = pltpu.SemaphoreType.DMA
        return [pltpu.VMEM((count, levels, 2) + piece, jnp.bfloat16)] + [
            dma((levels - 1, count)) for _ in range(4)
        ] + [dma((2 * levels - 1, count)) for _ in range(2)]

    def copy(self, ref, sent, got, target):
        return pltpu.make_async_remote_copy(
            src_ref=ref, dst_ref=ref, send_sem=sent, recv_sem=got, device_id=target, device_id_type=MESH
        )

    def up(self, k, hop, origin, sem):
        group, level, core = self.at
        target = (group, lax.rem(level + 1, self.levels), core)
        return self.copy(self.full.at[k, origin, core], self.sent_up.at[sem, k], self.got_up.at[sem, k], target)

    def down(self, k, hop, origin, sem):
        group, level, core = self.at
        target = (group, lax.rem(level + self.levels - 1, self.levels), core)
        return self.copy(
            self.full.at[k, origin, core], self.sent_down.at[sem, k], self.got_down.at[sem, k], target
        )

    def across(self, k, origin, side, sem):
        group, level, core = self.at
        return self.copy(
            self.full.at[k, origin, side], self.sent_core.at[sem, k], self.got_core.at[sem, k], (group, level, 1 - core)
        )

    def start(self, k):
        group, level, core = self.at

        @pl.when(level < self.levels - 1)
        def _():
            self.up(k, 0, level, 0).start()

        @pl.when(level > 0)
        def _():
            self.down(k, 0, level, 0).start()

        self.across(k, level, core, 0).start()

    def hop(self, k, hop):
        group, level, core = self.at
        last = self.levels - 1

        @pl.when(level >= hop)
        def _():
            origin = level - hop
            self.up(k, hop, origin, hop - 1).wait_recv()
            if hop < last:

                @pl.when(level < last)
                def _():
                    self.up(k, hop, origin, hop).start()

            self.across(k, origin, core, hop).start()

        @pl.when(level + hop <= last)
        def _():
            origin = level + hop
            self.down(k, hop, origin, hop - 1).wait_recv()
            if hop < last:

                @pl.when(level > 0)
                def _():
                    self.down(k, hop, origin, hop).start()

            self.across(k, origin, core, last + hop).start()

    def ready(self, k):
        group, level, core = self.at
        last = self.levels - 1
        self.across(k, level, 1 - core, 0).wait_recv()
        for hop in range(1, self.levels):

            @pl.when(level >= hop)
            def _():
                self.across(k, level - hop, 1 - core, hop).wait_recv()

            @pl.when(level + hop <= last)
            def _():
                self.across(k, level + hop, 1 - core, last + hop).wait_recv()

    def drain(self):
        group, level, core = self.at
        last = self.levels - 1

        def one(k, _):
            self.across(k, level, core, 0).wait_send()
            for hop in range(self.levels):
                if hop < last:

                    @pl.when((level >= hop) & (level < last))
                    def _():
                        self.up(k, hop, level - hop, hop).wait_send()

                    @pl.when((level + hop <= last) & (level > 0))
                    def _():
                        self.down(k, hop, level + hop, hop).wait_send()

                if hop > 0:

                    @pl.when(level >= hop)
                    def _():
                        self.across(k, level - hop, core, hop).wait_send()

                    @pl.when(level + hop <= last)
                    def _():
                        self.across(k, level + hop, core, last + hop).wait_send()

            return 0

        lax.fori_loop(0, self.count, one, 0)


class Scatter:
    REFS = 4

    def __init__(self, at, sizes, count, refs):
        self.at, self.levels, self.count = at, sizes[1], count
        self.part, self.cross, self.inbox, self.total = refs[:4]
        self.sent_core, self.got_core, self.sent_up, self.got_up, self.sent_down, self.got_down = refs[4:]

    @staticmethod
    def scratch(count, sizes, piece):
        levels = sizes[1]
        dma = pltpu.SemaphoreType.DMA
        return (
            [
                pltpu.VMEM((2, levels, 2) + piece, jnp.bfloat16),
                pltpu.VMEM((count, levels) + piece, jnp.bfloat16),
                pltpu.VMEM((count, levels + 1) + piece, jnp.bfloat16),
                pltpu.VMEM(piece, jnp.float32),
            ]
            + [dma((count,)) for _ in range(2)]
            + [dma((levels, count)) for _ in range(4)]
        )

    def across(self, k):
        group, level, core = self.at
        return pltpu.make_async_remote_copy(
            src_ref=self.part.at[lax.rem(k, 2), :, 1 - core],
            dst_ref=self.cross.at[k],
            send_sem=self.sent_core.at[k],
            recv_sem=self.got_core.at[k],
            device_id=(group, level, 1 - core),
            device_id_type=MESH,
        )

    def up(self, k, owner):
        group, level, core = self.at
        return pltpu.make_async_remote_copy(
            src_ref=self.cross.at[k, owner],
            dst_ref=self.inbox.at[k, owner + 1],
            send_sem=self.sent_up.at[owner, k],
            recv_sem=self.got_up.at[owner, k],
            device_id=(group, lax.rem(level + 1, self.levels), core),
            device_id_type=MESH,
        )

    def down(self, k, owner):
        group, level, core = self.at
        return pltpu.make_async_remote_copy(
            src_ref=self.cross.at[k, owner],
            dst_ref=self.inbox.at[k, owner],
            send_sem=self.sent_down.at[owner, k],
            recv_sem=self.got_down.at[owner, k],
            device_id=(group, lax.rem(level + self.levels - 1, self.levels), core),
            device_id_type=MESH,
        )

    def free(self, k):
        @pl.when(k >= 2)
        def _():
            self.across(k - 2).wait_send()

    def start(self, k):
        self.across(k).start()

    def join(self, k):
        core = self.at[2]
        self.across(k).wait_recv()
        for owner in range(self.levels):
            self.cross[k, owner] = lowered(
                wide(self.part[lax.rem(k, 2), owner, core]) + wide(self.cross[k, owner])
            )

    def step_up(self, k):
        level = self.at[1]
        for owner in range(self.levels - 1, 0, -1):

            @pl.when(level < owner)
            def _():
                @pl.when(level > 0)
                def _():
                    self.up(k, owner).wait_recv()
                    self.cross[k, owner] = lowered(wide(self.cross[k, owner]) + wide(self.inbox[k, owner + 1]))

                self.up(k, owner).start()

    def step_down(self, k):
        level = self.at[1]
        for owner in range(self.levels - 1):

            @pl.when(level > owner)
            def _():
                @pl.when(level < self.levels - 1)
                def _():
                    self.down(k, owner).wait_recv()
                    self.cross[k, owner] = lowered(wide(self.cross[k, owner]) + wide(self.inbox[k, owner]))

                self.down(k, owner).start()

    def steps(self, wave):
        level = self.at[1]
        above = wave - level
        below = wave - (self.levels - 1 - level)

        @pl.when(within(above, self.count))
        def _():
            self.step_up(above)

        @pl.when(within(below, self.count))
        def _():
            self.step_down(below)

    def finish(self, k):
        level = self.at[1]
        self.total[...] = wide(self.cross[k, level])

        @pl.when(level > 0)
        def _():
            self.up(k, level).wait_recv()
            self.total[...] += wide(self.inbox[k, level + 1])

        @pl.when(level < self.levels - 1)
        def _():
            self.down(k, level).wait_recv()
            self.total[...] += wide(self.inbox[k, level])

    def drain(self):
        level = self.at[1]

        def one(k, _):
            @pl.when(k >= self.count - 2)
            def _():
                self.across(k).wait_send()

            for owner in range(self.levels):

                @pl.when(level < owner)
                def _():
                    self.up(k, owner).wait_send()

                @pl.when(level > owner)
                def _():
                    self.down(k, owner).wait_send()

            return 0

        lax.fori_loop(0, self.count, one, 0)


def in_order(count, step):
    def body(number, carry):
        step(number)
        return carry

    lax.fori_loop(0, count, body, 0)


def span(number, size):
    return pl.ds(pl.multiple_of(number * size, size), size)


class Moves:
    def __init__(self, pairs, sems):
        self.pairs, self.sems = pairs, sems

    def copy(self, number):
        return pltpu.make_async_copy(*self.pairs[number], self.sems.at[number])

    def start(self, *numbers):
        for number in numbers:
            self.copy(number).start()

    def wait(self, *numbers):
        for number in numbers:
            self.copy(number).wait()


class Chunks:
    def __init__(self, pairs, size, sems):
        self.pairs, self.size, self.sems = pairs, size, sems

    def start(self, k):
        for number, (source, target) in enumerate(self.pairs):
            rows = span(k, self.size)
            pltpu.make_async_copy(source.at[rows], target.at[rows], self.sems.at[number, k]).start()

    def wait(self, count):
        def one(k, carry):
            for number, (source, target) in enumerate(self.pairs):
                rows = span(k, self.size)
                pltpu.make_async_copy(source.at[rows], target.at[rows], self.sems.at[number, k]).wait()
            return carry

        lax.fori_loop(0, count, one, 0)


def matmul(left, right):
    return jnp.dot(left, right, preferred_element_type=jnp.float32)


def decay_tile(near, far, size, bounds, rate):
    rows = near * size + lax.broadcasted_iota(jnp.int32, (size, 1), 0)
    columns = far * size + lax.broadcasted_iota(jnp.int32, (1, size), 1)
    row_seq, column_seq = jnp.zeros((size, 1), jnp.int32), jnp.zeros((1, size), jnp.int32)
    for number in range(1, SEQ_DEV):
        row_seq += (rows >= bounds[number]).astype(jnp.int32)
        column_seq += (columns >= bounds[number]).astype(jnp.int32)
    distance = rows - columns
    valid = (distance >= 0) & (row_seq == column_seq)
    return (
        jnp.where(valid, jnp.exp(jnp.maximum(distance, 0).astype(jnp.float32) * rate[0]), 0.0)
        * QK_DIM ** (-0.5)
    )


class Swap:
    def __init__(self, at, sizes, items, sems):
        self.at, self.count, self.items = at, sizes[0], items
        self.local, self.sent, self.got = sems

    scratch = Spread.scratch

    def block(self, number, owner):
        source, target, axis = self.items[number]
        size = source.shape[axis] // self.count
        window = pl.ds(pl.multiple_of(owner * size, size), size)
        return source.at[window] if axis == 0 else source.at[:, window]

    def own(self, number):
        return pltpu.make_async_copy(
            self.block(number, self.at[0]), self.items[number][1].at[0], self.local.at[number]
        )

    def away(self, number, k):
        peer = lax.rem(self.at[0] + k, self.count)
        return pltpu.make_async_remote_copy(
            src_ref=self.block(number, peer),
            dst_ref=self.items[number][1].at[k],
            send_sem=self.sent.at[number, k - 1],
            recv_sem=self.got.at[number, k - 1],
            device_id=(peer,) + self.at[1:],
            device_id_type=MESH,
        )

    def start(self, number):
        self.own(number).start()
        for k in range(1, self.count):
            self.away(number, k).start()

    def wait(self, number):
        self.own(number).wait()
        for k in range(1, self.count):
            self.away(number, k).wait()


def deal_kernel(sizes, tokens, gains, *refs):
    masters, refs = refs[:8], refs[8:]
    tokens_out, gains_out, *refs = refs
    rounded_out, refs = refs[:8], refs[8:]
    spread_sems, refs = refs[:3], refs[3:]
    held, refs = refs[:8], refs[8:]
    rounded, refs = refs[:8], refs[8:]
    load_sems, store_sems = refs
    at = around(AXES)
    loads = Moves(list(zip(masters, held)), load_sems)
    stores = Moves(list(zip(rounded, rounded_out)), store_sems)
    loads.start(*range(8))
    greet(plane_peers(at, sizes))
    spread = Spread(at, sizes, [(tokens, tokens_out, 0), (gains, gains_out, 0)], spread_sems)
    spread.start(0)
    spread.start(1)
    for number in range(8):
        loads.wait(number)

        def block(k):
            rows = span(k, 32)
            rounded[number][rows, :] = lowered(held[number][rows, :])

        in_order(held[number].shape[0] // 32, block)
        stores.start(number)
    stores.wait(*range(8))
    spread.wait(0)
    spread.wait(1)
    spread.drain(0)
    spread.drain(1)


def open_kernel(sizes, shards, gain, *refs):
    x_part, gain, *refs = (shards, gain) + refs
    sources, refs = refs[:5], refs[5:]
    normed_out, query_out, key_out, value_out, swish_out, *refs = refs
    weight_outs, refs = refs[:5], refs[5:]
    rows_out, unit_out, scale_out, *refs = refs
    full, *refs = refs
    gather_sems, refs = refs[:6], refs[6:]
    spread_sems, refs = refs[:3], refs[3:]
    weights, refs = refs[:4], refs[4:]
    normed, query, keys, values, swish, load_sem, out_sem, weight_sem, normed_sem = refs
    at = around(AXES)
    group, level, core = at
    place = 2 * level + core
    count, levels, _, chunk, width = full.shape
    ranks = 2 * levels
    load = pltpu.make_async_copy(x_part, full.at[:, level, core], load_sem)
    load.start()
    greet(plane_peers(at, sizes) + column_peers(at, sizes))
    items = [(s, t, 0) for s, t in zip(sources[:4], weights)] + [(sources[4], weight_outs[4], 1)]
    spread = Spread(at, sizes, items, spread_sems)
    gather = Gather(at, sizes, count, full, gather_sems)
    load.wait()
    gather.start(0)
    for number in range(5):
        spread.start(number)
    piece = chunk // ranks

    def norm(k):
        def block(number, carry):
            rows = span(number, 16)
            value = jnp.concatenate(
                [wide(full[k, q, c, rows, :]) for q in range(levels) for c in range(2)], axis=1
            )
            unit, scale = layer_norm(value, EPSILON)
            where = pl.ds(pl.multiple_of(k * chunk + number * 16, 16), 16)
            normed[where, :] = lowered(unit * gain[...])
            mine = wide(full[k, level, core, rows, :])
            mean = jnp.mean(value, -1, keepdims=True)
            unit_out[where, :] = (mine - mean) * scale
            scale_out[where, :] = jnp.broadcast_to(scale, (16, 128))
            return carry

        lax.fori_loop(0, chunk // 16, block, 0)
        mine = span(place, piece)
        rows_out[span(k, piece), :] = jnp.concatenate(
            [full[k, q, c, mine, :] for q in range(levels) for c in range(2)], axis=1
        )
        pltpu.make_async_copy(
            normed.at[span(k, chunk)], normed_out.at[span(k, chunk)], normed_sem.at[k]
        ).start()

    def wave(number):
        @pl.when(number + 1 < count)
        def _():
            gather.start(number + 1)

        for hop in range(1, levels):

            @pl.when(within(number - hop, count))
            def _():
                gather.hop(number - hop, hop)

        @pl.when(within(number - levels, count))
        def _():
            gather.ready(number - levels)
            norm(number - levels)

    in_order(count + levels, wave)
    outs = [(query, query_out), (keys, key_out), (values, value_out), (swish, swish_out)]
    for number, (held, out) in enumerate(outs):
        spread.wait(number)
        pltpu.make_async_copy(weights[number], weight_outs[number], weight_sem.at[number]).start()

        def rows(k):
            where = span(k, chunk)
            held[where, :] = matmul(normed[where, :], weights[number][...]).astype(held.dtype)

        in_order(count, rows)
        pltpu.make_async_copy(held, out, out_sem.at[number]).start()
    spread.wait(4)
    for number, (held, out) in enumerate(outs):
        pltpu.make_async_copy(held, out, out_sem.at[number]).wait()
        pltpu.make_async_copy(weights[number], weight_outs[number], weight_sem.at[number]).wait()
    for number in range(5):
        spread.drain(number)
    gather.drain()

    def stored(k):
        pltpu.make_async_copy(
            normed.at[span(k, chunk)], normed_out.at[span(k, chunk)], normed_sem.at[k]
        ).wait()

    in_order(count, stored)


def middle_kernel(sizes, bounds, rate, gain, *refs):
    ins, refs = refs[:6], refs[6:]
    sources, refs = refs[:4], refs[4:]
    normed_out, gate_out, up_out, hidden_out, resid_out, retained_out, mixed_out, *refs = refs
    gate_w_out, up_w_out, down_w_out, dy_out, *refs = refs
    held, refs = refs[:6], refs[6:]
    query, keys, values, swish, out_w, x_rows = held
    scatter_refs, refs = refs[:10], refs[10:]
    full, *refs = refs
    gather_sems, refs = refs[:6], refs[6:]
    spread_sems, refs = refs[:3], refs[3:]
    gate_w, up_w, gate, up, hidden, resid, retained, mixed_in, refs = *refs[:8], refs[8:]
    load_sems, chunk_sems, normed_sems, weight_sems, resid_sem = refs
    at = around(AXES)
    group, level, core = at
    count, levels, _, piece, width = full.shape
    chunk = 2 * levels * piece
    loads = Moves(list(zip(ins, held)), load_sems)
    loads.start(*range(6))
    greet(plane_peers(at, sizes) + column_peers(at, sizes))
    spread = Spread(
        at,
        sizes,
        [
            (sources[0], gate_w, 0),
            (sources[1], up_w, 0),
            (sources[2], down_w_out, 1),
            (sources[3], dy_out, 0),
        ],
        spread_sems,
    )
    for number in range(4):
        spread.start(number)
    scatter = Scatter(at, sizes, count, scatter_refs)
    gather = Gather(at, sizes, count, full, gather_sems)
    weights = Moves([(gate_w, gate_w_out), (up_w, up_w_out)], weight_sems)
    early = Chunks([(retained, retained_out), (mixed_in, mixed_out)], chunk, chunk_sems.at[:2])
    late = Chunks([(gate, gate_out), (up, up_out), (hidden, hidden_out)], chunk, chunk_sems.at[2:])
    loads.wait(*range(6))
    tile = 512

    def stores(k):
        copies = []
        for q in range(levels):
            for c in range(2):
                rows = pl.ds(pl.multiple_of(k * chunk + (2 * q + c) * piece, piece), piece)
                copies.append(
                    pltpu.make_async_copy(full.at[k, q, c], normed_out.at[rows], normed_sems.at[2 * q + c, k])
                )
        return copies

    def first(k):
        where = span(k, chunk)
        retained[where, :] = jnp.zeros((chunk, retained.shape[1]), jnp.float32)

        def block(j, carry):
            there = span(j, chunk)
            decay = decay_tile(k, j, chunk, bounds, rate)
            weight = lowered(inner_rows(query[where, :], keys[there, :]) * decay)
            retained[where, :] += matmul(weight, values[there, :])
            return carry

        lax.fori_loop(0, k + 1, block, 0)
        normed, _ = layer_norm(retained[where, :], GROUP_EPS)
        value = swish[where, :]
        mixed_in[where, :] = lowered(value * jax.nn.sigmoid(value) * normed)
        early.start(k)
        scatter.free(k)
        rows = mixed_in[where, :]
        for column in range(0, width, tile):
            value = matmul(rows, out_w[:, column : column + tile])
            scatter.part[lax.rem(k, 2), :, :, :, column : column + tile] = lowered(value).reshape(
                levels, 2, piece, tile
            )
        scatter.start(k)

    def norm(k):
        scatter.finish(k)

        def block(number, carry):
            sub = span(number, 16)
            where = pl.ds(pl.multiple_of(k * piece + number * 16, 16), 16)
            value = wide(x_rows[where, :]) + scatter.total[sub, :]
            resid[where, :] = value
            unit, _ = layer_norm(value, EPSILON)
            full[k, level, core, sub, :] = lowered(unit * gain[...])
            return carry

        lax.fori_loop(0, piece // 16, block, 0)
        gather.start(k)

    def last(k):
        gather.ready(k)
        for copy in stores(k):
            copy.start()
        rows = full[k].reshape(chunk, width)
        where = span(k, chunk)
        gate[where, :] = matmul(rows, gate_w[...])
        up[where, :] = matmul(rows, up_w[...])
        hidden[where, :] = lowered(jax.nn.gelu(gate[where, :]) * up[where, :])
        late.start(k)

    lag = levels - 1

    def wave(number):
        @pl.when(number < count)
        def _():
            first(number)

        for hop in range(1, levels):

            @pl.when(within(number - lag - hop, count))
            def _():
                gather.hop(number - lag - hop, hop)

        @pl.when(number == 2 * lag + 1)
        def _():
            spread.wait(0)
            spread.wait(1)
            weights.start(0, 1)

        @pl.when(within(number - 2 * lag - 1, count))
        def _():
            last(number - 2 * lag - 1)

        @pl.when(number < count)
        def _():
            scatter.join(number)

        scatter.steps(number)

        @pl.when(within(number - lag, count))
        def _():
            norm(number - lag)

    in_order(count + 2 * lag + 1, wave)
    store_resid = pltpu.make_async_copy(resid, resid_out, resid_sem)
    store_resid.start()
    spread.wait(2)
    spread.wait(3)
    for number in range(4):
        spread.drain(number)
    scatter.drain()
    gather.drain()
    weights.wait(0, 1)
    store_resid.wait()
    early.wait(count)
    late.wait(count)

    def stored(k):
        for copy in stores(k):
            copy.wait()

    in_order(count, stored)


def feed_kernel(sizes, dy_part, *refs):
    ins, refs = refs[:5], refs[5:]
    mixed_out, gate_grad_out, up_grad_out, dy_rows_out, down_grad_out, *refs = refs
    held, refs = refs[:5], refs[5:]
    hidden, down_w, resid, gate, up = held
    scatter_refs, refs = refs[:10], refs[10:]
    full, *refs = refs
    gather_sems, refs = refs[:6], refs[6:]
    tile_acc, down_acc, down_grad, mixed, gate_grad, up_grad, dy_rows, refs = *refs[:7], refs[7:]
    load_sem, load_sems, chunk_sems, end_sems = refs
    at = around(AXES)
    group, level, core = at
    place = 2 * level + core
    count, levels, _, chunk, width = full.shape
    ranks = 2 * levels
    piece = chunk // ranks
    load = pltpu.make_async_copy(dy_part, full.at[:, level, core], load_sem)
    load.start()
    loads = Moves(list(zip(ins, held)), load_sems)
    loads.start(*range(5))
    greet(column_peers(at, sizes))
    scatter = Scatter(at, sizes, count, scatter_refs)
    gather = Gather(at, sizes, count, full, gather_sems)
    store = Chunks(
        [(mixed, mixed_out), (gate_grad, gate_grad_out), (up_grad, up_grad_out)], chunk, chunk_sems
    )
    early = Chunks(store.pairs[:1], chunk, chunk_sems.at[:1])
    late = Chunks(store.pairs[1:], chunk, chunk_sems.at[1:])
    load.wait()
    gather.start(0)
    loads.wait(0, 1, 2)
    down_acc[...] = jnp.zeros(down_acc.shape, jnp.float32)

    def first(k):
        scatter.free(k)
        rows = hidden[span(k, chunk), :]
        mine = span(place, piece)
        for rank in range(ranks):
            columns = slice(rank * width, (rank + 1) * width)
            tile_acc[...] = matmul(rows, down_w[:, columns])
            tile_acc[mine, :] += resid[span(k, piece), columns]
            scatter.part[lax.rem(k, 2), rank // 2, rank % 2] = lowered(tile_acc[...])
        scatter.start(k)

    def last(k):
        gather.ready(k)
        where = span(k, chunk)
        rows = jnp.concatenate([full[k, q, c] for q in range(levels) for c in range(2)], axis=1)
        back = inner_rows(rows, down_w[...])
        mine = span(place, piece)
        dy_rows[span(k, piece), :] = jnp.concatenate(
            [full[k, q, c, mine, :] for q in range(levels) for c in range(2)], axis=1
        )
        g, u = gate[where, :], up[where, :]
        root = 0.7978845608028654
        bend = jnp.tanh(root * (g + 0.044715 * g * g * g))
        curve = 0.5 * (1.0 + bend)
        slope = curve + 0.5 * g * (1.0 - bend * bend) * root * (1.0 + 0.134145 * g * g)
        gate_grad[where, :] = lowered(back * u * slope)
        up_grad[where, :] = lowered(back * g * curve)
        late.start(k)
        for rank in range(ranks):
            columns = slice(rank * width, (rank + 1) * width)
            down_acc[:, columns] += inner_cols(hidden[where, :], full[k, rank // 2, rank % 2])

    lag = levels - 1

    def wave(number):
        @pl.when(number + 1 < count)
        def _():
            gather.start(number + 1)

        @pl.when(number < count)
        def _():
            first(number)

        for hop in range(1, levels):

            @pl.when(within(number - hop, count))
            def _():
                gather.hop(number - hop, hop)

        @pl.when(number < count)
        def _():
            scatter.join(number)

        scatter.steps(number)

        @pl.when(within(number - lag, count))
        def _():
            scatter.finish(number - lag)
            mixed[span(number - lag, chunk), :] = lowered(scatter.total[...])
            early.start(number - lag)

        @pl.when(number == levels)
        def _():
            loads.wait(3, 4)

        @pl.when(within(number - levels, count))
        def _():
            last(number - levels)

    in_order(count + levels, wave)
    down_grad[...] = lowered(down_acc[...])
    ends = Moves([(down_grad, down_grad_out), (dy_rows, dy_rows_out)], end_sems)
    ends.start(0, 1)
    scatter.drain()
    gather.drain()
    store.wait(count)
    ends.wait(0, 1)


def back_kernel(sizes, bounds, rate, gain, *refs):
    ins, refs = refs[:13], refs[13:]
    mixed_src, down_src, *refs = refs
    branch_out, swish_out, query_out, key_out, value_out, gain_out, *refs = refs
    mixed_dst, down_dst, gate_dst, up_dst, *refs = refs
    held, refs = refs[:13], refs[13:]
    gate_grad, up_grad, gate_w, up_w, resid, dy_rows, normed_mid, out_w, retained, swish, *held_qkv = held
    query, keys, values = held_qkv
    scatter_refs, refs = refs[:10], refs[10:]
    full, *refs = refs
    gather_sems, refs = refs[:6], refs[6:]
    spread_sems, refs = refs[:3], refs[3:]
    swap_sems, refs = refs[:3], refs[3:]
    gate_total, up_total, swish_grad, delta, query_acc, key_acc, value_acc, refs = *refs[:7], refs[7:]
    load_sems, chunk_sems, store_sems, end_sems = refs
    at = around(AXES)
    group, level, core = at
    count, levels, _, piece, width = full.shape
    chunk = 2 * levels * piece
    loads = Moves(list(zip(ins, held)), load_sems)
    loads.start(*range(13))
    greet(plane_peers(at, sizes) + column_peers(at, sizes))
    spread = Spread(at, sizes, [(mixed_src, mixed_dst, 0)], spread_sems)
    swap = Swap(at, sizes, [(down_src, down_dst, 1), (gate_total, gate_dst, 0), (up_total, up_dst, 0)], swap_sems)
    spread.start(0)
    swap.start(0)
    scatter = Scatter(at, sizes, count, scatter_refs)
    gather = Gather(at, sizes, count, full, gather_sems)
    store = Chunks([(swish_grad, swish_out), (query, query_out)], chunk, chunk_sems)
    gain_out[...] = jnp.zeros(gain_out.shape, jnp.float32)
    key_acc[...] = jnp.zeros(key_acc.shape, jnp.float32)
    value_acc[...] = jnp.zeros(value_acc.shape, jnp.float32)
    loads.wait(0, 1, 2, 3)
    tile = 512

    def stores(k):
        copies = []
        for q in range(levels):
            for c in range(2):
                rows = pl.ds(pl.multiple_of(k * chunk + (2 * q + c) * piece, piece), piece)
                copies.append(
                    pltpu.make_async_copy(full.at[k, q, c], branch_out.at[rows], store_sems.at[2 * q + c, k])
                )
        return copies

    def first(k):
        scatter.free(k)
        where = span(k, chunk)
        for column in range(0, width, tile):
            columns = slice(column, column + tile)
            value = inner_rows(gate_grad[where, :], gate_w[columns, :])
            value += inner_rows(up_grad[where, :], up_w[columns, :])
            scatter.part[lax.rem(k, 2), :, :, :, columns] = lowered(value).reshape(levels, 2, piece, tile)
        scatter.start(k)

    def weigh(k):
        columns = span(k, chunk)
        rows = normed_mid[:, columns]
        gate_total[columns, :] = lowered(inner_cols(rows, gate_grad[...]))
        up_total[columns, :] = lowered(inner_cols(rows, up_grad[...]))

    def norm(k):
        scatter.finish(k)

        def block(number, carry):
            sub = span(number, 16)
            where = pl.ds(pl.multiple_of(k * piece + number * 16, 16), 16)
            unit, scale = layer_norm(resid[where, :], EPSILON)
            grad = scatter.total[sub, :]
            outer = grad * unit
            gain_out[...] += outer[:8] + outer[8:]
            value = wide(dy_rows[where, :]) + norm_back(grad * gain[...], unit, scale)
            full[k, level, core, sub, :] = lowered(value)
            return carry

        lax.fori_loop(0, piece // 16, block, 0)
        gather.start(k)

    def last(k):
        gather.ready(k)
        for copy in stores(k):
            copy.start()
        rows = full[k].reshape(chunk, width)
        where = span(k, chunk)
        grad = inner_rows(rows, out_w[...])
        normed, scale = layer_norm(retained[where, :], GROUP_EPS)
        value = swish[where, :]
        gated = jax.nn.sigmoid(value)
        swish_grad[where, :] = lowered(grad * normed * gated * (1.0 + value * (1.0 - gated)))
        delta[...] = lowered(norm_back(grad * value * gated, normed, scale))
        query_acc[...] = jnp.zeros(query_acc.shape, jnp.float32)

        def block(j, carry):
            there = span(j, chunk)
            decay = decay_tile(k, j, chunk, bounds, rate)
            weight = lowered(inner_rows(query[where, :], keys[there, :]) * decay)
            score = lowered(inner_rows(delta[...], values[there, :]) * decay)
            query_acc[...] += matmul(score, keys[there, :])
            key_acc[there, :] += inner_cols(score, query[where, :])
            value_acc[there, :] += inner_cols(weight, delta[...])
            return carry

        lax.fori_loop(0, k + 1, block, 0)
        query[where, :] = lowered(query_acc[...])
        store.start(k)

    lag = levels - 1
    tiles = width // chunk

    def wave(number):
        @pl.when(number < count)
        def _():
            first(number)

        for hop in range(1, levels):

            @pl.when(within(number - lag - hop, count))
            def _():
                gather.hop(number - lag - hop, hop)

        @pl.when(number == 2 * lag + 1)
        def _():
            loads.wait(7, 8, 9, 10, 11, 12)

        @pl.when(within(number - 2 * lag - 1, count))
        def _():
            last(number - 2 * lag - 1)

        @pl.when(number < count)
        def _():
            scatter.join(number)

        scatter.steps(number)

        @pl.when(number == lag)
        def _():
            loads.wait(4, 5)

        @pl.when(within(number - lag, count))
        def _():
            norm(number - lag)

        @pl.when(number == 0)
        def _():
            loads.wait(6)

        @pl.when(number < tiles)
        def _():
            weigh(number)

        @pl.when(number == tiles)
        def _():
            swap.start(1)
            swap.start(2)

    in_order(count + 2 * lag + 1, wave)
    keys[...] = lowered(key_acc[...])
    values[...] = lowered(value_acc[...])
    ends = Moves([(keys, key_out), (values, value_out)], end_sems)
    ends.start(0, 1)
    spread.wait(0)
    for number in range(3):
        swap.wait(number)
    spread.drain(0)
    scatter.drain()
    gather.drain()
    store.wait(count)
    ends.wait(0, 1)

    def stored(k):
        for copy in stores(k):
            copy.wait()

    in_order(count, stored)


def close_kernel(sizes, gain, gain_two, *refs):
    ins, refs = refs[:13], refs[13:]
    grad_out, gains_out, *refs = refs
    targets, refs = refs[:5], refs[5:]
    held, refs = refs[:13], refs[13:]
    deltas, weights = held[:4], held[4:8]
    normed_in, branch, mixed_in, unit, scale = held[8:]
    grads, refs = refs[:5], refs[5:]
    scatter_refs, refs = refs[:10], refs[10:]
    swap_sems, refs = refs[:3], refs[3:]
    sums, line_one, share, packed, gains, gains_in, refs = *refs[:6], refs[6:]
    load_sems, sums_sent, sums_got, gain_sent, gain_got, deal_sent, deal_got, deal_own = refs
    at = around(AXES)
    group, level, core = at
    place = 2 * level + core
    groups = sizes[0]
    scatter = Scatter(at, sizes, sums.shape[1], scatter_refs)
    _, levels, _, chunk, width = scatter.part.shape
    count, ranks = sums.shape[1], 2 * levels
    rows_all = count * chunk
    loads = Moves(list(zip(ins, held)), load_sems)
    loads.start(*range(13))
    greet(plane_peers(at, sizes) + column_all(at, sizes))
    swap = Swap(at, sizes, list(zip(grads, targets, SWAP_AXES)) + [(gains, gains_in, 1)], swap_sems)
    line_one[...] = jnp.zeros(line_one.shape, jnp.float32)
    loads.wait(*range(9))
    mine = pl.ds(pl.multiple_of(place * width, width), width)

    def first(k):
        scatter.free(k)
        where = span(k, chunk)
        rows = [d[where, :] for d in deltas]
        one = jnp.zeros((chunk, width), jnp.float32)
        two = jnp.zeros((chunk, width), jnp.float32)
        for rank in range(ranks):
            columns = slice(rank * width, (rank + 1) * width)
            value = inner_rows(rows[0], weights[0][columns, :])
            for row, weight in zip(rows[1:], weights[1:]):
                value += inner_rows(row, weight[columns, :])
            scatter.part[lax.rem(k, 2), rank // 2, rank % 2] = lowered(value)
            one += value * gain[:, columns]
            two += value * wide(normed_in[where, columns])
        scatter.start(k)
        ones = jnp.ones((8, width), jnp.float32)
        flat = [
            lax.dot_general(
                ones,
                item,
                (((1,), (1,)), ((), ())),
                precision=lax.Precision.HIGHEST,
                preferred_element_type=jnp.float32,
            )
            for item in (one, two)
        ]
        line = lax.broadcasted_iota(jnp.int32, (8, chunk), 0)
        sums[place, k] = jnp.where(line == 0, flat[0], flat[1])
        for j in range(1, ranks):
            sums_copy(k, j, place).start()

    def sums_copy(k, j, owner):
        peer = lax.rem(place + j, ranks)
        return pltpu.make_async_remote_copy(
            src_ref=sums.at[owner, k],
            dst_ref=sums.at[owner, k],
            send_sem=sums_sent.at[j - 1, k],
            recv_sem=sums_got.at[j - 1, k],
            device_id=(group, peer // 2, lax.rem(peer, 2)),
            device_id_type=MESH,
        )

    def pack_copy(j, owner):
        peer = lax.rem(place + j, ranks)
        return pltpu.make_async_remote_copy(
            src_ref=packed.at[owner],
            dst_ref=packed.at[owner],
            send_sem=gain_sent.at[j - 1],
            recv_sem=gain_got.at[j - 1],
            device_id=(group, peer // 2, lax.rem(peer, 2)),
            device_id_type=MESH,
        )

    def sender(j):
        return lax.rem(place + ranks - j, ranks)

    def deal(k, j, owner):
        rows = pl.ds(pl.multiple_of(owner * rows_all + k * chunk, chunk), chunk)
        return pltpu.make_async_remote_copy(
            src_ref=share.at[span(k, chunk)],
            dst_ref=grad_out.at[rows],
            send_sem=deal_sent.at[j - 1, k],
            recv_sem=deal_got.at[j - 1, k],
            device_id=(lax.rem(group + j, groups), level, core),
            device_id_type=MESH,
        )

    def deal_here(k):
        rows = pl.ds(pl.multiple_of(group * rows_all + k * chunk, chunk), chunk)
        return pltpu.make_async_copy(share.at[span(k, chunk)], grad_out.at[rows], deal_own.at[k])

    def finish(k):
        scatter.finish(k)
        for j in range(1, ranks):
            sums_copy(k, j, sender(j)).wait_recv()
        line = lax.broadcasted_iota(jnp.int32, (8, 128), 0)
        lane = lax.broadcasted_iota(jnp.int32, (8, 128), 1)
        means = lax.dot_general(
            jnp.sum(sums[:, k], 0),
            jnp.where(line == lane, 1.0 / (ranks * width), 0.0),
            (((0,), (0,)), ((), ())),
            precision=lax.Precision.HIGHEST,
            preferred_element_type=jnp.float32,
        )
        where = span(k, chunk)
        value, normed = scatter.total[...], unit[where, :]
        outer = value * normed
        line_one[...] += jnp.sum(outer.reshape(chunk // 8, 8, width), 0)
        back = value * gain[:, mine] - means[:, :1] - normed * means[:, 1:2]
        share[where, :] = lowered(wide(branch[where, mine]) + scale[where, :1] * back)
        deal_here(k).start()
        for j in range(1, groups):
            deal(k, j, group).start()

    def weigh(number):
        if number == 4:

            def part(k):
                columns = span(k, chunk)
                grads[4][:, columns] = lowered(inner_cols(mixed_in[...], branch[:, columns]))
        else:

            def part(k):
                columns = span(k, chunk)
                grads[number][columns, :] = lowered(inner_cols(normed_in[:, columns], deltas[number][...]))

        in_order(ranks * width // chunk, part)
        swap.start(number)

    lag = levels - 1

    def wave(number):
        @pl.when(number < count)
        def _():
            first(number)

        @pl.when(number == 0)
        def _():
            weigh(3)

        for step, which in ((1, 2), (2, 0), (3, 1)):

            @pl.when(number == step)
            def _():
                weigh(which)

        @pl.when(number < count)
        def _():
            scatter.join(number)

        scatter.steps(number)

        @pl.when(number == lag)
        def _():
            loads.wait(9, 10, 11, 12)

        @pl.when(within(number - lag, count))
        def _():
            finish(number - lag)

        @pl.when(number == lag + 1)
        def _():
            weigh(4)

    in_order(count + lag, wave)
    total = jnp.sum(gain_two[...], 0, keepdims=True)
    packed[place] = jnp.concatenate([total, jnp.sum(line_one[...], 0, keepdims=True)], axis=1)
    for j in range(1, ranks):
        pack_copy(j, place).start()
    for j in range(1, ranks):
        pack_copy(j, sender(j)).wait_recv()
    everything = ranks * width
    line = lax.broadcasted_iota(jnp.int32, (8, everything), 0)
    two = sum(packed[rank, :, :everything] for rank in range(ranks))
    one = jnp.concatenate([packed[rank, :, everything:] for rank in range(ranks)], axis=1)
    gains[...] = jnp.where(line == 0, one, two)
    swap.start(5)
    for number in range(6):
        swap.wait(number)
    gains_out[...] = jnp.sum(gains_in[...], 0)
    for j in range(1, ranks):
        pack_copy(j, place).wait_send()
    scatter.drain()

    def drain(k):
        deal_here(k).wait()
        for j in range(1, groups):
            deal(k, j, lax.rem(group + groups - j, groups)).wait_recv()
            deal(k, j, group).wait_send()
        for j in range(1, ranks):
            sums_copy(k, j, place).wait_send()

    in_order(count, drain)


def column_all(at, sizes):
    group, level, core = at
    return column_peers(at, sizes) + [
        (group, lax.rem(level + k, sizes[1]), 1 - core) for k in range(1, sizes[1])
    ]


def struct(shape, kind=jnp.bfloat16):
    return jax.ShapeDtypeStruct(shape, kind)


VMEM = pltpu.VMEM
DMA = pltpu.SemaphoreType.DMA


def kernel_call(body, number, ins, outs, scratch):
    places = {
        "vmem": pl.BlockSpec(memory_space=pltpu.VMEM),
        "smem": pl.BlockSpec(memory_space=pltpu.SMEM),
        "any": pl.BlockSpec(memory_space=pl.ANY),
    }
    return pl.pallas_call(
        body,
        out_shape=[shape for _, shape in outs],
        in_specs=[places[inside] for inside, _ in ins],
        out_specs=[places[inside] for inside, _ in outs],
        scratch_shapes=scratch,
        compiler_params=pltpu.CompilerParams(
            collective_id=number, has_side_effects=True, vmem_limit_bytes=60 * 2**20
        ),
    )(*[array for _, array in ins])


def spread_shape(shard, axis, sizes):
    shape = list(shard.shape)
    shape[axis] *= sizes[0]
    return struct(tuple(shape), shard.dtype)


def swap_shape(whole, axis, sizes):
    shape = list(whole.shape)
    shape[axis] //= sizes[0]
    return struct((sizes[0],) + tuple(shape), whole.dtype)


def anywhere(items):
    return [("any", item) for item in items]


def held_like(arrays):
    return [VMEM(a.shape, a.dtype) for a in arrays]


def pick(rows, whole):
    return whole.at[rows].get(mode="promise_in_bounds")


def shards(
    tokens,
    cotangent,
    lengths,
    dealing,
    w_query,
    w_key,
    w_value,
    w_swish,
    w_out,
    w_gate,
    w_up,
    w_down,
    gain_attn,
    gain_mlp,
):
    group = lax.axis_index("dp")
    place = lax.axis_index(("heads", "tensor"))
    rows_dev = tokens.shape[0]
    slice_width = tokens.shape[1]
    seq_count = lengths.shape[0]
    ident = jnp.arange(seq_count, dtype=jnp.int32)
    starts = jnp.cumsum(lengths) - lengths
    picked = lax.dynamic_slice_in_dim(dealing, group * SEQ_DEV, SEQ_DEV)
    match = picked[:, None] == ident[None, :]
    dealt_len = jnp.sum(jnp.where(match, lengths[None, :], 0), 1)
    home_start = jnp.sum(jnp.where(match, starts[None, :], 0), 1)
    dealt_start = jnp.cumsum(dealt_len) - dealt_len
    rows = jnp.arange(rows_dev, dtype=jnp.int32)
    seq_ids = jnp.sum((rows[:, None] >= dealt_start[None, :]).astype(jnp.int32), 1) - 1
    member = seq_ids[:, None] == jnp.arange(SEQ_DEV, dtype=jnp.int32)[None, :]
    source = jnp.sum(jnp.where(member, (home_start - dealt_start)[None, :], 0), 1) + rows
    sizes = (lax.axis_size("dp"), lax.axis_size("heads"))
    ranks = sizes[1] * lax.axis_size("tensor")
    chunk = ranks * PIECE
    count = rows_dev // chunk
    width = slice_width * ranks
    own = rows_dev // ranks
    qk_dim, v_dim, ff_dim = w_query.shape[1], w_value.shape[1], w_gate.shape[1]
    f32 = jnp.float32
    masters = (w_query, w_key, w_value, w_swish, w_out, w_gate, w_up, w_down)
    axes = (0, 0, 0, 0, 1, 0, 0, 1)
    gain_rows = jnp.pad(jnp.stack([gain_attn, gain_mlp]), ((0, 6), (0, 0)))
    rounded = [struct(w.shape) for w in masters]
    x_all, gains_all, *low = kernel_call(
        functools.partial(deal_kernel, sizes),
        0,
        anywhere((tokens, gain_rows) + masters),
        anywhere([spread_shape(tokens, 0, sizes), spread_shape(gain_rows, 0, sizes)] + rounded),
        Spread.scratch(2, sizes) + held_like(masters) + held_like(rounded) + [DMA((8,)), DMA((8,))],
    )
    full_w = [spread_shape(w, a, sizes) for w, a in zip(low, axes)]
    gains_all = wide(lowered(gains_all.reshape(sizes[0], 8, -1)))
    wide_one = gains_all[:, 0].reshape(1, width)
    wide_two = gains_all[:, 1].reshape(1, width)
    x_part = pick(source, x_all)
    (
        normed_in,
        query,
        keys,
        values,
        swish_in,
        query_w,
        key_w,
        value_w,
        swish_w,
        out_w,
        x_rows,
        unit_share,
        scale_one,
    ) = kernel_call(
        functools.partial(open_kernel, sizes),
        1,
        [("any", x_part.reshape(count, chunk, slice_width)), ("vmem", wide_one)] + anywhere(low[:5]),
        anywhere(
            [
                struct((rows_dev, width)),
                struct((rows_dev, qk_dim)),
                struct((rows_dev, qk_dim)),
                struct((rows_dev, v_dim)),
                struct((rows_dev, v_dim), f32),
            ]
            + full_w[:5]
        )
        + [
            ("vmem", struct((own, width))),
            ("vmem", struct((rows_dev, slice_width), f32)),
            ("vmem", struct((rows_dev, 128), f32)),
        ],
        Gather.scratch(count, sizes, (chunk, slice_width))
        + Spread.scratch(5, sizes)
        + held_like(full_w[:4])
        + [
            VMEM((rows_dev, width), jnp.bfloat16),
            VMEM((rows_dev, qk_dim), jnp.bfloat16),
            VMEM((rows_dev, qk_dim), jnp.bfloat16),
            VMEM((rows_dev, v_dim), jnp.bfloat16),
            VMEM((rows_dev, v_dim), f32),
            DMA,
            DMA((4,)),
            DMA((4,)),
            DMA((count,)),
        ],
    )
    rate = jnp.log1p(-jnp.exp2(-5.0 - place.astype(f32))).reshape(1)
    middle_ins = (query, keys, values, swish_in, out_w, x_rows)
    normed_mid, gate, up_proj, hidden, resid, retained, mixed_in, gate_w, up_w, down_w, dy_all = kernel_call(
        functools.partial(middle_kernel, sizes),
        2,
        [("smem", dealt_start), ("smem", rate), ("vmem", wide_two)]
        + anywhere(middle_ins)
        + anywhere(low[5:] + [cotangent]),
        anywhere(
            [
                struct((rows_dev, width)),
                struct((rows_dev, ff_dim), f32),
                struct((rows_dev, ff_dim), f32),
                struct((rows_dev, ff_dim)),
                struct((own, width), f32),
                struct((rows_dev, v_dim), f32),
                struct((rows_dev, v_dim)),
            ]
            + full_w[5:]
            + [spread_shape(cotangent, 0, sizes)]
        ),
        held_like(middle_ins)
        + Scatter.scratch(count, sizes, (PIECE, width))
        + Gather.scratch(count, sizes, (PIECE, width))
        + Spread.scratch(4, sizes)
        + held_like(full_w[5:7])
        + [
            VMEM((rows_dev, ff_dim), f32),
            VMEM((rows_dev, ff_dim), f32),
            VMEM((rows_dev, ff_dim), jnp.bfloat16),
            VMEM((own, width), f32),
            VMEM((rows_dev, v_dim), f32),
            VMEM((rows_dev, v_dim), jnp.bfloat16),
            DMA((6,)),
            DMA((5, count)),
            DMA((ranks, count)),
            DMA((2,)),
            DMA,
        ],
    )
    dy_part = pick(source, dy_all)
    feed_ins = (hidden, down_w, resid, gate, up_proj)
    mixed_share, delta_gate, delta_up, dy_rows, grad_down = kernel_call(
        functools.partial(feed_kernel, sizes),
        3,
        anywhere((dy_part.reshape(count, chunk, slice_width),) + feed_ins),
        anywhere(
            [
                struct((rows_dev, slice_width)),
                struct((rows_dev, ff_dim)),
                struct((rows_dev, ff_dim)),
                struct((own, width)),
                struct((ff_dim, width)),
            ]
        ),
        held_like(feed_ins)
        + Scatter.scratch(count, sizes, (chunk, slice_width))
        + Gather.scratch(count, sizes, (chunk, slice_width))
        + [
            VMEM((chunk, slice_width), f32),
            VMEM((ff_dim, width), f32),
            VMEM((ff_dim, width), jnp.bfloat16),
            VMEM((rows_dev, slice_width), jnp.bfloat16),
            VMEM((rows_dev, ff_dim), jnp.bfloat16),
            VMEM((rows_dev, ff_dim), jnp.bfloat16),
            VMEM((own, width), jnp.bfloat16),
            DMA,
            DMA((5,)),
            DMA((3, count)),
            DMA((2,)),
        ],
    )
    back_ins = (
        delta_gate,
        delta_up,
        gate_w,
        up_w,
        resid,
        dy_rows,
        normed_mid,
        out_w,
        retained,
        swish_in,
        query,
        keys,
        values,
    )
    delta_branch, delta_swish, delta_query, delta_keys, delta_values, gain_two_part, mixed_all, *ff_grads = (
        kernel_call(
            functools.partial(back_kernel, sizes),
            4,
            [("smem", dealt_start), ("smem", rate), ("vmem", wide_two)]
            + anywhere(back_ins)
            + anywhere((mixed_share, grad_down)),
            anywhere(
                [
                    struct((rows_dev, width)),
                    struct((rows_dev, v_dim)),
                    struct((rows_dev, qk_dim)),
                    struct((rows_dev, qk_dim)),
                    struct((rows_dev, v_dim)),
                ]
            )
            + [("vmem", struct((8, width), f32))]
            + anywhere(
                [
                    spread_shape(mixed_share, 0, sizes),
                    swap_shape(full_w[7], 1, sizes),
                    swap_shape(full_w[5], 0, sizes),
                    swap_shape(full_w[6], 0, sizes),
                ]
            ),
            held_like(back_ins)
            + Scatter.scratch(count, sizes, (PIECE, width))
            + Gather.scratch(count, sizes, (PIECE, width))
            + Spread.scratch(1, sizes)
            + Swap.scratch(3, sizes)
            + held_like(full_w[5:7])
            + [
                VMEM((rows_dev, v_dim), jnp.bfloat16),
                VMEM((chunk, v_dim), jnp.bfloat16),
                VMEM((chunk, qk_dim), f32),
                VMEM((rows_dev, qk_dim), f32),
                VMEM((rows_dev, v_dim), f32),
                DMA((13,)),
                DMA((2, count)),
                DMA((ranks, count)),
                DMA((2,)),
            ],
        )
    )
    close_ins = (
        delta_query,
        delta_keys,
        delta_values,
        delta_swish,
        query_w,
        key_w,
        value_w,
        swish_w,
        normed_in,
        delta_branch,
        mixed_in,
        unit_share,
        scale_one,
    )
    swaps = len(SWAP_AXES)
    grad_all, gains, *attn_grads = kernel_call(
        functools.partial(close_kernel, sizes),
        5,
        [("vmem", wide_one), ("vmem", gain_two_part)] + anywhere(close_ins),
        anywhere([struct((sizes[0] * rows_dev, slice_width))])
        + [("vmem", struct((8, gain_attn.shape[0]), f32))]
        + anywhere([swap_shape(w, a, sizes) for w, a in zip(full_w[:5], SWAP_AXES)]),
        held_like(close_ins)
        + held_like(full_w[:5])
        + Scatter.scratch(count, sizes, (chunk, slice_width))
        + Swap.scratch(swaps + 1, sizes)
        + [
            VMEM((ranks, count, 8, chunk), f32),
            VMEM((8, slice_width), f32),
            VMEM((rows_dev, slice_width), jnp.bfloat16),
            VMEM((ranks, 1, width + slice_width), f32),
            VMEM((8, width), f32),
            VMEM((sizes[0], 8, gain_attn.shape[0]), f32),
            DMA((len(close_ins),)),
            DMA((ranks - 1, count)),
            DMA((ranks - 1, count)),
            DMA((ranks - 1,)),
            DMA((ranks - 1,)),
            DMA((sizes[0] - 1, count)),
            DMA((sizes[0] - 1, count)),
            DMA((count,)),
        ],
    )
    grads = [jnp.sum(wide(g), 0) for g in attn_grads + ff_grads[1:] + ff_grads[:1]]
    slot_match = dealing[:, None] == ident[None, :]
    slot_len = jnp.sum(jnp.where(slot_match, lengths[None, :], 0), 1)
    slot_home = jnp.sum(jnp.where(slot_match, starts[None, :], 0), 1)
    per_group = slot_len.reshape(-1, SEQ_DEV)
    slot_start = (jnp.cumsum(per_group, 1) - per_group).reshape(-1)
    slot_base = ident // SEQ_DEV * rows_dev + slot_start - slot_home
    owner_base = jnp.sum(jnp.where(dealing[None, :] == ident[:, None], slot_base[None, :], 0), 1)
    global_rows = group * rows_dev + rows
    seq_of = jnp.sum((global_rows[:, None] >= starts[None, :]).astype(jnp.int32), 1) - 1
    targets = (
        jnp.sum(jnp.where(seq_of[:, None] == ident[None, :], owner_base[None, :], 0), 1)
        + global_rows
    )
    mixed_rows, grad_rows = pick(targets, mixed_all), pick(targets, grad_all)
    return (
        mixed_rows,
        grad_rows,
        grads[0],
        grads[1],
        grads[2],
        grads[3],
        grads[4],
        grads[5],
        grads[6],
        grads[7],
        gains[0],
        gains[1],
    )


def solution(mesh):
    in_specs = (
        P("dp", ("heads", "tensor")),
        P("dp", ("heads", "tensor")),
        P(),
        P(),
        P("dp", ("heads", "tensor")),
        P("dp", ("heads", "tensor")),
        P("dp", ("heads", "tensor")),
        P("dp", ("heads", "tensor")),
        P(("heads", "tensor"), "dp"),
        P("dp", ("heads", "tensor")),
        P("dp", ("heads", "tensor")),
        P(("heads", "tensor"), "dp"),
        P("dp"),
        P("dp"),
    )
    out_specs = (
        P("dp", ("heads", "tensor")),
        P("dp", ("heads", "tensor")),
        P("dp", ("heads", "tensor")),
        P("dp", ("heads", "tensor")),
        P("dp", ("heads", "tensor")),
        P("dp", ("heads", "tensor")),
        P(("heads", "tensor"), "dp"),
        P("dp", ("heads", "tensor")),
        P("dp", ("heads", "tensor")),
        P(("heads", "tensor"), "dp"),
        P("dp"),
        P("dp"),
    )
    return jax.shard_map(shards, mesh=mesh, in_specs=in_specs, out_specs=out_specs, check_vma=False)
```

```python
import functools

import jax
import jax.numpy as jnp
from jax import lax
from jax.experimental import pallas as pl
from jax.experimental.pallas import tpu as pltpu
from jax.sharding import PartitionSpec as P

QK_DIM = 256
SEQ_DEV = 3
PIECE = 32
AXES = ("dp", "heads", "tensor")
SWAP_AXES = (0, 0, 0, 0, 1)
MESH = pl.DeviceIdType.MESH


EPSILON = 1e-05
GROUP_EPS = 1.0


def layer_norm(values, epsilon):
    center = values - jnp.mean(values, -1, keepdims=True)
    scale = lax.rsqrt(jnp.mean(center * center, -1, keepdims=True) + epsilon)
    return (center * scale, scale)


def norm_back(grad, normed, scale):
    return scale * (
        grad
        - jnp.mean(grad, -1, keepdims=True)
        - normed * jnp.mean(grad * normed, -1, keepdims=True)
    )


def product(left, right):
    return jnp.dot(left, right, preferred_element_type=jnp.float32)


def inner_rows(left, right):
    return lax.dot_general(
        left, right, (((1,), (1,)), ((), ())), preferred_element_type=jnp.float32
    )


def inner_cols(left, right):
    return lax.dot_general(
        left, right, (((0,), (0,)), ((), ())), preferred_element_type=jnp.float32
    )


def lowered(value):
    return value.astype(jnp.bfloat16)


def around(axes):
    return tuple(lax.axis_index(name) for name in axes)


def wide(value):
    return value.astype(jnp.float32)


def within(number, count):
    return (number >= 0) & (number < count)


def greet(others):
    barrier = pltpu.get_barrier_semaphore()
    for other in others:
        pl.semaphore_signal(barrier, inc=1, device_id=other, device_id_type=MESH)
    pl.semaphore_wait(barrier, len(others))


def plane_peers(at, sizes):
    group, level, core = at
    return [(lax.rem(group + k, sizes[0]), level, core) for k in range(1, sizes[0])]


def column_peers(at, sizes):
    group, level, core = at
    return [(group, lax.rem(level + k, sizes[1]), core) for k in range(1, sizes[1])] + [
        (group, level, 1 - core)
    ]


def beside(group):
    return group + 1 - 2 * lax.rem(group, 2), lax.rem(group + 2, 4), 3 - group


class Spread:
    def __init__(self, at, sizes, items, sems, relay=True):
        self.at, self.count, self.items = at, sizes[0], items
        self.local, self.sent, self.got = sems
        self.plane = relay and sizes[0] == 4

    @staticmethod
    def scratch(items, sizes):
        ways = max(4, sizes[0] - 1)
        return [
            pltpu.SemaphoreType.DMA((items,)),
            pltpu.SemaphoreType.DMA((items, ways)),
            pltpu.SemaphoreType.DMA((items, ways)),
        ]

    def place(self, number, owner, half=None):
        source, target, axis, *where = self.items[number]
        rows, columns = source.shape
        size = source.shape[axis]
        step, offset = where or (size, 0)
        start = owner * step + offset
        if half is None:
            begin, height = 0, rows
        else:
            begin, height = half * (rows // 2), rows // 2
        if axis == 0:
            return target.at[pl.ds(pl.multiple_of(start + begin, height), height)]
        return target.at[pl.ds(begin, height), pl.ds(pl.multiple_of(start, size), size)]

    def own(self, number):
        return pltpu.make_async_copy(
            self.items[number][0], self.place(number, self.at[0]), self.local.at[number]
        )

    def copy(self, number, source, place, way, peer):
        return pltpu.make_async_remote_copy(
            src_ref=source,
            dst_ref=place,
            send_sem=self.sent.at[number, way],
            recv_sem=self.got.at[number, way],
            device_id=(peer,) + self.at[1:],
            device_id_type=MESH,
        )

    def away(self, number, k):
        peer = lax.rem(self.at[0] + k, self.count)
        return self.copy(number, self.items[number][0], self.place(number, self.at[0]), k - 1, peer)

    def landed(self, number, k):
        owner = lax.rem(self.at[0] + self.count - k, self.count)
        return self.copy(number, self.items[number][0], self.place(number, owner), k - 1, owner)

    def to(self, number, way):
        peer = beside(self.at[0])[way]
        return self.copy(number, self.items[number][0], self.place(number, self.at[0]), way, peer)

    def of(self, number, way):
        peer = beside(self.at[0])[way]
        return self.copy(number, self.items[number][0], self.place(number, peer), way, peer)

    def on(self, number, way):
        near = beside(self.at[0])
        ref = self.place(number, near[way], way)
        return self.copy(number, ref, ref, 2 + way, near[1 - way])

    def last(self, number, way):
        near = beside(self.at[0])
        ref = self.place(number, near[2], way)
        return self.copy(number, ref, ref, 2 + way, near[1 - way])

    def start(self, *numbers):
        for number in numbers:
            if self.plane:
                self.to(number, 0).start()
                self.to(number, 1).start()
            else:
                for k in range(1, self.count):
                    self.away(number, k).start()
            self.own(number).start()

    def relay(self, *numbers):
        if self.plane:
            for number in numbers:
                for way in range(2):
                    self.of(number, way).wait_recv()
                    self.on(number, way).start()

    def wait(self, *numbers):
        for number in numbers:
            self.own(number).wait()
            if self.plane:
                self.last(number, 0).wait_recv()
                self.last(number, 1).wait_recv()
            else:
                for k in range(1, self.count):
                    self.landed(number, k).wait_recv()

    def drain(self, *numbers):
        for number in numbers:
            if self.plane:
                for way in range(2):
                    self.to(number, way).wait_send()
                    self.on(number, way).wait_send()
            else:
                for k in range(1, self.count):
                    self.away(number, k).wait_send()


class Gather:
    def __init__(self, at, sizes, count, full, sems):
        self.at, self.levels, self.count, self.full = at, sizes[1], count, full
        self.sent_up, self.got_up, self.sent_down, self.got_down, self.sent_core, self.got_core = sems

    @staticmethod
    def scratch(count, sizes, piece):
        levels = sizes[1]
        dma = pltpu.SemaphoreType.DMA
        return [pltpu.VMEM((count, levels, 2) + piece, jnp.bfloat16)] + [
            dma((levels - 1, count)) for _ in range(4)
        ] + [dma((2 * levels - 1, count)) for _ in range(2)]

    def copy(self, ref, sent, got, target):
        return pltpu.make_async_remote_copy(
            src_ref=ref, dst_ref=ref, send_sem=sent, recv_sem=got, device_id=target, device_id_type=MESH
        )

    def up(self, k, hop, origin, sem):
        group, level, core = self.at
        target = (group, lax.rem(level + 1, self.levels), core)
        return self.copy(self.full.at[k, origin, core], self.sent_up.at[sem, k], self.got_up.at[sem, k], target)

    def down(self, k, hop, origin, sem):
        group, level, core = self.at
        target = (group, lax.rem(level + self.levels - 1, self.levels), core)
        return self.copy(
            self.full.at[k, origin, core], self.sent_down.at[sem, k], self.got_down.at[sem, k], target
        )

    def across(self, k, origin, side, sem):
        group, level, core = self.at
        return self.copy(
            self.full.at[k, origin, side], self.sent_core.at[sem, k], self.got_core.at[sem, k], (group, level, 1 - core)
        )

    def start(self, k):
        group, level, core = self.at

        @pl.when(level < self.levels - 1)
        def _():
            self.up(k, 0, level, 0).start()

        @pl.when(level > 0)
        def _():
            self.down(k, 0, level, 0).start()

        self.across(k, level, core, 0).start()

    def hop(self, k, hop):
        group, level, core = self.at
        last = self.levels - 1

        @pl.when(level >= hop)
        def _():
            origin = level - hop
            self.up(k, hop, origin, hop - 1).wait_recv()
            if hop < last:

                @pl.when(level < last)
                def _():
                    self.up(k, hop, origin, hop).start()

            self.across(k, origin, core, hop).start()

        @pl.when(level + hop <= last)
        def _():
            origin = level + hop
            self.down(k, hop, origin, hop - 1).wait_recv()
            if hop < last:

                @pl.when(level > 0)
                def _():
                    self.down(k, hop, origin, hop).start()

            self.across(k, origin, core, last + hop).start()

    def ready(self, k):
        group, level, core = self.at
        last = self.levels - 1
        self.across(k, level, 1 - core, 0).wait_recv()
        for hop in range(1, self.levels):

            @pl.when(level >= hop)
            def _():
                self.across(k, level - hop, 1 - core, hop).wait_recv()

            @pl.when(level + hop <= last)
            def _():
                self.across(k, level + hop, 1 - core, last + hop).wait_recv()

    def drain(self):
        group, level, core = self.at
        last = self.levels - 1

        def one(k, _):
            self.across(k, level, core, 0).wait_send()
            for hop in range(self.levels):
                if hop < last:

                    @pl.when((level >= hop) & (level < last))
                    def _():
                        self.up(k, hop, level - hop, hop).wait_send()

                    @pl.when((level + hop <= last) & (level > 0))
                    def _():
                        self.down(k, hop, level + hop, hop).wait_send()

                if hop > 0:

                    @pl.when(level >= hop)
                    def _():
                        self.across(k, level - hop, core, hop).wait_send()

                    @pl.when(level + hop <= last)
                    def _():
                        self.across(k, level + hop, core, last + hop).wait_send()

            return 0

        lax.fori_loop(0, self.count, one, 0)


class Scatter:
    REFS = 4

    def __init__(self, at, sizes, count, refs):
        self.at, self.levels, self.count = at, sizes[1], count
        self.part, self.cross, self.inbox, self.total = refs[:4]
        self.sent_core, self.got_core, self.sent_up, self.got_up, self.sent_down, self.got_down = refs[4:]

    @staticmethod
    def scratch(count, sizes, piece):
        levels = sizes[1]
        dma = pltpu.SemaphoreType.DMA
        return (
            [
                pltpu.VMEM((2, levels, 2) + piece, jnp.bfloat16),
                pltpu.VMEM((count, levels) + piece, jnp.bfloat16),
                pltpu.VMEM((count, levels + 1) + piece, jnp.bfloat16),
                pltpu.VMEM(piece, jnp.float32),
            ]
            + [dma((count,)) for _ in range(2)]
            + [dma((levels, count)) for _ in range(4)]
        )

    def across(self, k):
        group, level, core = self.at
        return pltpu.make_async_remote_copy(
            src_ref=self.part.at[lax.rem(k, 2), :, 1 - core],
            dst_ref=self.cross.at[k],
            send_sem=self.sent_core.at[k],
            recv_sem=self.got_core.at[k],
            device_id=(group, level, 1 - core),
            device_id_type=MESH,
        )

    def up(self, k, owner):
        group, level, core = self.at
        return pltpu.make_async_remote_copy(
            src_ref=self.cross.at[k, owner],
            dst_ref=self.inbox.at[k, owner + 1],
            send_sem=self.sent_up.at[owner, k],
            recv_sem=self.got_up.at[owner, k],
            device_id=(group, lax.rem(level + 1, self.levels), core),
            device_id_type=MESH,
        )

    def down(self, k, owner):
        group, level, core = self.at
        return pltpu.make_async_remote_copy(
            src_ref=self.cross.at[k, owner],
            dst_ref=self.inbox.at[k, owner],
            send_sem=self.sent_down.at[owner, k],
            recv_sem=self.got_down.at[owner, k],
            device_id=(group, lax.rem(level + self.levels - 1, self.levels), core),
            device_id_type=MESH,
        )

    def free(self, k):
        @pl.when(k >= 2)
        def _():
            self.across(k - 2).wait_send()

    def start(self, k):
        self.across(k).start()

    def join(self, k):
        core = self.at[2]
        self.across(k).wait_recv()
        for owner in range(self.levels):
            self.cross[k, owner] = lowered(
                wide(self.part[lax.rem(k, 2), owner, core]) + wide(self.cross[k, owner])
            )

    def step_up(self, k):
        level = self.at[1]
        for owner in range(self.levels - 1, 0, -1):

            @pl.when(level < owner)
            def _():
                @pl.when(level > 0)
                def _():
                    self.up(k, owner).wait_recv()
                    self.cross[k, owner] = lowered(wide(self.cross[k, owner]) + wide(self.inbox[k, owner + 1]))

                self.up(k, owner).start()

    def step_down(self, k):
        level = self.at[1]
        for owner in range(self.levels - 1):

            @pl.when(level > owner)
            def _():
                @pl.when(level < self.levels - 1)
                def _():
                    self.down(k, owner).wait_recv()
                    self.cross[k, owner] = lowered(wide(self.cross[k, owner]) + wide(self.inbox[k, owner]))

                self.down(k, owner).start()

    def steps(self, wave):
        level = self.at[1]
        above = wave - level
        below = wave - (self.levels - 1 - level)

        @pl.when(within(above, self.count) & (level < self.levels // 2))
        def _():
            self.step_up(above)

        @pl.when(within(below, self.count))
        def _():
            self.step_down(below)

        @pl.when(within(above, self.count) & (level >= self.levels // 2))
        def _():
            self.step_up(above)

    def finish(self, k):
        level = self.at[1]
        self.total[...] = wide(self.cross[k, level])

        @pl.when(level > 0)
        def _():
            self.up(k, level).wait_recv()
            self.total[...] += wide(self.inbox[k, level + 1])

        @pl.when(level < self.levels - 1)
        def _():
            self.down(k, level).wait_recv()
            self.total[...] += wide(self.inbox[k, level])

    def drain(self):
        level = self.at[1]

        def one(k, _):
            @pl.when(k >= self.count - 2)
            def _():
                self.across(k).wait_send()

            for owner in range(self.levels):

                @pl.when(level < owner)
                def _():
                    self.up(k, owner).wait_send()

                @pl.when(level > owner)
                def _():
                    self.down(k, owner).wait_send()

            return 0

        lax.fori_loop(0, self.count, one, 0)


def in_order(count, step):
    def body(number, carry):
        step(number)
        return carry

    lax.fori_loop(0, count, body, 0)


def span(number, size):
    return pl.ds(pl.multiple_of(number * size, size), size)


class Moves:
    def __init__(self, pairs, sems):
        self.pairs, self.sems = pairs, sems

    def copy(self, number):
        return pltpu.make_async_copy(*self.pairs[number], self.sems.at[number])

    def start(self, *numbers):
        for number in numbers:
            self.copy(number).start()

    def wait(self, *numbers):
        for number in numbers:
            self.copy(number).wait()


class Chunks:
    def __init__(self, pairs, size, sems):
        self.pairs, self.size, self.sems = pairs, size, sems

    def start(self, k):
        for number, (source, target) in enumerate(self.pairs):
            rows = span(k, self.size)
            pltpu.make_async_copy(source.at[rows], target.at[rows], self.sems.at[number, k]).start()

    def wait(self, count):
        def one(k, carry):
            for number, (source, target) in enumerate(self.pairs):
                rows = span(k, self.size)
                pltpu.make_async_copy(source.at[rows], target.at[rows], self.sems.at[number, k]).wait()
            return carry

        lax.fori_loop(0, count, one, 0)


def matmul(left, right):
    return jnp.dot(left, right, preferred_element_type=jnp.float32)


def decay_tile(near, far, size, bounds, rate):
    rows = near * size + lax.broadcasted_iota(jnp.int32, (size, 1), 0)
    columns = far * size + lax.broadcasted_iota(jnp.int32, (1, size), 1)
    row_seq, column_seq = jnp.zeros((size, 1), jnp.int32), jnp.zeros((1, size), jnp.int32)
    for number in range(1, SEQ_DEV):
        row_seq += (rows >= bounds[number]).astype(jnp.int32)
        column_seq += (columns >= bounds[number]).astype(jnp.int32)
    distance = rows - columns
    valid = (distance >= 0) & (row_seq == column_seq)
    return (
        jnp.where(valid, jnp.exp(jnp.maximum(distance, 0).astype(jnp.float32) * rate[0]), 0.0)
        * QK_DIM ** (-0.5)
    )


class Swap:
    def __init__(self, at, sizes, items, sems, halves=None):
        self.at, self.count, self.items = at, sizes[0], items
        self.local, self.sent, self.got = sems
        self.halves = halves
        self.plane = halves is not None and sizes[0] == 4

    @staticmethod
    def scratch(items, sizes):
        ways = max(6, sizes[0] - 1)
        return [
            pltpu.SemaphoreType.DMA((items,)),
            pltpu.SemaphoreType.DMA((items, ways)),
            pltpu.SemaphoreType.DMA((items, ways)),
        ]

    def block(self, number, owner, half=None):
        source, target, axis = self.items[number]
        rows, columns = source.shape
        size = source.shape[axis] // self.count
        height = size if axis == 0 else rows
        begin = 0
        if half is not None:
            height //= 2
            begin = half * height
        if axis == 0:
            return source.at[pl.ds(pl.multiple_of(owner * size + begin, height), height)]
        return source.at[pl.ds(begin, height), pl.ds(pl.multiple_of(owner * size, size), size)]

    def half(self, number, slot, half):
        target = self.items[number][1]
        height = target.shape[1] // 2
        return target.at[slot, pl.ds(half * height, height)]

    def copy(self, number, source, place, way, peer):
        return pltpu.make_async_remote_copy(
            src_ref=source,
            dst_ref=place,
            send_sem=self.sent.at[number, way],
            recv_sem=self.got.at[number, way],
            device_id=(peer,) + self.at[1:],
            device_id_type=MESH,
        )

    def own(self, number):
        return pltpu.make_async_copy(
            self.block(number, self.at[0]), self.items[number][1].at[0], self.local.at[number]
        )

    def away(self, number, k):
        peer = lax.rem(self.at[0] + k, self.count)
        return self.copy(number, self.block(number, peer), self.items[number][1].at[k], k - 1, peer)

    def across(self, number, way):
        near = beside(self.at[0])
        return self.copy(
            number, self.block(number, near[2], way), self.halves[number].at[way], way, near[way]
        )

    def direct(self, number, way):
        near = beside(self.at[0])
        return self.copy(
            number, self.block(number, near[way], way), self.half(number, 1 + way, way), 2 + way, near[way]
        )

    def added(self, number, way):
        peer = beside(self.at[0])[1 - way]
        return self.copy(
            number, self.block(number, peer, way), self.half(number, 2 - way, way), 4 + way, peer
        )

    def start(self, *numbers):
        for number in numbers:
            if self.plane:
                for way in range(2):
                    self.across(number, way).start()
                for way in range(2):
                    self.direct(number, way).start()
            else:
                for k in range(1, self.count):
                    self.away(number, k).start()
            self.own(number).start()

    def relay(self, *numbers):
        if self.plane:
            near = beside(self.at[0])
            for number in numbers:
                for way in range(2):
                    self.across(number, way).wait_recv()
                    part = self.block(number, near[1 - way], way)
                    part[...] = lowered(wide(part[...]) + wide(self.halves[number][way]))
                    self.added(number, way).start()

    def wait(self, *numbers):
        for number in numbers:
            self.own(number).wait()
            if self.plane:
                for way in range(2):
                    self.across(number, way).wait_send()
                    self.direct(number, way).wait()
                    self.added(number, way).wait()
            else:
                for k in range(1, self.count):
                    self.away(number, k).wait()


def half_blocks(items, sizes):
    room = []
    for whole, axis in items:
        shape = list(whole.shape)
        shape[axis] //= sizes[0]
        room.append(pltpu.VMEM((2, shape[0] // 2, shape[1]), jnp.bfloat16))
    return room


def quarters(source, target):
    rows = source.shape[0]
    run = rows // 4
    return [(source.at[pl.ds(k * run, run)], target, 0, rows, k * run) for k in range(4)]


def deal_kernel(sizes, tokens, gains, *refs):
    masters, refs = refs[:8], refs[8:]
    tokens_out, gains_out, *refs = refs
    rounded_out, refs = refs[:8], refs[8:]
    spread_sems, refs = refs[:3], refs[3:]
    small_sems, refs = refs[:3], refs[3:]
    held, refs = refs[:8], refs[8:]
    rounded, refs = refs[:8], refs[8:]
    load_sems, store_sems, tokens_held, gains_held = refs
    at = around(AXES)
    loads = Moves(list(zip(masters, held)) + [(tokens, tokens_held), (gains, gains_held)], load_sems)
    stores = Moves(list(zip(rounded, rounded_out)), store_sems)
    loads.start(8, 9, *range(8))
    greet(plane_peers(at, sizes))
    loads.wait(8, 9)
    spread = Spread(at, sizes, quarters(tokens_held, tokens_out), spread_sems)
    small = Spread(at, sizes, [(gains_held, gains_out, 0)], small_sems, relay=False)
    spread.start(*range(4))
    small.start(0)
    for number in range(8):
        loads.wait(number)

        def block(k):
            rows = span(k, 32)
            rounded[number][rows, :] = lowered(held[number][rows, :])

        in_order(held[number].shape[0] // 32, block)
        stores.start(number)
    for number in range(4):
        spread.relay(number)
    stores.wait(*range(8))
    small.wait(0)
    spread.wait(*range(4))
    small.drain(0)
    spread.drain(*range(4))


def open_kernel(sizes, shards, gain, *refs):
    x_part, gain, *refs = (shards, gain) + refs
    sources, refs = refs[:5], refs[5:]
    normed_out, query_out, key_out, value_out, swish_out, *refs = refs
    weight_outs, refs = refs[:5], refs[5:]
    rows_out, unit_out, scale_out, *refs = refs
    full, *refs = refs
    gather_sems, refs = refs[:6], refs[6:]
    spread_sems, refs = refs[:3], refs[3:]
    weights, refs = refs[:4], refs[4:]
    normed, query, keys, values, swish, load_sem, out_sem, weight_sem, normed_sem, shard = refs
    at = around(AXES)
    group, level, core = at
    place = 2 * level + core
    count, levels, _, chunk, width = full.shape
    ranks = 2 * levels
    load = pltpu.make_async_copy(x_part, full.at[:, level, core], load_sem)
    load.start()
    load_shard = pltpu.make_async_copy(sources[4], shard, weight_sem.at[4])
    load_shard.start()
    greet(plane_peers(at, sizes) + column_peers(at, sizes))
    items = [(s, t, 0) for s, t in zip(sources[:4], weights)] + [(shard, weight_outs[4], 1)]
    spread = Spread(at, sizes, items, spread_sems)
    gather = Gather(at, sizes, count, full, gather_sems)
    load.wait()
    gather.start(0)
    load_shard.wait()
    spread.start(0, 1, 2)
    piece = chunk // ranks

    def norm(k):
        def block(number, carry):
            rows = span(number, 16)
            value = jnp.concatenate(
                [wide(full[k, q, c, rows, :]) for q in range(levels) for c in range(2)], axis=1
            )
            unit, scale = layer_norm(value, EPSILON)
            where = pl.ds(pl.multiple_of(k * chunk + number * 16, 16), 16)
            normed[where, :] = lowered(unit * gain[...])
            mine = wide(full[k, level, core, rows, :])
            mean = jnp.mean(value, -1, keepdims=True)
            unit_out[where, :] = (mine - mean) * scale
            scale_out[where, :] = jnp.broadcast_to(scale, (16, 128))
            return carry

        lax.fori_loop(0, chunk // 16, block, 0)
        mine = span(place, piece)
        rows_out[span(k, piece), :] = jnp.concatenate(
            [full[k, q, c, mine, :] for q in range(levels) for c in range(2)], axis=1
        )
        pltpu.make_async_copy(
            normed.at[span(k, chunk)], normed_out.at[span(k, chunk)], normed_sem.at[k]
        ).start()

    def wave(number):
        @pl.when(number + 1 < count)
        def _():
            gather.start(number + 1)

        for hop in range(levels - 1, 0, -1):

            @pl.when(within(number - hop, count))
            def _():
                gather.hop(number - hop, hop)

        for step, relayed, started in ((1, 0, None), (2, 1, 3), (4, 2, 4), (7, 3, None)):

            @pl.when(number == step)
            def _():
                spread.relay(relayed)
                if started is not None:
                    spread.start(started)

        @pl.when(within(number - levels, count))
        def _():
            gather.ready(number - levels)
            norm(number - levels)

    in_order(count + levels, wave)
    spread.relay(4)
    outs = [(query, query_out), (keys, key_out), (values, value_out), (swish, swish_out)]
    for number, (held, out) in enumerate(outs):
        spread.wait(number)
        pltpu.make_async_copy(weights[number], weight_outs[number], weight_sem.at[number]).start()

        def rows(k):
            where = span(k, chunk)
            held[where, :] = matmul(normed[where, :], weights[number][...]).astype(held.dtype)

        in_order(count, rows)
        pltpu.make_async_copy(held, out, out_sem.at[number]).start()
    spread.wait(4)
    for number, (held, out) in enumerate(outs):
        pltpu.make_async_copy(held, out, out_sem.at[number]).wait()
        pltpu.make_async_copy(weights[number], weight_outs[number], weight_sem.at[number]).wait()
    spread.drain(*range(5))
    gather.drain()

    def stored(k):
        pltpu.make_async_copy(
            normed.at[span(k, chunk)], normed_out.at[span(k, chunk)], normed_sem.at[k]
        ).wait()

    in_order(count, stored)


def middle_kernel(sizes, bounds, rate, gain, *refs):
    ins, refs = refs[:6], refs[6:]
    sources, refs = refs[:4], refs[4:]
    normed_out, gate_out, up_out, hidden_out, resid_out, retained_out, mixed_out, *refs = refs
    gate_w_out, up_w_out, down_w_out, dy_out, *refs = refs
    held, refs = refs[:6], refs[6:]
    query, keys, values, swish, out_w, x_rows = held
    scatter_refs, refs = refs[:10], refs[10:]
    full, *refs = refs
    gather_sems, refs = refs[:6], refs[6:]
    spread_sems, refs = refs[:3], refs[3:]
    gate_w, up_w, gate, up, hidden, resid, retained, mixed_in, refs = *refs[:8], refs[8:]
    load_sems, chunk_sems, normed_sems, weight_sems, resid_sem, down_shard, dy_shard = refs
    at = around(AXES)
    group, level, core = at
    count, levels, _, piece, width = full.shape
    chunk = 2 * levels * piece
    loads = Moves(list(zip(ins, held)) + [(sources[2], down_shard), (sources[3], dy_shard)], load_sems)
    loads.start(6, 7, *range(6))
    greet(plane_peers(at, sizes) + column_peers(at, sizes))
    spread = Spread(
        at,
        sizes,
        [
            (sources[0], gate_w, 0),
            (sources[1], up_w, 0),
            (down_shard, down_w_out, 1),
        ]
        + quarters(dy_shard, dy_out),
        spread_sems,
    )
    loads.wait(6, 7)
    spread.start(0, 1)
    scatter = Scatter(at, sizes, count, scatter_refs)
    gather = Gather(at, sizes, count, full, gather_sems)
    weights = Moves([(gate_w, gate_w_out), (up_w, up_w_out)], weight_sems)
    early = Chunks([(retained, retained_out), (mixed_in, mixed_out)], chunk, chunk_sems.at[:2])
    late = Chunks([(gate, gate_out), (up, up_out), (hidden, hidden_out)], chunk, chunk_sems.at[2:])
    loads.wait(*range(6))
    tile = 512

    def stores(k):
        copies = []
        for q in range(levels):
            for c in range(2):
                rows = pl.ds(pl.multiple_of(k * chunk + (2 * q + c) * piece, piece), piece)
                copies.append(
                    pltpu.make_async_copy(full.at[k, q, c], normed_out.at[rows], normed_sems.at[2 * q + c, k])
                )
        return copies

    def first(k):
        where = span(k, chunk)
        retained[where, :] = jnp.zeros((chunk, retained.shape[1]), jnp.float32)

        def block(j, carry):
            there = span(j, chunk)
            decay = decay_tile(k, j, chunk, bounds, rate)
            weight = lowered(inner_rows(query[where, :], keys[there, :]) * decay)
            retained[where, :] += matmul(weight, values[there, :])
            return carry

        lax.fori_loop(0, k + 1, block, 0)
        normed, _ = layer_norm(retained[where, :], GROUP_EPS)
        value = swish[where, :]
        mixed_in[where, :] = lowered(value * jax.nn.sigmoid(value) * normed)
        early.start(k)
        scatter.free(k)
        rows = mixed_in[where, :]
        for column in range(0, width, tile):
            value = matmul(rows, out_w[:, column : column + tile])
            scatter.part[lax.rem(k, 2), :, :, :, column : column + tile] = lowered(value).reshape(
                levels, 2, piece, tile
            )
        scatter.start(k)

    def norm(k):
        scatter.finish(k)

        def block(number, carry):
            sub = span(number, 16)
            where = pl.ds(pl.multiple_of(k * piece + number * 16, 16), 16)
            value = wide(x_rows[where, :]) + scatter.total[sub, :]
            resid[where, :] = value
            unit, _ = layer_norm(value, EPSILON)
            full[k, level, core, sub, :] = lowered(unit * gain[...])
            return carry

        lax.fori_loop(0, piece // 16, block, 0)
        gather.start(k)

    def last(k):
        gather.ready(k)
        for copy in stores(k):
            copy.start()
        rows = full[k].reshape(chunk, width)
        where = span(k, chunk)
        gate[where, :] = matmul(rows, gate_w[...])
        up[where, :] = matmul(rows, up_w[...])
        hidden[where, :] = lowered(jax.nn.gelu(gate[where, :]) * up[where, :])
        late.start(k)

    lag = levels

    def wave(number):
        @pl.when(number < count)
        def _():
            first(number)

        for hop in range(levels - 1, 0, -1):

            @pl.when(within(number - lag - hop, count))
            def _():
                gather.hop(number - lag - hop, hop)

        @pl.when(within(number - lag, count))
        def _():
            norm(number - lag)

        @pl.when(within(number - 1, count))
        def _():
            scatter.join(number - 1)

        scatter.steps(number - 1)

        for step, relayed, started in (
            (2, (0,), (2,)),
            (4, (1,), (3, 4)),
            (6, (2,), (5, 6)),
            (8, (3,), ()),
            (9, (4,), ()),
            (11, (5,), ()),
        ):

            @pl.when(number == step)
            def _():
                spread.relay(*relayed)
                spread.start(*started)

        @pl.when(number == 2 * lag - 1)
        def _():
            spread.wait(0, 1)
            weights.start(0, 1)

        @pl.when(within(number - 2 * lag + 1, count))
        def _():
            last(number - 2 * lag + 1)

    in_order(count + 2 * lag - 1, wave)
    store_resid = pltpu.make_async_copy(resid, resid_out, resid_sem)
    store_resid.start()
    spread.relay(6)
    spread.wait(2, 3, 4, 5, 6)
    spread.drain(*range(7))
    scatter.drain()
    gather.drain()
    weights.wait(0, 1)
    store_resid.wait()
    early.wait(count)
    late.wait(count)

    def stored(k):
        for copy in stores(k):
            copy.wait()

    in_order(count, stored)


def feed_kernel(sizes, dy_part, *refs):
    ins, refs = refs[:5], refs[5:]
    mixed_out, gate_grad_out, up_grad_out, dy_rows_out, down_grad_out, *refs = refs
    held, refs = refs[:5], refs[5:]
    hidden, down_w, resid, gate, up = held
    scatter_refs, refs = refs[:10], refs[10:]
    full, *refs = refs
    gather_sems, refs = refs[:6], refs[6:]
    tile_acc, down_acc, down_grad, mixed, gate_grad, up_grad, dy_rows, refs = *refs[:7], refs[7:]
    load_sem, load_sems, chunk_sems, end_sems = refs
    at = around(AXES)
    group, level, core = at
    place = 2 * level + core
    count, levels, _, chunk, width = full.shape
    ranks = 2 * levels
    piece = chunk // ranks
    load = pltpu.make_async_copy(dy_part, full.at[:, level, core], load_sem)
    load.start()
    loads = Moves(list(zip(ins, held)), load_sems)
    loads.start(*range(5))
    greet(column_peers(at, sizes))
    scatter = Scatter(at, sizes, count, scatter_refs)
    gather = Gather(at, sizes, count, full, gather_sems)
    store = Chunks(
        [(mixed, mixed_out), (gate_grad, gate_grad_out), (up_grad, up_grad_out)], chunk, chunk_sems
    )
    early = Chunks(store.pairs[:1], chunk, chunk_sems.at[:1])
    late = Chunks(store.pairs[1:], chunk, chunk_sems.at[1:])
    load.wait()
    gather.start(0)
    loads.wait(0, 1, 2)
    down_acc[...] = jnp.zeros(down_acc.shape, jnp.float32)

    def first(k):
        scatter.free(k)
        rows = hidden[span(k, chunk), :]
        mine = span(place, piece)
        for rank in range(ranks):
            columns = slice(rank * width, (rank + 1) * width)
            tile_acc[...] = matmul(rows, down_w[:, columns])
            tile_acc[mine, :] += resid[span(k, piece), columns]
            scatter.part[lax.rem(k, 2), rank // 2, rank % 2] = lowered(tile_acc[...])
        scatter.start(k)

    def last(k):
        gather.ready(k)
        where = span(k, chunk)
        rows = jnp.concatenate([full[k, q, c] for q in range(levels) for c in range(2)], axis=1)
        back = inner_rows(rows, down_w[...])
        mine = span(place, piece)
        dy_rows[span(k, piece), :] = jnp.concatenate(
            [full[k, q, c, mine, :] for q in range(levels) for c in range(2)], axis=1
        )
        g, u = gate[where, :], up[where, :]
        root = 0.7978845608028654
        bend = jnp.tanh(root * (g + 0.044715 * g * g * g))
        curve = 0.5 * (1.0 + bend)
        slope = curve + 0.5 * g * (1.0 - bend * bend) * root * (1.0 + 0.134145 * g * g)
        gate_grad[where, :] = lowered(back * u * slope)
        up_grad[where, :] = lowered(back * g * curve)
        late.start(k)
        for rank in range(ranks):
            columns = slice(rank * width, (rank + 1) * width)
            down_acc[:, columns] += inner_cols(hidden[where, :], full[k, rank // 2, rank % 2])

    lag = levels - 1

    def wave(number):
        @pl.when(number + 1 < count)
        def _():
            gather.start(number + 1)

        @pl.when(number < count)
        def _():
            first(number)

        for hop in range(levels - 1, 0, -1):

            @pl.when(within(number - hop, count))
            def _():
                gather.hop(number - hop, hop)

        @pl.when(number < count)
        def _():
            scatter.join(number)

        scatter.steps(number)

        @pl.when(within(number - lag, count))
        def _():
            scatter.finish(number - lag)
            mixed[span(number - lag, chunk), :] = lowered(scatter.total[...])
            early.start(number - lag)

        @pl.when(number == levels)
        def _():
            loads.wait(3, 4)

        @pl.when(within(number - levels, count))
        def _():
            last(number - levels)

    in_order(count + levels, wave)
    down_grad[...] = lowered(down_acc[...])
    ends = Moves([(down_grad, down_grad_out), (dy_rows, dy_rows_out)], end_sems)
    ends.start(0, 1)
    scatter.drain()
    gather.drain()
    store.wait(count)
    ends.wait(0, 1)


def back_kernel(sizes, bounds, rate, gain, *refs):
    ins, refs = refs[:13], refs[13:]
    mixed_src, down_src, *refs = refs
    branch_out, swish_out, query_out, key_out, value_out, gain_out, *refs = refs
    mixed_dst, down_dst, gate_dst, up_dst, *refs = refs
    held, refs = refs[:13], refs[13:]
    gate_grad, up_grad, gate_w, up_w, resid, dy_rows, normed_mid, out_w, retained, swish, *held_qkv = held
    query, keys, values = held_qkv
    scatter_refs, refs = refs[:10], refs[10:]
    full, *refs = refs
    gather_sems, refs = refs[:6], refs[6:]
    spread_sems, refs = refs[:3], refs[3:]
    swap_sems, refs = refs[:3], refs[3:]
    gate_total, up_total, swish_grad, delta, query_acc, key_acc, value_acc, refs = *refs[:7], refs[7:]
    load_sems, chunk_sems, store_sems, end_sems, mixed_held, down_held, *halves = refs
    at = around(AXES)
    group, level, core = at
    count, levels, _, piece, width = full.shape
    chunk = 2 * levels * piece
    loads = Moves(list(zip(ins, held)) + [(mixed_src, mixed_held), (down_src, down_held)], load_sems)
    loads.start(13, 14, *range(13))
    greet(plane_peers(at, sizes) + column_peers(at, sizes))
    loads.wait(13, 14)
    spread = Spread(at, sizes, quarters(mixed_held, mixed_dst), spread_sems)
    swap = Swap(at, sizes, [(down_held, down_dst, 1), (gate_total, gate_dst, 0), (up_total, up_dst, 0)], swap_sems, halves)
    spread.start(*range(4))
    scatter = Scatter(at, sizes, count, scatter_refs)
    gather = Gather(at, sizes, count, full, gather_sems)
    store = Chunks([(swish_grad, swish_out), (query, query_out)], chunk, chunk_sems)
    gain_out[...] = jnp.zeros(gain_out.shape, jnp.float32)
    key_acc[...] = jnp.zeros(key_acc.shape, jnp.float32)
    value_acc[...] = jnp.zeros(value_acc.shape, jnp.float32)
    loads.wait(0, 1, 2, 3)
    tile = 512

    def stores(k):
        copies = []
        for q in range(levels):
            for c in range(2):
                rows = pl.ds(pl.multiple_of(k * chunk + (2 * q + c) * piece, piece), piece)
                copies.append(
                    pltpu.make_async_copy(full.at[k, q, c], branch_out.at[rows], store_sems.at[2 * q + c, k])
                )
        return copies

    def first(k):
        scatter.free(k)
        where = span(k, chunk)
        for column in range(0, width, tile):
            columns = slice(column, column + tile)
            value = inner_rows(gate_grad[where, :], gate_w[columns, :])
            value += inner_rows(up_grad[where, :], up_w[columns, :])
            scatter.part[lax.rem(k, 2), :, :, :, columns] = lowered(value).reshape(levels, 2, piece, tile)
        scatter.start(k)

    def weigh(k):
        columns = span(k, chunk)
        rows = normed_mid[:, columns]
        gate_total[columns, :] = lowered(inner_cols(rows, gate_grad[...]))
        up_total[columns, :] = lowered(inner_cols(rows, up_grad[...]))

    def norm(k):
        scatter.finish(k)

        def block(number, carry):
            sub = span(number, 16)
            where = pl.ds(pl.multiple_of(k * piece + number * 16, 16), 16)
            unit, scale = layer_norm(resid[where, :], EPSILON)
            grad = scatter.total[sub, :]
            outer = grad * unit
            gain_out[...] += outer[:8] + outer[8:]
            value = wide(dy_rows[where, :]) + norm_back(grad * gain[...], unit, scale)
            full[k, level, core, sub, :] = lowered(value)
            return carry

        lax.fori_loop(0, piece // 16, block, 0)
        gather.start(k)

    def last(k):
        gather.ready(k)
        for copy in stores(k):
            copy.start()
        rows = full[k].reshape(chunk, width)
        where = span(k, chunk)
        grad = inner_rows(rows, out_w[...])
        normed, scale = layer_norm(retained[where, :], GROUP_EPS)
        value = swish[where, :]
        gated = jax.nn.sigmoid(value)
        swish_grad[where, :] = lowered(grad * normed * gated * (1.0 + value * (1.0 - gated)))
        delta[...] = lowered(norm_back(grad * value * gated, normed, scale))
        query_acc[...] = jnp.zeros(query_acc.shape, jnp.float32)

        def block(j, carry):
            there = span(j, chunk)
            decay = decay_tile(k, j, chunk, bounds, rate)
            weight = lowered(inner_rows(query[where, :], keys[there, :]) * decay)
            score = lowered(inner_rows(delta[...], values[there, :]) * decay)
            query_acc[...] += matmul(score, keys[there, :])
            key_acc[there, :] += inner_cols(score, query[where, :])
            value_acc[there, :] += inner_cols(weight, delta[...])
            return carry

        lax.fori_loop(0, k + 1, block, 0)
        query[where, :] = lowered(query_acc[...])
        store.start(k)

    lag = levels
    tiles = width // chunk

    def wave(number):
        @pl.when(number < count)
        def _():
            first(number)

        for hop in range(levels - 1, 0, -1):

            @pl.when(within(number - lag - hop, count))
            def _():
                gather.hop(number - lag - hop, hop)

        @pl.when(number == lag)
        def _():
            loads.wait(4, 5)

        @pl.when(within(number - lag, count))
        def _():
            norm(number - lag)

        @pl.when(within(number - 1, count))
        def _():
            scatter.join(number - 1)

        scatter.steps(number - 1)

        @pl.when(number == 2 * lag - 1)
        def _():
            loads.wait(7, 8, 9, 10, 11, 12)

        @pl.when(within(number - 2 * lag + 1, count))
        def _():
            last(number - 2 * lag + 1)

        @pl.when(number == 0)
        def _():
            loads.wait(6)

        @pl.when(number < tiles // 2)
        def _():
            weigh(2 * number)
            weigh(2 * number + 1)

        for step, relayed in ((1, 0), (2, 1), (3, 2), (4, 3)):

            @pl.when(number == step)
            def _():
                spread.relay(relayed)

        @pl.when(number == 1)
        def _():
            swap.start(0)

        @pl.when(number == tiles // 2)
        def _():
            swap.start(1, 2)

        for step, relayed in ((5, 0), (7, 1), (9, 2)):

            @pl.when(number == step)
            def _():
                swap.relay(relayed)

    in_order(count + 2 * lag - 1, wave)
    keys[...] = lowered(key_acc[...])
    values[...] = lowered(value_acc[...])
    ends = Moves([(keys, key_out), (values, value_out)], end_sems)
    ends.start(0, 1)
    spread.wait(*range(4))
    swap.wait(0, 1, 2)
    spread.drain(*range(4))
    scatter.drain()
    gather.drain()
    store.wait(count)
    ends.wait(0, 1)

    def stored(k):
        for copy in stores(k):
            copy.wait()

    in_order(count, stored)


def close_kernel(sizes, gain, gain_two, *refs):
    ins, refs = refs[:13], refs[13:]
    grad_out, gains_out, *refs = refs
    targets, refs = refs[:5], refs[5:]
    held, refs = refs[:13], refs[13:]
    deltas, weights = held[:4], held[4:8]
    normed_in, branch, mixed_in, unit, scale = held[8:]
    grads, refs = refs[:5], refs[5:]
    scatter_refs, refs = refs[:10], refs[10:]
    swap_sems, refs = refs[:3], refs[3:]
    sums, line_one, share, packed, gains, gains_in, refs = *refs[:6], refs[6:]
    load_sems, sums_sent, sums_got, gain_sent, gain_got, refs = *refs[:5], refs[5:]
    spread_sems, refs = refs[:3], refs[3:]
    small_sems, halves = refs[:3], refs[3:]
    at = around(AXES)
    group, level, core = at
    place = 2 * level + core
    groups = sizes[0]
    scatter = Scatter(at, sizes, sums.shape[1], scatter_refs)
    _, levels, _, chunk, width = scatter.part.shape
    count, ranks = sums.shape[1], 2 * levels
    rows_all = count * chunk
    loads = Moves(list(zip(ins, held)), load_sems)
    loads.start(*range(13))
    greet(plane_peers(at, sizes) + column_all(at, sizes))
    swap = Swap(at, sizes, list(zip(grads, targets, SWAP_AXES)), swap_sems, halves)
    small = Swap(at, sizes, [(gains, gains_in, 1)], small_sems)
    spread = Spread(
        at,
        sizes,
        [(share.at[pl.ds(k * chunk, chunk)], grad_out, 0, rows_all, k * chunk) for k in range(count)],
        spread_sems,
    )
    line_one[...] = jnp.zeros(line_one.shape, jnp.float32)
    loads.wait(*range(9))
    mine = pl.ds(pl.multiple_of(place * width, width), width)

    def first(k):
        scatter.free(k)
        where = span(k, chunk)
        rows = [d[where, :] for d in deltas]
        one = jnp.zeros((chunk, width), jnp.float32)
        two = jnp.zeros((chunk, width), jnp.float32)
        for rank in range(ranks):
            columns = slice(rank * width, (rank + 1) * width)
            value = inner_rows(rows[0], weights[0][columns, :])
            for row, weight in zip(rows[1:], weights[1:]):
                value += inner_rows(row, weight[columns, :])
            scatter.part[lax.rem(k, 2), rank // 2, rank % 2] = lowered(value)
            one += value * gain[:, columns]
            two += value * wide(normed_in[where, columns])
        scatter.start(k)
        ones = jnp.ones((8, width), jnp.float32)
        flat = [
            lax.dot_general(
                ones,
                item,
                (((1,), (1,)), ((), ())),
                precision=lax.Precision.HIGHEST,
                preferred_element_type=jnp.float32,
            )
            for item in (one, two)
        ]
        line = lax.broadcasted_iota(jnp.int32, (8, chunk), 0)
        sums[place, k] = jnp.where(line == 0, flat[0], flat[1])
        for j in range(1, ranks):
            sums_copy(k, j, place).start()

    def sums_copy(k, j, owner):
        peer = lax.rem(place + j, ranks)
        return pltpu.make_async_remote_copy(
            src_ref=sums.at[owner, k],
            dst_ref=sums.at[owner, k],
            send_sem=sums_sent.at[j - 1, k],
            recv_sem=sums_got.at[j - 1, k],
            device_id=(group, peer // 2, lax.rem(peer, 2)),
            device_id_type=MESH,
        )

    def pack_copy(j, owner):
        peer = lax.rem(place + j, ranks)
        return pltpu.make_async_remote_copy(
            src_ref=packed.at[owner],
            dst_ref=packed.at[owner],
            send_sem=gain_sent.at[j - 1],
            recv_sem=gain_got.at[j - 1],
            device_id=(group, peer // 2, lax.rem(peer, 2)),
            device_id_type=MESH,
        )

    def sender(j):
        return lax.rem(place + ranks - j, ranks)

    def finish(k):
        scatter.finish(k)
        for j in range(1, ranks):
            sums_copy(k, j, sender(j)).wait_recv()
        line = lax.broadcasted_iota(jnp.int32, (8, 128), 0)
        lane = lax.broadcasted_iota(jnp.int32, (8, 128), 1)
        means = lax.dot_general(
            jnp.sum(sums[:, k], 0),
            jnp.where(line == lane, 1.0 / (ranks * width), 0.0),
            (((0,), (0,)), ((), ())),
            precision=lax.Precision.HIGHEST,
            preferred_element_type=jnp.float32,
        )
        where = span(k, chunk)
        value, normed = scatter.total[...], unit[where, :]
        outer = value * normed
        line_one[...] += jnp.sum(outer.reshape(chunk // 8, 8, width), 0)
        back = value * gain[:, mine] - means[:, :1] - normed * means[:, 1:2]
        share[where, :] = lowered(wide(branch[where, mine]) + scale[where, :1] * back)

    def weigh(number):
        if number == 4:

            def part(k):
                columns = span(k, chunk)
                grads[4][:, columns] = lowered(inner_cols(mixed_in[...], branch[:, columns]))
        else:

            def part(k):
                columns = span(k, chunk)
                grads[number][columns, :] = lowered(inner_cols(normed_in[:, columns], deltas[number][...]))

        in_order(ranks * width // chunk, part)
        swap.start(number)

    lag = levels - 1

    def wave(number):
        @pl.when(number < count)
        def _():
            first(number)

        @pl.when(number == 0)
        def _():
            weigh(3)

        for step, which in ((1, 2), (2, 0), (3, 1)):

            @pl.when(number == step)
            def _():
                weigh(which)

        @pl.when(number < count)
        def _():
            scatter.join(number)

        scatter.steps(number)

        @pl.when(number == lag)
        def _():
            loads.wait(9, 10, 11, 12)

        @pl.when(within(number - lag, count))
        def _():
            finish(number - lag)

        for k in range(count):

            @pl.when(number == lag + k)
            def _():
                spread.start(k)

            @pl.when(number == lag + k + 2)
            def _():
                spread.relay(k)

        @pl.when(number == lag + 1)
        def _():
            weigh(4)

        for step, relayed in ((2, 3), (4, 2), (5, 0), (6, 1), (8, 4)):

            @pl.when(number == step)
            def _():
                swap.relay(relayed)

    in_order(count + lag, wave)
    for k in (count - 2, count - 1):
        spread.relay(k)
    total = jnp.sum(gain_two[...], 0, keepdims=True)
    packed[place] = jnp.concatenate([total, jnp.sum(line_one[...], 0, keepdims=True)], axis=1)
    for j in range(1, ranks):
        pack_copy(j, place).start()
    for j in range(1, ranks):
        pack_copy(j, sender(j)).wait_recv()
    everything = ranks * width
    line = lax.broadcasted_iota(jnp.int32, (8, everything), 0)
    two = sum(packed[rank, :, :everything] for rank in range(ranks))
    one = jnp.concatenate([packed[rank, :, everything:] for rank in range(ranks)], axis=1)
    gains[...] = jnp.where(line == 0, one, two)
    small.start(0)
    small.wait(0)
    swap.wait(*range(5))
    spread.wait(*range(count))
    spread.drain(*range(count))
    gains_out[...] = jnp.sum(gains_in[...], 0)
    for j in range(1, ranks):
        pack_copy(j, place).wait_send()
    scatter.drain()

    def drain(k):
        for j in range(1, ranks):
            sums_copy(k, j, place).wait_send()

    in_order(count, drain)


def column_all(at, sizes):
    group, level, core = at
    return column_peers(at, sizes) + [
        (group, lax.rem(level + k, sizes[1]), 1 - core) for k in range(1, sizes[1])
    ]


def struct(shape, kind=jnp.bfloat16):
    return jax.ShapeDtypeStruct(shape, kind)


VMEM = pltpu.VMEM
DMA = pltpu.SemaphoreType.DMA


def kernel_call(body, number, ins, outs, scratch):
    places = {
        "vmem": pl.BlockSpec(memory_space=pltpu.VMEM),
        "smem": pl.BlockSpec(memory_space=pltpu.SMEM),
        "any": pl.BlockSpec(memory_space=pl.ANY),
    }
    return pl.pallas_call(
        body,
        out_shape=[shape for _, shape in outs],
        in_specs=[places[inside] for inside, _ in ins],
        out_specs=[places[inside] for inside, _ in outs],
        scratch_shapes=scratch,
        compiler_params=pltpu.CompilerParams(
            collective_id=number, has_side_effects=True, vmem_limit_bytes=60 * 2**20
        ),
    )(*[array for _, array in ins])


def spread_shape(shard, axis, sizes):
    shape = list(shard.shape)
    shape[axis] *= sizes[0]
    return struct(tuple(shape), shard.dtype)


def swap_shape(whole, axis, sizes):
    shape = list(whole.shape)
    shape[axis] //= sizes[0]
    return struct((3 if sizes[0] == 4 else sizes[0],) + tuple(shape), whole.dtype)


def anywhere(items):
    return [("any", item) for item in items]


def held_like(arrays):
    return [VMEM(a.shape, a.dtype) for a in arrays]


def pick(rows, whole):
    return whole.at[rows].get(mode="promise_in_bounds")


def shards(
    tokens,
    cotangent,
    lengths,
    dealing,
    w_query,
    w_key,
    w_value,
    w_swish,
    w_out,
    w_gate,
    w_up,
    w_down,
    gain_attn,
    gain_mlp,
):
    group = lax.axis_index("dp")
    place = lax.axis_index(("heads", "tensor"))
    rows_dev = tokens.shape[0]
    slice_width = tokens.shape[1]
    seq_count = lengths.shape[0]
    ident = jnp.arange(seq_count, dtype=jnp.int32)
    starts = jnp.cumsum(lengths) - lengths
    picked = lax.dynamic_slice_in_dim(dealing, group * SEQ_DEV, SEQ_DEV)
    match = picked[:, None] == ident[None, :]
    dealt_len = jnp.sum(jnp.where(match, lengths[None, :], 0), 1)
    home_start = jnp.sum(jnp.where(match, starts[None, :], 0), 1)
    dealt_start = jnp.cumsum(dealt_len) - dealt_len
    rows = jnp.arange(rows_dev, dtype=jnp.int32)
    seq_ids = jnp.sum((rows[:, None] >= dealt_start[None, :]).astype(jnp.int32), 1) - 1
    member = seq_ids[:, None] == jnp.arange(SEQ_DEV, dtype=jnp.int32)[None, :]
    source = jnp.sum(jnp.where(member, (home_start - dealt_start)[None, :], 0), 1) + rows
    sizes = (lax.axis_size("dp"), lax.axis_size("heads"))
    ranks = sizes[1] * lax.axis_size("tensor")
    chunk = ranks * PIECE
    count = rows_dev // chunk
    width = slice_width * ranks
    own = rows_dev // ranks
    qk_dim, v_dim, ff_dim = w_query.shape[1], w_value.shape[1], w_gate.shape[1]
    f32 = jnp.float32
    masters = (w_query, w_key, w_value, w_swish, w_out, w_gate, w_up, w_down)
    axes = (0, 0, 0, 0, 1, 0, 0, 1)
    gain_rows = jnp.pad(jnp.stack([gain_attn, gain_mlp]), ((0, 6), (0, 0)))
    rounded = [struct(w.shape) for w in masters]
    x_all, gains_all, *low = kernel_call(
        functools.partial(deal_kernel, sizes),
        0,
        anywhere((tokens, gain_rows) + masters),
        anywhere([spread_shape(tokens, 0, sizes), spread_shape(gain_rows, 0, sizes)] + rounded),
        Spread.scratch(4, sizes) + Spread.scratch(1, sizes) + held_like(masters) + held_like(rounded) + [DMA((10,)), DMA((8,))] + held_like((tokens, gain_rows)),
    )
    full_w = [spread_shape(w, a, sizes) for w, a in zip(low, axes)]
    gains_all = wide(lowered(gains_all.reshape(sizes[0], 8, -1)))
    wide_one = gains_all[:, 0].reshape(1, width)
    wide_two = gains_all[:, 1].reshape(1, width)
    x_part = pick(source, x_all)
    (
        normed_in,
        query,
        keys,
        values,
        swish_in,
        query_w,
        key_w,
        value_w,
        swish_w,
        out_w,
        x_rows,
        unit_share,
        scale_one,
    ) = kernel_call(
        functools.partial(open_kernel, sizes),
        1,
        [("any", x_part.reshape(count, chunk, slice_width)), ("vmem", wide_one)] + anywhere(low[:5]),
        anywhere(
            [
                struct((rows_dev, width)),
                struct((rows_dev, qk_dim)),
                struct((rows_dev, qk_dim)),
                struct((rows_dev, v_dim)),
                struct((rows_dev, v_dim), f32),
            ]
            + full_w[:5]
        )
        + [
            ("vmem", struct((own, width))),
            ("vmem", struct((rows_dev, slice_width), f32)),
            ("vmem", struct((rows_dev, 128), f32)),
        ],
        Gather.scratch(count, sizes, (chunk, slice_width))
        + Spread.scratch(5, sizes)
        + held_like(full_w[:4])
        + [
            VMEM((rows_dev, width), jnp.bfloat16),
            VMEM((rows_dev, qk_dim), jnp.bfloat16),
            VMEM((rows_dev, qk_dim), jnp.bfloat16),
            VMEM((rows_dev, v_dim), jnp.bfloat16),
            VMEM((rows_dev, v_dim), f32),
            DMA,
            DMA((4,)),
            DMA((5,)),
            DMA((count,)),
            VMEM(w_out.shape, jnp.bfloat16),
        ],
    )
    rate = jnp.log1p(-jnp.exp2(-5.0 - place.astype(f32))).reshape(1)
    middle_ins = (query, keys, values, swish_in, out_w, x_rows)
    normed_mid, gate, up_proj, hidden, resid, retained, mixed_in, gate_w, up_w, down_w, dy_all = kernel_call(
        functools.partial(middle_kernel, sizes),
        2,
        [("smem", dealt_start), ("smem", rate), ("vmem", wide_two)]
        + anywhere(middle_ins)
        + anywhere(low[5:] + [cotangent]),
        anywhere(
            [
                struct((rows_dev, width)),
                struct((rows_dev, ff_dim), f32),
                struct((rows_dev, ff_dim), f32),
                struct((rows_dev, ff_dim)),
                struct((own, width), f32),
                struct((rows_dev, v_dim), f32),
                struct((rows_dev, v_dim)),
            ]
            + full_w[5:]
            + [spread_shape(cotangent, 0, sizes)]
        ),
        held_like(middle_ins)
        + Scatter.scratch(count, sizes, (PIECE, width))
        + Gather.scratch(count, sizes, (PIECE, width))
        + Spread.scratch(7, sizes)
        + held_like(full_w[5:7])
        + [
            VMEM((rows_dev, ff_dim), f32),
            VMEM((rows_dev, ff_dim), f32),
            VMEM((rows_dev, ff_dim), jnp.bfloat16),
            VMEM((own, width), f32),
            VMEM((rows_dev, v_dim), f32),
            VMEM((rows_dev, v_dim), jnp.bfloat16),
            DMA((8,)),
            DMA((5, count)),
            DMA((ranks, count)),
            DMA((2,)),
            DMA,
        ]
        + held_like((low[7], cotangent)),
    )
    dy_part = pick(source, dy_all)
    feed_ins = (hidden, down_w, resid, gate, up_proj)
    mixed_share, delta_gate, delta_up, dy_rows, grad_down = kernel_call(
        functools.partial(feed_kernel, sizes),
        3,
        anywhere((dy_part.reshape(count, chunk, slice_width),) + feed_ins),
        anywhere(
            [
                struct((rows_dev, slice_width)),
                struct((rows_dev, ff_dim)),
                struct((rows_dev, ff_dim)),
                struct((own, width)),
                struct((ff_dim, width)),
            ]
        ),
        held_like(feed_ins)
        + Scatter.scratch(count, sizes, (chunk, slice_width))
        + Gather.scratch(count, sizes, (chunk, slice_width))
        + [
            VMEM((chunk, slice_width), f32),
            VMEM((ff_dim, width), f32),
            VMEM((ff_dim, width), jnp.bfloat16),
            VMEM((rows_dev, slice_width), jnp.bfloat16),
            VMEM((rows_dev, ff_dim), jnp.bfloat16),
            VMEM((rows_dev, ff_dim), jnp.bfloat16),
            VMEM((own, width), jnp.bfloat16),
            DMA,
            DMA((5,)),
            DMA((3, count)),
            DMA((2,)),
        ],
    )
    back_ins = (
        delta_gate,
        delta_up,
        gate_w,
        up_w,
        resid,
        dy_rows,
        normed_mid,
        out_w,
        retained,
        swish_in,
        query,
        keys,
        values,
    )
    delta_branch, delta_swish, delta_query, delta_keys, delta_values, gain_two_part, mixed_all, *ff_grads = (
        kernel_call(
            functools.partial(back_kernel, sizes),
            4,
            [("smem", dealt_start), ("smem", rate), ("vmem", wide_two)]
            + anywhere(back_ins)
            + anywhere((mixed_share, grad_down)),
            anywhere(
                [
                    struct((rows_dev, width)),
                    struct((rows_dev, v_dim)),
                    struct((rows_dev, qk_dim)),
                    struct((rows_dev, qk_dim)),
                    struct((rows_dev, v_dim)),
                ]
            )
            + [("vmem", struct((8, width), f32))]
            + anywhere(
                [
                    spread_shape(mixed_share, 0, sizes),
                    swap_shape(full_w[7], 1, sizes),
                    swap_shape(full_w[5], 0, sizes),
                    swap_shape(full_w[6], 0, sizes),
                ]
            ),
            held_like(back_ins)
            + Scatter.scratch(count, sizes, (PIECE, width))
            + Gather.scratch(count, sizes, (PIECE, width))
            + Spread.scratch(4, sizes)
            + Swap.scratch(3, sizes)
            + held_like(full_w[5:7])
            + [
                VMEM((rows_dev, v_dim), jnp.bfloat16),
                VMEM((chunk, v_dim), jnp.bfloat16),
                VMEM((chunk, qk_dim), f32),
                VMEM((rows_dev, qk_dim), f32),
                VMEM((rows_dev, v_dim), f32),
                DMA((15,)),
                DMA((2, count)),
                DMA((ranks, count)),
                DMA((2,)),
            ]
            + held_like((mixed_share, grad_down))
            + half_blocks([(full_w[7], 1), (full_w[5], 0), (full_w[6], 0)], sizes),
        )
    )
    close_ins = (
        delta_query,
        delta_keys,
        delta_values,
        delta_swish,
        query_w,
        key_w,
        value_w,
        swish_w,
        normed_in,
        delta_branch,
        mixed_in,
        unit_share,
        scale_one,
    )
    swaps = len(SWAP_AXES)
    grad_all, gains, *attn_grads = kernel_call(
        functools.partial(close_kernel, sizes),
        5,
        [("vmem", wide_one), ("vmem", gain_two_part)] + anywhere(close_ins),
        anywhere([struct((sizes[0] * rows_dev, slice_width))])
        + [("vmem", struct((8, gain_attn.shape[0]), f32))]
        + anywhere([swap_shape(w, a, sizes) for w, a in zip(full_w[:5], SWAP_AXES)]),
        held_like(close_ins)
        + held_like(full_w[:5])
        + Scatter.scratch(count, sizes, (chunk, slice_width))
        + Swap.scratch(swaps, sizes)
        + [
            VMEM((ranks, count, 8, chunk), f32),
            VMEM((8, slice_width), f32),
            VMEM((rows_dev, slice_width), jnp.bfloat16),
            VMEM((ranks, 1, width + slice_width), f32),
            VMEM((8, width), f32),
            VMEM((sizes[0], 8, gain_attn.shape[0]), f32),
            DMA((len(close_ins),)),
            DMA((ranks - 1, count)),
            DMA((ranks - 1, count)),
            DMA((ranks - 1,)),
            DMA((ranks - 1,)),
        ]
        + Spread.scratch(count, sizes)
        + Swap.scratch(1, sizes)
        + half_blocks(list(zip(full_w[:5], SWAP_AXES)), sizes),
    )
    grads = [jnp.sum(wide(g), 0) for g in attn_grads + ff_grads[1:] + ff_grads[:1]]
    slot_match = dealing[:, None] == ident[None, :]
    slot_len = jnp.sum(jnp.where(slot_match, lengths[None, :], 0), 1)
    slot_home = jnp.sum(jnp.where(slot_match, starts[None, :], 0), 1)
    per_group = slot_len.reshape(-1, SEQ_DEV)
    slot_start = (jnp.cumsum(per_group, 1) - per_group).reshape(-1)
    slot_base = ident // SEQ_DEV * rows_dev + slot_start - slot_home
    owner_base = jnp.sum(jnp.where(dealing[None, :] == ident[:, None], slot_base[None, :], 0), 1)
    global_rows = group * rows_dev + rows
    seq_of = jnp.sum((global_rows[:, None] >= starts[None, :]).astype(jnp.int32), 1) - 1
    targets = (
        jnp.sum(jnp.where(seq_of[:, None] == ident[None, :], owner_base[None, :], 0), 1)
        + global_rows
    )
    mixed_rows, grad_rows = pick(targets, mixed_all), pick(targets, grad_all)
    return (
        mixed_rows,
        grad_rows,
        grads[0],
        grads[1],
        grads[2],
        grads[3],
        grads[4],
        grads[5],
        grads[6],
        grads[7],
        gains[0],
        gains[1],
    )


def solution(mesh):
    in_specs = (
        P("dp", ("heads", "tensor")),
        P("dp", ("heads", "tensor")),
        P(),
        P(),
        P("dp", ("heads", "tensor")),
        P("dp", ("heads", "tensor")),
        P("dp", ("heads", "tensor")),
        P("dp", ("heads", "tensor")),
        P(("heads", "tensor"), "dp"),
        P("dp", ("heads", "tensor")),
        P("dp", ("heads", "tensor")),
        P(("heads", "tensor"), "dp"),
        P("dp"),
        P("dp"),
    )
    out_specs = (
        P("dp", ("heads", "tensor")),
        P("dp", ("heads", "tensor")),
        P("dp", ("heads", "tensor")),
        P("dp", ("heads", "tensor")),
        P("dp", ("heads", "tensor")),
        P("dp", ("heads", "tensor")),
        P(("heads", "tensor"), "dp"),
        P("dp", ("heads", "tensor")),
        P("dp", ("heads", "tensor")),
        P(("heads", "tensor"), "dp"),
        P("dp"),
        P("dp"),
    )
    return jax.shard_map(shards, mesh=mesh, in_specs=in_specs, out_specs=out_specs, check_vma=False)
```

```python
import functools

import jax
import jax.numpy as jnp
from jax import lax
from jax.experimental import pallas as pl
from jax.experimental.pallas import tpu as pltpu
from jax.sharding import PartitionSpec as P

QK_DIM = 256
SEQ_DEV = 3
PIECE = 32
AXES = ("dp", "heads", "tensor")
SWAP_AXES = (0, 0, 0, 0, 1)
MESH = pl.DeviceIdType.MESH


EPSILON = 1e-05
GROUP_EPS = 1.0


def layer_norm(values, epsilon):
    center = values - jnp.mean(values, -1, keepdims=True)
    scale = lax.rsqrt(jnp.mean(center * center, -1, keepdims=True) + epsilon)
    return (center * scale, scale)


def norm_back(grad, normed, scale):
    return scale * (
        grad
        - jnp.mean(grad, -1, keepdims=True)
        - normed * jnp.mean(grad * normed, -1, keepdims=True)
    )


def product(left, right):
    return jnp.dot(left, right, preferred_element_type=jnp.float32)


def inner_rows(left, right):
    return lax.dot_general(
        left, right, (((1,), (1,)), ((), ())), preferred_element_type=jnp.float32
    )


def inner_cols(left, right):
    return lax.dot_general(
        left, right, (((0,), (0,)), ((), ())), preferred_element_type=jnp.float32
    )


def lowered(value):
    return value.astype(jnp.bfloat16)


def around(axes):
    return tuple(lax.axis_index(name) for name in axes)


def wide(value):
    return value.astype(jnp.float32)


def within(number, count):
    return (number >= 0) & (number < count)


def greet(others):
    barrier = pltpu.get_barrier_semaphore()
    for other in others:
        pl.semaphore_signal(barrier, inc=1, device_id=other, device_id_type=MESH)
    pl.semaphore_wait(barrier, len(others))


def plane_peers(at, sizes):
    group, level, core = at
    return [(lax.rem(group + k, sizes[0]), level, core) for k in range(1, sizes[0])]


def column_peers(at, sizes):
    group, level, core = at
    return [(group, lax.rem(level + k, sizes[1]), core) for k in range(1, sizes[1])] + [
        (group, level, 1 - core)
    ]


def beside(group):
    return group + 1 - 2 * lax.rem(group, 2), lax.rem(group + 2, 4), 3 - group


class Spread:
    def __init__(self, at, sizes, items, sems, relay=True):
        self.at, self.count, self.items = at, sizes[0], items
        self.local, self.sent, self.got = sems
        self.plane = relay and sizes[0] == 4

    @staticmethod
    def scratch(items, sizes):
        ways = max(4, sizes[0] - 1)
        return [
            pltpu.SemaphoreType.DMA((items,)),
            pltpu.SemaphoreType.DMA((items, ways)),
            pltpu.SemaphoreType.DMA((items, ways)),
        ]

    def place(self, number, owner, half=None):
        source, target, axis, *where = self.items[number]
        rows, columns = source.shape
        size = source.shape[axis]
        step, offset = where or (size, 0)
        start = owner * step + offset
        if half is None:
            begin, height = 0, rows
        else:
            begin, height = half * (rows // 2), rows // 2
        if axis == 0:
            return target.at[pl.ds(pl.multiple_of(start + begin, height), height)]
        return target.at[pl.ds(begin, height), pl.ds(pl.multiple_of(start, size), size)]

    def own(self, number):
        return pltpu.make_async_copy(
            self.items[number][0], self.place(number, self.at[0]), self.local.at[number]
        )

    def copy(self, number, source, place, way, peer):
        return pltpu.make_async_remote_copy(
            src_ref=source,
            dst_ref=place,
            send_sem=self.sent.at[number, way],
            recv_sem=self.got.at[number, way],
            device_id=(peer,) + self.at[1:],
            device_id_type=MESH,
        )

    def away(self, number, k):
        peer = lax.rem(self.at[0] + k, self.count)
        return self.copy(number, self.items[number][0], self.place(number, self.at[0]), k - 1, peer)

    def landed(self, number, k):
        owner = lax.rem(self.at[0] + self.count - k, self.count)
        return self.copy(number, self.items[number][0], self.place(number, owner), k - 1, owner)

    def to(self, number, way):
        peer = beside(self.at[0])[way]
        return self.copy(number, self.items[number][0], self.place(number, self.at[0]), way, peer)

    def of(self, number, way):
        peer = beside(self.at[0])[way]
        return self.copy(number, self.items[number][0], self.place(number, peer), way, peer)

    def on(self, number, way):
        near = beside(self.at[0])
        ref = self.place(number, near[way], way)
        return self.copy(number, ref, ref, 2 + way, near[1 - way])

    def last(self, number, way):
        near = beside(self.at[0])
        ref = self.place(number, near[2], way)
        return self.copy(number, ref, ref, 2 + way, near[1 - way])

    def start(self, *numbers):
        for number in numbers:
            if self.plane:
                self.to(number, 0).start()
                self.to(number, 1).start()
            else:
                for k in range(1, self.count):
                    self.away(number, k).start()
            self.own(number).start()

    def relay(self, *numbers):
        if self.plane:
            for number in numbers:
                for way in range(2):
                    self.of(number, way).wait_recv()
                    self.on(number, way).start()

    def wait(self, *numbers):
        for number in numbers:
            self.own(number).wait()
            if self.plane:
                self.last(number, 0).wait_recv()
                self.last(number, 1).wait_recv()
            else:
                for k in range(1, self.count):
                    self.landed(number, k).wait_recv()

    def drain(self, *numbers):
        for number in numbers:
            if self.plane:
                for way in range(2):
                    self.to(number, way).wait_send()
                    self.on(number, way).wait_send()
            else:
                for k in range(1, self.count):
                    self.away(number, k).wait_send()


class Gather:
    def __init__(self, at, sizes, count, full, sems):
        self.at, self.levels, self.count, self.full = at, sizes[1], count, full
        self.sent_up, self.got_up, self.sent_down, self.got_down, self.sent_core, self.got_core = sems

    @staticmethod
    def scratch(count, sizes, piece):
        levels = sizes[1]
        dma = pltpu.SemaphoreType.DMA
        return [pltpu.VMEM((count, levels, 2) + piece, jnp.bfloat16)] + [
            dma((levels - 1, count)) for _ in range(4)
        ] + [dma((2 * levels - 1, count)) for _ in range(2)]

    def copy(self, ref, sent, got, target):
        return pltpu.make_async_remote_copy(
            src_ref=ref, dst_ref=ref, send_sem=sent, recv_sem=got, device_id=target, device_id_type=MESH
        )

    def up(self, k, hop, origin, sem):
        group, level, core = self.at
        target = (group, lax.rem(level + 1, self.levels), core)
        return self.copy(self.full.at[k, origin, core], self.sent_up.at[sem, k], self.got_up.at[sem, k], target)

    def down(self, k, hop, origin, sem):
        group, level, core = self.at
        target = (group, lax.rem(level + self.levels - 1, self.levels), core)
        return self.copy(
            self.full.at[k, origin, core], self.sent_down.at[sem, k], self.got_down.at[sem, k], target
        )

    def across(self, k, origin, side, sem):
        group, level, core = self.at
        return self.copy(
            self.full.at[k, origin, side], self.sent_core.at[sem, k], self.got_core.at[sem, k], (group, level, 1 - core)
        )

    def start(self, k):
        group, level, core = self.at

        @pl.when(level < self.levels - 1)
        def _():
            self.up(k, 0, level, 0).start()

        @pl.when(level > 0)
        def _():
            self.down(k, 0, level, 0).start()

        self.across(k, level, core, 0).start()

    def hop(self, k, hop):
        group, level, core = self.at
        last = self.levels - 1

        @pl.when(level >= hop)
        def _():
            origin = level - hop
            self.up(k, hop, origin, hop - 1).wait_recv()
            if hop < last:

                @pl.when(level < last)
                def _():
                    self.up(k, hop, origin, hop).start()

            self.across(k, origin, core, hop).start()

        @pl.when(level + hop <= last)
        def _():
            origin = level + hop
            self.down(k, hop, origin, hop - 1).wait_recv()
            if hop < last:

                @pl.when(level > 0)
                def _():
                    self.down(k, hop, origin, hop).start()

            self.across(k, origin, core, last + hop).start()

    def ready(self, k):
        group, level, core = self.at
        last = self.levels - 1
        self.across(k, level, 1 - core, 0).wait_recv()
        for hop in range(1, self.levels):

            @pl.when(level >= hop)
            def _():
                self.across(k, level - hop, 1 - core, hop).wait_recv()

            @pl.when(level + hop <= last)
            def _():
                self.across(k, level + hop, 1 - core, last + hop).wait_recv()

    def drain(self):
        group, level, core = self.at
        last = self.levels - 1

        def one(k, _):
            self.across(k, level, core, 0).wait_send()
            for hop in range(self.levels):
                if hop < last:

                    @pl.when((level >= hop) & (level < last))
                    def _():
                        self.up(k, hop, level - hop, hop).wait_send()

                    @pl.when((level + hop <= last) & (level > 0))
                    def _():
                        self.down(k, hop, level + hop, hop).wait_send()

                if hop > 0:

                    @pl.when(level >= hop)
                    def _():
                        self.across(k, level - hop, core, hop).wait_send()

                    @pl.when(level + hop <= last)
                    def _():
                        self.across(k, level + hop, core, last + hop).wait_send()

            return 0

        lax.fori_loop(0, self.count, one, 0)


class Scatter:
    REFS = 4

    def __init__(self, at, sizes, count, refs):
        self.at, self.levels, self.count = at, sizes[1], count
        self.part, self.cross, self.inbox, self.total = refs[:4]
        self.sent_core, self.got_core, self.sent_up, self.got_up, self.sent_down, self.got_down = refs[4:]

    @staticmethod
    def rooms(count, sizes, piece):
        levels = sizes[1]
        return [
            pltpu.VMEM((2, levels, 2) + piece, jnp.bfloat16),
            pltpu.VMEM((count, levels) + piece, jnp.bfloat16),
            pltpu.VMEM((count, levels + 1) + piece, jnp.bfloat16),
            pltpu.VMEM(piece, jnp.float32),
        ]

    @staticmethod
    def sems(count, sizes):
        dma = pltpu.SemaphoreType.DMA
        return [dma((count,)) for _ in range(2)] + [dma((sizes[1], count)) for _ in range(4)]

    @staticmethod
    def scratch(count, sizes, piece):
        return Scatter.rooms(count, sizes, piece) + Scatter.sems(count, sizes)

    def across(self, k):
        group, level, core = self.at
        return pltpu.make_async_remote_copy(
            src_ref=self.part.at[lax.rem(k, 2), :, 1 - core],
            dst_ref=self.cross.at[k],
            send_sem=self.sent_core.at[k],
            recv_sem=self.got_core.at[k],
            device_id=(group, level, 1 - core),
            device_id_type=MESH,
        )

    def up(self, k, owner):
        group, level, core = self.at
        return pltpu.make_async_remote_copy(
            src_ref=self.cross.at[k, owner],
            dst_ref=self.inbox.at[k, owner + 1],
            send_sem=self.sent_up.at[owner, k],
            recv_sem=self.got_up.at[owner, k],
            device_id=(group, lax.rem(level + 1, self.levels), core),
            device_id_type=MESH,
        )

    def down(self, k, owner):
        group, level, core = self.at
        return pltpu.make_async_remote_copy(
            src_ref=self.cross.at[k, owner],
            dst_ref=self.inbox.at[k, owner],
            send_sem=self.sent_down.at[owner, k],
            recv_sem=self.got_down.at[owner, k],
            device_id=(group, lax.rem(level + self.levels - 1, self.levels), core),
            device_id_type=MESH,
        )

    def free(self, k, before=None):
        @pl.when(k >= 2)
        def _():
            self.across(k - 2).wait_send()

        if before is not None:

            @pl.when(k < 2)
            def _():
                before.across(self.count - 2 + k).wait_send()

    def start(self, k):
        self.across(k).start()

    def join(self, k):
        core = self.at[2]
        self.across(k).wait_recv()
        for owner in range(self.levels):
            self.cross[k, owner] = lowered(
                wide(self.part[lax.rem(k, 2), owner, core]) + wide(self.cross[k, owner])
            )

    def step_up(self, k):
        level = self.at[1]
        for owner in range(self.levels - 1, 0, -1):

            @pl.when(level < owner)
            def _():
                @pl.when(level > 0)
                def _():
                    self.up(k, owner).wait_recv()
                    self.cross[k, owner] = lowered(wide(self.cross[k, owner]) + wide(self.inbox[k, owner + 1]))

                self.up(k, owner).start()

    def step_down(self, k):
        level = self.at[1]
        for owner in range(self.levels - 1):

            @pl.when(level > owner)
            def _():
                @pl.when(level < self.levels - 1)
                def _():
                    self.down(k, owner).wait_recv()
                    self.cross[k, owner] = lowered(wide(self.cross[k, owner]) + wide(self.inbox[k, owner]))

                self.down(k, owner).start()

    def steps(self, wave):
        level = self.at[1]
        above = wave - level
        below = wave - (self.levels - 1 - level)

        @pl.when(within(above, self.count) & (level < self.levels // 2))
        def _():
            self.step_up(above)

        @pl.when(within(below, self.count))
        def _():
            self.step_down(below)

        @pl.when(within(above, self.count) & (level >= self.levels // 2))
        def _():
            self.step_up(above)

    def finish(self, k):
        level = self.at[1]
        self.total[...] = wide(self.cross[k, level])

        @pl.when(level > 0)
        def _():
            self.up(k, level).wait_recv()
            self.total[...] += wide(self.inbox[k, level + 1])

        @pl.when(level < self.levels - 1)
        def _():
            self.down(k, level).wait_recv()
            self.total[...] += wide(self.inbox[k, level])

    def sent(self, k):
        level = self.at[1]
        for owner in range(self.levels):

            @pl.when(level < owner)
            def _():
                self.up(k, owner).wait_send()

            @pl.when(level > owner)
            def _():
                self.down(k, owner).wait_send()

    def drain(self):
        self.across(self.count - 2).wait_send()
        self.across(self.count - 1).wait_send()
        in_order(self.count, self.sent)


def in_order(count, step):
    def body(number, carry):
        step(number)
        return carry

    lax.fori_loop(0, count, body, 0)


def span(number, size):
    return pl.ds(pl.multiple_of(number * size, size), size)


class Moves:
    def __init__(self, pairs, sems):
        self.pairs, self.sems = pairs, sems

    def copy(self, number):
        return pltpu.make_async_copy(*self.pairs[number], self.sems.at[number])

    def start(self, *numbers):
        for number in numbers:
            self.copy(number).start()

    def wait(self, *numbers):
        for number in numbers:
            self.copy(number).wait()


class Chunks:
    def __init__(self, pairs, size, sems):
        self.pairs, self.size, self.sems = pairs, size, sems

    def start(self, k):
        for number, (source, target) in enumerate(self.pairs):
            rows = span(k, self.size)
            pltpu.make_async_copy(source.at[rows], target.at[rows], self.sems.at[number, k]).start()

    def wait(self, count):
        def one(k, carry):
            for number, (source, target) in enumerate(self.pairs):
                rows = span(k, self.size)
                pltpu.make_async_copy(source.at[rows], target.at[rows], self.sems.at[number, k]).wait()
            return carry

        lax.fori_loop(0, count, one, 0)


def matmul(left, right):
    return jnp.dot(left, right, preferred_element_type=jnp.float32)


def decay_tile(near, far, size, bounds, rate):
    rows = near * size + lax.broadcasted_iota(jnp.int32, (size, 1), 0)
    columns = far * size + lax.broadcasted_iota(jnp.int32, (1, size), 1)
    row_seq, column_seq = jnp.zeros((size, 1), jnp.int32), jnp.zeros((1, size), jnp.int32)
    for number in range(1, SEQ_DEV):
        row_seq += (rows >= bounds[number]).astype(jnp.int32)
        column_seq += (columns >= bounds[number]).astype(jnp.int32)
    distance = rows - columns
    valid = (distance >= 0) & (row_seq == column_seq)
    return (
        jnp.where(valid, jnp.exp(jnp.maximum(distance, 0).astype(jnp.float32) * rate[0]), 0.0)
        * QK_DIM ** (-0.5)
    )


class Swap:
    def __init__(self, at, sizes, items, sems, halves=None):
        self.at, self.count, self.items = at, sizes[0], items
        self.local, self.sent, self.got = sems
        self.halves = halves
        self.plane = halves is not None and sizes[0] == 4

    @staticmethod
    def scratch(items, sizes):
        ways = max(6, sizes[0] - 1)
        return [
            pltpu.SemaphoreType.DMA((items,)),
            pltpu.SemaphoreType.DMA((items, ways)),
            pltpu.SemaphoreType.DMA((items, ways)),
        ]

    def block(self, number, owner, half=None):
        source, target, axis = self.items[number]
        rows, columns = source.shape
        size = source.shape[axis] // self.count
        height = size if axis == 0 else rows
        begin = 0
        if half is not None:
            height //= 2
            begin = half * height
        if axis == 0:
            return source.at[pl.ds(pl.multiple_of(owner * size + begin, height), height)]
        return source.at[pl.ds(begin, height), pl.ds(pl.multiple_of(owner * size, size), size)]

    def half(self, number, slot, half):
        target = self.items[number][1]
        height = target.shape[1] // 2
        return target.at[slot, pl.ds(half * height, height)]

    def copy(self, number, source, place, way, peer):
        return pltpu.make_async_remote_copy(
            src_ref=source,
            dst_ref=place,
            send_sem=self.sent.at[number, way],
            recv_sem=self.got.at[number, way],
            device_id=(peer,) + self.at[1:],
            device_id_type=MESH,
        )

    def own(self, number):
        return pltpu.make_async_copy(
            self.block(number, self.at[0]), self.items[number][1].at[0], self.local.at[number]
        )

    def away(self, number, k):
        peer = lax.rem(self.at[0] + k, self.count)
        return self.copy(number, self.block(number, peer), self.items[number][1].at[k], k - 1, peer)

    def across(self, number, way):
        near = beside(self.at[0])
        return self.copy(
            number, self.block(number, near[2], way), self.halves[number].at[way], way, near[way]
        )

    def direct(self, number, way):
        near = beside(self.at[0])
        return self.copy(
            number, self.block(number, near[way], way), self.half(number, 1 + way, way), 2 + way, near[way]
        )

    def added(self, number, way):
        peer = beside(self.at[0])[1 - way]
        return self.copy(
            number, self.block(number, peer, way), self.half(number, 2 - way, way), 4 + way, peer
        )

    def start(self, *numbers):
        for number in numbers:
            if self.plane:
                for way in range(2):
                    self.across(number, way).start()
                for way in range(2):
                    self.direct(number, way).start()
            else:
                for k in range(1, self.count):
                    self.away(number, k).start()
            self.own(number).start()

    def relay(self, *numbers):
        if self.plane:
            near = beside(self.at[0])
            for number in numbers:
                for way in range(2):
                    self.across(number, way).wait_recv()
                    part = self.block(number, near[1 - way], way)
                    part[...] = lowered(wide(part[...]) + wide(self.halves[number][way]))
                    self.added(number, way).start()

    def wait(self, *numbers):
        for number in numbers:
            self.own(number).wait()
            if self.plane:
                for way in range(2):
                    self.across(number, way).wait_send()
                    self.direct(number, way).wait()
                    self.added(number, way).wait()
            else:
                for k in range(1, self.count):
                    self.away(number, k).wait()


def half_blocks(items, sizes):
    room = []
    for whole, axis in items:
        shape = list(whole.shape)
        shape[axis] //= sizes[0]
        room.append(pltpu.VMEM((2, shape[0] // 2, shape[1]), jnp.bfloat16))
    return room


def quarters(source, target):
    rows = source.shape[0]
    run = rows // 4
    return [(source.at[pl.ds(k * run, run)], target, 0, rows, k * run) for k in range(4)]


def deal_kernel(sizes, tokens, gains, *refs):
    masters, refs = refs[:8], refs[8:]
    tokens_out, gains_out, *refs = refs
    rounded_out, refs = refs[:8], refs[8:]
    spread_sems, refs = refs[:3], refs[3:]
    small_sems, refs = refs[:3], refs[3:]
    held, refs = refs[:8], refs[8:]
    rounded, refs = refs[:8], refs[8:]
    load_sems, store_sems, tokens_held, gains_held = refs
    at = around(AXES)
    loads = Moves(list(zip(masters, held)) + [(tokens, tokens_held), (gains, gains_held)], load_sems)
    stores = Moves(list(zip(rounded, rounded_out)), store_sems)
    loads.start(8, 9, *range(8))
    greet(plane_peers(at, sizes))
    loads.wait(8, 9)
    spread = Spread(at, sizes, quarters(tokens_held, tokens_out), spread_sems)
    small = Spread(at, sizes, [(gains_held, gains_out, 0)], small_sems, relay=False)
    spread.start(*range(4))
    small.start(0)
    for number in range(8):
        loads.wait(number)

        def block(k):
            rows = span(k, 32)
            rounded[number][rows, :] = lowered(held[number][rows, :])

        in_order(held[number].shape[0] // 32, block)
        stores.start(number)
    for number in range(4):
        spread.relay(number)
    stores.wait(*range(8))
    small.wait(0)
    spread.wait(*range(4))
    small.drain(0)
    spread.drain(*range(4))


def open_kernel(sizes, shards, gain, *refs):
    x_part, gain, *refs = (shards, gain) + refs
    sources, refs = refs[:5], refs[5:]
    normed_out, query_out, key_out, value_out, swish_out, *refs = refs
    weight_outs, dy_out, refs = refs[:4], refs[4], refs[5:]
    rows_out, unit_out, scale_out, *refs = refs
    full, *refs = refs
    gather_sems, refs = refs[:6], refs[6:]
    spread_sems, refs = refs[:3], refs[3:]
    weights, refs = refs[:4], refs[4:]
    normed, query, keys, values, swish, load_sem, out_sem, weight_sem, normed_sem, shard = refs
    at = around(AXES)
    group, level, core = at
    place = 2 * level + core
    count, levels, _, chunk, width = full.shape
    ranks = 2 * levels
    load = pltpu.make_async_copy(x_part, full.at[:, level, core], load_sem)
    load.start()
    load_shard = pltpu.make_async_copy(sources[4], shard, weight_sem.at[4])
    load_shard.start()
    greet(plane_peers(at, sizes) + column_peers(at, sizes))
    items = [(s, t, 0) for s, t in zip(sources[:4], weights)] + quarters(shard, dy_out)
    spread = Spread(at, sizes, items, spread_sems)
    gather = Gather(at, sizes, count, full, gather_sems)
    load.wait()
    gather.start(0)
    load_shard.wait()
    spread.start(0, 1, 2)
    piece = chunk // ranks

    def norm(k):
        def block(number, carry):
            rows = span(number, 16)
            value = jnp.concatenate(
                [wide(full[k, q, c, rows, :]) for q in range(levels) for c in range(2)], axis=1
            )
            unit, scale = layer_norm(value, EPSILON)
            where = pl.ds(pl.multiple_of(k * chunk + number * 16, 16), 16)
            normed[where, :] = lowered(unit * gain[...])
            mine = wide(full[k, level, core, rows, :])
            mean = jnp.mean(value, -1, keepdims=True)
            unit_out[where, :] = (mine - mean) * scale
            scale_out[where, :] = jnp.broadcast_to(scale, (16, 128))
            return carry

        lax.fori_loop(0, chunk // 16, block, 0)
        mine = span(place, piece)
        rows_out[span(k, piece), :] = jnp.concatenate(
            [full[k, q, c, mine, :] for q in range(levels) for c in range(2)], axis=1
        )
        pltpu.make_async_copy(
            normed.at[span(k, chunk)], normed_out.at[span(k, chunk)], normed_sem.at[k]
        ).start()

    def wave(number):
        @pl.when(number + 1 < count)
        def _():
            gather.start(number + 1)

        for hop in range(levels - 1, 0, -1):

            @pl.when(within(number - hop, count))
            def _():
                gather.hop(number - hop, hop)

        for step, relayed, started in (
            (1, (0,), ()),
            (2, (1,), (3,)),
            (4, (2,), (4, 5)),
            (6, (3,), (6, 7)),
            (8, (4,), ()),
            (9, (5,), ()),
        ):

            @pl.when(number == step)
            def _():
                spread.relay(*relayed)
                spread.start(*started)

        @pl.when(within(number - levels, count))
        def _():
            gather.ready(number - levels)
            norm(number - levels)

    in_order(count + levels, wave)
    spread.relay(6)
    outs = [(query, query_out), (keys, key_out), (values, value_out), (swish, swish_out)]
    for number, (held, out) in enumerate(outs):
        spread.wait(number)
        pltpu.make_async_copy(weights[number], weight_outs[number], weight_sem.at[number]).start()

        def rows(k):
            where = span(k, chunk)
            held[where, :] = matmul(normed[where, :], weights[number][...]).astype(held.dtype)

        in_order(count, rows)
        pltpu.make_async_copy(held, out, out_sem.at[number]).start()
    spread.relay(7)
    spread.wait(4, 5, 6, 7)
    for number, (held, out) in enumerate(outs):
        pltpu.make_async_copy(held, out, out_sem.at[number]).wait()
        pltpu.make_async_copy(weights[number], weight_outs[number], weight_sem.at[number]).wait()
    spread.drain(*range(8))
    gather.drain()

    def stored(k):
        pltpu.make_async_copy(
            normed.at[span(k, chunk)], normed_out.at[span(k, chunk)], normed_sem.at[k]
        ).wait()

    in_order(count, stored)


class Ring:
    def __init__(self, slots, whole, size, sems):
        self.slots, self.whole, self.size, self.sems = slots, whole, size, sems

    def load(self, k):
        return pltpu.make_async_copy(
            self.whole.at[span(k, self.size)], self.slots.at[lax.rem(k, 2)], self.sems.at[k]
        )

    def store(self, k):
        return pltpu.make_async_copy(
            self.slots.at[lax.rem(k, 2)], self.whole.at[span(k, self.size)], self.sems.at[k]
        )

    def free(self, k):
        @pl.when(k >= 2)
        def _():
            self.store(k - 2).wait()


def core_kernel(sizes, bounds, rate, gain, *refs):
    query_src, key_src, value_src, rows_src, dy_src, swish_src, *refs = refs
    shards, refs = refs[:4], refs[4:]
    mixed_in_out, retained_out, branch_out, swish_out, query_out, key_out, value_out, *refs = refs
    gain_out, mixed_dst, down_dst, gate_dst, up_dst, *refs = refs
    query, keys, values, x_rows, out_w, gate_w, up_w, down_w, *refs = refs
    rooms, refs = refs[:4], refs[4:]
    (other_part,), refs = refs[:1], refs[1:]
    sems_one, sems_two, sems_three, refs = refs[:6], refs[6:12], refs[12:18], refs[18:]
    normed_mid, refs = refs[0], refs[1:]
    normed_sems, refs = refs[:6], refs[6:]
    dy, refs = refs[0], refs[1:]
    dy_sems, refs = refs[:6], refs[6:]
    branch, refs = refs[0], refs[1:]
    branch_sems, refs = refs[:6], refs[6:]
    spread_sems, refs = refs[:3], refs[3:]
    deal_sems, refs = refs[:3], refs[3:]
    swap_sems, refs = refs[:3], refs[3:]
    hidden, gate_grad, up_grad, resid, swish_slots, retained_slots, mixed_in_slots, grad_slots, *refs = refs
    key_acc, value_acc, query_acc, delta, down_grad, mixed, *refs = refs
    load_sems, ring_sems, branch_store, query_store, end_sems, *halves = refs
    at = around(AXES)
    group, level, core = at
    place = 2 * level + core
    count, levels, _, piece, width = normed_mid.shape
    ranks = 2 * levels
    chunk = ranks * piece
    part_width = width // ranks
    loads = Moves(
        [
            (dy_src, dy.at[:, level, core]),
            (query_src, query),
            (key_src, keys),
            (value_src, values),
            (rows_src, x_rows),
        ],
        load_sems,
    )
    loads.start(*range(5))
    swish_one = Ring(swish_slots, swish_src, chunk, ring_sems.at[0])
    swish_two = Ring(swish_slots, swish_src, chunk, ring_sems.at[1])
    retained_one = Ring(retained_slots, retained_out, chunk, ring_sems.at[2])
    retained_two = Ring(retained_slots, retained_out, chunk, ring_sems.at[3])
    mixed_in_ring = Ring(mixed_in_slots, mixed_in_out, chunk, ring_sems.at[4])
    grad_ring = Ring(grad_slots, swish_out, chunk, ring_sems.at[5])
    query_ends = Chunks([(query, query_out)], chunk, query_store)
    swish_one.load(0).start()
    swish_one.load(1).start()
    greet(plane_peers(at, sizes) + column_peers(at, sizes))
    spread = Spread(
        at,
        sizes,
        [(shards[0], out_w, 1), (shards[1], gate_w, 0), (shards[2], up_w, 0), (shards[3], down_w, 1)],
        spread_sems,
    )
    deal = Spread(
        at,
        sizes,
        [
            (mixed.at[pl.ds(k * chunk, chunk)], mixed_dst, 0, count * chunk, k * chunk)
            for k in range(count)
        ],
        deal_sems,
    )
    swap = Swap(
        at, sizes, [(down_grad, down_dst, 1), (gate_w, gate_dst, 0), (up_w, up_dst, 0)], swap_sems, halves
    )
    spread.start(0, 1)
    one = Scatter(at, sizes, count, list(rooms) + list(sems_one))
    two = Scatter(at, sizes, count, [other_part] + list(rooms[1:]) + list(sems_two))
    three = Scatter(at, sizes, count, list(rooms) + list(sems_three))
    total = rooms[3]
    mid_gather = Gather(at, sizes, count, normed_mid, normed_sems)
    dy_gather = Gather(at, sizes, count, dy, dy_sems)
    branch_gather = Gather(at, sizes, count, branch, branch_sems)
    gain_out[...] = jnp.zeros(gain_out.shape, jnp.float32)
    key_acc[...] = jnp.zeros(key_acc.shape, jnp.float32)
    value_acc[...] = jnp.zeros(value_acc.shape, jnp.float32)
    loads.wait(0)
    dy_gather.start(0)
    loads.wait(1, 2, 3, 4)
    tile = 512

    def branch_stores(k):
        copies = []
        for q in range(levels):
            for c in range(2):
                rows = pl.ds(pl.multiple_of(k * chunk + (2 * q + c) * piece, piece), piece)
                copies.append(
                    pltpu.make_async_copy(branch.at[k, q, c], branch_out.at[rows], branch_store.at[2 * q + c, k])
                )
        return copies

    def first(k):
        where = span(k, chunk)
        slot = lax.rem(k, 2)
        retained_one.free(k)
        retained_slots[slot] = jnp.zeros((chunk, values.shape[1]), jnp.float32)

        def block(j, carry):
            there = span(j, chunk)
            decay = decay_tile(k, j, chunk, bounds, rate)
            weight = lowered(inner_rows(query[where, :], keys[there, :]) * decay)
            retained_slots[slot] += matmul(weight, values[there, :])
            return carry

        lax.fori_loop(0, k + 1, block, 0)
        retained_one.store(k).start()
        normed, _ = layer_norm(retained_slots[slot], GROUP_EPS)
        swish_one.load(k).wait()
        value = swish_slots[slot]
        mixed_in_ring.free(k)
        mixed_in_slots[slot] = lowered(value * jax.nn.sigmoid(value) * normed)
        mixed_in_ring.store(k).start()

        @pl.when(k + 2 < count)
        def _():
            swish_one.load(k + 2).start()

        @pl.when(k == 0)
        def _():
            spread.wait(0)

        one.free(k)
        rows = mixed_in_slots[slot]
        for column in range(0, width, tile):
            value = matmul(rows, out_w[:, column : column + tile])
            one.part[slot, :, :, :, column : column + tile] = lowered(value).reshape(levels, 2, piece, tile)
        one.start(k)

    def mid_norm(k):
        one.finish(k)

        def block(number, carry):
            sub = span(number, 16)
            where = pl.ds(pl.multiple_of(k * piece + number * 16, 16), 16)
            value = wide(x_rows[where, :]) + total[sub, :]
            resid[where, :] = value
            unit, _ = layer_norm(value, EPSILON)
            normed_mid[k, level, core, sub, :] = lowered(unit * gain[...])
            return carry

        lax.fori_loop(0, piece // 16, block, 0)
        mid_gather.start(k)

    def turn(k):
        mid_gather.ready(k)
        rows = normed_mid[k].reshape(chunk, width)
        where = span(k, chunk)
        g = matmul(rows, gate_w[...])
        u = matmul(rows, up_w[...])
        root = 0.7978845608028654
        bend = jnp.tanh(root * (g + 0.044715 * g * g * g))
        curve = 0.5 * (1.0 + bend)
        active = g * curve
        hidden[where, :] = lowered(active * u)
        slope = curve + 0.5 * g * (1.0 - bend * bend) * root * (1.0 + 0.134145 * g * g)
        dy_gather.ready(k)
        rows = jnp.concatenate([dy[k, q, c] for q in range(levels) for c in range(2)], axis=1)
        back = inner_rows(rows, down_w[...])
        gate_grad[where, :] = lowered(back * u * slope)
        up_grad[where, :] = lowered(back * active)
        two.free(k)
        for column in range(0, width, tile):
            columns = slice(column, column + tile)
            value = inner_rows(gate_grad[where, :], gate_w[columns, :])
            value += inner_rows(up_grad[where, :], up_w[columns, :])
            two.part[lax.rem(k, 2), :, :, :, columns] = lowered(value).reshape(levels, 2, piece, tile)
        two.start(k)

    def branch_norm(k):
        two.finish(k)

        def block(number, carry):
            sub = span(number, 16)
            where = pl.ds(pl.multiple_of(k * piece + number * 16, 16), 16)
            unit, scale = layer_norm(resid[where, :], EPSILON)
            grad = total[sub, :]
            outer = grad * unit
            gain_out[...] += outer[:8] + outer[8:]
            mine = pl.ds(pl.multiple_of(place * piece + number * 16, 16), 16)
            upstream = jnp.concatenate(
                [dy[k, q, c, mine, :] for q in range(levels) for c in range(2)], axis=1
            )
            value = wide(upstream) + norm_back(grad * gain[...], unit, scale)
            branch[k, level, core, sub, :] = lowered(value)
            return carry

        lax.fori_loop(0, piece // 16, block, 0)
        branch_gather.start(k)

    def last(k):
        branch_gather.ready(k)
        for copy in branch_stores(k):
            copy.start()
        rows = branch[k].reshape(chunk, width)
        where = span(k, chunk)
        slot = lax.rem(k, 2)
        grad = inner_rows(rows, out_w[...])
        retained_two.load(k).wait()
        swish_two.load(k).wait()
        normed, scale = layer_norm(retained_slots[slot], GROUP_EPS)
        value = swish_slots[slot]
        gated = jax.nn.sigmoid(value)
        grad_ring.free(k)
        grad_slots[slot] = lowered(grad * normed * gated * (1.0 + value * (1.0 - gated)))
        grad_ring.store(k).start()
        delta[...] = lowered(norm_back(grad * value * gated, normed, scale))

        @pl.when(k + 2 < count)
        def _():
            retained_two.load(k + 2).start()
            swish_two.load(k + 2).start()

        query_acc[...] = jnp.zeros(query_acc.shape, jnp.float32)

        def block(j, carry):
            there = span(j, chunk)
            decay = decay_tile(k, j, chunk, bounds, rate)
            weight = lowered(inner_rows(query[where, :], keys[there, :]) * decay)
            score = lowered(inner_rows(delta[...], values[there, :]) * decay)
            query_acc[...] += matmul(score, keys[there, :])
            key_acc[there, :] += inner_cols(score, query[where, :])
            value_acc[there, :] += inner_cols(weight, delta[...])
            return carry

        lax.fori_loop(0, k + 1, block, 0)
        query[where, :] = lowered(query_acc[...])
        query_ends.start(k)

    def out_part(k):
        three.free(k, one)
        rows = hidden[span(k, chunk), :]
        mine = pl.ds(pl.multiple_of(k * piece, piece), piece)
        for rank in range(ranks):
            columns = slice(rank * part_width, (rank + 1) * part_width)
            value = matmul(rows, down_w[:, columns])
            for run in range(ranks):
                held = jnp.where(place == run, resid[mine, columns], 0.0)
                three.part[
                    lax.rem(k, 2), rank // 2, rank % 2, :, run * part_width : (run + 1) * part_width
                ] = lowered(value[run * piece : (run + 1) * piece, :] + held)
        three.start(k)

    def out_finish(k):
        three.finish(k)
        for run in range(ranks):
            where = pl.ds(pl.multiple_of(k * chunk + run * piece, piece), piece)
            mixed[where, :] = lowered(total[:, run * part_width : (run + 1) * part_width])

    def weigh(which):
        def part(k):
            columns = span(k, chunk)
            if which == 0:
                down = jnp.zeros((hidden.shape[1], part_width), jnp.float32)
                for j in range(count):
                    down += inner_cols(hidden[j * chunk : (j + 1) * chunk, :], dy[j, k // 2, lax.rem(k, 2)])
                there = pl.ds(pl.multiple_of(k * part_width, part_width), part_width)
                down_grad[:, there] = lowered(down)
            else:
                target, source = ((gate_w, gate_grad), (up_w, up_grad))[which - 1]
                rows = jnp.concatenate(
                    [
                        normed_mid[j, q, c, :, columns]
                        for j in range(count)
                        for q in range(levels)
                        for c in range(2)
                    ],
                    axis=0,
                )
                target[columns, :] = lowered(inner_cols(rows, source[...]))

        in_order(width // chunk, part)
        swap.start(which)

    lead = 2
    mid_lag = lead + levels
    turn_lag = mid_lag + levels - 1
    branch_lag = turn_lag + levels
    last_lag = branch_lag + levels - 1

    def at_wave(number, lag, step):
        @pl.when(within(number - lag, count))
        def _():
            step(number - lag)

    def wave(number):
        at_wave(number, lead, first)
        for gather, lag, scatter in ((branch_gather, branch_lag, two), (mid_gather, mid_lag, one)):
            at_wave(number, lag + 1, scatter.sent)
            for hop in range(levels - 1, 0, -1):
                at_wave(number, lag + hop, functools.partial(hop_on, gather, hop))
        at_wave(number, branch_lag, branch_norm)
        at_wave(number, mid_lag, mid_norm)
        at_wave(number, -1, next_dy)
        for hop in range(levels - 1, 0, -1):
            at_wave(number, hop, functools.partial(hop_on, dy_gather, hop))
        for scatter, lag in ((two, turn_lag), (one, lead)):
            at_wave(number, lag + 1, scatter.join)
            scatter.steps(number - lag - 1)
        for step, relayed, started in ((1, (0,), (2,)), (3, (1,), (3,)), (5, (2,), ()), (7, (3,), ())):

            @pl.when(number == step)
            def _():
                spread.relay(*relayed)
                spread.start(*started)

        @pl.when(number == turn_lag)
        def _():
            spread.wait(1, 2, 3)

        at_wave(number, turn_lag, turn)

        @pl.when(number == turn_lag + 1)
        def _():
            retained_one.store(count - 2).wait()
            retained_one.store(count - 1).wait()
            for k in range(2):
                retained_two.load(k).start()
                swish_two.load(k).start()

        @pl.when(number == turn_lag + count)
        def _():
            spread.drain(*range(4))

        for step, which in ((0, 1), (1, 2), (2, 0)):

            @pl.when(number == turn_lag + count + step)
            def _():
                weigh(which)

        for step, which in ((2, 1), (4, 2), (6, 0)):

            @pl.when(number == turn_lag + count + step)
            def _():
                swap.relay(which)

        at_wave(number, last_lag, last)
        at_wave(number, last_lag, out_part)
        at_wave(number, last_lag + 1, three.join)
        three.steps(number - last_lag - 1)
        at_wave(number, last_lag + levels, out_finish)
        for k in range(count):

            @pl.when(number == last_lag + levels + k)
            def _():
                deal.start(k)

            @pl.when(number == last_lag + levels + k + 2)
            def _():
                deal.relay(k)

    def hop_on(gather, hop, k):
        gather.hop(k, hop)

    def next_dy(k):
        @pl.when(k > 0)
        def _():
            dy_gather.start(k)

    in_order(count + last_lag + levels, wave)
    deal.relay(count - 2, count - 1)
    keys[...] = lowered(key_acc[...])
    values[...] = lowered(value_acc[...])
    ends = Moves([(keys, key_out), (values, value_out)], end_sems)
    ends.start(0, 1)
    swap.wait(0, 1, 2)
    deal.wait(*range(count))
    deal.drain(*range(count))
    two.across(count - 2).wait_send()
    two.across(count - 1).wait_send()
    three.drain()
    mid_gather.drain()
    dy_gather.drain()
    branch_gather.drain()
    ends.wait(0, 1)
    query_ends.wait(count)
    for k in (count - 2, count - 1):
        mixed_in_ring.store(k).wait()
        grad_ring.store(k).wait()

    def stored(k):
        for copy in branch_stores(k):
            copy.wait()

    in_order(count, stored)


def close_kernel(sizes, gain, gain_two, *refs):
    ins, refs = refs[:13], refs[13:]
    grad_out, gains_out, *refs = refs
    targets, refs = refs[:5], refs[5:]
    held, refs = refs[:13], refs[13:]
    deltas, weights = held[:4], held[4:8]
    normed_in, branch, mixed_in, unit, scale = held[8:]
    grads, refs = refs[:5], refs[5:]
    scatter_refs, refs = refs[:10], refs[10:]
    swap_sems, refs = refs[:3], refs[3:]
    sums, line_one, share, packed, gains, gains_in, refs = *refs[:6], refs[6:]
    load_sems, sums_sent, sums_got, gain_sent, gain_got, refs = *refs[:5], refs[5:]
    spread_sems, refs = refs[:3], refs[3:]
    small_sems, halves = refs[:3], refs[3:]
    at = around(AXES)
    group, level, core = at
    place = 2 * level + core
    groups = sizes[0]
    scatter = Scatter(at, sizes, sums.shape[1], scatter_refs)
    _, levels, _, chunk, width = scatter.part.shape
    count, ranks = sums.shape[1], 2 * levels
    rows_all = count * chunk
    loads = Moves(list(zip(ins, held)), load_sems)
    loads.start(*range(13))
    greet(plane_peers(at, sizes) + column_all(at, sizes))
    swap = Swap(at, sizes, list(zip(grads, targets, SWAP_AXES)), swap_sems, halves)
    small = Swap(at, sizes, [(gains, gains_in, 1)], small_sems)
    spread = Spread(
        at,
        sizes,
        [(share.at[pl.ds(k * chunk, chunk)], grad_out, 0, rows_all, k * chunk) for k in range(count)],
        spread_sems,
    )
    line_one[...] = jnp.zeros(line_one.shape, jnp.float32)
    loads.wait(*range(9))
    mine = pl.ds(pl.multiple_of(place * width, width), width)

    def first(k):
        scatter.free(k)
        where = span(k, chunk)
        rows = [d[where, :] for d in deltas]
        one = jnp.zeros((chunk, width), jnp.float32)
        two = jnp.zeros((chunk, width), jnp.float32)
        for rank in range(ranks):
            columns = slice(rank * width, (rank + 1) * width)
            value = inner_rows(rows[0], weights[0][columns, :])
            for row, weight in zip(rows[1:], weights[1:]):
                value += inner_rows(row, weight[columns, :])
            scatter.part[lax.rem(k, 2), rank // 2, rank % 2] = lowered(value)
            one += value * gain[:, columns]
            two += value * wide(normed_in[where, columns])
        scatter.start(k)
        ones = jnp.ones((8, width), jnp.float32)
        flat = [
            lax.dot_general(
                ones,
                item,
                (((1,), (1,)), ((), ())),
                precision=lax.Precision.HIGHEST,
                preferred_element_type=jnp.float32,
            )
            for item in (one, two)
        ]
        line = lax.broadcasted_iota(jnp.int32, (8, chunk), 0)
        sums[place, k] = jnp.where(line == 0, flat[0], flat[1])
        for j in range(1, ranks):
            sums_copy(k, j, place).start()

    def sums_copy(k, j, owner):
        peer = lax.rem(place + j, ranks)
        return pltpu.make_async_remote_copy(
            src_ref=sums.at[owner, k],
            dst_ref=sums.at[owner, k],
            send_sem=sums_sent.at[j - 1, k],
            recv_sem=sums_got.at[j - 1, k],
            device_id=(group, peer // 2, lax.rem(peer, 2)),
            device_id_type=MESH,
        )

    def pack_copy(j, owner):
        peer = lax.rem(place + j, ranks)
        return pltpu.make_async_remote_copy(
            src_ref=packed.at[owner],
            dst_ref=packed.at[owner],
            send_sem=gain_sent.at[j - 1],
            recv_sem=gain_got.at[j - 1],
            device_id=(group, peer // 2, lax.rem(peer, 2)),
            device_id_type=MESH,
        )

    def sender(j):
        return lax.rem(place + ranks - j, ranks)

    def finish(k):
        scatter.finish(k)
        for j in range(1, ranks):
            sums_copy(k, j, sender(j)).wait_recv()
        line = lax.broadcasted_iota(jnp.int32, (8, 128), 0)
        lane = lax.broadcasted_iota(jnp.int32, (8, 128), 1)
        means = lax.dot_general(
            jnp.sum(sums[:, k], 0),
            jnp.where(line == lane, 1.0 / (ranks * width), 0.0),
            (((0,), (0,)), ((), ())),
            precision=lax.Precision.HIGHEST,
            preferred_element_type=jnp.float32,
        )
        where = span(k, chunk)
        value, normed = scatter.total[...], unit[where, :]
        outer = value * normed
        line_one[...] += jnp.sum(outer.reshape(chunk // 8, 8, width), 0)
        back = value * gain[:, mine] - means[:, :1] - normed * means[:, 1:2]
        share[where, :] = lowered(wide(branch[where, mine]) + scale[where, :1] * back)

    def weigh(number):
        if number == 4:

            def part(k):
                columns = span(k, chunk)
                grads[4][:, columns] = lowered(inner_cols(mixed_in[...], branch[:, columns]))
        else:

            def part(k):
                columns = span(k, chunk)
                grads[number][columns, :] = lowered(inner_cols(normed_in[:, columns], deltas[number][...]))

        in_order(ranks * width // chunk, part)
        swap.start(number)

    lag = levels - 1

    def wave(number):
        @pl.when(number < count)
        def _():
            first(number)

        @pl.when(number == 0)
        def _():
            weigh(3)

        for step, which in ((1, 2), (2, 0), (3, 1)):

            @pl.when(number == step)
            def _():
                weigh(which)

        @pl.when(number < count)
        def _():
            scatter.join(number)

        scatter.steps(number)

        @pl.when(number == lag)
        def _():
            loads.wait(9, 10, 11, 12)

        @pl.when(within(number - lag, count))
        def _():
            finish(number - lag)

        for k in range(count):

            @pl.when(number == lag + k)
            def _():
                spread.start(k)

            @pl.when(number == lag + k + 2)
            def _():
                spread.relay(k)

        @pl.when(number == lag + 1)
        def _():
            weigh(4)

        for step, relayed in ((2, 3), (4, 2), (5, 0), (6, 1), (8, 4)):

            @pl.when(number == step)
            def _():
                swap.relay(relayed)

    in_order(count + lag, wave)
    for k in (count - 2, count - 1):
        spread.relay(k)
    total = jnp.sum(gain_two[...], 0, keepdims=True)
    packed[place] = jnp.concatenate([total, jnp.sum(line_one[...], 0, keepdims=True)], axis=1)
    for j in range(1, ranks):
        pack_copy(j, place).start()
    for j in range(1, ranks):
        pack_copy(j, sender(j)).wait_recv()
    everything = ranks * width
    line = lax.broadcasted_iota(jnp.int32, (8, everything), 0)
    two = sum(packed[rank, :, :everything] for rank in range(ranks))
    one = jnp.concatenate([packed[rank, :, everything:] for rank in range(ranks)], axis=1)
    gains[...] = jnp.where(line == 0, one, two)
    small.start(0)
    small.wait(0)
    swap.wait(*range(5))
    spread.wait(*range(count))
    spread.drain(*range(count))
    gains_out[...] = jnp.sum(gains_in[...], 0)
    for j in range(1, ranks):
        pack_copy(j, place).wait_send()
    scatter.drain()

    def drain(k):
        for j in range(1, ranks):
            sums_copy(k, j, place).wait_send()

    in_order(count, drain)


def column_all(at, sizes):
    group, level, core = at
    return column_peers(at, sizes) + [
        (group, lax.rem(level + k, sizes[1]), 1 - core) for k in range(1, sizes[1])
    ]


def struct(shape, kind=jnp.bfloat16):
    return jax.ShapeDtypeStruct(shape, kind)


VMEM = pltpu.VMEM
DMA = pltpu.SemaphoreType.DMA


def kernel_call(body, number, ins, outs, scratch):
    places = {
        "vmem": pl.BlockSpec(memory_space=pltpu.VMEM),
        "smem": pl.BlockSpec(memory_space=pltpu.SMEM),
        "any": pl.BlockSpec(memory_space=pl.ANY),
    }
    return pl.pallas_call(
        body,
        out_shape=[shape for _, shape in outs],
        in_specs=[places[inside] for inside, _ in ins],
        out_specs=[places[inside] for inside, _ in outs],
        scratch_shapes=scratch,
        compiler_params=pltpu.CompilerParams(
            collective_id=number, has_side_effects=True, vmem_limit_bytes=63 * 2**20
        ),
    )(*[array for _, array in ins])


def spread_shape(shard, axis, sizes):
    shape = list(shard.shape)
    shape[axis] *= sizes[0]
    return struct(tuple(shape), shard.dtype)


def swap_shape(whole, axis, sizes):
    shape = list(whole.shape)
    shape[axis] //= sizes[0]
    return struct((3 if sizes[0] == 4 else sizes[0],) + tuple(shape), whole.dtype)


def anywhere(items):
    return [("any", item) for item in items]


def held_like(arrays):
    return [VMEM(a.shape, a.dtype) for a in arrays]


def pick(rows, whole):
    return whole.at[rows].get(mode="promise_in_bounds")


def shards(
    tokens,
    cotangent,
    lengths,
    dealing,
    w_query,
    w_key,
    w_value,
    w_swish,
    w_out,
    w_gate,
    w_up,
    w_down,
    gain_attn,
    gain_mlp,
):
    group = lax.axis_index("dp")
    place = lax.axis_index(("heads", "tensor"))
    rows_dev = tokens.shape[0]
    slice_width = tokens.shape[1]
    seq_count = lengths.shape[0]
    ident = jnp.arange(seq_count, dtype=jnp.int32)
    starts = jnp.cumsum(lengths) - lengths
    picked = lax.dynamic_slice_in_dim(dealing, group * SEQ_DEV, SEQ_DEV)
    match = picked[:, None] == ident[None, :]
    dealt_len = jnp.sum(jnp.where(match, lengths[None, :], 0), 1)
    home_start = jnp.sum(jnp.where(match, starts[None, :], 0), 1)
    dealt_start = jnp.cumsum(dealt_len) - dealt_len
    rows = jnp.arange(rows_dev, dtype=jnp.int32)
    seq_ids = jnp.sum((rows[:, None] >= dealt_start[None, :]).astype(jnp.int32), 1) - 1
    member = seq_ids[:, None] == jnp.arange(SEQ_DEV, dtype=jnp.int32)[None, :]
    source = jnp.sum(jnp.where(member, (home_start - dealt_start)[None, :], 0), 1) + rows
    sizes = (lax.axis_size("dp"), lax.axis_size("heads"))
    ranks = sizes[1] * lax.axis_size("tensor")
    chunk = ranks * PIECE
    count = rows_dev // chunk
    width = slice_width * ranks
    own = rows_dev // ranks
    qk_dim, v_dim, ff_dim = w_query.shape[1], w_value.shape[1], w_gate.shape[1]
    f32 = jnp.float32
    masters = (w_query, w_key, w_value, w_swish, w_out, w_gate, w_up, w_down)
    axes = (0, 0, 0, 0, 1, 0, 0, 1)
    gain_rows = jnp.pad(jnp.stack([gain_attn, gain_mlp]), ((0, 6), (0, 0)))
    rounded = [struct(w.shape) for w in masters]
    x_all, gains_all, *low = kernel_call(
        functools.partial(deal_kernel, sizes),
        0,
        anywhere((tokens, gain_rows) + masters),
        anywhere([spread_shape(tokens, 0, sizes), spread_shape(gain_rows, 0, sizes)] + rounded),
        Spread.scratch(4, sizes) + Spread.scratch(1, sizes) + held_like(masters) + held_like(rounded) + [DMA((10,)), DMA((8,))] + held_like((tokens, gain_rows)),
    )
    full_w = [spread_shape(w, a, sizes) for w, a in zip(low, axes)]
    gains_all = wide(lowered(gains_all.reshape(sizes[0], 8, -1)))
    wide_one = gains_all[:, 0].reshape(1, width)
    wide_two = gains_all[:, 1].reshape(1, width)
    x_part = pick(source, x_all)
    (
        normed_in,
        query,
        keys,
        values,
        swish_in,
        query_w,
        key_w,
        value_w,
        swish_w,
        dy_all,
        x_rows,
        unit_share,
        scale_one,
    ) = kernel_call(
        functools.partial(open_kernel, sizes),
        1,
        [("any", x_part.reshape(count, chunk, slice_width)), ("vmem", wide_one)] + anywhere(low[:4] + [cotangent]),
        anywhere(
            [
                struct((rows_dev, width)),
                struct((rows_dev, qk_dim)),
                struct((rows_dev, qk_dim)),
                struct((rows_dev, v_dim)),
                struct((rows_dev, v_dim), f32),
            ]
            + full_w[:4]
            + [spread_shape(cotangent, 0, sizes)]
        )
        + [
            ("vmem", struct((own, width))),
            ("vmem", struct((rows_dev, slice_width), f32)),
            ("vmem", struct((rows_dev, 128), f32)),
        ],
        Gather.scratch(count, sizes, (chunk, slice_width))
        + Spread.scratch(8, sizes)
        + held_like(full_w[:4])
        + [
            VMEM((rows_dev, width), jnp.bfloat16),
            VMEM((rows_dev, qk_dim), jnp.bfloat16),
            VMEM((rows_dev, qk_dim), jnp.bfloat16),
            VMEM((rows_dev, v_dim), jnp.bfloat16),
            VMEM((rows_dev, v_dim), f32),
            DMA,
            DMA((4,)),
            DMA((5,)),
            DMA((count,)),
            VMEM(cotangent.shape, jnp.bfloat16),
        ],
    )
    rate = jnp.log1p(-jnp.exp2(-5.0 - place.astype(f32))).reshape(1)
    dy_part = pick(source, dy_all)
    by_rows = (PIECE, width)
    bf16 = jnp.bfloat16
    (
        mixed_in,
        _,
        delta_branch,
        delta_swish,
        delta_query,
        delta_keys,
        delta_values,
        gain_two_part,
        mixed_all,
        *ff_grads,
    ) = kernel_call(
        functools.partial(core_kernel, sizes),
        2,
        [("smem", dealt_start), ("smem", rate), ("vmem", wide_two)]
        + anywhere((query, keys, values, x_rows, dy_part.reshape(count, chunk, slice_width), swish_in))
        + anywhere(low[4:]),
        anywhere(
            [
                struct((rows_dev, v_dim)),
                struct((rows_dev, v_dim), f32),
                struct((rows_dev, width)),
                struct((rows_dev, v_dim)),
                struct((rows_dev, qk_dim)),
                struct((rows_dev, qk_dim)),
                struct((rows_dev, v_dim)),
            ]
        )
        + [("vmem", struct((8, width), f32))]
        + anywhere(
            [
                struct((sizes[0] * rows_dev, slice_width)),
                swap_shape(full_w[7], 1, sizes),
                swap_shape(full_w[5], 0, sizes),
                swap_shape(full_w[6], 0, sizes),
            ]
        ),
        held_like((query, keys, values, x_rows))
        + held_like(full_w[4:])
        + Scatter.rooms(count, sizes, by_rows)
        + Scatter.rooms(count, sizes, by_rows)[:1]
        + Scatter.sems(count, sizes) * 3
        + Gather.scratch(count, sizes, by_rows)
        + Gather.scratch(count, sizes, (chunk, slice_width))
        + Gather.scratch(count, sizes, by_rows)
        + Spread.scratch(4, sizes)
        + Spread.scratch(count, sizes)
        + Swap.scratch(3, sizes)
        + [
            VMEM((rows_dev, ff_dim), bf16),
            VMEM((rows_dev, ff_dim), bf16),
            VMEM((rows_dev, ff_dim), bf16),
            VMEM((own, width), f32),
            VMEM((2, chunk, v_dim), f32),
            VMEM((2, chunk, v_dim), f32),
            VMEM((2, chunk, v_dim), bf16),
            VMEM((2, chunk, v_dim), bf16),
            VMEM((rows_dev, qk_dim), f32),
            VMEM((rows_dev, v_dim), f32),
            VMEM((chunk, qk_dim), f32),
            VMEM((chunk, v_dim), bf16),
            VMEM((ff_dim, width), bf16),
            VMEM((rows_dev, slice_width), bf16),
            DMA((5,)),
            DMA((6, count)),
            DMA((ranks, count)),
            DMA((1, count)),
            DMA((2,)),
        ]
        + half_blocks([(full_w[7], 1), (full_w[5], 0), (full_w[6], 0)], sizes),
    )
    close_ins = (
        delta_query,
        delta_keys,
        delta_values,
        delta_swish,
        query_w,
        key_w,
        value_w,
        swish_w,
        normed_in,
        delta_branch,
        mixed_in,
        unit_share,
        scale_one,
    )
    swaps = len(SWAP_AXES)
    grad_all, gains, *attn_grads = kernel_call(
        functools.partial(close_kernel, sizes),
        3,
        [("vmem", wide_one), ("vmem", gain_two_part)] + anywhere(close_ins),
        anywhere([struct((sizes[0] * rows_dev, slice_width))])
        + [("vmem", struct((8, gain_attn.shape[0]), f32))]
        + anywhere([swap_shape(w, a, sizes) for w, a in zip(full_w[:5], SWAP_AXES)]),
        held_like(close_ins)
        + held_like(full_w[:5])
        + Scatter.scratch(count, sizes, (chunk, slice_width))
        + Swap.scratch(swaps, sizes)
        + [
            VMEM((ranks, count, 8, chunk), f32),
            VMEM((8, slice_width), f32),
            VMEM((rows_dev, slice_width), jnp.bfloat16),
            VMEM((ranks, 1, width + slice_width), f32),
            VMEM((8, width), f32),
            VMEM((sizes[0], 8, gain_attn.shape[0]), f32),
            DMA((len(close_ins),)),
            DMA((ranks - 1, count)),
            DMA((ranks - 1, count)),
            DMA((ranks - 1,)),
            DMA((ranks - 1,)),
        ]
        + Spread.scratch(count, sizes)
        + Swap.scratch(1, sizes)
        + half_blocks(list(zip(full_w[:5], SWAP_AXES)), sizes),
    )
    grads = [jnp.sum(wide(g), 0) for g in attn_grads + ff_grads[1:] + ff_grads[:1]]
    slot_match = dealing[:, None] == ident[None, :]
    slot_len = jnp.sum(jnp.where(slot_match, lengths[None, :], 0), 1)
    slot_home = jnp.sum(jnp.where(slot_match, starts[None, :], 0), 1)
    per_group = slot_len.reshape(-1, SEQ_DEV)
    slot_start = (jnp.cumsum(per_group, 1) - per_group).reshape(-1)
    slot_base = ident // SEQ_DEV * rows_dev + slot_start - slot_home
    owner_base = jnp.sum(jnp.where(dealing[None, :] == ident[:, None], slot_base[None, :], 0), 1)
    global_rows = group * rows_dev + rows
    seq_of = jnp.sum((global_rows[:, None] >= starts[None, :]).astype(jnp.int32), 1) - 1
    targets = (
        jnp.sum(jnp.where(seq_of[:, None] == ident[None, :], owner_base[None, :], 0), 1)
        + global_rows
    )
    mixed_rows, grad_rows = pick(targets, mixed_all), pick(targets, grad_all)
    return (
        mixed_rows,
        grad_rows,
        grads[0],
        grads[1],
        grads[2],
        grads[3],
        grads[4],
        grads[5],
        grads[6],
        grads[7],
        gains[0],
        gains[1],
    )


def solution(mesh):
    in_specs = (
        P("dp", ("heads", "tensor")),
        P("dp", ("heads", "tensor")),
        P(),
        P(),
        P("dp", ("heads", "tensor")),
        P("dp", ("heads", "tensor")),
        P("dp", ("heads", "tensor")),
        P("dp", ("heads", "tensor")),
        P(("heads", "tensor"), "dp"),
        P("dp", ("heads", "tensor")),
        P("dp", ("heads", "tensor")),
        P(("heads", "tensor"), "dp"),
        P("dp"),
        P("dp"),
    )
    out_specs = (
        P("dp", ("heads", "tensor")),
        P("dp", ("heads", "tensor")),
        P("dp", ("heads", "tensor")),
        P("dp", ("heads", "tensor")),
        P("dp", ("heads", "tensor")),
        P("dp", ("heads", "tensor")),
        P(("heads", "tensor"), "dp"),
        P("dp", ("heads", "tensor")),
        P("dp", ("heads", "tensor")),
        P(("heads", "tensor"), "dp"),
        P("dp"),
        P("dp"),
    )
    return jax.shard_map(shards, mesh=mesh, in_specs=in_specs, out_specs=out_specs, check_vma=False)
```

```python
import functools

import jax
import jax.numpy as jnp
from jax import lax
from jax.experimental import pallas as pl
from jax.experimental.pallas import tpu as pltpu
from jax.sharding import PartitionSpec as P

QK_DIM = 256
SEQ_DEV = 3
PIECE = 32
AXES = ("dp", "heads", "tensor")
SWAP_AXES = (0, 0, 0, 0, 1)
MESH = pl.DeviceIdType.MESH


EPSILON = 1e-05
GROUP_EPS = 1.0


def layer_norm(values, epsilon):
    center = values - jnp.mean(values, -1, keepdims=True)
    scale = lax.rsqrt(jnp.mean(center * center, -1, keepdims=True) + epsilon)
    return (center * scale, scale)


def norm_back(grad, normed, scale):
    return scale * (
        grad
        - jnp.mean(grad, -1, keepdims=True)
        - normed * jnp.mean(grad * normed, -1, keepdims=True)
    )


def product(left, right):
    return jnp.dot(left, right, preferred_element_type=jnp.float32)


def inner_rows(left, right):
    return lax.dot_general(
        left, right, (((1,), (1,)), ((), ())), preferred_element_type=jnp.float32
    )


def inner_cols(left, right):
    return lax.dot_general(
        left, right, (((0,), (0,)), ((), ())), preferred_element_type=jnp.float32
    )


def lowered(value):
    return value.astype(jnp.bfloat16)


def around(axes):
    return tuple(lax.axis_index(name) for name in axes)


def wide(value):
    return value.astype(jnp.float32)


def within(number, count):
    return (number >= 0) & (number < count)


def greet(others):
    barrier = pltpu.get_barrier_semaphore()
    for other in others:
        pl.semaphore_signal(barrier, inc=1, device_id=other, device_id_type=MESH)
    pl.semaphore_wait(barrier, len(others))


def plane_peers(at, sizes):
    group, level, core = at
    return [(lax.rem(group + k, sizes[0]), level, core) for k in range(1, sizes[0])]


def column_peers(at, sizes):
    group, level, core = at
    return [(group, lax.rem(level + k, sizes[1]), core) for k in range(1, sizes[1])] + [
        (group, level, 1 - core)
    ]


def beside(group):
    return group + 1 - 2 * lax.rem(group, 2), lax.rem(group + 2, 4), 3 - group


class Spread:
    def __init__(self, at, sizes, items, sems, relay=True):
        self.at, self.count, self.items = at, sizes[0], items
        self.local, self.sent, self.got = sems
        self.plane = relay and sizes[0] == 4

    @staticmethod
    def scratch(items, sizes):
        ways = max(4, sizes[0] - 1)
        return [
            pltpu.SemaphoreType.DMA((items,)),
            pltpu.SemaphoreType.DMA((items, ways)),
            pltpu.SemaphoreType.DMA((items, ways)),
        ]

    def place(self, number, owner, half=None):
        source, target, axis, *where = self.items[number]
        rows = source.shape[0]
        size = source.shape[axis]
        step, offset = where or (size, 0)
        start = owner * step + offset
        if half is None:
            begin, height = 0, rows
        else:
            begin, height = half * (rows // 2), rows // 2
        if axis == 0:
            return target.at[pl.ds(pl.multiple_of(start + begin, height), height)]
        return target.at[pl.ds(begin, height), pl.ds(pl.multiple_of(start, size), size)]

    def own(self, number):
        return pltpu.make_async_copy(
            self.items[number][0], self.place(number, self.at[0]), self.local.at[number]
        )

    def copy(self, number, source, place, way, peer):
        return pltpu.make_async_remote_copy(
            src_ref=source,
            dst_ref=place,
            send_sem=self.sent.at[number, way],
            recv_sem=self.got.at[number, way],
            device_id=(peer,) + self.at[1:],
            device_id_type=MESH,
        )

    def away(self, number, k):
        peer = lax.rem(self.at[0] + k, self.count)
        return self.copy(number, self.items[number][0], self.place(number, self.at[0]), k - 1, peer)

    def landed(self, number, k):
        owner = lax.rem(self.at[0] + self.count - k, self.count)
        return self.copy(number, self.items[number][0], self.place(number, owner), k - 1, owner)

    def to(self, number, way):
        peer = beside(self.at[0])[way]
        return self.copy(number, self.items[number][0], self.place(number, self.at[0]), way, peer)

    def of(self, number, way):
        peer = beside(self.at[0])[way]
        return self.copy(number, self.items[number][0], self.place(number, peer), way, peer)

    def on(self, number, way):
        near = beside(self.at[0])
        ref = self.place(number, near[way], way)
        return self.copy(number, ref, ref, 2 + way, near[1 - way])

    def last(self, number, way):
        near = beside(self.at[0])
        ref = self.place(number, near[2], way)
        return self.copy(number, ref, ref, 2 + way, near[1 - way])

    def start(self, *numbers):
        for number in numbers:
            if self.plane:
                self.to(number, 0).start()
                self.to(number, 1).start()
            else:
                for k in range(1, self.count):
                    self.away(number, k).start()
            self.own(number).start()

    def relay(self, *numbers):
        if self.plane:
            for number in numbers:
                for way in range(2):
                    self.of(number, way).wait_recv()
                    self.on(number, way).start()

    def wait(self, *numbers):
        for number in numbers:
            self.own(number).wait()
            if self.plane:
                self.last(number, 0).wait_recv()
                self.last(number, 1).wait_recv()
            else:
                for k in range(1, self.count):
                    self.landed(number, k).wait_recv()

    def drain(self, *numbers):
        for number in numbers:
            if self.plane:
                for way in range(2):
                    self.to(number, way).wait_send()
                    self.on(number, way).wait_send()
            else:
                for k in range(1, self.count):
                    self.away(number, k).wait_send()


class Gather:
    def __init__(self, at, sizes, count, full, sems):
        self.at, self.levels, self.count, self.full = at, sizes[1], count, full
        self.sent_up, self.got_up, self.sent_down, self.got_down, self.sent_core, self.got_core = sems

    @staticmethod
    def scratch(count, sizes, piece):
        levels = sizes[1]
        dma = pltpu.SemaphoreType.DMA
        return [pltpu.VMEM((count, levels, 2) + piece, jnp.bfloat16)] + [
            dma((levels - 1, count)) for _ in range(4)
        ] + [dma((2 * levels - 1, count)) for _ in range(2)]

    def copy(self, ref, sent, got, target):
        return pltpu.make_async_remote_copy(
            src_ref=ref, dst_ref=ref, send_sem=sent, recv_sem=got, device_id=target, device_id_type=MESH
        )

    def up(self, k, hop, origin, sem):
        group, level, core = self.at
        target = (group, lax.rem(level + 1, self.levels), core)
        return self.copy(self.full.at[k, origin, core], self.sent_up.at[sem, k], self.got_up.at[sem, k], target)

    def down(self, k, hop, origin, sem):
        group, level, core = self.at
        target = (group, lax.rem(level + self.levels - 1, self.levels), core)
        return self.copy(
            self.full.at[k, origin, core], self.sent_down.at[sem, k], self.got_down.at[sem, k], target
        )

    def across(self, k, origin, side, sem):
        group, level, core = self.at
        return self.copy(
            self.full.at[k, origin, side], self.sent_core.at[sem, k], self.got_core.at[sem, k], (group, level, 1 - core)
        )

    def start(self, k):
        group, level, core = self.at

        @pl.when(level < self.levels - 1)
        def _():
            self.up(k, 0, level, 0).start()

        @pl.when(level > 0)
        def _():
            self.down(k, 0, level, 0).start()

        self.across(k, level, core, 0).start()

    def hop(self, k, hop):
        group, level, core = self.at
        last = self.levels - 1

        @pl.when(level >= hop)
        def _():
            origin = level - hop
            self.up(k, hop, origin, hop - 1).wait_recv()
            if hop < last:

                @pl.when(level < last)
                def _():
                    self.up(k, hop, origin, hop).start()

            self.across(k, origin, core, hop).start()

        @pl.when(level + hop <= last)
        def _():
            origin = level + hop
            self.down(k, hop, origin, hop - 1).wait_recv()
            if hop < last:

                @pl.when(level > 0)
                def _():
                    self.down(k, hop, origin, hop).start()

            self.across(k, origin, core, last + hop).start()

    def ready(self, k):
        group, level, core = self.at
        last = self.levels - 1
        self.across(k, level, 1 - core, 0).wait_recv()
        for hop in range(1, self.levels):

            @pl.when(level >= hop)
            def _():
                self.across(k, level - hop, 1 - core, hop).wait_recv()

            @pl.when(level + hop <= last)
            def _():
                self.across(k, level + hop, 1 - core, last + hop).wait_recv()

    def drain(self):
        group, level, core = self.at
        last = self.levels - 1

        def one(k, _):
            self.across(k, level, core, 0).wait_send()
            for hop in range(self.levels):
                if hop < last:

                    @pl.when((level >= hop) & (level < last))
                    def _():
                        self.up(k, hop, level - hop, hop).wait_send()

                    @pl.when((level + hop <= last) & (level > 0))
                    def _():
                        self.down(k, hop, level + hop, hop).wait_send()

                if hop > 0:

                    @pl.when(level >= hop)
                    def _():
                        self.across(k, level - hop, core, hop).wait_send()

                    @pl.when(level + hop <= last)
                    def _():
                        self.across(k, level + hop, core, last + hop).wait_send()

            return 0

        lax.fori_loop(0, self.count, one, 0)


class Scatter:
    REFS = 4

    def __init__(self, at, sizes, count, refs):
        self.at, self.levels, self.count = at, sizes[1], count
        self.part, self.cross, self.inbox, self.total = refs[:4]
        self.sent_core, self.got_core, self.sent_up, self.got_up, self.sent_down, self.got_down = refs[4:]

    @staticmethod
    def rooms(count, sizes, piece):
        levels = sizes[1]
        return [
            pltpu.VMEM((2, levels, 2) + piece, jnp.bfloat16),
            pltpu.VMEM((count, levels) + piece, jnp.bfloat16),
            pltpu.VMEM((count, levels + 1) + piece, jnp.bfloat16),
            pltpu.VMEM(piece, jnp.float32),
        ]

    @staticmethod
    def sems(count, sizes):
        dma = pltpu.SemaphoreType.DMA
        return [dma((count,)) for _ in range(2)] + [dma((sizes[1], count)) for _ in range(4)]

    @staticmethod
    def scratch(count, sizes, piece):
        return Scatter.rooms(count, sizes, piece) + Scatter.sems(count, sizes)

    def across(self, k):
        group, level, core = self.at
        return pltpu.make_async_remote_copy(
            src_ref=self.part.at[lax.rem(k, 2), :, 1 - core],
            dst_ref=self.cross.at[k],
            send_sem=self.sent_core.at[k],
            recv_sem=self.got_core.at[k],
            device_id=(group, level, 1 - core),
            device_id_type=MESH,
        )

    def up(self, k, owner):
        group, level, core = self.at
        return pltpu.make_async_remote_copy(
            src_ref=self.cross.at[k, owner],
            dst_ref=self.inbox.at[k, owner + 1],
            send_sem=self.sent_up.at[owner, k],
            recv_sem=self.got_up.at[owner, k],
            device_id=(group, lax.rem(level + 1, self.levels), core),
            device_id_type=MESH,
        )

    def down(self, k, owner):
        group, level, core = self.at
        return pltpu.make_async_remote_copy(
            src_ref=self.cross.at[k, owner],
            dst_ref=self.inbox.at[k, owner],
            send_sem=self.sent_down.at[owner, k],
            recv_sem=self.got_down.at[owner, k],
            device_id=(group, lax.rem(level + self.levels - 1, self.levels), core),
            device_id_type=MESH,
        )

    def free(self, k, before=None):
        @pl.when(k >= 2)
        def _():
            self.across(k - 2).wait_send()

        if before is not None:

            @pl.when(k < 2)
            def _():
                before.across(self.count - 2 + k).wait_send()

    def start(self, k):
        self.across(k).start()

    def join(self, k):
        core = self.at[2]
        self.across(k).wait_recv()
        for owner in range(self.levels):
            self.cross[k, owner] = lowered(
                wide(self.part[lax.rem(k, 2), owner, core]) + wide(self.cross[k, owner])
            )

    def step_up(self, k):
        level = self.at[1]
        for owner in range(self.levels - 1, 0, -1):

            @pl.when(level < owner)
            def _():
                @pl.when(level > 0)
                def _():
                    self.up(k, owner).wait_recv()
                    self.cross[k, owner] = lowered(wide(self.cross[k, owner]) + wide(self.inbox[k, owner + 1]))

                self.up(k, owner).start()

    def step_down(self, k):
        level = self.at[1]
        for owner in range(self.levels - 1):

            @pl.when(level > owner)
            def _():
                @pl.when(level < self.levels - 1)
                def _():
                    self.down(k, owner).wait_recv()
                    self.cross[k, owner] = lowered(wide(self.cross[k, owner]) + wide(self.inbox[k, owner]))

                self.down(k, owner).start()

    def steps(self, wave):
        level = self.at[1]
        above = wave - level
        below = wave - (self.levels - 1 - level)

        @pl.when(within(above, self.count) & (level < self.levels // 2))
        def _():
            self.step_up(above)

        @pl.when(within(below, self.count))
        def _():
            self.step_down(below)

        @pl.when(within(above, self.count) & (level >= self.levels // 2))
        def _():
            self.step_up(above)

    def finish(self, k):
        level = self.at[1]
        self.total[...] = wide(self.cross[k, level])

        @pl.when(level > 0)
        def _():
            self.up(k, level).wait_recv()
            self.total[...] += wide(self.inbox[k, level + 1])

        @pl.when(level < self.levels - 1)
        def _():
            self.down(k, level).wait_recv()
            self.total[...] += wide(self.inbox[k, level])

    def sent(self, k):
        level = self.at[1]
        for owner in range(self.levels):

            @pl.when(level < owner)
            def _():
                self.up(k, owner).wait_send()

            @pl.when(level > owner)
            def _():
                self.down(k, owner).wait_send()

    def drain(self):
        self.across(self.count - 2).wait_send()
        self.across(self.count - 1).wait_send()
        in_order(self.count, self.sent)


def in_order(count, step):
    def body(number, carry):
        step(number)
        return carry

    lax.fori_loop(0, count, body, 0)


def span(number, size):
    return pl.ds(pl.multiple_of(number * size, size), size)


class Moves:
    def __init__(self, pairs, sems):
        self.pairs, self.sems = pairs, sems

    def copy(self, number):
        return pltpu.make_async_copy(*self.pairs[number], self.sems.at[number])

    def start(self, *numbers):
        for number in numbers:
            self.copy(number).start()

    def wait(self, *numbers):
        for number in numbers:
            self.copy(number).wait()


class Chunks:
    def __init__(self, pairs, size, sems):
        self.pairs, self.size, self.sems = pairs, size, sems

    def start(self, k):
        for number, (source, target) in enumerate(self.pairs):
            rows = span(k, self.size)
            pltpu.make_async_copy(source.at[rows], target.at[rows], self.sems.at[number, k]).start()

    def wait(self, count):
        def one(k, carry):
            for number, (source, target) in enumerate(self.pairs):
                rows = span(k, self.size)
                pltpu.make_async_copy(source.at[rows], target.at[rows], self.sems.at[number, k]).wait()
            return carry

        lax.fori_loop(0, count, one, 0)


def matmul(left, right):
    return jnp.dot(left, right, preferred_element_type=jnp.float32)


def decay_tile(near, far, size, bounds, rate):
    rows = near * size + lax.broadcasted_iota(jnp.int32, (size, 1), 0)
    columns = far * size + lax.broadcasted_iota(jnp.int32, (1, size), 1)
    row_seq, column_seq = jnp.zeros((size, 1), jnp.int32), jnp.zeros((1, size), jnp.int32)
    for number in range(1, SEQ_DEV):
        row_seq += (rows >= bounds[number]).astype(jnp.int32)
        column_seq += (columns >= bounds[number]).astype(jnp.int32)
    distance = rows - columns
    valid = (distance >= 0) & (row_seq == column_seq)
    return (
        jnp.where(valid, jnp.exp(jnp.maximum(distance, 0).astype(jnp.float32) * rate[0]), 0.0)
        * QK_DIM ** (-0.5)
    )


class Swap:
    def __init__(self, at, sizes, items, sems, halves=None):
        self.at, self.count, self.items = at, sizes[0], items
        self.local, self.sent, self.got = sems
        self.halves = halves
        self.plane = halves is not None and sizes[0] == 4

    @staticmethod
    def scratch(items, sizes):
        ways = max(6, sizes[0] - 1)
        return [
            pltpu.SemaphoreType.DMA((items,)),
            pltpu.SemaphoreType.DMA((items, ways)),
            pltpu.SemaphoreType.DMA((items, ways)),
        ]

    def block(self, number, owner, half=None):
        source, target, axis = self.items[number]
        rows, columns = source.shape
        size = source.shape[axis] // self.count
        height = size if axis == 0 else rows
        begin = 0
        if half is not None:
            height //= 2
            begin = half * height
        if axis == 0:
            return source.at[pl.ds(pl.multiple_of(owner * size + begin, height), height)]
        return source.at[pl.ds(begin, height), pl.ds(pl.multiple_of(owner * size, size), size)]

    def half(self, number, slot, half):
        target = self.items[number][1]
        height = target.shape[1] // 2
        return target.at[slot, pl.ds(half * height, height)]

    def copy(self, number, source, place, way, peer):
        return pltpu.make_async_remote_copy(
            src_ref=source,
            dst_ref=place,
            send_sem=self.sent.at[number, way],
            recv_sem=self.got.at[number, way],
            device_id=(peer,) + self.at[1:],
            device_id_type=MESH,
        )

    def own(self, number):
        return pltpu.make_async_copy(
            self.block(number, self.at[0]), self.items[number][1].at[0], self.local.at[number]
        )

    def away(self, number, k):
        peer = lax.rem(self.at[0] + k, self.count)
        return self.copy(number, self.block(number, peer), self.items[number][1].at[k], k - 1, peer)

    def across(self, number, way):
        near = beside(self.at[0])
        return self.copy(
            number, self.block(number, near[2], way), self.halves[number].at[way], way, near[way]
        )

    def direct(self, number, way):
        near = beside(self.at[0])
        return self.copy(
            number, self.block(number, near[way], way), self.half(number, 1 + way, way), 2 + way, near[way]
        )

    def added(self, number, way):
        peer = beside(self.at[0])[1 - way]
        return self.copy(
            number, self.block(number, peer, way), self.half(number, 2 - way, way), 4 + way, peer
        )

    def start(self, *numbers):
        for number in numbers:
            if self.plane:
                for way in range(2):
                    self.across(number, way).start()
                for way in range(2):
                    self.direct(number, way).start()
            else:
                for k in range(1, self.count):
                    self.away(number, k).start()
            self.own(number).start()

    def relay(self, *numbers):
        if self.plane:
            near = beside(self.at[0])
            for number in numbers:
                for way in range(2):
                    self.across(number, way).wait_recv()
                    part = self.block(number, near[1 - way], way)
                    part[...] = lowered(wide(part[...]) + wide(self.halves[number][way]))
                    self.added(number, way).start()

    def wait(self, *numbers):
        for number in numbers:
            self.own(number).wait()
            if self.plane:
                for way in range(2):
                    self.across(number, way).wait_send()
                    self.direct(number, way).wait()
                    self.added(number, way).wait()
            else:
                for k in range(1, self.count):
                    self.away(number, k).wait()


def half_blocks(items, sizes):
    room = []
    for whole, axis in items:
        shape = list(whole.shape)
        shape[axis] //= sizes[0]
        room.append(pltpu.VMEM((2, shape[0] // 2, shape[1]), jnp.bfloat16))
    return room


def quarters(source, target):
    rows = source.shape[0]
    run = rows // 4
    return [(source.at[pl.ds(k * run, run)], target, 0, rows, k * run) for k in range(4)]


def pick_rows(whole, number, first, rows, bounds, shifts, begins):
    window = 2 * rows
    lane = lax.broadcasted_iota(jnp.int32, (rows, window), 1)
    slot = jnp.zeros((rows, 1), jnp.int32)
    own = first + lax.broadcasted_iota(jnp.int32, (rows, 1), 0)
    for item in range(1, SEQ_DEV):
        slot += (own >= bounds[item]).astype(jnp.int32)
    chosen, windows = [], []
    for item in range(SEQ_DEV):
        start = begins[number * SEQ_DEV + item]
        wanted = jnp.where(slot == item, own + shifts[item] - 16 * start, -1)
        chosen.append(jnp.where(lane == wanted, 1.0, 0.0).astype(jnp.bfloat16))
        windows += [whole[start + k] for k in range(window // 16)]
    return lowered(matmul(jnp.concatenate(chosen, axis=1), jnp.concatenate(windows, axis=0)))


def front_kernel(sizes, bounds, shifts, begins, tokens, cotangent, gain_rows, *refs):
    masters, refs = refs[:8], refs[8:]
    normed_out, query_out, key_out, value_out, swish_out, dy_out, *refs = refs
    weight_outs, rounded_outs, refs = refs[:4], refs[4:8], refs[8:]
    gain_one, gain_two, rows_out, unit_out, scale_out, *refs = refs
    full, *refs = refs
    gather_sems, refs = refs[:6], refs[6:]
    spread_sems, small_sems, refs = refs[:3], refs[3:6], refs[6:]
    held, rounded, weights, refs = refs[:8], refs[8:16], refs[16:20], refs[20:]
    tokens_held, dy_held, gains_held, tokens_all, dy_all, gains_all, dy_part, *refs = refs
    normed, query, keys, values, swish, load_sems, store_sems, out_sems, normed_sem = refs
    at = around(AXES)
    group, level, core = at
    place = 2 * level + core
    count, levels, _, chunk, width = full.shape
    ranks = 2 * levels
    piece = chunk // ranks
    loads = Moves(
        list(zip(masters, held)) + [(tokens, tokens_held), (gain_rows, gains_held), (cotangent, dy_held)], load_sems
    )
    loads.start(8, 9, 2, 3, 1, 0, 10, 4, 5, 6, 7)
    greet(plane_peers(at, sizes) + column_peers(at, sizes))
    loads.wait(8, 9)
    spread = Spread(
        at,
        sizes,
        quarters(tokens_held, tokens_all)
        + [(rounded[2], weights[2], 0), (rounded[3], weights[3], 0)]
        + quarters(dy_held, dy_all)
        + [(rounded[1], weights[1], 0), (rounded[0], weights[0], 0)],
        spread_sems,
    )
    small = Spread(at, sizes, [(gains_held, gains_all, 0)], small_sems, relay=False)
    spread.start(*range(4))
    small.start(0)
    gather = Gather(at, sizes, count, full, gather_sems)

    def cast(number):
        loads.wait(number)
        rows = min(32, held[number].shape[0])

        def block(k):
            held_rows = span(k, rows)
            rounded[number][held_rows, :] = lowered(held[number][held_rows, :])

        in_order(held[number].shape[0] // rows, block)

    stores = Moves(list(zip(rounded[4:], rounded_outs)), store_sems)
    cast(2)
    spread.start(4)
    for number in (3, 1, 0, 4, 5, 6, 7):
        cast(number)
    loads.wait(10)
    stores.start(*range(4))
    for number in range(4):
        spread.relay(number)
    spread.start(5, 6, 7)
    small.wait(0)
    own = gains_held.shape[0]
    for row, gain in enumerate((gain_one, gain_two)):
        gain[...] = wide(
            lowered(
                jnp.concatenate([gains_all[own * k + row : own * k + row + 1, :] for k in range(sizes[0])], axis=1)
            )
        )
    spread.wait(*range(4))
    run = chunk // 2

    def pick_chunk(whole, k, half):
        return pick_rows(whole, 2 * k + half, k * chunk + half * run, run, bounds, shifts, begins)

    def begin(k):
        for half in range(2):
            full[k, level, core, half * run : (half + 1) * run, :] = pick_chunk(tokens_all, k, half)
        gather.start(k)

    def norm(k):
        def block(number, carry):
            rows = span(number, 16)
            value = jnp.concatenate(
                [wide(full[k, q, c, rows, :]) for q in range(levels) for c in range(2)], axis=1
            )
            unit, scale = layer_norm(value, EPSILON)
            where = pl.ds(pl.multiple_of(k * chunk + number * 16, 16), 16)
            normed[where, :] = lowered(unit * gain_one[...])
            mine = wide(full[k, level, core, rows, :])
            mean = jnp.mean(value, -1, keepdims=True)
            unit_out[where, :] = (mine - mean) * scale
            scale_out[where, :] = jnp.broadcast_to(scale, (16, 128))
            return carry

        lax.fori_loop(0, chunk // 16, block, 0)
        mine = span(place, piece)
        rows_out[span(k, piece), :] = jnp.concatenate(
            [full[k, q, c, mine, :] for q in range(levels) for c in range(2)], axis=1
        )
        pltpu.make_async_copy(
            normed.at[span(k, chunk)], normed_out.at[span(k, chunk)], normed_sem.at[k]
        ).start()

    begin(0)
    outs = [(query, query_out), (keys, key_out), (values, value_out), (swish, swish_out)]
    ends = Moves(outs + list(zip(weights, weight_outs)) + [(dy_part, dy_out)], out_sems)

    def project_rows(number, k):
        where = span(k, chunk)
        target = outs[number][0]
        target[where, :] = matmul(normed[where, :], weights[number][...]).astype(target.dtype)

    def wave(number):
        @pl.when(number + 1 < count)
        def _():
            begin(number + 1)

        for hop in range(levels - 1, 0, -1):

            @pl.when(within(number - hop, count))
            def _():
                gather.hop(number - hop, hop)

        for step, relayed, started in (
            (1, (4,), (8, 9)),
            (3, (5,), (10, 11)),
            (5, (6, 7), ()),
            (6, (8, 9), ()),
            (8, (10,), ()),
        ):

            @pl.when(number == step)
            def _():
                spread.relay(*relayed)
                spread.start(*started)

        @pl.when(within(number - levels, count))
        def _():
            gather.ready(number - levels)
            norm(number - levels)

        @pl.when(number == levels + 3)
        def _():
            spread.wait(4)
            ends.start(6)
            for k in range(3):
                project_rows(2, k)

        @pl.when(number >= levels + 3)
        def _():
            project_rows(2, number - levels)

    in_order(count + levels, wave)

    def project(number, item):
        if item is not None:
            spread.wait(item)
            ends.start(4 + number)
            in_order(count, functools.partial(project_rows, number))
        ends.start(number)

    spread.relay(11)
    project(2, None)
    project(3, 5)
    spread.wait(*range(6, 10))

    def dy_chunk(k):
        for half in range(2):
            dy_part[k, half * run : (half + 1) * run, :] = pick_chunk(dy_all, k, half)

    in_order(count, dy_chunk)
    ends.start(8)
    project(1, 10)
    project(0, 11)
    small.drain(0)
    spread.drain(*range(12))
    gather.drain()
    stores.wait(*range(4))
    ends.wait(*range(9))

    def stored(k):
        pltpu.make_async_copy(
            normed.at[span(k, chunk)], normed_out.at[span(k, chunk)], normed_sem.at[k]
        ).wait()

    in_order(count, stored)


class Ring:
    def __init__(self, slots, whole, size, sems):
        self.slots, self.whole, self.size, self.sems = slots, whole, size, sems

    def load(self, k):
        return pltpu.make_async_copy(
            self.whole.at[span(k, self.size)], self.slots.at[lax.rem(k, 2)], self.sems.at[k]
        )

    def store(self, k):
        return pltpu.make_async_copy(
            self.slots.at[lax.rem(k, 2)], self.whole.at[span(k, self.size)], self.sems.at[k]
        )

    def free(self, k):
        @pl.when(k >= 2)
        def _():
            self.store(k - 2).wait()


def core_kernel(sizes, bounds, rate, gain, *refs):
    query_src, key_src, value_src, rows_src, dy_src, swish_src, *refs = refs
    shards, refs = refs[:4], refs[4:]
    mixed_in_out, retained_out, branch_out, swish_out, query_out, key_out, value_out, *refs = refs
    gain_out, mixed_dst, down_dst, gate_dst, up_dst, *refs = refs
    query, keys, values, x_rows, out_w, gate_w, up_w, down_w, *refs = refs
    rooms, refs = refs[:4], refs[4:]
    (other_part,), refs = refs[:1], refs[1:]
    sems_one, sems_two, sems_three, refs = refs[:6], refs[6:12], refs[12:18], refs[18:]
    normed_mid, refs = refs[0], refs[1:]
    normed_sems, refs = refs[:6], refs[6:]
    dy, refs = refs[0], refs[1:]
    dy_sems, refs = refs[:6], refs[6:]
    branch, refs = refs[0], refs[1:]
    branch_sems, refs = refs[:6], refs[6:]
    spread_sems, refs = refs[:3], refs[3:]
    deal_sems, refs = refs[:3], refs[3:]
    swap_sems, refs = refs[:3], refs[3:]
    hidden, gate_grad, up_grad, resid, swish_slots, retained_slots, mixed_in_slots, grad_slots, *refs = refs
    key_acc, value_acc, query_acc, delta, down_grad, mixed, *refs = refs
    load_sems, ring_sems, branch_store, query_store, end_sems, *halves = refs
    at = around(AXES)
    group, level, core = at
    place = 2 * level + core
    count, levels, _, piece, width = normed_mid.shape
    ranks = 2 * levels
    chunk = ranks * piece
    part_width = width // ranks
    loads = Moves(
        [
            (dy_src, dy.at[:, level, core]),
            (query_src, query),
            (key_src, keys),
            (value_src, values),
            (rows_src, x_rows),
        ],
        load_sems,
    )
    loads.start(*range(5))
    swish_one = Ring(swish_slots, swish_src, chunk, ring_sems.at[0])
    swish_two = Ring(swish_slots, swish_src, chunk, ring_sems.at[1])
    retained_one = Ring(retained_slots, retained_out, chunk, ring_sems.at[2])
    retained_two = Ring(retained_slots, retained_out, chunk, ring_sems.at[3])
    mixed_in_ring = Ring(mixed_in_slots, mixed_in_out, chunk, ring_sems.at[4])
    grad_ring = Ring(grad_slots, swish_out, chunk, ring_sems.at[5])
    query_ends = Chunks([(query, query_out)], chunk, query_store)
    swish_one.load(0).start()
    swish_one.load(1).start()
    greet(plane_peers(at, sizes) + column_peers(at, sizes))
    spread = Spread(
        at,
        sizes,
        [(shards[0], out_w, 1), (shards[1], gate_w, 0), (shards[2], up_w, 0), (shards[3], down_w, 1)],
        spread_sems,
    )
    deal = Spread(
        at,
        sizes,
        [
            (mixed.at[pl.ds(k * chunk, chunk)], mixed_dst, 0, count * chunk, k * chunk)
            for k in range(count)
        ],
        deal_sems,
    )
    swap = Swap(
        at, sizes, [(down_grad, down_dst, 1), (gate_w, gate_dst, 0), (up_w, up_dst, 0)], swap_sems, halves
    )
    spread.start(0)
    one = Scatter(at, sizes, count, list(rooms) + list(sems_one))
    two = Scatter(at, sizes, count, [other_part] + list(rooms[1:]) + list(sems_two))
    three = Scatter(at, sizes, count, list(rooms) + list(sems_three))
    total = rooms[3]
    mid_gather = Gather(at, sizes, count, normed_mid, normed_sems)
    dy_gather = Gather(at, sizes, count, dy, dy_sems)
    branch_gather = Gather(at, sizes, count, branch, branch_sems)
    gain_out[...] = jnp.zeros(gain_out.shape, jnp.float32)
    key_acc[...] = jnp.zeros(key_acc.shape, jnp.float32)
    value_acc[...] = jnp.zeros(value_acc.shape, jnp.float32)
    loads.wait(0)
    dy_gather.start(0)
    loads.wait(1, 2, 3, 4)
    tile = 512

    def branch_stores(k):
        copies = []
        for q in range(levels):
            for c in range(2):
                rows = pl.ds(pl.multiple_of(k * chunk + (2 * q + c) * piece, piece), piece)
                copies.append(
                    pltpu.make_async_copy(branch.at[k, q, c], branch_out.at[rows], branch_store.at[2 * q + c, k])
                )
        return copies

    def first(k):
        where = span(k, chunk)
        slot = lax.rem(k, 2)
        retained_one.free(k)
        retained_slots[slot] = jnp.zeros((chunk, values.shape[1]), jnp.float32)

        def block(j, carry):
            there = span(j, chunk)
            decay = decay_tile(k, j, chunk, bounds, rate)
            weight = lowered(inner_rows(query[where, :], keys[there, :]) * decay)
            retained_slots[slot] += matmul(weight, values[there, :])
            return carry

        lax.fori_loop(0, k + 1, block, 0)
        retained_one.store(k).start()
        normed, _ = layer_norm(retained_slots[slot], GROUP_EPS)
        swish_one.load(k).wait()
        value = swish_slots[slot]
        mixed_in_ring.free(k)
        mixed_in_slots[slot] = lowered(value * jax.nn.sigmoid(value) * normed)
        mixed_in_ring.store(k).start()

        @pl.when(k + 2 < count)
        def _():
            swish_one.load(k + 2).start()

        @pl.when(k == 0)
        def _():
            spread.wait(0)

        one.free(k)
        rows = mixed_in_slots[slot]
        for column in range(0, width, tile):
            value = matmul(rows, out_w[:, column : column + tile])
            one.part[slot, :, :, :, column : column + tile] = lowered(value).reshape(levels, 2, piece, tile)
        one.start(k)

    def mid_norm(k):
        one.finish(k)

        def block(number, carry):
            sub = span(number, 16)
            where = pl.ds(pl.multiple_of(k * piece + number * 16, 16), 16)
            value = wide(x_rows[where, :]) + total[sub, :]
            resid[where, :] = value
            unit, _ = layer_norm(value, EPSILON)
            normed_mid[k, level, core, sub, :] = lowered(unit * gain[...])
            return carry

        lax.fori_loop(0, piece // 16, block, 0)
        mid_gather.start(k)

    def turn(k):
        mid_gather.ready(k)
        rows = normed_mid[k].reshape(chunk, width)
        where = span(k, chunk)
        g = matmul(rows, gate_w[...])
        u = matmul(rows, up_w[...])
        root = 0.7978845608028654
        bend = jnp.tanh(root * (g + 0.044715 * g * g * g))
        curve = 0.5 * (1.0 + bend)
        active = g * curve
        hidden[where, :] = lowered(active * u)
        slope = curve + 0.5 * g * (1.0 - bend * bend) * root * (1.0 + 0.134145 * g * g)
        dy_gather.ready(k)
        rows = jnp.concatenate([dy[k, q, c] for q in range(levels) for c in range(2)], axis=1)
        back = inner_rows(rows, down_w[...])
        gate_grad[where, :] = lowered(back * u * slope)
        up_grad[where, :] = lowered(back * active)
        two.free(k)
        for column in range(0, width, tile):
            columns = slice(column, column + tile)
            value = inner_rows(gate_grad[where, :], gate_w[columns, :])
            value += inner_rows(up_grad[where, :], up_w[columns, :])
            two.part[lax.rem(k, 2), :, :, :, columns] = lowered(value).reshape(levels, 2, piece, tile)
        two.start(k)

    def branch_norm(k):
        two.finish(k)

        def block(number, carry):
            sub = span(number, 16)
            where = pl.ds(pl.multiple_of(k * piece + number * 16, 16), 16)
            unit, scale = layer_norm(resid[where, :], EPSILON)
            grad = total[sub, :]
            outer = grad * unit
            gain_out[...] += outer[:8] + outer[8:]
            mine = pl.ds(pl.multiple_of(place * piece + number * 16, 16), 16)
            upstream = jnp.concatenate(
                [dy[k, q, c, mine, :] for q in range(levels) for c in range(2)], axis=1
            )
            value = wide(upstream) + norm_back(grad * gain[...], unit, scale)
            branch[k, level, core, sub, :] = lowered(value)
            return carry

        lax.fori_loop(0, piece // 16, block, 0)
        branch_gather.start(k)

    def last(k):
        branch_gather.ready(k)
        for copy in branch_stores(k):
            copy.start()
        rows = branch[k].reshape(chunk, width)
        where = span(k, chunk)
        slot = lax.rem(k, 2)
        grad = inner_rows(rows, out_w[...])
        retained_two.load(k).wait()
        swish_two.load(k).wait()
        normed, scale = layer_norm(retained_slots[slot], GROUP_EPS)
        value = swish_slots[slot]
        gated = jax.nn.sigmoid(value)
        grad_ring.free(k)
        grad_slots[slot] = lowered(grad * normed * gated * (1.0 + value * (1.0 - gated)))
        grad_ring.store(k).start()
        delta[...] = lowered(norm_back(grad * value * gated, normed, scale))

        @pl.when(k + 2 < count)
        def _():
            retained_two.load(k + 2).start()
            swish_two.load(k + 2).start()

        query_acc[...] = jnp.zeros(query_acc.shape, jnp.float32)

        def block(j, carry):
            there = span(j, chunk)
            decay = decay_tile(k, j, chunk, bounds, rate)
            weight = lowered(inner_rows(query[where, :], keys[there, :]) * decay)
            score = lowered(inner_rows(delta[...], values[there, :]) * decay)
            query_acc[...] += matmul(score, keys[there, :])
            key_acc[there, :] += inner_cols(score, query[where, :])
            value_acc[there, :] += inner_cols(weight, delta[...])
            return carry

        lax.fori_loop(0, k + 1, block, 0)
        query[where, :] = lowered(query_acc[...])
        query_ends.start(k)

    def out_part(k):
        three.free(k, one)
        rows = hidden[span(k, chunk), :]
        mine = pl.ds(pl.multiple_of(k * piece, piece), piece)
        for rank in range(ranks):
            columns = slice(rank * part_width, (rank + 1) * part_width)
            value = matmul(rows, down_w[:, columns])
            for run in range(ranks):
                held = jnp.where(place == run, resid[mine, columns], 0.0)
                three.part[
                    lax.rem(k, 2), rank // 2, rank % 2, :, run * part_width : (run + 1) * part_width
                ] = lowered(value[run * piece : (run + 1) * piece, :] + held)
        three.start(k)

    def out_finish(k):
        three.finish(k)
        for run in range(ranks):
            where = pl.ds(pl.multiple_of(k * chunk + run * piece, piece), piece)
            mixed[where, :] = lowered(total[:, run * part_width : (run + 1) * part_width])

    def weigh(which):
        def part(k):
            columns = span(k, chunk)
            if which == 0:
                down = jnp.zeros((hidden.shape[1], part_width), jnp.float32)
                for j in range(count):
                    down += inner_cols(hidden[j * chunk : (j + 1) * chunk, :], dy[j, k // 2, lax.rem(k, 2)])
                there = pl.ds(pl.multiple_of(k * part_width, part_width), part_width)
                down_grad[:, there] = lowered(down)
            else:
                target, source = ((gate_w, gate_grad), (up_w, up_grad))[which - 1]
                rows = jnp.concatenate(
                    [
                        normed_mid[j, q, c, :, columns]
                        for j in range(count)
                        for q in range(levels)
                        for c in range(2)
                    ],
                    axis=0,
                )
                target[columns, :] = lowered(inner_cols(rows, source[...]))

        in_order(width // chunk, part)
        swap.start(which)

    lead = 3
    mid_lag = lead + levels
    turn_lag = mid_lag + levels - 1
    branch_lag = turn_lag + levels
    last_lag = branch_lag + levels - 1

    def at_wave(number, lag, step):
        @pl.when(within(number - lag, count))
        def _():
            step(number - lag)

    def wave(number):
        at_wave(number, lead, first)
        for gather, lag, scatter in ((branch_gather, branch_lag, two), (mid_gather, mid_lag, one)):
            at_wave(number, lag + 1, scatter.sent)
            for hop in range(levels - 1, 0, -1):
                at_wave(number, lag + hop, functools.partial(hop_on, gather, hop))
        at_wave(number, branch_lag, branch_norm)
        at_wave(number, mid_lag, mid_norm)
        at_wave(number, -1, next_dy)
        for hop in range(levels - 1, 0, -1):
            at_wave(number, hop, functools.partial(hop_on, dy_gather, hop))
        for scatter, lag in ((two, turn_lag), (one, lead)):
            at_wave(number, lag + 1, scatter.join)
            scatter.steps(number - lag - 1)
        for step, relayed, started in ((1, (0,), (1, 2)), (4, (1,), (3,)), (6, (2,), ()), (8, (3,), ())):

            @pl.when(number == step)
            def _():
                spread.relay(*relayed)
                spread.start(*started)

        @pl.when(number == turn_lag)
        def _():
            spread.wait(1, 2, 3)

        at_wave(number, turn_lag, turn)

        @pl.when(number == turn_lag + 1)
        def _():
            retained_one.store(count - 2).wait()
            retained_one.store(count - 1).wait()
            for k in range(2):
                retained_two.load(k).start()
                swish_two.load(k).start()

        @pl.when(number == turn_lag + count)
        def _():
            spread.drain(*range(4))

        for step, which in ((0, 1), (1, 2), (2, 0)):

            @pl.when(number == turn_lag + count + step)
            def _():
                weigh(which)

        for step, which in ((2, 1), (4, 2), (6, 0)):

            @pl.when(number == turn_lag + count + step)
            def _():
                swap.relay(which)

        at_wave(number, last_lag, last)
        at_wave(number, last_lag, out_part)
        at_wave(number, last_lag + 1, three.join)
        three.steps(number - last_lag - 1)
        at_wave(number, last_lag + levels, out_finish)
        for k in range(count):

            @pl.when(number == last_lag + levels + k)
            def _():
                deal.start(k)

            @pl.when(number == last_lag + levels + k + 2)
            def _():
                deal.relay(k)

    def hop_on(gather, hop, k):
        gather.hop(k, hop)

    def next_dy(k):
        @pl.when(k > 0)
        def _():
            dy_gather.start(k)

    in_order(count + last_lag + levels, wave)
    deal.relay(count - 2, count - 1)
    keys[...] = lowered(key_acc[...])
    values[...] = lowered(value_acc[...])
    ends = Moves([(keys, key_out), (values, value_out)], end_sems)
    ends.start(0, 1)
    swap.wait(0, 1, 2)
    deal.wait(*range(count))
    deal.drain(*range(count))
    two.across(count - 2).wait_send()
    two.across(count - 1).wait_send()
    three.drain()
    mid_gather.drain()
    dy_gather.drain()
    branch_gather.drain()
    ends.wait(0, 1)
    query_ends.wait(count)
    for k in (count - 2, count - 1):
        mixed_in_ring.store(k).wait()
        grad_ring.store(k).wait()

    def stored(k):
        for copy in branch_stores(k):
            copy.wait()

    in_order(count, stored)


def close_kernel(sizes, gain, gain_two, *refs):
    ins, refs = refs[:13], refs[13:]
    grad_out, gains_out, *refs = refs
    targets, refs = refs[:5], refs[5:]
    held, refs = refs[:13], refs[13:]
    deltas, weights = held[:4], held[4:8]
    normed_in, branch, mixed_in, unit, scale = held[8:]
    grads, refs = refs[:5], refs[5:]
    scatter_refs, refs = refs[:10], refs[10:]
    swap_sems, refs = refs[:3], refs[3:]
    sums, line_one, share, packed, gains, gains_in, refs = *refs[:6], refs[6:]
    load_sems, sums_sent, sums_got, gain_sent, gain_got, refs = *refs[:5], refs[5:]
    spread_sems, refs = refs[:3], refs[3:]
    small_sems, halves = refs[:3], refs[3:]
    at = around(AXES)
    group, level, core = at
    place = 2 * level + core
    groups = sizes[0]
    scatter = Scatter(at, sizes, sums.shape[1], scatter_refs)
    _, levels, _, chunk, width = scatter.part.shape
    count, ranks = sums.shape[1], 2 * levels
    rows_all = count * chunk
    loads = Moves(list(zip(ins, held)), load_sems)
    loads.start(8, 3, 4, 5, 6, 7, 0, 1, 2, 9, 10, 11, 12)
    greet(plane_peers(at, sizes) + column_all(at, sizes))
    swap = Swap(at, sizes, list(zip(grads, targets, SWAP_AXES)), swap_sems, halves)
    small = Swap(at, sizes, [(gains, gains_in, 1)], small_sems)
    spread = Spread(
        at,
        sizes,
        [(share.at[pl.ds(k * chunk, chunk)], grad_out, 0, rows_all, k * chunk) for k in range(count)],
        spread_sems,
    )
    line_one[...] = jnp.zeros(line_one.shape, jnp.float32)
    mine = pl.ds(pl.multiple_of(place * width, width), width)

    def first(k):
        scatter.free(k)
        where = span(k, chunk)
        rows = [d[where, :] for d in deltas]
        one = jnp.zeros((chunk, width), jnp.float32)
        two = jnp.zeros((chunk, width), jnp.float32)
        for rank in range(ranks):
            columns = slice(rank * width, (rank + 1) * width)
            value = inner_rows(rows[0], weights[0][columns, :])
            for row, weight in zip(rows[1:], weights[1:]):
                value += inner_rows(row, weight[columns, :])
            scatter.part[lax.rem(k, 2), rank // 2, rank % 2] = lowered(value)
            one += value * gain[:, columns]
            two += value * wide(normed_in[where, columns])
        scatter.start(k)
        ones = jnp.ones((8, width), jnp.float32)
        flat = [
            lax.dot_general(
                ones,
                item,
                (((1,), (1,)), ((), ())),
                precision=lax.Precision.HIGHEST,
                preferred_element_type=jnp.float32,
            )
            for item in (one, two)
        ]
        line = lax.broadcasted_iota(jnp.int32, (8, chunk), 0)
        sums[place, k] = jnp.where(line == 0, flat[0], flat[1])
        for j in range(1, ranks):
            sums_copy(k, j, place).start()

    def sums_copy(k, j, owner):
        peer = lax.rem(place + j, ranks)
        return pltpu.make_async_remote_copy(
            src_ref=sums.at[owner, k],
            dst_ref=sums.at[owner, k],
            send_sem=sums_sent.at[j - 1, k],
            recv_sem=sums_got.at[j - 1, k],
            device_id=(group, peer // 2, lax.rem(peer, 2)),
            device_id_type=MESH,
        )

    def pack_copy(j, owner):
        peer = lax.rem(place + j, ranks)
        return pltpu.make_async_remote_copy(
            src_ref=packed.at[owner],
            dst_ref=packed.at[owner],
            send_sem=gain_sent.at[j - 1],
            recv_sem=gain_got.at[j - 1],
            device_id=(group, peer // 2, lax.rem(peer, 2)),
            device_id_type=MESH,
        )

    def sender(j):
        return lax.rem(place + ranks - j, ranks)

    def finish(k):
        scatter.finish(k)
        for j in range(1, ranks):
            sums_copy(k, j, sender(j)).wait_recv()
        line = lax.broadcasted_iota(jnp.int32, (8, 128), 0)
        lane = lax.broadcasted_iota(jnp.int32, (8, 128), 1)
        means = lax.dot_general(
            jnp.sum(sums[:, k], 0),
            jnp.where(line == lane, 1.0 / (ranks * width), 0.0),
            (((0,), (0,)), ((), ())),
            precision=lax.Precision.HIGHEST,
            preferred_element_type=jnp.float32,
        )
        where = span(k, chunk)
        value, normed = scatter.total[...], unit[where, :]
        outer = value * normed
        line_one[...] += jnp.sum(outer.reshape(chunk // 8, 8, width), 0)
        back = value * gain[:, mine] - means[:, :1] - normed * means[:, 1:2]
        share[where, :] = lowered(wide(branch[where, mine]) + scale[where, :1] * back)

    def weigh(number):
        if number == 4:

            def part(k):
                columns = span(k, chunk)
                grads[4][:, columns] = lowered(inner_cols(mixed_in[...], branch[:, columns]))
        else:

            def part(k):
                columns = span(k, chunk)
                grads[number][columns, :] = lowered(inner_cols(normed_in[:, columns], deltas[number][...]))

        in_order(ranks * width // chunk, part)
        swap.start(number)

    lag = levels - 1

    def wave(number):
        @pl.when(number < count)
        def _():
            first(number)

        for step, which in ((1, 2), (2, 0), (3, 1)):

            @pl.when(number == step)
            def _():
                weigh(which)

        @pl.when(number < count)
        def _():
            scatter.join(number)

        scatter.steps(number)

        @pl.when(number == lag)
        def _():
            loads.wait(9, 10, 11, 12)

        @pl.when(within(number - lag, count))
        def _():
            finish(number - lag)

        for k in range(count):

            @pl.when(number == lag + k)
            def _():
                spread.start(k)

            @pl.when(number == lag + k + 2)
            def _():
                spread.relay(k)

        @pl.when(number == lag + 1)
        def _():
            weigh(4)

        for step, relayed in ((2, 3), (4, 2), (5, 0), (6, 1), (8, 4)):

            @pl.when(number == step)
            def _():
                swap.relay(relayed)

    loads.wait(3, 8)
    weigh(3)
    loads.wait(0, 1, 2, 4, 5, 6, 7)
    in_order(count + lag, wave)
    for k in (count - 2, count - 1):
        spread.relay(k)
    total = jnp.sum(gain_two[...], 0, keepdims=True)
    packed[place] = jnp.concatenate([total, jnp.sum(line_one[...], 0, keepdims=True)], axis=1)
    for j in range(1, ranks):
        pack_copy(j, place).start()
    for j in range(1, ranks):
        pack_copy(j, sender(j)).wait_recv()
    everything = ranks * width
    line = lax.broadcasted_iota(jnp.int32, (8, everything), 0)
    two = sum(packed[rank, :, :everything] for rank in range(ranks))
    one = jnp.concatenate([packed[rank, :, everything:] for rank in range(ranks)], axis=1)
    gains[...] = jnp.where(line == 0, one, two)
    small.start(0)
    small.wait(0)
    swap.wait(*range(5))
    spread.wait(*range(count))
    spread.drain(*range(count))
    gains_out[...] = jnp.sum(gains_in[...], 0)
    for j in range(1, ranks):
        pack_copy(j, place).wait_send()
    scatter.drain()

    def drain(k):
        for j in range(1, ranks):
            sums_copy(k, j, place).wait_send()

    in_order(count, drain)


def column_all(at, sizes):
    group, level, core = at
    return column_peers(at, sizes) + [
        (group, lax.rem(level + k, sizes[1]), 1 - core) for k in range(1, sizes[1])
    ]


def struct(shape, kind=jnp.bfloat16):
    return jax.ShapeDtypeStruct(shape, kind)


VMEM = pltpu.VMEM
DMA = pltpu.SemaphoreType.DMA


def kernel_call(body, number, ins, outs, scratch):
    places = {
        "vmem": pl.BlockSpec(memory_space=pltpu.VMEM),
        "smem": pl.BlockSpec(memory_space=pltpu.SMEM),
        "any": pl.BlockSpec(memory_space=pl.ANY),
    }
    return pl.pallas_call(
        body,
        out_shape=[shape for _, shape in outs],
        in_specs=[places[inside] for inside, _ in ins],
        out_specs=[places[inside] for inside, _ in outs],
        scratch_shapes=scratch,
        compiler_params=pltpu.CompilerParams(
            collective_id=number, has_side_effects=True, vmem_limit_bytes=63 * 2**20
        ),
    )(*[array for _, array in ins])


def spread_shape(shard, axis, sizes):
    shape = list(shard.shape)
    shape[axis] *= sizes[0]
    return struct(tuple(shape), shard.dtype)


def swap_shape(whole, axis, sizes):
    shape = list(whole.shape)
    shape[axis] //= sizes[0]
    return struct((3 if sizes[0] == 4 else sizes[0],) + tuple(shape), whole.dtype)


def anywhere(items):
    return [("any", item) for item in items]


def held_like(arrays):
    return [VMEM(a.shape, a.dtype) for a in arrays]


def pick(rows, whole):
    return whole.at[rows].get(mode="promise_in_bounds")


def shards(
    tokens,
    cotangent,
    lengths,
    dealing,
    w_query,
    w_key,
    w_value,
    w_swish,
    w_out,
    w_gate,
    w_up,
    w_down,
    gain_attn,
    gain_mlp,
):
    group = lax.axis_index("dp")
    place = lax.axis_index(("heads", "tensor"))
    rows_dev = tokens.shape[0]
    slice_width = tokens.shape[1]
    seq_count = lengths.shape[0]
    ident = jnp.arange(seq_count, dtype=jnp.int32)
    starts = jnp.cumsum(lengths) - lengths
    picked = lax.dynamic_slice_in_dim(dealing, group * SEQ_DEV, SEQ_DEV)
    match = picked[:, None] == ident[None, :]
    dealt_len = jnp.sum(jnp.where(match, lengths[None, :], 0), 1)
    home_start = jnp.sum(jnp.where(match, starts[None, :], 0), 1)
    dealt_start = jnp.cumsum(dealt_len) - dealt_len
    rows = jnp.arange(rows_dev, dtype=jnp.int32)
    seq_ids = jnp.sum((rows[:, None] >= dealt_start[None, :]).astype(jnp.int32), 1) - 1
    sizes = (lax.axis_size("dp"), lax.axis_size("heads"))
    ranks = sizes[1] * lax.axis_size("tensor")
    chunk = ranks * PIECE
    count = rows_dev // chunk
    width = slice_width * ranks
    own = rows_dev // ranks
    qk_dim, v_dim, ff_dim = w_query.shape[1], w_value.shape[1], w_gate.shape[1]
    f32 = jnp.float32
    masters = (w_query, w_key, w_value, w_swish, w_out, w_gate, w_up, w_down)
    axes = (0, 0, 0, 0, 1, 0, 0, 1)
    gain_rows = jnp.pad(jnp.stack([gain_attn, gain_mlp]), ((0, 6), (0, 0)))
    shifts = home_start - dealt_start
    firsts = jnp.arange(2 * count, dtype=jnp.int32) * (chunk // 2)
    begins = jnp.clip(firsts[:, None] + shifts[None, :], 0, sizes[0] * rows_dev - chunk) // 16
    bf16 = jnp.bfloat16
    rounded = [struct(w.shape) for w in masters]
    full_w = [spread_shape(w, a, sizes) for w, a in zip(rounded, axes)]
    by_runs = struct((rows_dev // 16, 16, slice_width))
    every = spread_shape(by_runs, 0, sizes)
    gains_all = struct((sizes[0] * 8, gain_rows.shape[1]), f32)
    (
        normed_in,
        query,
        keys,
        values,
        swish_in,
        dy_part,
        query_w,
        key_w,
        value_w,
        swish_w,
        *low,
        wide_one,
        wide_two,
        x_rows,
        unit_share,
        scale_one,
    ) = kernel_call(
        functools.partial(front_kernel, sizes),
        0,
        [("smem", dealt_start), ("smem", shifts), ("smem", begins.reshape(-1))]
        + anywhere((tokens.reshape(by_runs.shape), cotangent.reshape(by_runs.shape), gain_rows) + masters),
        anywhere(
            [
                struct((rows_dev, width)),
                struct((rows_dev, qk_dim)),
                struct((rows_dev, qk_dim)),
                struct((rows_dev, v_dim)),
                struct((rows_dev, v_dim), f32),
                struct((count, chunk, slice_width)),
            ]
            + full_w[:4]
            + rounded[4:]
        )
        + [
            ("vmem", struct((1, width), f32)),
            ("vmem", struct((1, width), f32)),
            ("vmem", struct((own, width))),
            ("vmem", struct((rows_dev, slice_width), f32)),
            ("vmem", struct((rows_dev, 128), f32)),
        ],
        Gather.scratch(count, sizes, (chunk, slice_width))
        + Spread.scratch(12, sizes)
        + Spread.scratch(1, sizes)
        + held_like(masters)
        + held_like(rounded)
        + held_like(full_w[:4])
        + held_like((by_runs, by_runs, gain_rows, every, every, gains_all))
        + [
            VMEM((count, chunk, slice_width), bf16),
            VMEM((rows_dev, width), bf16),
            VMEM((rows_dev, qk_dim), bf16),
            VMEM((rows_dev, qk_dim), bf16),
            VMEM((rows_dev, v_dim), bf16),
            VMEM((rows_dev, v_dim), f32),
            DMA((11,)),
            DMA((4,)),
            DMA((9,)),
            DMA((count,)),
        ],
    )
    rate = jnp.log1p(-jnp.exp2(-5.0 - place.astype(f32))).reshape(1)
    by_rows = (PIECE, width)
    (
        mixed_in,
        _,
        delta_branch,
        delta_swish,
        delta_query,
        delta_keys,
        delta_values,
        gain_two_part,
        mixed_all,
        *ff_grads,
    ) = kernel_call(
        functools.partial(core_kernel, sizes),
        1,
        [("smem", dealt_start), ("smem", rate), ("vmem", wide_two)]
        + anywhere((query, keys, values, x_rows, dy_part, swish_in))
        + anywhere(low),
        anywhere(
            [
                struct((rows_dev, v_dim)),
                struct((rows_dev, v_dim), f32),
                struct((rows_dev, width)),
                struct((rows_dev, v_dim)),
                struct((rows_dev, qk_dim)),
                struct((rows_dev, qk_dim)),
                struct((rows_dev, v_dim)),
            ]
        )
        + [("vmem", struct((8, width), f32))]
        + anywhere(
            [
                struct((sizes[0] * rows_dev, slice_width)),
                swap_shape(full_w[7], 1, sizes),
                swap_shape(full_w[5], 0, sizes),
                swap_shape(full_w[6], 0, sizes),
            ]
        ),
        held_like((query, keys, values, x_rows))
        + held_like(full_w[4:])
        + Scatter.rooms(count, sizes, by_rows)
        + Scatter.rooms(count, sizes, by_rows)[:1]
        + Scatter.sems(count, sizes) * 3
        + Gather.scratch(count, sizes, by_rows)
        + Gather.scratch(count, sizes, (chunk, slice_width))
        + Gather.scratch(count, sizes, by_rows)
        + Spread.scratch(4, sizes)
        + Spread.scratch(count, sizes)
        + Swap.scratch(3, sizes)
        + [
            VMEM((rows_dev, ff_dim), bf16),
            VMEM((rows_dev, ff_dim), bf16),
            VMEM((rows_dev, ff_dim), bf16),
            VMEM((own, width), f32),
            VMEM((2, chunk, v_dim), f32),
            VMEM((2, chunk, v_dim), f32),
            VMEM((2, chunk, v_dim), bf16),
            VMEM((2, chunk, v_dim), bf16),
            VMEM((rows_dev, qk_dim), f32),
            VMEM((rows_dev, v_dim), f32),
            VMEM((chunk, qk_dim), f32),
            VMEM((chunk, v_dim), bf16),
            VMEM((ff_dim, width), bf16),
            VMEM((rows_dev, slice_width), bf16),
            DMA((5,)),
            DMA((6, count)),
            DMA((ranks, count)),
            DMA((1, count)),
            DMA((2,)),
        ]
        + half_blocks([(full_w[7], 1), (full_w[5], 0), (full_w[6], 0)], sizes),
    )
    close_ins = (
        delta_query,
        delta_keys,
        delta_values,
        delta_swish,
        query_w,
        key_w,
        value_w,
        swish_w,
        normed_in,
        delta_branch,
        mixed_in,
        unit_share,
        scale_one,
    )
    swaps = len(SWAP_AXES)
    grad_all, gains, *attn_grads = kernel_call(
        functools.partial(close_kernel, sizes),
        2,
        [("vmem", wide_one), ("vmem", gain_two_part)] + anywhere(close_ins),
        anywhere([struct((sizes[0] * rows_dev, slice_width))])
        + [("vmem", struct((8, gain_attn.shape[0]), f32))]
        + anywhere([swap_shape(w, a, sizes) for w, a in zip(full_w[:5], SWAP_AXES)]),
        held_like(close_ins)
        + held_like(full_w[:5])
        + Scatter.scratch(count, sizes, (chunk, slice_width))
        + Swap.scratch(swaps, sizes)
        + [
            VMEM((ranks, count, 8, chunk), f32),
            VMEM((8, slice_width), f32),
            VMEM((rows_dev, slice_width), jnp.bfloat16),
            VMEM((ranks, 1, width + slice_width), f32),
            VMEM((8, width), f32),
            VMEM((sizes[0], 8, gain_attn.shape[0]), f32),
            DMA((len(close_ins),)),
            DMA((ranks - 1, count)),
            DMA((ranks - 1, count)),
            DMA((ranks - 1,)),
            DMA((ranks - 1,)),
        ]
        + Spread.scratch(count, sizes)
        + Swap.scratch(1, sizes)
        + half_blocks(list(zip(full_w[:5], SWAP_AXES)), sizes),
    )
    grads = [jnp.sum(wide(g), 0) for g in attn_grads + ff_grads[1:] + ff_grads[:1]]
    slot_match = dealing[:, None] == ident[None, :]
    slot_len = jnp.sum(jnp.where(slot_match, lengths[None, :], 0), 1)
    slot_home = jnp.sum(jnp.where(slot_match, starts[None, :], 0), 1)
    per_group = slot_len.reshape(-1, SEQ_DEV)
    slot_start = (jnp.cumsum(per_group, 1) - per_group).reshape(-1)
    slot_base = ident // SEQ_DEV * rows_dev + slot_start - slot_home
    owner_base = jnp.sum(jnp.where(dealing[None, :] == ident[:, None], slot_base[None, :], 0), 1)
    global_rows = group * rows_dev + rows
    seq_of = jnp.sum((global_rows[:, None] >= starts[None, :]).astype(jnp.int32), 1) - 1
    targets = (
        jnp.sum(jnp.where(seq_of[:, None] == ident[None, :], owner_base[None, :], 0), 1)
        + global_rows
    )
    mixed_rows, grad_rows = pick(targets, mixed_all), pick(targets, grad_all)
    return (
        mixed_rows,
        grad_rows,
        grads[0],
        grads[1],
        grads[2],
        grads[3],
        grads[4],
        grads[5],
        grads[6],
        grads[7],
        gains[0],
        gains[1],
    )


def solution(mesh):
    in_specs = (
        P("dp", ("heads", "tensor")),
        P("dp", ("heads", "tensor")),
        P(),
        P(),
        P("dp", ("heads", "tensor")),
        P("dp", ("heads", "tensor")),
        P("dp", ("heads", "tensor")),
        P("dp", ("heads", "tensor")),
        P(("heads", "tensor"), "dp"),
        P("dp", ("heads", "tensor")),
        P("dp", ("heads", "tensor")),
        P(("heads", "tensor"), "dp"),
        P("dp"),
        P("dp"),
    )
    out_specs = (
        P("dp", ("heads", "tensor")),
        P("dp", ("heads", "tensor")),
        P("dp", ("heads", "tensor")),
        P("dp", ("heads", "tensor")),
        P("dp", ("heads", "tensor")),
        P("dp", ("heads", "tensor")),
        P(("heads", "tensor"), "dp"),
        P("dp", ("heads", "tensor")),
        P("dp", ("heads", "tensor")),
        P(("heads", "tensor"), "dp"),
        P("dp"),
        P("dp"),
    )
    return jax.shard_map(shards, mesh=mesh, in_specs=in_specs, out_specs=out_specs, check_vma=False)
```

```python
import functools

import jax
import jax.numpy as jnp
from jax import lax
from jax.experimental import pallas as pl
from jax.experimental.pallas import tpu as pltpu
from jax.sharding import PartitionSpec as P

QK_DIM = 256
SEQ_DEV = 3
PIECE = 32
AXES = ("dp", "heads", "tensor")
MESH = pl.DeviceIdType.MESH


EPSILON = 1e-05
GROUP_EPS = 1.0


def layer_norm(values, epsilon):
    center = values - jnp.mean(values, -1, keepdims=True)
    scale = lax.rsqrt(jnp.mean(center * center, -1, keepdims=True) + epsilon)
    return (center * scale, scale)


def norm_back(grad, normed, scale):
    return scale * (
        grad
        - jnp.mean(grad, -1, keepdims=True)
        - normed * jnp.mean(grad * normed, -1, keepdims=True)
    )


def product(left, right):
    return jnp.dot(left, right, preferred_element_type=jnp.float32)


def inner_rows(left, right):
    return lax.dot_general(
        left, right, (((1,), (1,)), ((), ())), preferred_element_type=jnp.float32
    )


def inner_cols(left, right):
    return lax.dot_general(
        left, right, (((0,), (0,)), ((), ())), preferred_element_type=jnp.float32
    )


def lowered(value):
    return value.astype(jnp.bfloat16)


def around(axes):
    return tuple(lax.axis_index(name) for name in axes)


def wide(value):
    return value.astype(jnp.float32)


def within(number, count):
    return (number >= 0) & (number < count)


def greet(others):
    barrier = pltpu.get_barrier_semaphore()
    for other in others:
        pl.semaphore_signal(barrier, inc=1, device_id=other, device_id_type=MESH)
    pl.semaphore_wait(barrier, len(others))


def plane_peers(at, sizes):
    group, level, core = at
    return [(lax.rem(group + k, sizes[0]), level, core) for k in range(1, sizes[0])]


def column_peers(at, sizes):
    group, level, core = at
    return [(group, lax.rem(level + k, sizes[1]), core) for k in range(1, sizes[1])] + [
        (group, level, 1 - core)
    ]


def beside(group):
    return group + 1 - 2 * lax.rem(group, 2), lax.rem(group + 2, 4), 3 - group


class Spread:
    def __init__(self, at, sizes, items, sems, relay=True):
        self.at, self.count, self.items = at, sizes[0], items
        self.local, self.sent, self.got = sems
        self.plane = relay and sizes[0] == 4

    @staticmethod
    def scratch(items, sizes):
        ways = max(4, sizes[0] - 1)
        return [
            pltpu.SemaphoreType.DMA((items,)),
            pltpu.SemaphoreType.DMA((items, ways)),
            pltpu.SemaphoreType.DMA((items, ways)),
        ]

    def place(self, number, owner, half=None):
        source, target, axis, *where = self.items[number]
        rows = source.shape[0]
        size = source.shape[axis]
        step, offset = where or (size, 0)
        start = owner * step + offset
        if half is None:
            begin, height = 0, rows
        else:
            begin, height = half * (rows // 2), rows // 2
        if axis == 0:
            return target.at[pl.ds(pl.multiple_of(start + begin, height), height)]
        return target.at[pl.ds(begin, height), pl.ds(pl.multiple_of(start, size), size)]

    def own(self, number):
        return pltpu.make_async_copy(
            self.items[number][0], self.place(number, self.at[0]), self.local.at[number]
        )

    def copy(self, number, source, place, way, peer):
        return pltpu.make_async_remote_copy(
            src_ref=source,
            dst_ref=place,
            send_sem=self.sent.at[number, way],
            recv_sem=self.got.at[number, way],
            device_id=(peer,) + self.at[1:],
            device_id_type=MESH,
        )

    def away(self, number, k):
        peer = lax.rem(self.at[0] + k, self.count)
        return self.copy(number, self.items[number][0], self.place(number, self.at[0]), k - 1, peer)

    def landed(self, number, k):
        owner = lax.rem(self.at[0] + self.count - k, self.count)
        return self.copy(number, self.items[number][0], self.place(number, owner), k - 1, owner)

    def to(self, number, way):
        peer = beside(self.at[0])[way]
        return self.copy(number, self.items[number][0], self.place(number, self.at[0]), way, peer)

    def of(self, number, way):
        peer = beside(self.at[0])[way]
        return self.copy(number, self.items[number][0], self.place(number, peer), way, peer)

    def on(self, number, way):
        near = beside(self.at[0])
        ref = self.place(number, near[way], way)
        return self.copy(number, ref, ref, 2 + way, near[1 - way])

    def last(self, number, way):
        near = beside(self.at[0])
        ref = self.place(number, near[2], way)
        return self.copy(number, ref, ref, 2 + way, near[1 - way])

    def start(self, *numbers):
        for number in numbers:
            if self.plane:
                self.to(number, 0).start()
                self.to(number, 1).start()
            else:
                for k in range(1, self.count):
                    self.away(number, k).start()
            self.own(number).start()

    def relay(self, *numbers):
        if self.plane:
            for number in numbers:
                for way in range(2):
                    self.of(number, way).wait_recv()
                    self.on(number, way).start()

    def wait(self, *numbers):
        for number in numbers:
            self.own(number).wait()
            if self.plane:
                self.last(number, 0).wait_recv()
                self.last(number, 1).wait_recv()
            else:
                for k in range(1, self.count):
                    self.landed(number, k).wait_recv()

    def drain(self, *numbers):
        for number in numbers:
            if self.plane:
                for way in range(2):
                    self.to(number, way).wait_send()
                    self.on(number, way).wait_send()
            else:
                for k in range(1, self.count):
                    self.away(number, k).wait_send()


class Gather:
    def __init__(self, at, sizes, count, full, sems):
        self.at, self.levels, self.count, self.full = at, sizes[1], count, full
        self.sent_up, self.got_up, self.sent_down, self.got_down, self.sent_core, self.got_core = sems

    @staticmethod
    def scratch(count, sizes, piece):
        levels = sizes[1]
        dma = pltpu.SemaphoreType.DMA
        return [pltpu.VMEM((count, levels, 2) + piece, jnp.bfloat16)] + [
            dma((levels - 1, count)) for _ in range(4)
        ] + [dma((2 * levels - 1, count)) for _ in range(2)]

    def copy(self, ref, sent, got, target):
        return pltpu.make_async_remote_copy(
            src_ref=ref, dst_ref=ref, send_sem=sent, recv_sem=got, device_id=target, device_id_type=MESH
        )

    def up(self, k, hop, origin, sem):
        group, level, core = self.at
        target = (group, lax.rem(level + 1, self.levels), core)
        return self.copy(self.full.at[k, origin, core], self.sent_up.at[sem, k], self.got_up.at[sem, k], target)

    def down(self, k, hop, origin, sem):
        group, level, core = self.at
        target = (group, lax.rem(level + self.levels - 1, self.levels), core)
        return self.copy(
            self.full.at[k, origin, core], self.sent_down.at[sem, k], self.got_down.at[sem, k], target
        )

    def across(self, k, origin, side, sem):
        group, level, core = self.at
        return self.copy(
            self.full.at[k, origin, side], self.sent_core.at[sem, k], self.got_core.at[sem, k], (group, level, 1 - core)
        )

    def start(self, k):
        group, level, core = self.at

        @pl.when(level < self.levels - 1)
        def _():
            self.up(k, 0, level, 0).start()

        @pl.when(level > 0)
        def _():
            self.down(k, 0, level, 0).start()

        self.across(k, level, core, 0).start()

    def hop(self, k, hop):
        group, level, core = self.at
        last = self.levels - 1

        @pl.when(level >= hop)
        def _():
            origin = level - hop
            self.up(k, hop, origin, hop - 1).wait_recv()
            if hop < last:

                @pl.when(level < last)
                def _():
                    self.up(k, hop, origin, hop).start()

            self.across(k, origin, core, hop).start()

        @pl.when(level + hop <= last)
        def _():
            origin = level + hop
            self.down(k, hop, origin, hop - 1).wait_recv()
            if hop < last:

                @pl.when(level > 0)
                def _():
                    self.down(k, hop, origin, hop).start()

            self.across(k, origin, core, last + hop).start()

    def ready(self, k):
        group, level, core = self.at
        last = self.levels - 1
        self.across(k, level, 1 - core, 0).wait_recv()
        for hop in range(1, self.levels):

            @pl.when(level >= hop)
            def _():
                self.across(k, level - hop, 1 - core, hop).wait_recv()

            @pl.when(level + hop <= last)
            def _():
                self.across(k, level + hop, 1 - core, last + hop).wait_recv()

    def drain(self):
        group, level, core = self.at
        last = self.levels - 1

        def one(k, _):
            self.across(k, level, core, 0).wait_send()
            for hop in range(self.levels):
                if hop < last:

                    @pl.when((level >= hop) & (level < last))
                    def _():
                        self.up(k, hop, level - hop, hop).wait_send()

                    @pl.when((level + hop <= last) & (level > 0))
                    def _():
                        self.down(k, hop, level + hop, hop).wait_send()

                if hop > 0:

                    @pl.when(level >= hop)
                    def _():
                        self.across(k, level - hop, core, hop).wait_send()

                    @pl.when(level + hop <= last)
                    def _():
                        self.across(k, level + hop, core, last + hop).wait_send()

            return 0

        lax.fori_loop(0, self.count, one, 0)


class Scatter:
    REFS = 4

    def __init__(self, at, sizes, count, refs):
        self.at, self.levels, self.count = at, sizes[1], count
        self.part, self.cross, self.inbox, self.total = refs[:4]
        self.sent_core, self.got_core, self.sent_up, self.got_up, self.sent_down, self.got_down = refs[4:]

    @staticmethod
    def rooms(count, sizes, piece):
        levels = sizes[1]
        return [
            pltpu.VMEM((2, levels, 2) + piece, jnp.bfloat16),
            pltpu.VMEM((count, levels) + piece, jnp.bfloat16),
            pltpu.VMEM((count, levels + 1) + piece, jnp.bfloat16),
            pltpu.VMEM(piece, jnp.float32),
        ]

    @staticmethod
    def sems(count, sizes):
        dma = pltpu.SemaphoreType.DMA
        return [dma((count,)) for _ in range(2)] + [dma((sizes[1], count)) for _ in range(4)]

    @staticmethod
    def scratch(count, sizes, piece):
        return Scatter.rooms(count, sizes, piece) + Scatter.sems(count, sizes)

    def across(self, k):
        group, level, core = self.at
        return pltpu.make_async_remote_copy(
            src_ref=self.part.at[lax.rem(k, 2), :, 1 - core],
            dst_ref=self.cross.at[k],
            send_sem=self.sent_core.at[k],
            recv_sem=self.got_core.at[k],
            device_id=(group, level, 1 - core),
            device_id_type=MESH,
        )

    def up(self, k, owner):
        group, level, core = self.at
        return pltpu.make_async_remote_copy(
            src_ref=self.cross.at[k, owner],
            dst_ref=self.inbox.at[k, owner + 1],
            send_sem=self.sent_up.at[owner, k],
            recv_sem=self.got_up.at[owner, k],
            device_id=(group, lax.rem(level + 1, self.levels), core),
            device_id_type=MESH,
        )

    def down(self, k, owner):
        group, level, core = self.at
        return pltpu.make_async_remote_copy(
            src_ref=self.cross.at[k, owner],
            dst_ref=self.inbox.at[k, owner],
            send_sem=self.sent_down.at[owner, k],
            recv_sem=self.got_down.at[owner, k],
            device_id=(group, lax.rem(level + self.levels - 1, self.levels), core),
            device_id_type=MESH,
        )

    def free(self, k, before=None):
        @pl.when(k >= 2)
        def _():
            self.across(k - 2).wait_send()

        if before is not None:

            @pl.when(k < 2)
            def _():
                before.across(self.count - 2 + k).wait_send()

    def start(self, k):
        self.across(k).start()

    def join(self, k):
        core = self.at[2]
        self.across(k).wait_recv()
        for owner in range(self.levels):
            self.cross[k, owner] = lowered(
                wide(self.part[lax.rem(k, 2), owner, core]) + wide(self.cross[k, owner])
            )

    def step_up(self, k):
        level = self.at[1]
        for owner in range(self.levels - 1, 0, -1):

            @pl.when(level < owner)
            def _():
                @pl.when(level > 0)
                def _():
                    self.up(k, owner).wait_recv()
                    self.cross[k, owner] = lowered(wide(self.cross[k, owner]) + wide(self.inbox[k, owner + 1]))

                self.up(k, owner).start()

    def step_down(self, k):
        level = self.at[1]
        for owner in range(self.levels - 1):

            @pl.when(level > owner)
            def _():
                @pl.when(level < self.levels - 1)
                def _():
                    self.down(k, owner).wait_recv()
                    self.cross[k, owner] = lowered(wide(self.cross[k, owner]) + wide(self.inbox[k, owner]))

                self.down(k, owner).start()

    def steps(self, wave):
        level = self.at[1]
        above = wave - level
        below = wave - (self.levels - 1 - level)

        @pl.when(within(above, self.count) & (level < self.levels // 2))
        def _():
            self.step_up(above)

        @pl.when(within(below, self.count))
        def _():
            self.step_down(below)

        @pl.when(within(above, self.count) & (level >= self.levels // 2))
        def _():
            self.step_up(above)

    def finish(self, k):
        level = self.at[1]
        self.total[...] = wide(self.cross[k, level])

        @pl.when(level > 0)
        def _():
            self.up(k, level).wait_recv()
            self.total[...] += wide(self.inbox[k, level + 1])

        @pl.when(level < self.levels - 1)
        def _():
            self.down(k, level).wait_recv()
            self.total[...] += wide(self.inbox[k, level])

    def sent(self, k):
        level = self.at[1]
        for owner in range(self.levels):

            @pl.when(level < owner)
            def _():
                self.up(k, owner).wait_send()

            @pl.when(level > owner)
            def _():
                self.down(k, owner).wait_send()

    def drain(self):
        self.across(self.count - 2).wait_send()
        self.across(self.count - 1).wait_send()
        in_order(self.count, self.sent)


def in_order(count, step):
    def body(number, carry):
        step(number)
        return carry

    lax.fori_loop(0, count, body, 0)


def span(number, size):
    return pl.ds(pl.multiple_of(number * size, size), size)


class Moves:
    def __init__(self, pairs, sems):
        self.pairs, self.sems = pairs, sems

    def copy(self, number):
        return pltpu.make_async_copy(*self.pairs[number], self.sems.at[number])

    def start(self, *numbers):
        for number in numbers:
            self.copy(number).start()

    def wait(self, *numbers):
        for number in numbers:
            self.copy(number).wait()


class Chunks:
    def __init__(self, pairs, size, sems):
        self.pairs, self.size, self.sems = pairs, size, sems

    def start(self, k):
        for number, (source, target) in enumerate(self.pairs):
            rows = span(k, self.size)
            pltpu.make_async_copy(source.at[rows], target.at[rows], self.sems.at[number, k]).start()

    def wait(self, count):
        def one(k, carry):
            for number, (source, target) in enumerate(self.pairs):
                rows = span(k, self.size)
                pltpu.make_async_copy(source.at[rows], target.at[rows], self.sems.at[number, k]).wait()
            return carry

        lax.fori_loop(0, count, one, 0)


def matmul(left, right):
    return jnp.dot(left, right, preferred_element_type=jnp.float32)


def decay_tile(near, far, size, bounds, rate):
    rows = near * size + lax.broadcasted_iota(jnp.int32, (size, 1), 0)
    columns = far * size + lax.broadcasted_iota(jnp.int32, (1, size), 1)
    row_seq, column_seq = jnp.zeros((size, 1), jnp.int32), jnp.zeros((1, size), jnp.int32)
    for number in range(1, SEQ_DEV):
        row_seq += (rows >= bounds[number]).astype(jnp.int32)
        column_seq += (columns >= bounds[number]).astype(jnp.int32)
    distance = rows - columns
    valid = (distance >= 0) & (row_seq == column_seq)
    return (
        jnp.where(valid, jnp.exp(jnp.maximum(distance, 0).astype(jnp.float32) * rate[0]), 0.0)
        * QK_DIM ** (-0.5)
    )


class Swap:
    def __init__(self, at, sizes, items, sems, halves=None):
        self.at, self.count, self.items = at, sizes[0], items
        self.local, self.sent, self.got = sems
        self.halves = halves
        self.plane = halves is not None and sizes[0] == 4

    @staticmethod
    def scratch(items, sizes):
        ways = max(6, sizes[0] - 1)
        return [
            pltpu.SemaphoreType.DMA((items,)),
            pltpu.SemaphoreType.DMA((items, ways)),
            pltpu.SemaphoreType.DMA((items, ways)),
        ]

    def block(self, number, owner, half=None):
        source, target, axis = self.items[number]
        rows = source.shape[0]
        size = source.shape[axis] // self.count
        height = size if axis == 0 else rows
        begin = 0
        if half is not None:
            height //= 2
            begin = half * height
        if axis == 0:
            return source.at[pl.ds(pl.multiple_of(owner * size + begin, height), height)]
        return source.at[pl.ds(begin, height), pl.ds(pl.multiple_of(owner * size, size), size)]

    def half(self, number, slot, half):
        target = self.items[number][1]
        height = target.shape[1] // 2
        return target.at[slot, pl.ds(half * height, height)]

    def copy(self, number, source, place, way, peer):
        return pltpu.make_async_remote_copy(
            src_ref=source,
            dst_ref=place,
            send_sem=self.sent.at[number, way],
            recv_sem=self.got.at[number, way],
            device_id=(peer,) + self.at[1:],
            device_id_type=MESH,
        )

    def own(self, number):
        return pltpu.make_async_copy(
            self.block(number, self.at[0]), self.items[number][1].at[0], self.local.at[number]
        )

    def away(self, number, k):
        peer = lax.rem(self.at[0] + k, self.count)
        return self.copy(number, self.block(number, peer), self.items[number][1].at[k], k - 1, peer)

    def across(self, number, way):
        near = beside(self.at[0])
        return self.copy(
            number, self.block(number, near[2], way), self.halves[number].at[way], way, near[way]
        )

    def direct(self, number, way):
        near = beside(self.at[0])
        return self.copy(
            number, self.block(number, near[way], way), self.half(number, 1 + way, way), 2 + way, near[way]
        )

    def added(self, number, way):
        peer = beside(self.at[0])[1 - way]
        return self.copy(
            number, self.block(number, peer, way), self.half(number, 2 - way, way), 4 + way, peer
        )

    def start(self, *numbers):
        for number in numbers:
            if self.plane:
                for way in range(2):
                    self.across(number, way).start()
                for way in range(2):
                    self.direct(number, way).start()
            else:
                for k in range(1, self.count):
                    self.away(number, k).start()
            self.own(number).start()

    def relay(self, *numbers):
        if self.plane:
            near = beside(self.at[0])
            for number in numbers:
                for way in range(2):
                    self.across(number, way).wait_recv()
                    part = self.block(number, near[1 - way], way)
                    part[...] = lowered(wide(part[...]) + wide(self.halves[number][way]))
                for way in range(2):
                    self.added(number, way).start()

    def wait(self, *numbers):
        for number in numbers:
            self.own(number).wait()
            if self.plane:
                for way in range(2):
                    self.across(number, way).wait_send()
                    self.direct(number, way).wait()
                    self.added(number, way).wait()
            else:
                for k in range(1, self.count):
                    self.away(number, k).wait()


def half_blocks(items, sizes):
    room = []
    for whole, axis in items:
        shape = list(whole.shape)
        shape[axis] //= sizes[0]
        room.append(pltpu.VMEM((2, shape[0] // 2, shape[1]), jnp.bfloat16))
    return room


def quarters(source, target):
    rows = source.shape[0]
    run = rows // 4
    return [(source.at[pl.ds(k * run, run)], target, 0, rows, k * run) for k in range(4)]


def pick_rows(whole, number, first, rows, bounds, shifts, begins):
    window = 2 * rows
    lane = lax.broadcasted_iota(jnp.int32, (rows, window), 1)
    slot = jnp.zeros((rows, 1), jnp.int32)
    own = first + lax.broadcasted_iota(jnp.int32, (rows, 1), 0)
    for item in range(1, SEQ_DEV):
        slot += (own >= bounds[item]).astype(jnp.int32)
    chosen, windows = [], []
    for item in range(SEQ_DEV):
        start = begins[number * SEQ_DEV + item]
        wanted = jnp.where(slot == item, own + shifts[item] - 16 * start, -1)
        chosen.append(jnp.where(lane == wanted, 1.0, 0.0).astype(jnp.bfloat16))
        windows += [whole[start + k] for k in range(window // 16)]
    return lowered(matmul(jnp.concatenate(chosen, axis=1), jnp.concatenate(windows, axis=0)))


def front_kernel(sizes, bounds, shifts, begins, tokens, cotangent, gain_rows, *refs):
    masters, refs = refs[:8], refs[8:]
    normed_out, query_out, key_out, value_out, swish_out, dy_out, *refs = refs
    weight_outs, rounded_outs, refs = refs[:4], refs[4:8], refs[8:]
    gain_one, gain_two, rows_out, unit_out, scale_out, *refs = refs
    full, *refs = refs
    gather_sems, refs = refs[:6], refs[6:]
    spread_sems, small_sems, refs = refs[:3], refs[3:6], refs[6:]
    held, rounded, weights, refs = refs[:8], refs[8:16], refs[16:20], refs[20:]
    tokens_held, dy_held, gains_held, tokens_all, dy_all, gains_all, dy_part, *refs = refs
    normed, query, keys, values, swish, load_sems, store_sems, out_sems, normed_sem = refs
    at = around(AXES)
    group, level, core = at
    place = 2 * level + core
    count, levels, _, chunk, width = full.shape
    ranks = 2 * levels
    piece = chunk // ranks
    loads = Moves(
        list(zip(masters, held)) + [(tokens, tokens_held), (gain_rows, gains_held), (cotangent, dy_held)], load_sems
    )
    loads.start(8, 9, 2, 3, 1, 0, 10, 4, 5, 6, 7)
    greet(plane_peers(at, sizes) + column_peers(at, sizes))
    loads.wait(8, 9)
    spread = Spread(
        at,
        sizes,
        quarters(tokens_held, tokens_all)
        + [(rounded[2], weights[2], 0), (rounded[3], weights[3], 0)]
        + quarters(dy_held, dy_all)
        + [(rounded[1], weights[1], 0), (rounded[0], weights[0], 0)],
        spread_sems,
    )
    small = Spread(at, sizes, [(gains_held, gains_all, 0)], small_sems, relay=False)
    spread.start(*range(4))
    small.start(0)
    gather = Gather(at, sizes, count, full, gather_sems)

    def cast(number):
        loads.wait(number)
        rows = min(32, held[number].shape[0])

        def block(k):
            held_rows = span(k, rows)
            rounded[number][held_rows, :] = lowered(held[number][held_rows, :])

        in_order(held[number].shape[0] // rows, block)

    stores = Moves(list(zip(rounded[4:], rounded_outs)), store_sems)
    cast(2)
    spread.start(4)
    for number in (3, 1, 0, 4, 5, 6, 7):
        cast(number)
    loads.wait(10)
    stores.start(*range(4))
    for number in range(4):
        spread.relay(number)
    spread.start(5, 6, 7)
    small.wait(0)
    own = gains_held.shape[0]
    for row, gain in enumerate((gain_one, gain_two)):
        gain[...] = wide(
            lowered(
                jnp.concatenate([gains_all[own * k + row : own * k + row + 1, :] for k in range(sizes[0])], axis=1)
            )
        )
    spread.wait(*range(4))
    run = chunk // 2

    def pick_chunk(whole, k, half):
        return pick_rows(whole, 2 * k + half, k * chunk + half * run, run, bounds, shifts, begins)

    def begin(k):
        for half in range(2):
            full[k, level, core, half * run : (half + 1) * run, :] = pick_chunk(tokens_all, k, half)
        gather.start(k)

    def norm(k):
        def block(number, carry):
            rows = span(number, 16)
            value = jnp.concatenate(
                [wide(full[k, q, c, rows, :]) for q in range(levels) for c in range(2)], axis=1
            )
            unit, scale = layer_norm(value, EPSILON)
            where = pl.ds(pl.multiple_of(k * chunk + number * 16, 16), 16)
            normed[where, :] = lowered(unit * gain_one[...])
            mine = wide(full[k, level, core, rows, :])
            mean = jnp.mean(value, -1, keepdims=True)
            unit_out[where, :] = (mine - mean) * scale
            scale_out[where, :] = jnp.broadcast_to(scale, (16, 128))
            return carry

        lax.fori_loop(0, chunk // 16, block, 0)
        mine = span(place, piece)
        rows_out[span(k, piece), :] = jnp.concatenate(
            [full[k, q, c, mine, :] for q in range(levels) for c in range(2)], axis=1
        )
        pltpu.make_async_copy(
            normed.at[span(k, chunk)], normed_out.at[span(k, chunk)], normed_sem.at[k]
        ).start()

    begin(0)
    outs = [(query, query_out), (keys, key_out), (values, value_out), (swish, swish_out)]
    ends = Moves(outs + list(zip(weights, weight_outs)) + [(dy_part, dy_out)], out_sems)

    def project_rows(number, k):
        where = span(k, chunk)
        target = outs[number][0]
        target[where, :] = matmul(normed[where, :], weights[number][...]).astype(target.dtype)

    def wave(number):
        @pl.when(number + 1 < count)
        def _():
            begin(number + 1)

        for hop in range(levels - 1, 0, -1):

            @pl.when(within(number - hop, count))
            def _():
                gather.hop(number - hop, hop)

        for step, relayed, started in (
            (1, (4,), (8, 9)),
            (3, (5,), (10, 11)),
            (5, (6, 7), ()),
            (6, (8, 9), ()),
            (8, (10,), ()),
        ):

            @pl.when(number == step)
            def _():
                spread.relay(*relayed)
                spread.start(*started)

        @pl.when(within(number - levels, count))
        def _():
            gather.ready(number - levels)
            norm(number - levels)

        @pl.when(number == levels + 3)
        def _():
            spread.wait(4)
            ends.start(6)
            for k in range(3):
                project_rows(2, k)

        @pl.when(number >= levels + 3)
        def _():
            project_rows(2, number - levels)

    in_order(count + levels, wave)

    def project(number, item):
        if item is not None:
            spread.wait(item)
            ends.start(4 + number)
            in_order(count, functools.partial(project_rows, number))
        ends.start(number)

    spread.relay(11)
    project(2, None)
    project(3, 5)
    spread.wait(*range(6, 10))

    def dy_chunk(k):
        for half in range(2):
            dy_part[k, half * run : (half + 1) * run, :] = pick_chunk(dy_all, k, half)

    in_order(count, dy_chunk)
    ends.start(8)
    project(1, 10)
    project(0, 11)
    small.drain(0)
    spread.drain(*range(12))
    gather.drain()
    stores.wait(*range(4))
    ends.wait(*range(9))

    def stored(k):
        pltpu.make_async_copy(
            normed.at[span(k, chunk)], normed_out.at[span(k, chunk)], normed_sem.at[k]
        ).wait()

    in_order(count, stored)


class Ring:
    def __init__(self, slots, whole, size, sems):
        self.slots, self.whole, self.size, self.sems = slots, whole, size, sems

    def load(self, k):
        return pltpu.make_async_copy(
            self.whole.at[span(k, self.size)], self.slots.at[lax.rem(k, 2)], self.sems.at[k]
        )

    def store(self, k):
        return pltpu.make_async_copy(
            self.slots.at[lax.rem(k, 2)], self.whole.at[span(k, self.size)], self.sems.at[k]
        )

    def free(self, k):
        @pl.when(k >= 2)
        def _():
            self.store(k - 2).wait()


def core_kernel(sizes, bounds, rate, gain, *refs):
    gain_first, *refs = refs
    query_src, key_src, value_src, rows_src, dy_src, swish_src, *refs = refs
    normed_src, unit_src, scale_src, *refs = refs
    project_src, refs = refs[:4], refs[4:]
    shards, refs = refs[:4], refs[4:]
    mixed_in_out, retained_out, gains_out, *refs = refs
    mixed_dst, grad_dst, down_dst, gate_dst, up_dst, *refs = refs
    late_dst, refs = refs[:5], refs[5:]
    query, keys, values, x_rows, out_w, gate_w, up_w, down_w, *refs = refs
    rooms, refs = refs[:4], refs[4:]
    (other_part,), refs = refs[:1], refs[1:]
    sems_one, sems_two, sems_three, sems_four, refs = refs[:6], refs[6:12], refs[12:18], refs[18:24], refs[24:]
    normed_mid, refs = refs[0], refs[1:]
    normed_sems, refs = refs[:6], refs[6:]
    dy, refs = refs[0], refs[1:]
    dy_sems, refs = refs[:6], refs[6:]
    branch, refs = refs[0], refs[1:]
    branch_sems, refs = refs[:6], refs[6:]
    spread_sems, refs = refs[:3], refs[3:]
    deal_sems, refs = refs[:3], refs[3:]
    swap_sems, late_sems, small_sems, refs = refs[:3], refs[3:6], refs[6:9], refs[9:]
    give_sems, refs = refs[:3], refs[3:]
    hidden, gate_grad, up_grad, resid, swish_slots, retained_slots, mixed_in_slots, *refs = refs
    key_acc, value_acc, query_acc, delta, down_grad, mixed, gain_acc, *refs = refs
    sums, line_one, packed, gains, gains_in, *refs = refs
    load_sems, ring_sems, late_load, unit_sems, room, sums_sent, sums_got, gain_sent, gain_got, *halves = refs
    at = around(AXES)
    group, level, core = at
    place = 2 * level + core
    count, levels, _, piece, width = normed_mid.shape
    ranks = 2 * levels
    chunk = ranks * piece
    part_width = width // ranks
    loads = Moves(
        [
            (dy_src, dy.at[:, level, core]),
            (query_src, query),
            (key_src, keys),
            (value_src, values),
            (rows_src, x_rows),
        ],
        load_sems,
    )
    loads.start(*range(5))
    swish_one = Ring(swish_slots, swish_src, chunk, ring_sems.at[0])
    swish_two = Ring(swish_slots, swish_src, chunk, ring_sems.at[1])
    retained_one = Ring(retained_slots, retained_out, chunk, ring_sems.at[2])
    retained_two = Ring(retained_slots, retained_out, chunk, ring_sems.at[3])
    mixed_in_ring = Ring(mixed_in_slots, mixed_in_out, chunk, ring_sems.at[4])
    groups, v_dim = sizes[0], values.shape[1]
    late_loads = Moves(
        [(normed_src, normed_mid), (mixed_in_out, up_grad), (project_src[0], dy.at[0]), (project_src[1], dy.at[1])]
        + [
            (project_src[2 + n // 2].at[:, :, :, pl.ds(n % 2 * part_width, part_width)], dy.at[2 + n])
            for n in range(4)
        ],
        late_load,
    )
    swish_one.load(0).start()
    swish_one.load(1).start()
    greet(plane_peers(at, sizes) + column_all(at, sizes))
    spread = Spread(
        at,
        sizes,
        [(shards[0], out_w, 1), (shards[1], gate_w, 0), (shards[2], up_w, 0), (shards[3], down_w, 1)],
        spread_sems,
    )
    deal = Spread(
        at,
        sizes,
        [
            (mixed.at[pl.ds(k * chunk, chunk)], mixed_dst, 0, count * chunk, k * chunk)
            for k in range(count)
        ],
        deal_sems,
    )
    swap = Swap(
        at, sizes, [(down_grad, down_dst, 1), (gate_w, gate_dst, 0), (up_w, up_dst, 0)], swap_sems, halves[:3]
    )
    qk_dim = query.shape[1]
    late = Swap(
        at,
        sizes,
        [
            (gate_w, late_dst[0], 0),
            (out_w, late_dst[1], 1),
            (up_w, late_dst[2], 0),
            (down_grad.at[pl.ds(0, qk_dim)], late_dst[3], 1),
            (down_grad.at[pl.ds(qk_dim, qk_dim)], late_dst[4], 1),
        ],
        late_sems,
        [halves[1], halves[0], halves[2], halves[3], halves[4]],
    )
    small = Swap(at, sizes, [(gains, gains_in, 1)], small_sems)
    give = Spread(
        at,
        sizes,
        [
            (hidden.at[pl.ds(k * chunk, chunk), pl.ds(0, part_width)], grad_dst, 0, count * chunk, k * chunk)
            for k in range(count)
        ],
        give_sems,
    )
    spread.start(0)
    one = Scatter(at, sizes, count, list(rooms) + list(sems_one))
    two = Scatter(at, sizes, count, [other_part] + list(rooms[1:]) + list(sems_two))
    three = Scatter(at, sizes, count, list(rooms) + list(sems_three))
    four = Scatter(at, sizes, count, [other_part] + list(rooms[1:]) + list(sems_four))
    total = rooms[3]
    mid_gather = Gather(at, sizes, count, normed_mid, normed_sems)
    dy_gather = Gather(at, sizes, count, dy, dy_sems)
    branch_gather = Gather(at, sizes, count, branch, branch_sems)
    gain_acc[...] = jnp.zeros(gain_acc.shape, jnp.float32)
    line_one[...] = jnp.zeros(line_one.shape, jnp.float32)
    key_acc[...] = jnp.zeros(key_acc.shape, jnp.float32)
    value_acc[...] = jnp.zeros(value_acc.shape, jnp.float32)
    loads.wait(0)
    dy_gather.start(0)
    loads.wait(1, 2, 3, 4)
    tile = 512

    def first(k):
        where = span(k, chunk)
        slot = lax.rem(k, 2)
        retained_one.free(k)
        retained_slots[slot] = jnp.zeros((chunk, values.shape[1]), jnp.float32)

        def block(j, carry):
            there = span(j, chunk)
            decay = decay_tile(k, j, chunk, bounds, rate)
            weight = lowered(inner_rows(query[where, :], keys[there, :]) * decay)
            retained_slots[slot] += matmul(weight, values[there, :])
            return carry

        lax.fori_loop(0, k + 1, block, 0)
        retained_one.store(k).start()
        normed, _ = layer_norm(retained_slots[slot], GROUP_EPS)
        swish_one.load(k).wait()
        value = swish_slots[slot]
        mixed_in_ring.free(k)
        mixed_in_slots[slot] = lowered(value * jax.nn.sigmoid(value) * normed)
        mixed_in_ring.store(k).start()

        @pl.when(k + 2 < count)
        def _():
            swish_one.load(k + 2).start()

        @pl.when(k == 0)
        def _():
            spread.wait(0)

        one.free(k)
        rows = mixed_in_slots[slot]
        for column in range(0, width, tile):
            value = matmul(rows, out_w[:, column : column + tile])
            one.part[slot, :, :, :, column : column + tile] = lowered(value).reshape(levels, 2, piece, tile)
        one.start(k)

    def mid_norm(k):
        one.finish(k)

        def block(number, carry):
            sub = span(number, 16)
            where = pl.ds(pl.multiple_of(k * piece + number * 16, 16), 16)
            value = wide(x_rows[where, :]) + total[sub, :]
            resid[where, :] = value
            unit, _ = layer_norm(value, EPSILON)
            normed_mid[k, level, core, sub, :] = lowered(unit * gain[...])
            return carry

        lax.fori_loop(0, piece // 16, block, 0)
        mid_gather.start(k)

    def turn(k):
        mid_gather.ready(k)
        rows = normed_mid[k].reshape(chunk, width)
        where = span(k, chunk)
        g = matmul(rows, gate_w[...])
        u = matmul(rows, up_w[...])
        root = 0.7978845608028654
        bend = jnp.tanh(root * (g + 0.044715 * g * g * g))
        curve = 0.5 * (1.0 + bend)
        active = g * curve
        hidden[where, :] = lowered(active * u)
        slope = curve + 0.5 * g * (1.0 - bend * bend) * root * (1.0 + 0.134145 * g * g)
        dy_gather.ready(k)
        rows = jnp.concatenate([dy[k, q, c] for q in range(levels) for c in range(2)], axis=1)
        back = inner_rows(rows, down_w[...])
        gate_grad[where, :] = lowered(back * u * slope)
        up_grad[where, :] = lowered(back * active)
        two.free(k)
        for column in range(0, width, tile):
            columns = slice(column, column + tile)
            value = inner_rows(gate_grad[where, :], gate_w[columns, :])
            value += inner_rows(up_grad[where, :], up_w[columns, :])
            two.part[lax.rem(k, 2), :, :, :, columns] = lowered(value).reshape(levels, 2, piece, tile)
        two.start(k)

    def branch_norm(k):
        two.finish(k)

        def block(number, carry):
            sub = span(number, 16)
            where = pl.ds(pl.multiple_of(k * piece + number * 16, 16), 16)
            unit, scale = layer_norm(resid[where, :], EPSILON)
            grad = total[sub, :]
            outer = grad * unit
            gain_acc[...] += outer[:8] + outer[8:]
            mine = pl.ds(pl.multiple_of(place * piece + number * 16, 16), 16)
            upstream = jnp.concatenate(
                [dy[k, q, c, mine, :] for q in range(levels) for c in range(2)], axis=1
            )
            value = wide(upstream) + norm_back(grad * gain[...], unit, scale)
            branch[k, level, core, sub, :] = lowered(value)
            return carry

        lax.fori_loop(0, piece // 16, block, 0)
        branch_gather.start(k)

    def last(k):
        branch_gather.ready(k)
        rows = branch[k].reshape(chunk, width)
        where = span(k, chunk)
        slot = lax.rem(k, 2)
        grad = inner_rows(rows, out_w[...])
        retained_two.load(k).wait()
        swish_two.load(k).wait()
        normed, scale = layer_norm(retained_slots[slot], GROUP_EPS)
        value = swish_slots[slot]
        gated = jax.nn.sigmoid(value)
        gate_grad[where, :] = lowered(grad * normed * gated * (1.0 + value * (1.0 - gated)))
        delta[...] = lowered(norm_back(grad * value * gated, normed, scale))

        @pl.when(k + 2 < count)
        def _():
            retained_two.load(k + 2).start()
            swish_two.load(k + 2).start()

        query_acc[...] = jnp.zeros(query_acc.shape, jnp.float32)

        def block(j, carry):
            there = span(j, chunk)
            decay = decay_tile(k, j, chunk, bounds, rate)
            weight = lowered(inner_rows(query[where, :], keys[there, :]) * decay)
            score = lowered(inner_rows(delta[...], values[there, :]) * decay)
            query_acc[...] += matmul(score, keys[there, :])
            key_acc[there, :] += inner_cols(score, query[where, :])
            value_acc[there, :] += inner_cols(weight, delta[...])
            return carry

        lax.fori_loop(0, k + 1, block, 0)
        query[where, :] = lowered(query_acc[...])

    def out_part(k):
        three.free(k, one)
        rows = hidden[span(k, chunk), :]
        mine = pl.ds(pl.multiple_of(k * piece, piece), piece)
        for rank in range(ranks):
            columns = slice(rank * part_width, (rank + 1) * part_width)
            value = matmul(rows, down_w[:, columns])
            for run in range(ranks):
                held = jnp.where(place == run, resid[mine, columns], 0.0)
                three.part[
                    lax.rem(k, 2), rank // 2, rank % 2, :, run * part_width : (run + 1) * part_width
                ] = lowered(value[run * piece : (run + 1) * piece, :] + held)
        three.start(k)

    def out_finish(k):
        three.finish(k)
        for run in range(ranks):
            where = pl.ds(pl.multiple_of(k * chunk + run * piece, piece), piece)
            mixed[where, :] = lowered(total[:, run * part_width : (run + 1) * part_width])

    def runs_of(ref, columns):
        return jnp.concatenate(
            [ref[j, q, c, :, columns] for j in range(count) for q in range(levels) for c in range(2)], axis=0
        )

    def weigh(which):
        def part(k):
            columns = span(k, chunk)
            if which == 0:
                down = jnp.zeros((hidden.shape[1], part_width), jnp.float32)
                for j in range(count):
                    down += inner_cols(hidden[j * chunk : (j + 1) * chunk, :], dy[j, k // 2, lax.rem(k, 2)])
                there = pl.ds(pl.multiple_of(k * part_width, part_width), part_width)
                down_grad[:, there] = lowered(down)
            else:
                target, source = ((gate_w, gate_grad), (up_w, up_grad))[which - 1]
                target[columns, :] = lowered(inner_cols(runs_of(normed_mid, columns), source[...]))

        in_order(width // chunk, part)
        swap.start(which)

    def weigh_late(which):
        def part(k):
            columns = span(k, chunk)
            if which == 0:
                gate_w[columns, :] = lowered(inner_cols(runs_of(normed_mid, columns), gate_grad[...]))
            elif which == 1:
                out_w[:, columns] = lowered(inner_cols(up_grad[...], runs_of(branch, columns)))
            elif which == 2:
                up_w[columns, :] = lowered(inner_cols(runs_of(normed_mid, columns), values[...]))
            else:
                rows = runs_of(normed_mid, columns)
                down_grad[:qk_dim, columns] = lowered(inner_cols(query[...], rows))
                down_grad[qk_dim:, columns] = lowered(inner_cols(keys[...], rows))

        in_order(width // chunk, part)
        late.start(*((which,) if which < 3 else (3, 4)))

    def units(k):
        slot = lax.rem(k, 2)
        return [
            pltpu.make_async_copy(
                unit_src.at[span(k, chunk)], swish_slots.at[slot, :, pl.ds(0, part_width)], unit_sems.at[0, k]
            ),
            pltpu.make_async_copy(
                scale_src.at[span(k, chunk)], retained_slots.at[slot, :, pl.ds(0, 128)], unit_sems.at[1, k]
            ),
        ]

    def peer_of(j):
        peer = lax.rem(place + j, ranks)
        return (group, peer // 2, lax.rem(peer, 2))

    def sender(j):
        return lax.rem(place + ranks - j, ranks)

    def sums_copy(k, j, owner):
        return pltpu.make_async_remote_copy(
            src_ref=sums.at[owner, k],
            dst_ref=sums.at[owner, k],
            send_sem=sums_sent.at[j - 1, k],
            recv_sem=sums_got.at[j - 1, k],
            device_id=peer_of(j),
            device_id_type=MESH,
        )

    def pack_copy(j, owner):
        return pltpu.make_async_remote_copy(
            src_ref=packed.at[owner],
            dst_ref=packed.at[owner],
            send_sem=gain_sent.at[j - 1],
            recv_sem=gain_got.at[j - 1],
            device_id=peer_of(j),
            device_id_type=MESH,
        )

    def make_room(k):
        three.sent(k)
        pl.semaphore_signal(room.at[0], inc=1, device_id=(group, level, 1 - core), device_id_type=MESH)

        @pl.when(level > 0)
        def _():
            pl.semaphore_signal(room.at[1], inc=1, device_id=(group, level - 1, core), device_id_type=MESH)

        @pl.when(level < levels - 1)
        def _():
            pl.semaphore_signal(room.at[2], inc=1, device_id=(group, level + 1, core), device_id_type=MESH)

    def in_part(k):
        four.free(k, two)
        where = span(k, chunk)
        slot = lax.rem(k, 2)
        rows = [query[where, :], keys[where, :]]
        for source in (values, gate_grad):
            rows += [source[where, n : n + part_width] for n in range(0, v_dim, part_width)]
        first_sum = jnp.zeros((chunk, part_width), jnp.float32)
        second_sum = jnp.zeros((chunk, part_width), jnp.float32)
        for rank in range(ranks):
            columns = slice(rank * part_width, (rank + 1) * part_width)
            value = inner_rows(rows[0], dy[0, rank // 2, rank % 2])
            for n in range(1, len(rows)):
                value += inner_rows(rows[n], dy[n, rank // 2, rank % 2])
            for run in range(ranks):
                four.part[
                    slot, rank // 2, rank % 2, :, run * part_width : (run + 1) * part_width
                ] = lowered(value[run * piece : (run + 1) * piece, :])
            first_sum += value * gain_first[:, columns]
            second_sum += value * wide(normed_mid[k, :, :, :, columns].reshape(chunk, part_width))
        pl.semaphore_wait(room.at[0], 1)
        four.start(k)
        ones = jnp.ones((8, part_width), jnp.float32)
        flat = [
            lax.dot_general(
                ones,
                item,
                (((1,), (1,)), ((), ())),
                precision=lax.Precision.HIGHEST,
                preferred_element_type=jnp.float32,
            )
            for item in (first_sum, second_sum)
        ]
        line = lax.broadcasted_iota(jnp.int32, (8, chunk), 0)
        sums[place, k] = jnp.where(line == 0, flat[0], flat[1])
        for j in range(1, ranks):
            sums_copy(k, j, place).start()

    def in_room(wave):
        @pl.when(within(wave - level, count) & (level < levels - 1))
        def _():
            pl.semaphore_wait(room.at[1], 1)

        @pl.when(within(wave - (levels - 1 - level), count) & (level > 0))
        def _():
            pl.semaphore_wait(room.at[2], 1)

    def in_finish(k):
        four.finish(k)
        for j in range(1, ranks):
            sums_copy(k, j, sender(j)).wait_recv()
        line = lax.broadcasted_iota(jnp.int32, (8, 128), 0)
        lane = lax.broadcasted_iota(jnp.int32, (8, 128), 1)
        means = lax.dot_general(
            jnp.sum(sums[:, k], 0),
            jnp.where(line == lane, 1.0 / width, 0.0),
            (((0,), (0,)), ((), ())),
            precision=lax.Precision.HIGHEST,
            preferred_element_type=jnp.float32,
        )
        slot = lax.rem(k, 2)
        for copy in units(k):
            copy.wait()
        mine = pl.ds(pl.multiple_of(place * part_width, part_width), part_width)
        value = jnp.concatenate(
            [total[:, run * part_width : (run + 1) * part_width] for run in range(ranks)], axis=0
        )
        normed = swish_slots[slot, :, :part_width]
        outer = value * normed
        line_one[...] += jnp.sum(outer.reshape(chunk // 8, 8, part_width), 0)
        back = value * gain_first[:, mine] - means[:, :1] - normed * means[:, 1:2]
        upstream = wide(branch[k, :, :, :, mine].reshape(chunk, part_width))
        hidden[span(k, chunk), :part_width] = lowered(upstream + retained_slots[slot, :, :1] * back)

        @pl.when(k + 2 < count)
        def _():
            for copy in units(k + 2):
                copy.start()

    lead = 3
    mid_lag = lead + levels
    turn_lag = mid_lag + levels - 1
    branch_lag = turn_lag + levels
    last_lag = branch_lag + levels - 1
    turned = turn_lag + count
    close_lag = last_lag + count

    def at_wave(number, lag, step):
        @pl.when(within(number - lag, count))
        def _():
            step(number - lag)

    def wave(number):
        at_wave(number, lead, first)
        for gather, lag, scatter in ((branch_gather, branch_lag, two), (mid_gather, mid_lag, one)):
            at_wave(number, lag + 1, scatter.sent)
            for hop in range(levels - 1, 0, -1):
                at_wave(number, lag + hop, functools.partial(hop_on, gather, hop))
        at_wave(number, branch_lag, branch_norm)
        at_wave(number, mid_lag, mid_norm)
        at_wave(number, -1, next_dy)
        for hop in range(levels - 1, 0, -1):
            at_wave(number, hop, functools.partial(hop_on, dy_gather, hop))
        for scatter, lag in ((two, turn_lag), (one, lead)):
            at_wave(number, lag + 1, scatter.join)
            scatter.steps(number - lag - 1)
        for step, relayed, started in ((1, (0,), (1, 2)), (4, (1,), (3,)), (6, (2,), ()), (8, (3,), ())):

            @pl.when(number == step)
            def _():
                spread.relay(*relayed)
                spread.start(*started)

        @pl.when(number == turn_lag)
        def _():
            spread.wait(1, 2, 3)

        at_wave(number, turn_lag, turn)

        @pl.when(number == turn_lag + 1)
        def _():
            retained_one.store(count - 2).wait()
            retained_one.store(count - 1).wait()
            for k in range(2):
                retained_two.load(k).start()
                swish_two.load(k).start()

        @pl.when(number == turned)
        def _():
            spread.drain(*range(4))

        for step, which in ((0, 1), (1, 2), (2, 0)):

            @pl.when(number == turned + step)
            def _():
                weigh(which)

        for step, which in ((2, 1), (4, 2), (6, 0)):

            @pl.when(number == turned + step)
            def _():
                swap.relay(which)

        @pl.when(number == turned + 2)
        def _():
            mid_gather.drain()
            mixed_in_ring.store(count - 2).wait()
            mixed_in_ring.store(count - 1).wait()
            late_loads.start(0, 1)

        @pl.when(number == branch_lag + count)
        def _():
            dy_gather.drain()
            late_loads.start(*range(2, 8))

        at_wave(number, last_lag, last)
        at_wave(number, last_lag, out_part)
        at_wave(number, last_lag + 1, three.join)
        three.steps(number - last_lag - 1)
        at_wave(number, last_lag + levels, out_finish)
        for k in range(count):

            @pl.when(number == last_lag + levels + k)
            def _():
                deal.start(k)

            @pl.when(number == last_lag + levels + k + 2)
            def _():
                deal.relay(k)

        at_wave(number, last_lag + levels + 1, make_room)

        @pl.when(number == close_lag)
        def _():
            keys[...] = lowered(key_acc[...])
            values[...] = lowered(value_acc[...])
            for k in range(2):
                for copy in units(k):
                    copy.start()
            late_loads.wait(*range(8))

        at_wave(number, close_lag, in_part)
        for step, before, which in ((0, 1, 0), (1, 0, 1), (2, 2, 2), (3, None, 3)):

            @pl.when(number == close_lag + step)
            def _():
                if before is not None:
                    swap.wait(before)
                weigh_late(which)

        at_wave(number, close_lag + 1, four.join)
        in_room(number - close_lag - 1)
        four.steps(number - close_lag - 1)
        at_wave(number, close_lag + levels, in_finish)
        for step, which in ((3, (0,)), (4, (1,)), (5, (2,)), (7, (3, 4))):

            @pl.when(number == close_lag + step)
            def _():
                late.relay(*which)

        for k in range(count):

            @pl.when(number == close_lag + levels + k)
            def _():
                give.start(k)

            @pl.when(number == close_lag + levels + k + 2)
            def _():
                give.relay(k)

    def hop_on(gather, hop, k):
        gather.hop(k, hop)

    def next_dy(k):
        @pl.when(k > 0)
        def _():
            dy_gather.start(k)

    in_order(close_lag + levels + count, wave)
    give.relay(count - 2, count - 1)
    packed[place] = jnp.concatenate(
        [jnp.sum(gain_acc[...], 0, keepdims=True), jnp.sum(line_one[...], 0, keepdims=True)], axis=1
    )
    for j in range(1, ranks):
        pack_copy(j, place).start()
    for j in range(1, ranks):
        pack_copy(j, sender(j)).wait_recv()
    line = lax.broadcasted_iota(jnp.int32, (8, width), 0)
    two_sum = sum(packed[rank, :, :width] for rank in range(ranks))
    one_sum = jnp.concatenate([packed[rank, :, width:] for rank in range(ranks)], axis=1)
    gains[...] = jnp.where(line == 0, one_sum, two_sum)
    small.start(0)
    small.wait(0)
    gains_out[...] = jnp.sum(gains_in[...], 0)
    late.wait(*range(5))
    give.wait(*range(count))
    give.drain(*range(count))
    deal.wait(*range(count))
    deal.drain(*range(count))
    four.drain()
    three.across(count - 2).wait_send()
    three.across(count - 1).wait_send()
    branch_gather.drain()
    for j in range(1, ranks):
        pack_copy(j, place).wait_send()

    def drain(k):
        for j in range(1, ranks):
            sums_copy(k, j, place).wait_send()

    in_order(count, drain)


def column_all(at, sizes):
    group, level, core = at
    return column_peers(at, sizes) + [
        (group, lax.rem(level + k, sizes[1]), 1 - core) for k in range(1, sizes[1])
    ]


def struct(shape, kind=jnp.bfloat16):
    return jax.ShapeDtypeStruct(shape, kind)


VMEM = pltpu.VMEM
DMA = pltpu.SemaphoreType.DMA


def kernel_call(body, number, ins, outs, scratch):
    places = {
        "vmem": pl.BlockSpec(memory_space=pltpu.VMEM),
        "smem": pl.BlockSpec(memory_space=pltpu.SMEM),
        "any": pl.BlockSpec(memory_space=pl.ANY),
    }
    return pl.pallas_call(
        body,
        out_shape=[shape for _, shape in outs],
        in_specs=[places[inside] for inside, _ in ins],
        out_specs=[places[inside] for inside, _ in outs],
        scratch_shapes=scratch,
        compiler_params=pltpu.CompilerParams(
            collective_id=number, has_side_effects=True, vmem_limit_bytes=63 * 2**20
        ),
    )(*[array for _, array in ins])


def spread_shape(shard, axis, sizes):
    shape = list(shard.shape)
    shape[axis] *= sizes[0]
    return struct(tuple(shape), shard.dtype)


def swap_shape(whole, axis, sizes):
    shape = list(whole.shape)
    shape[axis] //= sizes[0]
    return struct((3 if sizes[0] == 4 else sizes[0],) + tuple(shape), whole.dtype)


def anywhere(items):
    return [("any", item) for item in items]


def held_like(arrays):
    return [VMEM(a.shape, a.dtype) for a in arrays]


def pick(rows, whole):
    return whole.at[rows].get(mode="promise_in_bounds")


def shards(
    tokens,
    cotangent,
    lengths,
    dealing,
    w_query,
    w_key,
    w_value,
    w_swish,
    w_out,
    w_gate,
    w_up,
    w_down,
    gain_attn,
    gain_mlp,
):
    group = lax.axis_index("dp")
    place = lax.axis_index(("heads", "tensor"))
    rows_dev = tokens.shape[0]
    slice_width = tokens.shape[1]
    seq_count = lengths.shape[0]
    ident = jnp.arange(seq_count, dtype=jnp.int32)
    starts = jnp.cumsum(lengths) - lengths
    picked = lax.dynamic_slice_in_dim(dealing, group * SEQ_DEV, SEQ_DEV)
    match = picked[:, None] == ident[None, :]
    dealt_len = jnp.sum(jnp.where(match, lengths[None, :], 0), 1)
    home_start = jnp.sum(jnp.where(match, starts[None, :], 0), 1)
    dealt_start = jnp.cumsum(dealt_len) - dealt_len
    rows = jnp.arange(rows_dev, dtype=jnp.int32)
    seq_ids = jnp.sum((rows[:, None] >= dealt_start[None, :]).astype(jnp.int32), 1) - 1
    sizes = (lax.axis_size("dp"), lax.axis_size("heads"))
    ranks = sizes[1] * lax.axis_size("tensor")
    chunk = ranks * PIECE
    count = rows_dev // chunk
    width = slice_width * ranks
    own = rows_dev // ranks
    qk_dim, v_dim, ff_dim = w_query.shape[1], w_value.shape[1], w_gate.shape[1]
    f32 = jnp.float32
    masters = (w_query, w_key, w_value, w_swish, w_out, w_gate, w_up, w_down)
    axes = (0, 0, 0, 0, 1, 0, 0, 1)
    gain_rows = jnp.pad(jnp.stack([gain_attn, gain_mlp]), ((0, 6), (0, 0)))
    shifts = home_start - dealt_start
    firsts = jnp.arange(2 * count, dtype=jnp.int32) * (chunk // 2)
    begins = jnp.clip(firsts[:, None] + shifts[None, :], 0, sizes[0] * rows_dev - chunk) // 16
    bf16 = jnp.bfloat16
    rounded = [struct(w.shape) for w in masters]
    full_w = [spread_shape(w, a, sizes) for w, a in zip(rounded, axes)]
    by_runs = struct((rows_dev // 16, 16, slice_width))
    every = spread_shape(by_runs, 0, sizes)
    gains_all = struct((sizes[0] * 8, gain_rows.shape[1]), f32)
    (
        normed_in,
        query,
        keys,
        values,
        swish_in,
        dy_part,
        query_w,
        key_w,
        value_w,
        swish_w,
        *low,
        wide_one,
        wide_two,
        x_rows,
        unit_share,
        scale_one,
    ) = kernel_call(
        functools.partial(front_kernel, sizes),
        0,
        [("smem", dealt_start), ("smem", shifts), ("smem", begins.reshape(-1))]
        + anywhere((tokens.reshape(by_runs.shape), cotangent.reshape(by_runs.shape), gain_rows) + masters),
        anywhere(
            [
                struct((rows_dev, width)),
                struct((rows_dev, qk_dim)),
                struct((rows_dev, qk_dim)),
                struct((rows_dev, v_dim)),
                struct((rows_dev, v_dim), f32),
                struct((count, chunk, slice_width)),
            ]
            + full_w[:4]
            + rounded[4:]
        )
        + [
            ("vmem", struct((1, width), f32)),
            ("vmem", struct((1, width), f32)),
            ("vmem", struct((own, width))),
            ("vmem", struct((rows_dev, slice_width), f32)),
            ("vmem", struct((rows_dev, 128), f32)),
        ],
        Gather.scratch(count, sizes, (chunk, slice_width))
        + Spread.scratch(12, sizes)
        + Spread.scratch(1, sizes)
        + held_like(masters)
        + held_like(rounded)
        + held_like(full_w[:4])
        + held_like((by_runs, by_runs, gain_rows, every, every, gains_all))
        + [
            VMEM((count, chunk, slice_width), bf16),
            VMEM((rows_dev, width), bf16),
            VMEM((rows_dev, qk_dim), bf16),
            VMEM((rows_dev, qk_dim), bf16),
            VMEM((rows_dev, v_dim), bf16),
            VMEM((rows_dev, v_dim), f32),
            DMA((11,)),
            DMA((4,)),
            DMA((9,)),
            DMA((count,)),
        ],
    )
    rate = jnp.log1p(-jnp.exp2(-5.0 - place.astype(f32))).reshape(1)
    by_rows = (PIECE, width)
    pieces = (count, sizes[1], 2) + by_rows
    blocks = (sizes[1], 2, slice_width)
    late_w = [struct(shape) for shape in ((width, v_dim), (v_dim, width), (width, v_dim), (qk_dim, width))]
    late_w.append(late_w[3])
    late_axes = (0, 1, 0, 1, 1)
    core_outs = kernel_call(
        functools.partial(core_kernel, sizes),
        1,
        [("smem", dealt_start), ("smem", rate), ("vmem", wide_two), ("vmem", wide_one)]
        + anywhere((query, keys, values, x_rows, dy_part, swish_in))
        + anywhere((normed_in.reshape(pieces), unit_share, scale_one))
        + anywhere([w.reshape(blocks + w.shape[1:]) for w in (query_w, key_w, value_w, swish_w)])
        + anywhere(low),
        anywhere([struct((rows_dev, v_dim)), struct((rows_dev, v_dim), f32)])
        + [("vmem", struct((8, gain_attn.shape[0]), f32))]
        + anywhere(
            [
                struct((sizes[0] * rows_dev, slice_width)),
                struct((sizes[0] * rows_dev, slice_width)),
                swap_shape(full_w[7], 1, sizes),
                swap_shape(full_w[5], 0, sizes),
                swap_shape(full_w[6], 0, sizes),
            ]
            + [swap_shape(w, a, sizes) for w, a in zip(late_w, late_axes)]
        ),
        held_like((query, keys, values, x_rows))
        + held_like(full_w[4:])
        + Scatter.rooms(count, sizes, by_rows)
        + Scatter.rooms(count, sizes, by_rows)[:1]
        + Scatter.sems(count, sizes) * 4
        + Gather.scratch(count, sizes, by_rows)
        + Gather.scratch(count, sizes, (chunk, slice_width))
        + Gather.scratch(count, sizes, by_rows)
        + Spread.scratch(4, sizes)
        + Spread.scratch(count, sizes)
        + Swap.scratch(3, sizes)
        + Swap.scratch(5, sizes)
        + Swap.scratch(1, sizes)
        + Spread.scratch(count, sizes)
        + [
            VMEM((rows_dev, ff_dim), bf16),
            VMEM((rows_dev, ff_dim), bf16),
            VMEM((rows_dev, ff_dim), bf16),
            VMEM((own, width), f32),
            VMEM((2, chunk, v_dim), f32),
            VMEM((2, chunk, v_dim), f32),
            VMEM((2, chunk, v_dim), bf16),
            VMEM((rows_dev, qk_dim), f32),
            VMEM((rows_dev, v_dim), f32),
            VMEM((chunk, qk_dim), f32),
            VMEM((chunk, v_dim), bf16),
            VMEM((ff_dim, width), bf16),
            VMEM((rows_dev, slice_width), bf16),
            VMEM((8, width), f32),
            VMEM((ranks, count, 8, chunk), f32),
            VMEM((8, slice_width), f32),
            VMEM((ranks, 1, width + slice_width), f32),
            VMEM((8, width), f32),
            VMEM((sizes[0], 8, gain_attn.shape[0]), f32),
            DMA((5,)),
            DMA((5, count)),
            DMA((8,)),
            DMA((2, count)),
            pltpu.SemaphoreType.REGULAR((3,)),
            DMA((ranks - 1, count)),
            DMA((ranks - 1, count)),
            DMA((ranks - 1,)),
            DMA((ranks - 1,)),
        ]
        + half_blocks([(full_w[7], 1), (full_w[5], 0), (full_w[6], 0)], sizes)
        + half_blocks(list(zip(late_w, late_axes))[3:], sizes),
    )
    _, _, gains, mixed_all, grad_all, *parts = core_outs
    down, gate, up, swish, out, value, query, key = (jnp.sum(wide(g), 0) for g in parts)
    grads = (query.T, key.T, value, swish, out, gate, up, down)
    slot_match = dealing[:, None] == ident[None, :]
    slot_len = jnp.sum(jnp.where(slot_match, lengths[None, :], 0), 1)
    slot_home = jnp.sum(jnp.where(slot_match, starts[None, :], 0), 1)
    per_group = slot_len.reshape(-1, SEQ_DEV)
    slot_start = (jnp.cumsum(per_group, 1) - per_group).reshape(-1)
    slot_base = ident // SEQ_DEV * rows_dev + slot_start - slot_home
    owner_base = jnp.sum(jnp.where(dealing[None, :] == ident[:, None], slot_base[None, :], 0), 1)
    global_rows = group * rows_dev + rows
    seq_of = jnp.sum((global_rows[:, None] >= starts[None, :]).astype(jnp.int32), 1) - 1
    targets = (
        jnp.sum(jnp.where(seq_of[:, None] == ident[None, :], owner_base[None, :], 0), 1)
        + global_rows
    )
    mixed_rows, grad_rows = pick(targets, mixed_all), pick(targets, grad_all)
    return (
        mixed_rows,
        grad_rows,
        grads[0],
        grads[1],
        grads[2],
        grads[3],
        grads[4],
        grads[5],
        grads[6],
        grads[7],
        gains[0],
        gains[1],
    )


def solution(mesh):
    in_specs = (
        P("dp", ("heads", "tensor")),
        P("dp", ("heads", "tensor")),
        P(),
        P(),
        P("dp", ("heads", "tensor")),
        P("dp", ("heads", "tensor")),
        P("dp", ("heads", "tensor")),
        P("dp", ("heads", "tensor")),
        P(("heads", "tensor"), "dp"),
        P("dp", ("heads", "tensor")),
        P("dp", ("heads", "tensor")),
        P(("heads", "tensor"), "dp"),
        P("dp"),
        P("dp"),
    )
    out_specs = (
        P("dp", ("heads", "tensor")),
        P("dp", ("heads", "tensor")),
        P("dp", ("heads", "tensor")),
        P("dp", ("heads", "tensor")),
        P("dp", ("heads", "tensor")),
        P("dp", ("heads", "tensor")),
        P(("heads", "tensor"), "dp"),
        P("dp", ("heads", "tensor")),
        P("dp", ("heads", "tensor")),
        P(("heads", "tensor"), "dp"),
        P("dp"),
        P("dp"),
    )
    return jax.shard_map(shards, mesh=mesh, in_specs=in_specs, out_specs=out_specs, check_vma=False)
```

```python
import functools

import jax
import jax.numpy as jnp
from jax import lax
from jax.experimental import pallas as pl
from jax.experimental.pallas import tpu as pltpu
from jax.sharding import PartitionSpec as P

QK_DIM = 256
SEQ_DEV = 3
PIECE = 32
AXES = ("dp", "heads", "tensor")
MESH = pl.DeviceIdType.MESH


EPSILON = 1e-05
GROUP_EPS = 1.0


def layer_norm(values, epsilon):
    center = values - jnp.mean(values, -1, keepdims=True)
    scale = lax.rsqrt(jnp.mean(center * center, -1, keepdims=True) + epsilon)
    return (center * scale, scale)


def norm_back(grad, normed, scale):
    return scale * (
        grad
        - jnp.mean(grad, -1, keepdims=True)
        - normed * jnp.mean(grad * normed, -1, keepdims=True)
    )


def product(left, right):
    return jnp.dot(left, right, preferred_element_type=jnp.float32)


def inner_rows(left, right):
    return lax.dot_general(
        left, right, (((1,), (1,)), ((), ())), preferred_element_type=jnp.float32
    )


def inner_cols(left, right):
    return lax.dot_general(
        left, right, (((0,), (0,)), ((), ())), preferred_element_type=jnp.float32
    )


def lowered(value):
    return value.astype(jnp.bfloat16)


def around(axes):
    return tuple(lax.axis_index(name) for name in axes)


def wide(value):
    return value.astype(jnp.float32)


def within(number, count):
    return (number >= 0) & (number < count)


def greet(others):
    barrier = pltpu.get_barrier_semaphore()
    for other in others:
        pl.semaphore_signal(barrier, inc=1, device_id=other, device_id_type=MESH)
    pl.semaphore_wait(barrier, len(others))


def plane_peers(at, sizes):
    group, level, core = at
    return [(lax.rem(group + k, sizes[0]), level, core) for k in range(1, sizes[0])]


def column_peers(at, sizes):
    group, level, core = at
    return [(group, lax.rem(level + k, sizes[1]), core) for k in range(1, sizes[1])] + [
        (group, level, 1 - core)
    ]


def beside(group):
    return group + 1 - 2 * lax.rem(group, 2), lax.rem(group + 2, 4), 3 - group


class Spread:
    def __init__(self, at, sizes, items, sems, relay=True):
        self.at, self.count, self.items = at, sizes[0], items
        self.local, self.sent, self.got = sems
        self.plane = relay and sizes[0] == 4

    @staticmethod
    def scratch(items, sizes):
        ways = max(4, sizes[0] - 1)
        return [
            pltpu.SemaphoreType.DMA((items,)),
            pltpu.SemaphoreType.DMA((items, ways)),
            pltpu.SemaphoreType.DMA((items, ways)),
        ]

    def place(self, number, owner, half=None):
        source, target, axis, *where = self.items[number]
        rows = source.shape[0]
        size = source.shape[axis]
        step, offset = where or (size, 0)
        start = owner * step + offset
        if half is None:
            begin, height = 0, rows
        else:
            begin, height = half * (rows // 2), rows // 2
        if axis == 0:
            return target.at[pl.ds(pl.multiple_of(start + begin, height), height)]
        return target.at[pl.ds(begin, height), pl.ds(pl.multiple_of(start, size), size)]

    def own(self, number):
        return pltpu.make_async_copy(
            self.items[number][0], self.place(number, self.at[0]), self.local.at[number]
        )

    def copy(self, number, source, place, way, peer):
        return pltpu.make_async_remote_copy(
            src_ref=source,
            dst_ref=place,
            send_sem=self.sent.at[number, way],
            recv_sem=self.got.at[number, way],
            device_id=(peer,) + self.at[1:],
            device_id_type=MESH,
        )

    def away(self, number, k):
        peer = lax.rem(self.at[0] + k, self.count)
        return self.copy(number, self.items[number][0], self.place(number, self.at[0]), k - 1, peer)

    def landed(self, number, k):
        owner = lax.rem(self.at[0] + self.count - k, self.count)
        return self.copy(number, self.items[number][0], self.place(number, owner), k - 1, owner)

    def to(self, number, way):
        peer = beside(self.at[0])[way]
        return self.copy(number, self.items[number][0], self.place(number, self.at[0]), way, peer)

    def of(self, number, way):
        peer = beside(self.at[0])[way]
        return self.copy(number, self.items[number][0], self.place(number, peer), way, peer)

    def on(self, number, way):
        near = beside(self.at[0])
        ref = self.place(number, near[way], way)
        return self.copy(number, ref, ref, 2 + way, near[1 - way])

    def last(self, number, way):
        near = beside(self.at[0])
        ref = self.place(number, near[2], way)
        return self.copy(number, ref, ref, 2 + way, near[1 - way])

    def start(self, *numbers):
        for number in numbers:
            if self.plane:
                self.to(number, 0).start()
                self.to(number, 1).start()
            else:
                for k in range(1, self.count):
                    self.away(number, k).start()
            self.own(number).start()

    def relay(self, *numbers):
        if self.plane:
            for number in numbers:
                for way in range(2):
                    self.of(number, way).wait_recv()
                    self.on(number, way).start()

    def wait(self, *numbers):
        for number in numbers:
            self.own(number).wait()
            if self.plane:
                self.last(number, 0).wait_recv()
                self.last(number, 1).wait_recv()
            else:
                for k in range(1, self.count):
                    self.landed(number, k).wait_recv()

    def drain(self, *numbers):
        for number in numbers:
            if self.plane:
                for way in range(2):
                    self.to(number, way).wait_send()
                    self.on(number, way).wait_send()
            else:
                for k in range(1, self.count):
                    self.away(number, k).wait_send()


class Gather:
    def __init__(self, at, sizes, count, full, sems):
        self.at, self.levels, self.count, self.full = at, sizes[1], count, full
        self.sent_up, self.got_up, self.sent_down, self.got_down, self.sent_core, self.got_core = sems

    @staticmethod
    def scratch(count, sizes, piece):
        levels = sizes[1]
        dma = pltpu.SemaphoreType.DMA
        return [pltpu.VMEM((count, levels, 2) + piece, jnp.bfloat16)] + [
            dma((levels - 1, count)) for _ in range(4)
        ] + [dma((2 * levels - 1, count)) for _ in range(2)]

    def copy(self, ref, sent, got, target):
        return pltpu.make_async_remote_copy(
            src_ref=ref, dst_ref=ref, send_sem=sent, recv_sem=got, device_id=target, device_id_type=MESH
        )

    def up(self, k, hop, origin, sem):
        group, level, core = self.at
        target = (group, lax.rem(level + 1, self.levels), core)
        return self.copy(self.full.at[k, origin, core], self.sent_up.at[sem, k], self.got_up.at[sem, k], target)

    def down(self, k, hop, origin, sem):
        group, level, core = self.at
        target = (group, lax.rem(level + self.levels - 1, self.levels), core)
        return self.copy(
            self.full.at[k, origin, core], self.sent_down.at[sem, k], self.got_down.at[sem, k], target
        )

    def across(self, k, origin, side, sem):
        group, level, core = self.at
        return self.copy(
            self.full.at[k, origin, side], self.sent_core.at[sem, k], self.got_core.at[sem, k], (group, level, 1 - core)
        )

    def start(self, k):
        group, level, core = self.at

        @pl.when(level < self.levels - 1)
        def _():
            self.up(k, 0, level, 0).start()

        @pl.when(level > 0)
        def _():
            self.down(k, 0, level, 0).start()

        self.across(k, level, core, 0).start()

    def hop(self, k, hop):
        group, level, core = self.at
        last = self.levels - 1

        @pl.when(level >= hop)
        def _():
            origin = level - hop
            self.up(k, hop, origin, hop - 1).wait_recv()
            if hop < last:

                @pl.when(level < last)
                def _():
                    self.up(k, hop, origin, hop).start()

            self.across(k, origin, core, hop).start()

        @pl.when(level + hop <= last)
        def _():
            origin = level + hop
            self.down(k, hop, origin, hop - 1).wait_recv()
            if hop < last:

                @pl.when(level > 0)
                def _():
                    self.down(k, hop, origin, hop).start()

            self.across(k, origin, core, last + hop).start()

    def ready(self, k):
        group, level, core = self.at
        last = self.levels - 1
        self.across(k, level, 1 - core, 0).wait_recv()
        for hop in range(1, self.levels):

            @pl.when(level >= hop)
            def _():
                self.across(k, level - hop, 1 - core, hop).wait_recv()

            @pl.when(level + hop <= last)
            def _():
                self.across(k, level + hop, 1 - core, last + hop).wait_recv()

    def drain(self):
        group, level, core = self.at
        last = self.levels - 1

        def one(k, _):
            self.across(k, level, core, 0).wait_send()
            for hop in range(self.levels):
                if hop < last:

                    @pl.when((level >= hop) & (level < last))
                    def _():
                        self.up(k, hop, level - hop, hop).wait_send()

                    @pl.when((level + hop <= last) & (level > 0))
                    def _():
                        self.down(k, hop, level + hop, hop).wait_send()

                if hop > 0:

                    @pl.when(level >= hop)
                    def _():
                        self.across(k, level - hop, core, hop).wait_send()

                    @pl.when(level + hop <= last)
                    def _():
                        self.across(k, level + hop, core, last + hop).wait_send()

            return 0

        lax.fori_loop(0, self.count, one, 0)


class Scatter:
    REFS = 4

    def __init__(self, at, sizes, count, refs):
        self.at, self.levels, self.count = at, sizes[1], count
        self.part, self.cross, self.inbox, self.total = refs[:4]
        self.sent_core, self.got_core, self.sent_up, self.got_up, self.sent_down, self.got_down = refs[4:]

    @staticmethod
    def rooms(count, sizes, piece):
        levels = sizes[1]
        return [
            pltpu.VMEM((2, levels, 2) + piece, jnp.bfloat16),
            pltpu.VMEM((count, levels) + piece, jnp.bfloat16),
            pltpu.VMEM((count, levels + 1) + piece, jnp.bfloat16),
            pltpu.VMEM(piece, jnp.float32),
        ]

    @staticmethod
    def sems(count, sizes):
        dma = pltpu.SemaphoreType.DMA
        return [dma((count,)) for _ in range(2)] + [dma((sizes[1], count)) for _ in range(4)]

    @staticmethod
    def scratch(count, sizes, piece):
        return Scatter.rooms(count, sizes, piece) + Scatter.sems(count, sizes)

    def across(self, k):
        group, level, core = self.at
        return pltpu.make_async_remote_copy(
            src_ref=self.part.at[lax.rem(k, 2), :, 1 - core],
            dst_ref=self.cross.at[k],
            send_sem=self.sent_core.at[k],
            recv_sem=self.got_core.at[k],
            device_id=(group, level, 1 - core),
            device_id_type=MESH,
        )

    def up(self, k, owner):
        group, level, core = self.at
        return pltpu.make_async_remote_copy(
            src_ref=self.cross.at[k, owner],
            dst_ref=self.inbox.at[k, owner + 1],
            send_sem=self.sent_up.at[owner, k],
            recv_sem=self.got_up.at[owner, k],
            device_id=(group, lax.rem(level + 1, self.levels), core),
            device_id_type=MESH,
        )

    def down(self, k, owner):
        group, level, core = self.at
        return pltpu.make_async_remote_copy(
            src_ref=self.cross.at[k, owner],
            dst_ref=self.inbox.at[k, owner],
            send_sem=self.sent_down.at[owner, k],
            recv_sem=self.got_down.at[owner, k],
            device_id=(group, lax.rem(level + self.levels - 1, self.levels), core),
            device_id_type=MESH,
        )

    def free(self, k, before=None):
        @pl.when(k >= 2)
        def _():
            self.across(k - 2).wait_send()

        if before is not None:

            @pl.when(k < 2)
            def _():
                before.across(self.count - 2 + k).wait_send()

    def start(self, k):
        self.across(k).start()

    def join(self, k):
        core = self.at[2]
        self.across(k).wait_recv()
        for owner in range(self.levels):
            self.cross[k, owner] = lowered(
                wide(self.part[lax.rem(k, 2), owner, core]) + wide(self.cross[k, owner])
            )

    def step_up(self, k):
        level = self.at[1]
        for owner in range(self.levels - 1, 0, -1):

            @pl.when(level < owner)
            def _():
                @pl.when(level > 0)
                def _():
                    self.up(k, owner).wait_recv()
                    self.cross[k, owner] = lowered(wide(self.cross[k, owner]) + wide(self.inbox[k, owner + 1]))

                self.up(k, owner).start()

    def step_down(self, k):
        level = self.at[1]
        for owner in range(self.levels - 1):

            @pl.when(level > owner)
            def _():
                @pl.when(level < self.levels - 1)
                def _():
                    self.down(k, owner).wait_recv()
                    self.cross[k, owner] = lowered(wide(self.cross[k, owner]) + wide(self.inbox[k, owner]))

                self.down(k, owner).start()

    def steps(self, wave):
        level = self.at[1]
        above = wave - level
        below = wave - (self.levels - 1 - level)

        @pl.when(within(above, self.count) & (level < self.levels // 2))
        def _():
            self.step_up(above)

        @pl.when(within(below, self.count))
        def _():
            self.step_down(below)

        @pl.when(within(above, self.count) & (level >= self.levels // 2))
        def _():
            self.step_up(above)

    def finish(self, k):
        level = self.at[1]
        self.total[...] = wide(self.cross[k, level])

        @pl.when(level > 0)
        def _():
            self.up(k, level).wait_recv()
            self.total[...] += wide(self.inbox[k, level + 1])

        @pl.when(level < self.levels - 1)
        def _():
            self.down(k, level).wait_recv()
            self.total[...] += wide(self.inbox[k, level])

    def sent(self, k):
        level = self.at[1]
        for owner in range(self.levels):

            @pl.when(level < owner)
            def _():
                self.up(k, owner).wait_send()

            @pl.when(level > owner)
            def _():
                self.down(k, owner).wait_send()

    def drain(self):
        self.across(self.count - 2).wait_send()
        self.across(self.count - 1).wait_send()
        in_order(self.count, self.sent)


def in_order(count, step):
    def body(number, carry):
        step(number)
        return carry

    lax.fori_loop(0, count, body, 0)


def span(number, size):
    return pl.ds(pl.multiple_of(number * size, size), size)


class Moves:
    def __init__(self, pairs, sems):
        self.pairs, self.sems = pairs, sems

    def copy(self, number):
        return pltpu.make_async_copy(*self.pairs[number], self.sems.at[number])

    def start(self, *numbers):
        for number in numbers:
            self.copy(number).start()

    def wait(self, *numbers):
        for number in numbers:
            self.copy(number).wait()


class Chunks:
    def __init__(self, pairs, size, sems):
        self.pairs, self.size, self.sems = pairs, size, sems

    def start(self, k):
        for number, (source, target) in enumerate(self.pairs):
            rows = span(k, self.size)
            pltpu.make_async_copy(source.at[rows], target.at[rows], self.sems.at[number, k]).start()

    def wait(self, count):
        def one(k, carry):
            for number, (source, target) in enumerate(self.pairs):
                rows = span(k, self.size)
                pltpu.make_async_copy(source.at[rows], target.at[rows], self.sems.at[number, k]).wait()
            return carry

        lax.fori_loop(0, count, one, 0)


def matmul(left, right):
    return jnp.dot(left, right, preferred_element_type=jnp.float32)


def decay_tile(near, far, size, bounds, rate):
    rows = near * size + lax.broadcasted_iota(jnp.int32, (size, 1), 0)
    columns = far * size + lax.broadcasted_iota(jnp.int32, (1, size), 1)
    row_seq, column_seq = jnp.zeros((size, 1), jnp.int32), jnp.zeros((1, size), jnp.int32)
    for number in range(1, SEQ_DEV):
        row_seq += (rows >= bounds[number]).astype(jnp.int32)
        column_seq += (columns >= bounds[number]).astype(jnp.int32)
    distance = rows - columns
    valid = (distance >= 0) & (row_seq == column_seq)
    return (
        jnp.where(valid, jnp.exp(jnp.maximum(distance, 0).astype(jnp.float32) * rate[0]), 0.0)
        * QK_DIM ** (-0.5)
    )


class Swap:
    def __init__(self, at, sizes, items, sems, halves=None):
        self.at, self.count, self.items = at, sizes[0], items
        self.local, self.sent, self.got = sems
        self.halves = halves
        self.plane = halves is not None and sizes[0] == 4

    @staticmethod
    def scratch(items, sizes):
        ways = max(6, sizes[0] - 1)
        return [
            pltpu.SemaphoreType.DMA((items,)),
            pltpu.SemaphoreType.DMA((items, ways)),
            pltpu.SemaphoreType.DMA((items, ways)),
        ]

    def block(self, number, owner, half=None):
        source, target, axis = self.items[number]
        rows = source.shape[0]
        size = source.shape[axis] // self.count
        height = size if axis == 0 else rows
        begin = 0
        if half is not None:
            height //= 2
            begin = half * height
        if axis == 0:
            return source.at[pl.ds(pl.multiple_of(owner * size + begin, height), height)]
        return source.at[pl.ds(begin, height), pl.ds(pl.multiple_of(owner * size, size), size)]

    def half(self, number, slot, half):
        target = self.items[number][1]
        height = target.shape[1] // 2
        return target.at[slot, pl.ds(half * height, height)]

    def copy(self, number, source, place, way, peer):
        return pltpu.make_async_remote_copy(
            src_ref=source,
            dst_ref=place,
            send_sem=self.sent.at[number, way],
            recv_sem=self.got.at[number, way],
            device_id=(peer,) + self.at[1:],
            device_id_type=MESH,
        )

    def own(self, number):
        return pltpu.make_async_copy(
            self.block(number, self.at[0]), self.items[number][1].at[0], self.local.at[number]
        )

    def away(self, number, k):
        peer = lax.rem(self.at[0] + k, self.count)
        return self.copy(number, self.block(number, peer), self.items[number][1].at[k], k - 1, peer)

    def across(self, number, way):
        near = beside(self.at[0])
        return self.copy(
            number, self.block(number, near[2], way), self.halves[number].at[way], way, near[way]
        )

    def direct(self, number, way):
        near = beside(self.at[0])
        return self.copy(
            number, self.block(number, near[way], way), self.half(number, 1 + way, way), 2 + way, near[way]
        )

    def added(self, number, way):
        peer = beside(self.at[0])[1 - way]
        return self.copy(
            number, self.block(number, peer, way), self.half(number, 2 - way, way), 4 + way, peer
        )

    def start(self, *numbers):
        for number in numbers:
            if self.plane:
                for way in range(2):
                    self.across(number, way).start()
                for way in range(2):
                    self.direct(number, way).start()
            else:
                for k in range(1, self.count):
                    self.away(number, k).start()
            self.own(number).start()

    def relay(self, *numbers):
        if self.plane:
            near = beside(self.at[0])
            for number in numbers:
                for way in range(2):
                    self.across(number, way).wait_recv()
                    part = self.block(number, near[1 - way], way)
                    part[...] = lowered(wide(part[...]) + wide(self.halves[number][way]))
                for way in range(2):
                    self.added(number, way).start()

    def wait(self, *numbers):
        for number in numbers:
            self.own(number).wait()
            if self.plane:
                for way in range(2):
                    self.across(number, way).wait_send()
                    self.direct(number, way).wait()
                    self.added(number, way).wait()
            else:
                for k in range(1, self.count):
                    self.away(number, k).wait()


def half_blocks(items, sizes):
    room = []
    for whole, axis in items:
        shape = list(whole.shape)
        shape[axis] //= sizes[0]
        room.append(pltpu.VMEM((2, shape[0] // 2, shape[1]), jnp.bfloat16))
    return room


def quarters(source, target):
    rows = source.shape[0]
    run = rows // 4
    return [(source.at[pl.ds(k * run, run)], target, 0, rows, k * run) for k in range(4)]


def pick_rows(whole, number, first, rows, bounds, shifts, begins):
    window = 2 * rows
    lane = lax.broadcasted_iota(jnp.int32, (rows, window), 1)
    slot = jnp.zeros((rows, 1), jnp.int32)
    own = first + lax.broadcasted_iota(jnp.int32, (rows, 1), 0)
    for item in range(1, SEQ_DEV):
        slot += (own >= bounds[item]).astype(jnp.int32)
    chosen, windows = [], []
    for item in range(SEQ_DEV):
        start = begins[number * SEQ_DEV + item]
        wanted = jnp.where(slot == item, own + shifts[item] - 16 * start, -1)
        chosen.append(jnp.where(lane == wanted, 1.0, 0.0).astype(jnp.bfloat16))
        windows += [whole[start + k] for k in range(window // 16)]
    return lowered(matmul(jnp.concatenate(chosen, axis=1), jnp.concatenate(windows, axis=0)))


def front_kernel(sizes, bounds, shifts, begins, tokens, cotangent, gain_rows, *refs):
    masters, refs = refs[:8], refs[8:]
    normed_out, query_out, key_out, value_out, swish_out, dy_out, *refs = refs
    weight_outs, rounded_outs, refs = refs[:4], refs[4:8], refs[8:]
    gain_one, gain_two, rows_out, unit_out, scale_out, *refs = refs
    full, *refs = refs
    gather_sems, refs = refs[:6], refs[6:]
    spread_sems, small_sems, refs = refs[:3], refs[3:6], refs[6:]
    held, rounded, weights, refs = refs[:8], refs[8:16], refs[16:20], refs[20:]
    tokens_held, dy_held, gains_held, tokens_all, dy_all, gains_all, dy_part, *refs = refs
    normed, query, keys, values, swish, load_sems, store_sems, out_sems, normed_sem = refs
    at = around(AXES)
    group, level, core = at
    place = 2 * level + core
    count, levels, _, chunk, width = full.shape
    ranks = 2 * levels
    piece = chunk // ranks
    loads = Moves(
        list(zip(masters, held)) + [(tokens, tokens_held), (gain_rows, gains_held), (cotangent, dy_held)], load_sems
    )
    loads.start(8, 9, 2, 3, 1, 0, 10, 4, 5, 6, 7)
    greet(plane_peers(at, sizes) + column_peers(at, sizes))
    loads.wait(8, 9)
    spread = Spread(
        at,
        sizes,
        quarters(tokens_held, tokens_all)
        + [(rounded[2], weights[2], 0), (rounded[3], weights[3], 0)]
        + quarters(dy_held, dy_all)
        + [(rounded[1], weights[1], 0), (rounded[0], weights[0], 0)],
        spread_sems,
    )
    small = Spread(at, sizes, [(gains_held, gains_all, 0)], small_sems, relay=False)
    spread.start(*range(4))
    small.start(0)
    gather = Gather(at, sizes, count, full, gather_sems)

    def cast(number):
        loads.wait(number)
        rows = min(32, held[number].shape[0])

        def block(k):
            held_rows = span(k, rows)
            rounded[number][held_rows, :] = lowered(held[number][held_rows, :])

        in_order(held[number].shape[0] // rows, block)

    stores = Moves(list(zip(rounded[4:], rounded_outs)), store_sems)
    cast(2)
    spread.start(4)
    for number in (3, 1, 0, 4, 5, 6, 7):
        cast(number)
    loads.wait(10)
    stores.start(*range(4))
    for number in range(4):
        spread.relay(number)
    spread.start(5, 6, 7)
    small.wait(0)
    own = gains_held.shape[0]
    for row, gain in enumerate((gain_one, gain_two)):
        gain[...] = wide(
            lowered(
                jnp.concatenate([gains_all[own * k + row : own * k + row + 1, :] for k in range(sizes[0])], axis=1)
            )
        )
    spread.wait(*range(4))
    run = chunk // 2

    def pick_chunk(whole, k, half):
        return pick_rows(whole, 2 * k + half, k * chunk + half * run, run, bounds, shifts, begins)

    def begin(k):
        for half in range(2):
            full[k, level, core, half * run : (half + 1) * run, :] = pick_chunk(tokens_all, k, half)
        gather.start(k)

    def norm(k):
        def block(number, carry):
            rows = span(number, 16)
            value = jnp.concatenate(
                [wide(full[k, q, c, rows, :]) for q in range(levels) for c in range(2)], axis=1
            )
            unit, scale = layer_norm(value, EPSILON)
            where = pl.ds(pl.multiple_of(k * chunk + number * 16, 16), 16)
            normed[where, :] = lowered(unit * gain_one[...])
            mine = wide(full[k, level, core, rows, :])
            mean = jnp.mean(value, -1, keepdims=True)
            unit_out[where, :] = (mine - mean) * scale
            scale_out[where, :] = jnp.broadcast_to(scale, (16, 128))
            return carry

        lax.fori_loop(0, chunk // 16, block, 0)
        mine = span(place, piece)
        rows_out[span(k, piece), :] = jnp.concatenate(
            [full[k, q, c, mine, :] for q in range(levels) for c in range(2)], axis=1
        )
        pltpu.make_async_copy(
            normed.at[span(k, chunk)], normed_out.at[span(k, chunk)], normed_sem.at[k]
        ).start()

    begin(0)
    outs = [(query, query_out), (keys, key_out), (values, value_out), (swish, swish_out)]
    ends = Moves(outs + list(zip(weights, weight_outs)) + [(dy_part, dy_out)], out_sems)

    def project_rows(number, k):
        where = span(k, chunk)
        target = outs[number][0]
        target[where, :] = matmul(normed[where, :], weights[number][...]).astype(target.dtype)

    def wave(number):
        @pl.when(number + 1 < count)
        def _():
            begin(number + 1)

        for hop in range(levels - 1, 0, -1):

            @pl.when(within(number - hop, count))
            def _():
                gather.hop(number - hop, hop)

        for step, relayed, started in (
            (1, (4,), (8, 9)),
            (3, (5,), (10, 11)),
            (5, (6, 7), ()),
            (6, (8, 9), ()),
            (8, (10,), ()),
        ):

            @pl.when(number == step)
            def _():
                spread.relay(*relayed)
                spread.start(*started)

        @pl.when(within(number - levels, count))
        def _():
            gather.ready(number - levels)
            norm(number - levels)

        @pl.when(number == levels + 3)
        def _():
            spread.wait(4)
            ends.start(6)
            for k in range(3):
                project_rows(2, k)

        @pl.when(number >= levels + 3)
        def _():
            project_rows(2, number - levels)

    in_order(count + levels, wave)

    def project(number, item):
        if item is not None:
            spread.wait(item)
            ends.start(4 + number)
            in_order(count, functools.partial(project_rows, number))
        ends.start(number)

    spread.relay(11)
    project(2, None)
    project(3, 5)
    spread.wait(*range(6, 10))

    def dy_chunk(k):
        for half in range(2):
            dy_part[k, half * run : (half + 1) * run, :] = pick_chunk(dy_all, k, half)

    in_order(count, dy_chunk)
    ends.start(8)
    project(1, 10)
    project(0, 11)
    small.drain(0)
    spread.drain(*range(12))
    gather.drain()
    stores.wait(*range(4))
    ends.wait(*range(9))

    def stored(k):
        pltpu.make_async_copy(
            normed.at[span(k, chunk)], normed_out.at[span(k, chunk)], normed_sem.at[k]
        ).wait()

    in_order(count, stored)


class Ring:
    def __init__(self, slots, whole, size, sems):
        self.slots, self.whole, self.size, self.sems = slots, whole, size, sems

    def load(self, k):
        return pltpu.make_async_copy(
            self.whole.at[span(k, self.size)], self.slots.at[lax.rem(k, 2)], self.sems.at[k]
        )

    def store(self, k):
        return pltpu.make_async_copy(
            self.slots.at[lax.rem(k, 2)], self.whole.at[span(k, self.size)], self.sems.at[k]
        )

    def free(self, k):
        @pl.when(k >= 2)
        def _():
            self.store(k - 2).wait()


def core_kernel(sizes, bounds, rate, gain, *refs):
    gain_first, *refs = refs
    query_src, key_src, value_src, rows_src, dy_src, swish_src, *refs = refs
    normed_src, unit_src, scale_src, *refs = refs
    project_src, refs = refs[:4], refs[4:]
    shards, refs = refs[:4], refs[4:]
    mixed_in_out, retained_out, gains_out, *refs = refs
    mixed_dst, grad_dst, down_dst, gate_dst, up_dst, *refs = refs
    late_dst, refs = refs[:5], refs[5:]
    query, keys, values, x_rows, out_w, gate_w, up_w, down_w, *refs = refs
    rooms, refs = refs[:4], refs[4:]
    (other_part,), refs = refs[:1], refs[1:]
    sems_one, sems_two, sems_three, sems_four, refs = refs[:6], refs[6:12], refs[12:18], refs[18:24], refs[24:]
    normed_mid, refs = refs[0], refs[1:]
    normed_sems, refs = refs[:6], refs[6:]
    dy, refs = refs[0], refs[1:]
    dy_sems, refs = refs[:6], refs[6:]
    branch, refs = refs[0], refs[1:]
    branch_sems, refs = refs[:6], refs[6:]
    spread_sems, refs = refs[:3], refs[3:]
    deal_sems, refs = refs[:3], refs[3:]
    swap_sems, late_sems, small_sems, refs = refs[:3], refs[3:6], refs[6:9], refs[9:]
    give_sems, refs = refs[:3], refs[3:]
    hidden, gate_grad, up_grad, resid, swish_slots, retained_slots, mixed_in_slots, *refs = refs
    key_acc, value_acc, query_acc, delta, down_grad, mixed, gain_acc, *refs = refs
    sums, line_one, packed, gains, gains_in, *refs = refs
    load_sems, ring_sems, late_load, unit_sems, room, sums_sent, sums_got, gain_sent, gain_got, *halves = refs
    at = around(AXES)
    group, level, core = at
    place = 2 * level + core
    count, levels, _, piece, width = normed_mid.shape
    ranks = 2 * levels
    chunk = ranks * piece
    part_width = width // ranks
    loads = Moves(
        [
            (dy_src, dy.at[:, level, core]),
            (query_src, query),
            (key_src, keys),
            (value_src, values),
            (rows_src, x_rows),
        ],
        load_sems,
    )
    loads.start(*range(5))
    swish_one = Ring(swish_slots, swish_src, chunk, ring_sems.at[0])
    swish_two = Ring(swish_slots, swish_src, chunk, ring_sems.at[1])
    retained_one = Ring(retained_slots, retained_out, chunk, ring_sems.at[2])
    retained_two = Ring(retained_slots, retained_out, chunk, ring_sems.at[3])
    mixed_in_ring = Ring(mixed_in_slots, mixed_in_out, chunk, ring_sems.at[4])
    groups, v_dim = sizes[0], values.shape[1]
    late_loads = Moves(
        [(normed_src, normed_mid), (mixed_in_out, up_grad), (project_src[0], dy.at[0]), (project_src[1], dy.at[1])]
        + [
            (project_src[2 + n // 2].at[:, :, :, pl.ds(n % 2 * part_width, part_width)], dy.at[2 + n])
            for n in range(4)
        ],
        late_load,
    )
    swish_one.load(0).start()
    swish_one.load(1).start()
    greet(plane_peers(at, sizes) + column_all(at, sizes))
    spread = Spread(
        at,
        sizes,
        [(shards[0], out_w, 1), (shards[1], gate_w, 0), (shards[2], up_w, 0), (shards[3], down_w, 1)],
        spread_sems,
    )
    deal = Spread(
        at,
        sizes,
        [
            (mixed.at[pl.ds(k * chunk, chunk)], mixed_dst, 0, count * chunk, k * chunk)
            for k in range(count)
        ],
        deal_sems,
    )
    swap = Swap(
        at, sizes, [(down_grad, down_dst, 1), (gate_w, gate_dst, 0), (up_w, up_dst, 0)], swap_sems, halves[:3]
    )
    qk_dim = query.shape[1]
    late = Swap(
        at,
        sizes,
        [
            (gate_w, late_dst[0], 0),
            (out_w, late_dst[1], 1),
            (up_w, late_dst[2], 0),
            (down_grad.at[pl.ds(0, qk_dim)], late_dst[3], 1),
            (down_grad.at[pl.ds(qk_dim, qk_dim)], late_dst[4], 1),
        ],
        late_sems,
        [halves[1], halves[0], halves[2], halves[3], halves[4]],
    )
    small = Swap(at, sizes, [(gains, gains_in, 1)], small_sems)
    give = Spread(
        at,
        sizes,
        [
            (hidden.at[pl.ds(k * chunk, chunk), pl.ds(0, part_width)], grad_dst, 0, count * chunk, k * chunk)
            for k in range(count)
        ],
        give_sems,
    )
    spread.start(0)
    one = Scatter(at, sizes, count, list(rooms) + list(sems_one))
    two = Scatter(at, sizes, count, [other_part] + list(rooms[1:]) + list(sems_two))
    three = Scatter(at, sizes, count, list(rooms) + list(sems_three))
    four = Scatter(at, sizes, count, [other_part] + list(rooms[1:]) + list(sems_four))
    total = rooms[3]
    mid_gather = Gather(at, sizes, count, normed_mid, normed_sems)
    dy_gather = Gather(at, sizes, count, dy, dy_sems)
    branch_gather = Gather(at, sizes, count, branch, branch_sems)
    gain_acc[...] = jnp.zeros(gain_acc.shape, jnp.float32)
    line_one[...] = jnp.zeros(line_one.shape, jnp.float32)
    key_acc[...] = jnp.zeros(key_acc.shape, jnp.float32)
    value_acc[...] = jnp.zeros(value_acc.shape, jnp.float32)
    loads.wait(0)
    dy_gather.start(0)
    loads.wait(1, 2, 3, 4)
    tile = 512

    def first(k):
        where = span(k, chunk)
        slot = lax.rem(k, 2)
        retained_one.free(k)
        retained_slots[slot] = jnp.zeros((chunk, values.shape[1]), jnp.float32)

        def block(j, carry):
            there = span(j, chunk)
            decay = decay_tile(k, j, chunk, bounds, rate)
            weight = lowered(inner_rows(query[where, :], keys[there, :]) * decay)
            retained_slots[slot] += matmul(weight, values[there, :])
            return carry

        lax.fori_loop(0, k + 1, block, 0)
        retained_one.store(k).start()
        normed, _ = layer_norm(retained_slots[slot], GROUP_EPS)
        swish_one.load(k).wait()
        value = swish_slots[slot]
        mixed_in_ring.free(k)
        mixed_in_slots[slot] = lowered(value * jax.nn.sigmoid(value) * normed)
        mixed_in_ring.store(k).start()

        @pl.when(k + 2 < count)
        def _():
            swish_one.load(k + 2).start()

        @pl.when(k == 0)
        def _():
            spread.wait(0)

        one.free(k)
        rows = mixed_in_slots[slot]
        for column in range(0, width, tile):
            value = matmul(rows, out_w[:, column : column + tile])
            one.part[slot, :, :, :, column : column + tile] = lowered(value).reshape(levels, 2, piece, tile)
        one.start(k)

    def mid_norm(k):
        one.finish(k)

        def block(number, carry):
            sub = span(number, 16)
            where = pl.ds(pl.multiple_of(k * piece + number * 16, 16), 16)
            value = wide(x_rows[where, :]) + total[sub, :]
            resid[where, :] = value
            unit, _ = layer_norm(value, EPSILON)
            normed_mid[k, level, core, sub, :] = lowered(unit * gain[...])
            return carry

        lax.fori_loop(0, piece // 16, block, 0)
        mid_gather.start(k)

    def turn(k):
        mid_gather.ready(k)
        rows = normed_mid[k].reshape(chunk, width)
        where = span(k, chunk)
        g = matmul(rows, gate_w[...])
        u = matmul(rows, up_w[...])
        root = 0.7978845608028654
        bend = jnp.tanh(root * (g + 0.044715 * g * g * g))
        curve = 0.5 * (1.0 + bend)
        active = g * curve
        hidden[where, :] = lowered(active * u)
        slope = curve + 0.5 * g * (1.0 - bend * bend) * root * (1.0 + 0.134145 * g * g)
        dy_gather.ready(k)
        rows = jnp.concatenate([dy[k, q, c] for q in range(levels) for c in range(2)], axis=1)
        back = inner_rows(rows, down_w[...])
        gate_grad[where, :] = lowered(back * u * slope)
        up_grad[where, :] = lowered(back * active)
        two.free(k)
        for column in range(0, width, tile):
            columns = slice(column, column + tile)
            value = inner_rows(gate_grad[where, :], gate_w[columns, :])
            value += inner_rows(up_grad[where, :], up_w[columns, :])
            two.part[lax.rem(k, 2), :, :, :, columns] = lowered(value).reshape(levels, 2, piece, tile)
        two.start(k)

    def branch_norm(k):
        two.finish(k)

        def block(number, carry):
            sub = span(number, 16)
            where = pl.ds(pl.multiple_of(k * piece + number * 16, 16), 16)
            unit, scale = layer_norm(resid[where, :], EPSILON)
            grad = total[sub, :]
            outer = grad * unit
            gain_acc[...] += outer[:8] + outer[8:]
            mine = pl.ds(pl.multiple_of(place * piece + number * 16, 16), 16)
            upstream = jnp.concatenate(
                [dy[k, q, c, mine, :] for q in range(levels) for c in range(2)], axis=1
            )
            value = wide(upstream) + norm_back(grad * gain[...], unit, scale)
            branch[k, level, core, sub, :] = lowered(value)
            return carry

        lax.fori_loop(0, piece // 16, block, 0)
        branch_gather.start(k)

    def last(k):
        branch_gather.ready(k)
        rows = branch[k].reshape(chunk, width)
        where = span(k, chunk)
        slot = lax.rem(k, 2)
        grad = inner_rows(rows, out_w[...])
        retained_two.load(k).wait()
        swish_two.load(k).wait()
        normed, scale = layer_norm(retained_slots[slot], GROUP_EPS)
        value = swish_slots[slot]
        gated = jax.nn.sigmoid(value)
        gate_grad[where, :] = lowered(grad * normed * gated * (1.0 + value * (1.0 - gated)))
        delta[...] = lowered(norm_back(grad * value * gated, normed, scale))

        @pl.when(k + 2 < count)
        def _():
            retained_two.load(k + 2).start()
            swish_two.load(k + 2).start()

        query_acc[...] = jnp.zeros(query_acc.shape, jnp.float32)

        def block(j, carry):
            there = span(j, chunk)
            decay = decay_tile(k, j, chunk, bounds, rate)
            weight = lowered(inner_rows(query[where, :], keys[there, :]) * decay)
            score = lowered(inner_rows(delta[...], values[there, :]) * decay)
            query_acc[...] += matmul(score, keys[there, :])
            key_acc[there, :] += inner_cols(score, query[where, :])
            value_acc[there, :] += inner_cols(weight, delta[...])
            return carry

        lax.fori_loop(0, k + 1, block, 0)
        query[where, :] = lowered(query_acc[...])

    def out_part(k):
        three.free(k, one)
        rows = hidden[span(k, chunk), :]
        mine = pl.ds(pl.multiple_of(k * piece, piece), piece)
        for rank in range(ranks):
            columns = slice(rank * part_width, (rank + 1) * part_width)
            value = matmul(rows, down_w[:, columns])
            for run in range(ranks):
                held = jnp.where(place == run, resid[mine, columns], 0.0)
                three.part[
                    lax.rem(k, 2), rank // 2, rank % 2, :, run * part_width : (run + 1) * part_width
                ] = lowered(value[run * piece : (run + 1) * piece, :] + held)
        pl.semaphore_wait(room.at[0, 0], 1)
        three.start(k)

    def out_finish(k):
        three.finish(k)
        for run in range(ranks):
            where = pl.ds(pl.multiple_of(k * chunk + run * piece, piece), piece)
            mixed[where, :] = lowered(total[:, run * part_width : (run + 1) * part_width])

    def runs_of(ref, columns):
        return jnp.concatenate(
            [ref[j, q, c, :, columns] for j in range(count) for q in range(levels) for c in range(2)], axis=0
        )

    def weigh(which):
        def part(k):
            columns = span(k, chunk)
            if which == 0:
                down = jnp.zeros((hidden.shape[1], part_width), jnp.float32)
                for j in range(count):
                    down += inner_cols(hidden[j * chunk : (j + 1) * chunk, :], dy[j, k // 2, lax.rem(k, 2)])
                there = pl.ds(pl.multiple_of(k * part_width, part_width), part_width)
                down_grad[:, there] = lowered(down)
            else:
                target, source = ((gate_w, gate_grad), (up_w, up_grad))[which - 1]
                target[columns, :] = lowered(inner_cols(runs_of(normed_mid, columns), source[...]))

        in_order(width // chunk, part)
        swap.start(which)

    def weigh_late(which):
        def part(k):
            columns = span(k, chunk)
            if which == 0:
                gate_w[columns, :] = lowered(inner_cols(runs_of(normed_mid, columns), gate_grad[...]))
            elif which == 1:
                out_w[:, columns] = lowered(inner_cols(up_grad[...], runs_of(branch, columns)))
            elif which == 2:
                up_w[columns, :] = lowered(inner_cols(runs_of(normed_mid, columns), values[...]))
            else:
                rows = runs_of(normed_mid, columns)
                down_grad[:qk_dim, columns] = lowered(inner_cols(query[...], rows))
                down_grad[qk_dim:, columns] = lowered(inner_cols(keys[...], rows))

        in_order(width // chunk, part)
        late.start(*((which,) if which < 3 else (3, 4)))

    def units(k):
        slot = lax.rem(k, 2)
        return [
            pltpu.make_async_copy(
                unit_src.at[span(k, chunk)], swish_slots.at[slot, :, pl.ds(0, part_width)], unit_sems.at[0, k]
            ),
            pltpu.make_async_copy(
                scale_src.at[span(k, chunk)], retained_slots.at[slot, :, pl.ds(0, 128)], unit_sems.at[1, k]
            ),
        ]

    def peer_of(j):
        peer = lax.rem(place + j, ranks)
        return (group, peer // 2, lax.rem(peer, 2))

    def sender(j):
        return lax.rem(place + ranks - j, ranks)

    def sums_copy(k, j, owner):
        return pltpu.make_async_remote_copy(
            src_ref=sums.at[owner, k],
            dst_ref=sums.at[owner, k],
            send_sem=sums_sent.at[j - 1, k],
            recv_sem=sums_got.at[j - 1, k],
            device_id=peer_of(j),
            device_id_type=MESH,
        )

    def pack_copy(j, owner):
        return pltpu.make_async_remote_copy(
            src_ref=packed.at[owner],
            dst_ref=packed.at[owner],
            send_sem=gain_sent.at[j - 1],
            recv_sem=gain_got.at[j - 1],
            device_id=peer_of(j),
            device_id_type=MESH,
        )

    def make_room(scatter, turn_of, k):
        scatter.sent(k)
        where = room.at[turn_of]
        pl.semaphore_signal(where.at[0], inc=1, device_id=(group, level, 1 - core), device_id_type=MESH)

        @pl.when(level > 0)
        def _():
            pl.semaphore_signal(where.at[1], inc=1, device_id=(group, level - 1, core), device_id_type=MESH)

        @pl.when(level < levels - 1)
        def _():
            pl.semaphore_signal(where.at[2], inc=1, device_id=(group, level + 1, core), device_id_type=MESH)

    def in_part(k):
        four.free(k, two)
        where = span(k, chunk)
        slot = lax.rem(k, 2)
        rows = [query[where, :], keys[where, :]]
        for source in (values, gate_grad):
            rows += [source[where, n : n + part_width] for n in range(0, v_dim, part_width)]
        first_sum = jnp.zeros((chunk, part_width), jnp.float32)
        second_sum = jnp.zeros((chunk, part_width), jnp.float32)
        for rank in range(ranks):
            columns = slice(rank * part_width, (rank + 1) * part_width)
            value = inner_rows(rows[0], dy[0, rank // 2, rank % 2])
            for n in range(1, len(rows)):
                value += inner_rows(rows[n], dy[n, rank // 2, rank % 2])
            for run in range(ranks):
                four.part[
                    slot, rank // 2, rank % 2, :, run * part_width : (run + 1) * part_width
                ] = lowered(value[run * piece : (run + 1) * piece, :])
            first_sum += value * gain_first[:, columns]
            second_sum += value * wide(normed_mid[k, :, :, :, columns].reshape(chunk, part_width))
        pl.semaphore_wait(room.at[1, 0], 1)
        four.start(k)
        ones = jnp.ones((8, part_width), jnp.float32)
        flat = [
            lax.dot_general(
                ones,
                item,
                (((1,), (1,)), ((), ())),
                precision=lax.Precision.HIGHEST,
                preferred_element_type=jnp.float32,
            )
            for item in (first_sum, second_sum)
        ]
        line = lax.broadcasted_iota(jnp.int32, (8, chunk), 0)
        sums[place, k] = jnp.where(line == 0, flat[0], flat[1])
        for j in range(1, ranks):
            sums_copy(k, j, place).start()

    def in_room(turn_of, wave):
        @pl.when(within(wave - level, count) & (level < levels - 1))
        def _():
            pl.semaphore_wait(room.at[turn_of, 1], 1)

        @pl.when(within(wave - (levels - 1 - level), count) & (level > 0))
        def _():
            pl.semaphore_wait(room.at[turn_of, 2], 1)

    def in_finish(k):
        four.finish(k)
        for j in range(1, ranks):
            sums_copy(k, j, sender(j)).wait_recv()
        line = lax.broadcasted_iota(jnp.int32, (8, 128), 0)
        lane = lax.broadcasted_iota(jnp.int32, (8, 128), 1)
        means = lax.dot_general(
            jnp.sum(sums[:, k], 0),
            jnp.where(line == lane, 1.0 / width, 0.0),
            (((0,), (0,)), ((), ())),
            precision=lax.Precision.HIGHEST,
            preferred_element_type=jnp.float32,
        )
        slot = lax.rem(k, 2)
        for copy in units(k):
            copy.wait()
        mine = pl.ds(pl.multiple_of(place * part_width, part_width), part_width)
        value = jnp.concatenate(
            [total[:, run * part_width : (run + 1) * part_width] for run in range(ranks)], axis=0
        )
        normed = swish_slots[slot, :, :part_width]
        outer = value * normed
        line_one[...] += jnp.sum(outer.reshape(chunk // 8, 8, part_width), 0)
        back = value * gain_first[:, mine] - means[:, :1] - normed * means[:, 1:2]
        upstream = wide(branch[k, :, :, :, mine].reshape(chunk, part_width))
        hidden[span(k, chunk), :part_width] = lowered(upstream + retained_slots[slot, :, :1] * back)

        @pl.when(k + 2 < count)
        def _():
            for copy in units(k + 2):
                copy.start()

    lead = 3
    mid_lag = lead + levels
    turn_lag = mid_lag + levels - 1
    branch_lag = turn_lag + levels
    last_lag = branch_lag + levels - 1
    turned = turn_lag + count
    close_lag = last_lag + count
    out_lag = last_lag - 2

    def at_wave(number, lag, step):
        @pl.when(within(number - lag, count))
        def _():
            step(number - lag)

    def wave(number):
        at_wave(number, lead, first)
        for gather, lag, sent in (
            (branch_gather, branch_lag, functools.partial(make_room, two, 0)),
            (mid_gather, mid_lag, one.sent),
        ):
            at_wave(number, lag + 1, sent)
            for hop in range(levels - 1, 0, -1):
                at_wave(number, lag + hop, functools.partial(hop_on, gather, hop))
        at_wave(number, branch_lag, branch_norm)
        at_wave(number, mid_lag, mid_norm)
        at_wave(number, -1, next_dy)
        for hop in range(levels - 1, 0, -1):
            at_wave(number, hop, functools.partial(hop_on, dy_gather, hop))
        for scatter, lag in ((two, turn_lag), (one, lead)):
            at_wave(number, lag + 1, scatter.join)
            scatter.steps(number - lag - 1)
        for step, relayed, started in ((1, (0,), (1, 2)), (4, (1,), (3,)), (6, (2,), ()), (8, (3,), ())):

            @pl.when(number == step)
            def _():
                spread.relay(*relayed)
                spread.start(*started)

        @pl.when(number == turn_lag)
        def _():
            spread.wait(1, 2, 3)

        at_wave(number, turn_lag, turn)

        @pl.when(number == turn_lag + 1)
        def _():
            retained_one.store(count - 2).wait()
            retained_one.store(count - 1).wait()
            for k in range(2):
                retained_two.load(k).start()
                swish_two.load(k).start()

        @pl.when(number == turned)
        def _():
            spread.drain(*range(4))

        for step, which in ((0, 1), (1, 2), (2, 0)):

            @pl.when(number == turned + step)
            def _():
                weigh(which)

        for step, which in ((2, 1), (4, 2), (6, 0)):

            @pl.when(number == turned + step)
            def _():
                swap.relay(which)

        @pl.when(number == turned + 2)
        def _():
            mid_gather.drain()
            mixed_in_ring.store(count - 2).wait()
            mixed_in_ring.store(count - 1).wait()
            late_loads.start(0, 1)

        @pl.when(number == branch_lag + count)
        def _():
            dy_gather.drain()
            late_loads.start(*range(2, 8))

        at_wave(number, last_lag, last)
        at_wave(number, out_lag, out_part)
        at_wave(number, out_lag + 1, three.join)
        in_room(0, number - out_lag - 1)
        three.steps(number - out_lag - 1)
        at_wave(number, out_lag + levels, out_finish)
        for k in range(count):

            @pl.when(number == out_lag + levels + k)
            def _():
                deal.start(k)

            @pl.when(number == out_lag + levels + k + 2)
            def _():
                deal.relay(k)

        at_wave(number, out_lag + levels + 1, functools.partial(make_room, three, 1))

        @pl.when(number == close_lag)
        def _():
            keys[...] = lowered(key_acc[...])
            values[...] = lowered(value_acc[...])
            for k in range(2):
                for copy in units(k):
                    copy.start()
            late_loads.wait(*range(8))

        for step, before, which in ((0, 1, 0), (1, 0, 1), (2, 2, 2), (3, None, 3)):

            @pl.when(number == close_lag + step)
            def _():
                if before is not None:
                    swap.wait(before)
                weigh_late(which)

        at_wave(number, close_lag, in_part)
        at_wave(number, close_lag + 1, four.join)
        in_room(1, number - close_lag - 1)
        four.steps(number - close_lag - 1)
        at_wave(number, close_lag + levels, in_finish)
        for step, which in ((3, (0,)), (4, (1,)), (5, (2,)), (7, (3, 4))):

            @pl.when(number == close_lag + step)
            def _():
                late.relay(*which)

        for k in range(count):

            @pl.when(number == close_lag + levels + k)
            def _():
                give.start(k)

            @pl.when(number == close_lag + levels + k + 2)
            def _():
                give.relay(k)

    def hop_on(gather, hop, k):
        gather.hop(k, hop)

    def next_dy(k):
        @pl.when(k > 0)
        def _():
            dy_gather.start(k)

    in_order(close_lag + levels + count, wave)
    give.relay(count - 2, count - 1)
    packed[place] = jnp.concatenate(
        [jnp.sum(gain_acc[...], 0, keepdims=True), jnp.sum(line_one[...], 0, keepdims=True)], axis=1
    )
    for j in range(1, ranks):
        pack_copy(j, place).start()
    for j in range(1, ranks):
        pack_copy(j, sender(j)).wait_recv()
    line = lax.broadcasted_iota(jnp.int32, (8, width), 0)
    two_sum = sum(packed[rank, :, :width] for rank in range(ranks))
    one_sum = jnp.concatenate([packed[rank, :, width:] for rank in range(ranks)], axis=1)
    gains[...] = jnp.where(line == 0, one_sum, two_sum)
    small.start(0)
    small.wait(0)
    gains_out[...] = jnp.sum(gains_in[...], 0)
    late.wait(*range(5))
    give.wait(*range(count))
    give.drain(*range(count))
    deal.wait(*range(count))
    deal.drain(*range(count))
    four.drain()
    three.across(count - 2).wait_send()
    three.across(count - 1).wait_send()
    branch_gather.drain()
    for j in range(1, ranks):
        pack_copy(j, place).wait_send()

    def drain(k):
        for j in range(1, ranks):
            sums_copy(k, j, place).wait_send()

    in_order(count, drain)


def column_all(at, sizes):
    group, level, core = at
    return column_peers(at, sizes) + [
        (group, lax.rem(level + k, sizes[1]), 1 - core) for k in range(1, sizes[1])
    ]


def struct(shape, kind=jnp.bfloat16):
    return jax.ShapeDtypeStruct(shape, kind)


VMEM = pltpu.VMEM
DMA = pltpu.SemaphoreType.DMA


def kernel_call(body, number, ins, outs, scratch):
    places = {
        "vmem": pl.BlockSpec(memory_space=pltpu.VMEM),
        "smem": pl.BlockSpec(memory_space=pltpu.SMEM),
        "any": pl.BlockSpec(memory_space=pl.ANY),
    }
    return pl.pallas_call(
        body,
        out_shape=[shape for _, shape in outs],
        in_specs=[places[inside] for inside, _ in ins],
        out_specs=[places[inside] for inside, _ in outs],
        scratch_shapes=scratch,
        compiler_params=pltpu.CompilerParams(
            collective_id=number, has_side_effects=True, vmem_limit_bytes=63 * 2**20
        ),
    )(*[array for _, array in ins])


def spread_shape(shard, axis, sizes):
    shape = list(shard.shape)
    shape[axis] *= sizes[0]
    return struct(tuple(shape), shard.dtype)


def swap_shape(whole, axis, sizes):
    shape = list(whole.shape)
    shape[axis] //= sizes[0]
    return struct((3 if sizes[0] == 4 else sizes[0],) + tuple(shape), whole.dtype)


def anywhere(items):
    return [("any", item) for item in items]


def held_like(arrays):
    return [VMEM(a.shape, a.dtype) for a in arrays]


def pick(rows, whole):
    return whole.at[rows].get(mode="promise_in_bounds")


def shards(
    tokens,
    cotangent,
    lengths,
    dealing,
    w_query,
    w_key,
    w_value,
    w_swish,
    w_out,
    w_gate,
    w_up,
    w_down,
    gain_attn,
    gain_mlp,
):
    group = lax.axis_index("dp")
    place = lax.axis_index(("heads", "tensor"))
    rows_dev = tokens.shape[0]
    slice_width = tokens.shape[1]
    seq_count = lengths.shape[0]
    ident = jnp.arange(seq_count, dtype=jnp.int32)
    starts = jnp.cumsum(lengths) - lengths
    picked = lax.dynamic_slice_in_dim(dealing, group * SEQ_DEV, SEQ_DEV)
    match = picked[:, None] == ident[None, :]
    dealt_len = jnp.sum(jnp.where(match, lengths[None, :], 0), 1)
    home_start = jnp.sum(jnp.where(match, starts[None, :], 0), 1)
    dealt_start = jnp.cumsum(dealt_len) - dealt_len
    rows = jnp.arange(rows_dev, dtype=jnp.int32)
    seq_ids = jnp.sum((rows[:, None] >= dealt_start[None, :]).astype(jnp.int32), 1) - 1
    sizes = (lax.axis_size("dp"), lax.axis_size("heads"))
    ranks = sizes[1] * lax.axis_size("tensor")
    chunk = ranks * PIECE
    count = rows_dev // chunk
    width = slice_width * ranks
    own = rows_dev // ranks
    qk_dim, v_dim, ff_dim = w_query.shape[1], w_value.shape[1], w_gate.shape[1]
    f32 = jnp.float32
    masters = (w_query, w_key, w_value, w_swish, w_out, w_gate, w_up, w_down)
    axes = (0, 0, 0, 0, 1, 0, 0, 1)
    gain_rows = jnp.pad(jnp.stack([gain_attn, gain_mlp]), ((0, 6), (0, 0)))
    shifts = home_start - dealt_start
    firsts = jnp.arange(2 * count, dtype=jnp.int32) * (chunk // 2)
    begins = jnp.clip(firsts[:, None] + shifts[None, :], 0, sizes[0] * rows_dev - chunk) // 16
    bf16 = jnp.bfloat16
    rounded = [struct(w.shape) for w in masters]
    full_w = [spread_shape(w, a, sizes) for w, a in zip(rounded, axes)]
    by_runs = struct((rows_dev // 16, 16, slice_width))
    every = spread_shape(by_runs, 0, sizes)
    gains_all = struct((sizes[0] * 8, gain_rows.shape[1]), f32)
    (
        normed_in,
        query,
        keys,
        values,
        swish_in,
        dy_part,
        query_w,
        key_w,
        value_w,
        swish_w,
        *low,
        wide_one,
        wide_two,
        x_rows,
        unit_share,
        scale_one,
    ) = kernel_call(
        functools.partial(front_kernel, sizes),
        0,
        [("smem", dealt_start), ("smem", shifts), ("smem", begins.reshape(-1))]
        + anywhere((tokens.reshape(by_runs.shape), cotangent.reshape(by_runs.shape), gain_rows) + masters),
        anywhere(
            [
                struct((rows_dev, width)),
                struct((rows_dev, qk_dim)),
                struct((rows_dev, qk_dim)),
                struct((rows_dev, v_dim)),
                struct((rows_dev, v_dim), f32),
                struct((count, chunk, slice_width)),
            ]
            + full_w[:4]
            + rounded[4:]
        )
        + [
            ("vmem", struct((1, width), f32)),
            ("vmem", struct((1, width), f32)),
            ("vmem", struct((own, width))),
            ("vmem", struct((rows_dev, slice_width), f32)),
            ("vmem", struct((rows_dev, 128), f32)),
        ],
        Gather.scratch(count, sizes, (chunk, slice_width))
        + Spread.scratch(12, sizes)
        + Spread.scratch(1, sizes)
        + held_like(masters)
        + held_like(rounded)
        + held_like(full_w[:4])
        + held_like((by_runs, by_runs, gain_rows, every, every, gains_all))
        + [
            VMEM((count, chunk, slice_width), bf16),
            VMEM((rows_dev, width), bf16),
            VMEM((rows_dev, qk_dim), bf16),
            VMEM((rows_dev, qk_dim), bf16),
            VMEM((rows_dev, v_dim), bf16),
            VMEM((rows_dev, v_dim), f32),
            DMA((11,)),
            DMA((4,)),
            DMA((9,)),
            DMA((count,)),
        ],
    )
    rate = jnp.log1p(-jnp.exp2(-5.0 - place.astype(f32))).reshape(1)
    by_rows = (PIECE, width)
    pieces = (count, sizes[1], 2) + by_rows
    blocks = (sizes[1], 2, slice_width)
    late_w = [struct(shape) for shape in ((width, v_dim), (v_dim, width), (width, v_dim), (qk_dim, width))]
    late_w.append(late_w[3])
    late_axes = (0, 1, 0, 1, 1)
    core_outs = kernel_call(
        functools.partial(core_kernel, sizes),
        1,
        [("smem", dealt_start), ("smem", rate), ("vmem", wide_two), ("vmem", wide_one)]
        + anywhere((query, keys, values, x_rows, dy_part, swish_in))
        + anywhere((normed_in.reshape(pieces), unit_share, scale_one))
        + anywhere([w.reshape(blocks + w.shape[1:]) for w in (query_w, key_w, value_w, swish_w)])
        + anywhere(low),
        anywhere([struct((rows_dev, v_dim)), struct((rows_dev, v_dim), f32)])
        + [("vmem", struct((8, gain_attn.shape[0]), f32))]
        + anywhere(
            [
                struct((sizes[0] * rows_dev, slice_width)),
                struct((sizes[0] * rows_dev, slice_width)),
                swap_shape(full_w[7], 1, sizes),
                swap_shape(full_w[5], 0, sizes),
                swap_shape(full_w[6], 0, sizes),
            ]
            + [swap_shape(w, a, sizes) for w, a in zip(late_w, late_axes)]
        ),
        held_like((query, keys, values, x_rows))
        + held_like(full_w[4:])
        + Scatter.rooms(count, sizes, by_rows)
        + Scatter.rooms(count, sizes, by_rows)[:1]
        + Scatter.sems(count, sizes) * 4
        + Gather.scratch(count, sizes, by_rows)
        + Gather.scratch(count, sizes, (chunk, slice_width))
        + Gather.scratch(count, sizes, by_rows)
        + Spread.scratch(4, sizes)
        + Spread.scratch(count, sizes)
        + Swap.scratch(3, sizes)
        + Swap.scratch(5, sizes)
        + Swap.scratch(1, sizes)
        + Spread.scratch(count, sizes)
        + [
            VMEM((rows_dev, ff_dim), bf16),
            VMEM((rows_dev, ff_dim), bf16),
            VMEM((rows_dev, ff_dim), bf16),
            VMEM((own, width), f32),
            VMEM((2, chunk, v_dim), f32),
            VMEM((2, chunk, v_dim), f32),
            VMEM((2, chunk, v_dim), bf16),
            VMEM((rows_dev, qk_dim), f32),
            VMEM((rows_dev, v_dim), f32),
            VMEM((chunk, qk_dim), f32),
            VMEM((chunk, v_dim), bf16),
            VMEM((ff_dim, width), bf16),
            VMEM((rows_dev, slice_width), bf16),
            VMEM((8, width), f32),
            VMEM((ranks, count, 8, chunk), f32),
            VMEM((8, slice_width), f32),
            VMEM((ranks, 1, width + slice_width), f32),
            VMEM((8, width), f32),
            VMEM((sizes[0], 8, gain_attn.shape[0]), f32),
            DMA((5,)),
            DMA((5, count)),
            DMA((8,)),
            DMA((2, count)),
            pltpu.SemaphoreType.REGULAR((2, 3)),
            DMA((ranks - 1, count)),
            DMA((ranks - 1, count)),
            DMA((ranks - 1,)),
            DMA((ranks - 1,)),
        ]
        + half_blocks([(full_w[7], 1), (full_w[5], 0), (full_w[6], 0)], sizes)
        + half_blocks(list(zip(late_w, late_axes))[3:], sizes),
    )
    _, _, gains, mixed_all, grad_all, *parts = core_outs
    down, gate, up, swish, out, value, query, key = (jnp.sum(wide(g), 0) for g in parts)
    grads = (query.T, key.T, value, swish, out, gate, up, down)
    slot_match = dealing[:, None] == ident[None, :]
    slot_len = jnp.sum(jnp.where(slot_match, lengths[None, :], 0), 1)
    slot_home = jnp.sum(jnp.where(slot_match, starts[None, :], 0), 1)
    per_group = slot_len.reshape(-1, SEQ_DEV)
    slot_start = (jnp.cumsum(per_group, 1) - per_group).reshape(-1)
    slot_base = ident // SEQ_DEV * rows_dev + slot_start - slot_home
    owner_base = jnp.sum(jnp.where(dealing[None, :] == ident[:, None], slot_base[None, :], 0), 1)
    global_rows = group * rows_dev + rows
    seq_of = jnp.sum((global_rows[:, None] >= starts[None, :]).astype(jnp.int32), 1) - 1
    targets = (
        jnp.sum(jnp.where(seq_of[:, None] == ident[None, :], owner_base[None, :], 0), 1)
        + global_rows
    )
    mixed_rows, grad_rows = pick(targets, mixed_all), pick(targets, grad_all)
    return (
        mixed_rows,
        grad_rows,
        grads[0],
        grads[1],
        grads[2],
        grads[3],
        grads[4],
        grads[5],
        grads[6],
        grads[7],
        gains[0],
        gains[1],
    )


def solution(mesh):
    in_specs = (
        P("dp", ("heads", "tensor")),
        P("dp", ("heads", "tensor")),
        P(),
        P(),
        P("dp", ("heads", "tensor")),
        P("dp", ("heads", "tensor")),
        P("dp", ("heads", "tensor")),
        P("dp", ("heads", "tensor")),
        P(("heads", "tensor"), "dp"),
        P("dp", ("heads", "tensor")),
        P("dp", ("heads", "tensor")),
        P(("heads", "tensor"), "dp"),
        P("dp"),
        P("dp"),
    )
    out_specs = (
        P("dp", ("heads", "tensor")),
        P("dp", ("heads", "tensor")),
        P("dp", ("heads", "tensor")),
        P("dp", ("heads", "tensor")),
        P("dp", ("heads", "tensor")),
        P("dp", ("heads", "tensor")),
        P(("heads", "tensor"), "dp"),
        P("dp", ("heads", "tensor")),
        P("dp", ("heads", "tensor")),
        P(("heads", "tensor"), "dp"),
        P("dp"),
        P("dp"),
    )
    return jax.shard_map(shards, mesh=mesh, in_specs=in_specs, out_specs=out_specs, check_vma=False)
```

```python
import functools

import jax
import jax.numpy as jnp
from jax import lax
from jax.experimental import pallas as pl
from jax.experimental.pallas import tpu as pltpu
from jax.sharding import PartitionSpec as P

QK_DIM = 256
SEQ_DEV = 3
PIECE = 32
AXES = ("dp", "heads", "tensor")
MESH = pl.DeviceIdType.MESH


EPSILON = 1e-05
GROUP_EPS = 1.0


def layer_norm(values, epsilon):
    center = values - jnp.mean(values, -1, keepdims=True)
    scale = lax.rsqrt(jnp.mean(center * center, -1, keepdims=True) + epsilon)
    return (center * scale, scale)


def norm_back(grad, normed, scale):
    return scale * (
        grad
        - jnp.mean(grad, -1, keepdims=True)
        - normed * jnp.mean(grad * normed, -1, keepdims=True)
    )


def product(left, right):
    return jnp.dot(left, right, preferred_element_type=jnp.float32)


def inner_rows(left, right):
    return lax.dot_general(
        left, right, (((1,), (1,)), ((), ())), preferred_element_type=jnp.float32
    )


def inner_cols(left, right):
    return lax.dot_general(
        left, right, (((0,), (0,)), ((), ())), preferred_element_type=jnp.float32
    )


def lowered(value):
    return value.astype(jnp.bfloat16)


def around(axes):
    return tuple(lax.axis_index(name) for name in axes)


def wide(value):
    return value.astype(jnp.float32)


def within(number, count):
    return (number >= 0) & (number < count)


def greet(others):
    barrier = pltpu.get_barrier_semaphore()
    for other in others:
        pl.semaphore_signal(barrier, inc=1, device_id=other, device_id_type=MESH)
    pl.semaphore_wait(barrier, len(others))


def plane_peers(at, sizes):
    group, level, core = at
    return [(lax.rem(group + k, sizes[0]), level, core) for k in range(1, sizes[0])]


def column_peers(at, sizes):
    group, level, core = at
    return [(group, lax.rem(level + k, sizes[1]), core) for k in range(1, sizes[1])] + [
        (group, level, 1 - core)
    ]


def beside(group):
    return group + 1 - 2 * lax.rem(group, 2), lax.rem(group + 2, 4), 3 - group


class Spread:
    def __init__(self, at, sizes, items, sems, relay=True):
        self.at, self.count, self.items = at, sizes[0], items
        self.local, self.sent, self.got = sems
        self.plane = relay and sizes[0] == 4

    @staticmethod
    def scratch(items, sizes):
        ways = max(4, sizes[0] - 1)
        return [
            pltpu.SemaphoreType.DMA((items,)),
            pltpu.SemaphoreType.DMA((items, ways)),
            pltpu.SemaphoreType.DMA((items, ways)),
        ]

    def place(self, number, owner, half=None):
        source, target, axis, *where = self.items[number]
        rows = source.shape[0]
        size = source.shape[axis]
        step, offset = where or (size, 0)
        start = owner * step + offset
        if half is None:
            begin, height = 0, rows
        else:
            begin, height = half * (rows // 2), rows // 2
        if axis == 0:
            return target.at[pl.ds(pl.multiple_of(start + begin, height), height)]
        return target.at[pl.ds(begin, height), pl.ds(pl.multiple_of(start, size), size)]

    def own(self, number):
        return pltpu.make_async_copy(
            self.items[number][0], self.place(number, self.at[0]), self.local.at[number]
        )

    def copy(self, number, source, place, way, peer):
        return pltpu.make_async_remote_copy(
            src_ref=source,
            dst_ref=place,
            send_sem=self.sent.at[number, way],
            recv_sem=self.got.at[number, way],
            device_id=(peer,) + self.at[1:],
            device_id_type=MESH,
        )

    def away(self, number, k):
        peer = lax.rem(self.at[0] + k, self.count)
        return self.copy(number, self.items[number][0], self.place(number, self.at[0]), k - 1, peer)

    def landed(self, number, k):
        owner = lax.rem(self.at[0] + self.count - k, self.count)
        return self.copy(number, self.items[number][0], self.place(number, owner), k - 1, owner)

    def to(self, number, way):
        peer = beside(self.at[0])[way]
        return self.copy(number, self.items[number][0], self.place(number, self.at[0]), way, peer)

    def of(self, number, way):
        peer = beside(self.at[0])[way]
        return self.copy(number, self.items[number][0], self.place(number, peer), way, peer)

    def on(self, number, way):
        near = beside(self.at[0])
        ref = self.place(number, near[way], way)
        return self.copy(number, ref, ref, 2 + way, near[1 - way])

    def last(self, number, way):
        near = beside(self.at[0])
        ref = self.place(number, near[2], way)
        return self.copy(number, ref, ref, 2 + way, near[1 - way])

    def start(self, *numbers):
        for number in numbers:
            if self.plane:
                self.to(number, 0).start()
                self.to(number, 1).start()
            else:
                for k in range(1, self.count):
                    self.away(number, k).start()
            self.own(number).start()

    def relay(self, *numbers):
        if self.plane:
            for number in numbers:
                for way in range(2):
                    self.of(number, way).wait_recv()
                    self.on(number, way).start()

    def wait(self, *numbers):
        for number in numbers:
            self.own(number).wait()
            if self.plane:
                self.last(number, 0).wait_recv()
                self.last(number, 1).wait_recv()
            else:
                for k in range(1, self.count):
                    self.landed(number, k).wait_recv()

    def drain(self, *numbers):
        for number in numbers:
            if self.plane:
                for way in range(2):
                    self.to(number, way).wait_send()
                    self.on(number, way).wait_send()
            else:
                for k in range(1, self.count):
                    self.away(number, k).wait_send()


class Gather:
    def __init__(self, at, sizes, count, full, sems):
        self.at, self.levels, self.count, self.full = at, sizes[1], count, full
        self.sent_up, self.got_up, self.sent_down, self.got_down, self.sent_core, self.got_core = sems

    @staticmethod
    def scratch(count, sizes, piece):
        levels = sizes[1]
        dma = pltpu.SemaphoreType.DMA
        return [pltpu.VMEM((count, levels, 2) + piece, jnp.bfloat16)] + [
            dma((levels - 1, count)) for _ in range(4)
        ] + [dma((2 * levels - 1, count)) for _ in range(2)]

    def copy(self, ref, sent, got, target):
        return pltpu.make_async_remote_copy(
            src_ref=ref, dst_ref=ref, send_sem=sent, recv_sem=got, device_id=target, device_id_type=MESH
        )

    def up(self, k, hop, origin, sem):
        group, level, core = self.at
        target = (group, lax.rem(level + 1, self.levels), core)
        return self.copy(self.full.at[k, origin, core], self.sent_up.at[sem, k], self.got_up.at[sem, k], target)

    def down(self, k, hop, origin, sem):
        group, level, core = self.at
        target = (group, lax.rem(level + self.levels - 1, self.levels), core)
        return self.copy(
            self.full.at[k, origin, core], self.sent_down.at[sem, k], self.got_down.at[sem, k], target
        )

    def across(self, k, origin, side, sem):
        group, level, core = self.at
        return self.copy(
            self.full.at[k, origin, side], self.sent_core.at[sem, k], self.got_core.at[sem, k], (group, level, 1 - core)
        )

    def start(self, k):
        group, level, core = self.at

        @pl.when(level < self.levels - 1)
        def _():
            self.up(k, 0, level, 0).start()

        @pl.when(level > 0)
        def _():
            self.down(k, 0, level, 0).start()

        self.across(k, level, core, 0).start()

    def hop(self, k, hop):
        group, level, core = self.at
        last = self.levels - 1

        @pl.when(level >= hop)
        def _():
            origin = level - hop
            self.up(k, hop, origin, hop - 1).wait_recv()
            if hop < last:

                @pl.when(level < last)
                def _():
                    self.up(k, hop, origin, hop).start()

            self.across(k, origin, core, hop).start()

        @pl.when(level + hop <= last)
        def _():
            origin = level + hop
            self.down(k, hop, origin, hop - 1).wait_recv()
            if hop < last:

                @pl.when(level > 0)
                def _():
                    self.down(k, hop, origin, hop).start()

            self.across(k, origin, core, last + hop).start()

    def ready(self, k):
        group, level, core = self.at
        last = self.levels - 1
        self.across(k, level, 1 - core, 0).wait_recv()
        for hop in range(1, self.levels):

            @pl.when(level >= hop)
            def _():
                self.across(k, level - hop, 1 - core, hop).wait_recv()

            @pl.when(level + hop <= last)
            def _():
                self.across(k, level + hop, 1 - core, last + hop).wait_recv()

    def drain(self):
        group, level, core = self.at
        last = self.levels - 1

        def one(k, _):
            self.across(k, level, core, 0).wait_send()
            for hop in range(self.levels):
                if hop < last:

                    @pl.when((level >= hop) & (level < last))
                    def _():
                        self.up(k, hop, level - hop, hop).wait_send()

                    @pl.when((level + hop <= last) & (level > 0))
                    def _():
                        self.down(k, hop, level + hop, hop).wait_send()

                if hop > 0:

                    @pl.when(level >= hop)
                    def _():
                        self.across(k, level - hop, core, hop).wait_send()

                    @pl.when(level + hop <= last)
                    def _():
                        self.across(k, level + hop, core, last + hop).wait_send()

            return 0

        lax.fori_loop(0, self.count, one, 0)


class Scatter:
    REFS = 4

    def __init__(self, at, sizes, count, refs):
        self.at, self.levels, self.count = at, sizes[1], count
        self.part, self.cross, self.inbox, self.total = refs[:4]
        self.sent_core, self.got_core, self.sent_up, self.got_up, self.sent_down, self.got_down = refs[4:]

    @staticmethod
    def rooms(count, sizes, piece):
        levels = sizes[1]
        return [
            pltpu.VMEM((2, levels, 2) + piece, jnp.bfloat16),
            pltpu.VMEM((count, levels) + piece, jnp.bfloat16),
            pltpu.VMEM((count, levels + 1) + piece, jnp.bfloat16),
            pltpu.VMEM(piece, jnp.float32),
        ]

    @staticmethod
    def sems(count, sizes):
        dma = pltpu.SemaphoreType.DMA
        return [dma((count,)) for _ in range(2)] + [dma((sizes[1], count)) for _ in range(4)]

    @staticmethod
    def scratch(count, sizes, piece):
        return Scatter.rooms(count, sizes, piece) + Scatter.sems(count, sizes)

    def across(self, k):
        group, level, core = self.at
        return pltpu.make_async_remote_copy(
            src_ref=self.part.at[lax.rem(k, 2), :, 1 - core],
            dst_ref=self.cross.at[k],
            send_sem=self.sent_core.at[k],
            recv_sem=self.got_core.at[k],
            device_id=(group, level, 1 - core),
            device_id_type=MESH,
        )

    def up(self, k, owner):
        group, level, core = self.at
        return pltpu.make_async_remote_copy(
            src_ref=self.cross.at[k, owner],
            dst_ref=self.inbox.at[k, owner + 1],
            send_sem=self.sent_up.at[owner, k],
            recv_sem=self.got_up.at[owner, k],
            device_id=(group, lax.rem(level + 1, self.levels), core),
            device_id_type=MESH,
        )

    def down(self, k, owner):
        group, level, core = self.at
        return pltpu.make_async_remote_copy(
            src_ref=self.cross.at[k, owner],
            dst_ref=self.inbox.at[k, owner],
            send_sem=self.sent_down.at[owner, k],
            recv_sem=self.got_down.at[owner, k],
            device_id=(group, lax.rem(level + self.levels - 1, self.levels), core),
            device_id_type=MESH,
        )

    def free(self, k, before=None):
        @pl.when(k >= 2)
        def _():
            self.across(k - 2).wait_send()

        if before is not None:

            @pl.when(k < 2)
            def _():
                before.across(self.count - 2 + k).wait_send()

    def start(self, k):
        self.across(k).start()

    def join(self, k):
        core = self.at[2]
        self.across(k).wait_recv()
        for owner in range(self.levels):
            self.cross[k, owner] = lowered(
                wide(self.part[lax.rem(k, 2), owner, core]) + wide(self.cross[k, owner])
            )

    def step_up(self, k):
        level = self.at[1]
        for owner in range(self.levels - 1, 0, -1):

            @pl.when(level < owner)
            def _():
                @pl.when(level > 0)
                def _():
                    self.up(k, owner).wait_recv()
                    self.cross[k, owner] = lowered(wide(self.cross[k, owner]) + wide(self.inbox[k, owner + 1]))

                self.up(k, owner).start()

    def step_down(self, k):
        level = self.at[1]
        for owner in range(self.levels - 1):

            @pl.when(level > owner)
            def _():
                @pl.when(level < self.levels - 1)
                def _():
                    self.down(k, owner).wait_recv()
                    self.cross[k, owner] = lowered(wide(self.cross[k, owner]) + wide(self.inbox[k, owner]))

                self.down(k, owner).start()

    def steps(self, wave):
        level = self.at[1]
        above = wave - level
        below = wave - (self.levels - 1 - level)

        @pl.when(within(above, self.count) & (level < self.levels // 2))
        def _():
            self.step_up(above)

        @pl.when(within(below, self.count))
        def _():
            self.step_down(below)

        @pl.when(within(above, self.count) & (level >= self.levels // 2))
        def _():
            self.step_up(above)

    def finish(self, k):
        level = self.at[1]
        self.total[...] = wide(self.cross[k, level])

        @pl.when(level > 0)
        def _():
            self.up(k, level).wait_recv()
            self.total[...] += wide(self.inbox[k, level + 1])

        @pl.when(level < self.levels - 1)
        def _():
            self.down(k, level).wait_recv()
            self.total[...] += wide(self.inbox[k, level])

    def sent(self, k):
        level = self.at[1]
        for owner in range(self.levels):

            @pl.when(level < owner)
            def _():
                self.up(k, owner).wait_send()

            @pl.when(level > owner)
            def _():
                self.down(k, owner).wait_send()

    def drain(self):
        self.across(self.count - 2).wait_send()
        self.across(self.count - 1).wait_send()
        in_order(self.count, self.sent)


def in_order(count, step):
    def body(number, carry):
        step(number)
        return carry

    lax.fori_loop(0, count, body, 0)


def span(number, size):
    return pl.ds(pl.multiple_of(number * size, size), size)


class Moves:
    def __init__(self, pairs, sems):
        self.pairs, self.sems = pairs, sems

    def copy(self, number):
        return pltpu.make_async_copy(*self.pairs[number], self.sems.at[number])

    def start(self, *numbers):
        for number in numbers:
            self.copy(number).start()

    def wait(self, *numbers):
        for number in numbers:
            self.copy(number).wait()


class Chunks:
    def __init__(self, pairs, size, sems):
        self.pairs, self.size, self.sems = pairs, size, sems

    def start(self, k):
        for number, (source, target) in enumerate(self.pairs):
            rows = span(k, self.size)
            pltpu.make_async_copy(source.at[rows], target.at[rows], self.sems.at[number, k]).start()

    def wait(self, count):
        def one(k, carry):
            for number, (source, target) in enumerate(self.pairs):
                rows = span(k, self.size)
                pltpu.make_async_copy(source.at[rows], target.at[rows], self.sems.at[number, k]).wait()
            return carry

        lax.fori_loop(0, count, one, 0)


def matmul(left, right):
    return jnp.dot(left, right, preferred_element_type=jnp.float32)


def decay_tile(near, far, size, bounds, rate):
    rows = near * size + lax.broadcasted_iota(jnp.int32, (size, 1), 0)
    columns = far * size + lax.broadcasted_iota(jnp.int32, (1, size), 1)
    row_seq, column_seq = jnp.zeros((size, 1), jnp.int32), jnp.zeros((1, size), jnp.int32)
    for number in range(1, SEQ_DEV):
        row_seq += (rows >= bounds[number]).astype(jnp.int32)
        column_seq += (columns >= bounds[number]).astype(jnp.int32)
    distance = rows - columns
    valid = (distance >= 0) & (row_seq == column_seq)
    return (
        jnp.where(valid, jnp.exp(jnp.maximum(distance, 0).astype(jnp.float32) * rate[0]), 0.0)
        * QK_DIM ** (-0.5)
    )


class Swap:
    def __init__(self, at, sizes, items, sems, halves=None):
        self.at, self.count, self.items = at, sizes[0], items
        self.local, self.sent, self.got = sems
        self.halves = halves
        self.plane = halves is not None and sizes[0] == 4

    @staticmethod
    def scratch(items, sizes):
        ways = max(6, sizes[0] - 1)
        return [
            pltpu.SemaphoreType.DMA((items,)),
            pltpu.SemaphoreType.DMA((items, ways)),
            pltpu.SemaphoreType.DMA((items, ways)),
        ]

    def block(self, number, owner, half=None):
        source, target, axis = self.items[number]
        rows = source.shape[0]
        size = source.shape[axis] // self.count
        height = size if axis == 0 else rows
        begin = 0
        if half is not None:
            height //= 2
            begin = half * height
        if axis == 0:
            return source.at[pl.ds(pl.multiple_of(owner * size + begin, height), height)]
        return source.at[pl.ds(begin, height), pl.ds(pl.multiple_of(owner * size, size), size)]

    def half(self, number, slot, half):
        target = self.items[number][1]
        height = target.shape[1] // 2
        return target.at[slot, pl.ds(half * height, height)]

    def copy(self, number, source, place, way, peer):
        return pltpu.make_async_remote_copy(
            src_ref=source,
            dst_ref=place,
            send_sem=self.sent.at[number, way],
            recv_sem=self.got.at[number, way],
            device_id=(peer,) + self.at[1:],
            device_id_type=MESH,
        )

    def own(self, number):
        return pltpu.make_async_copy(
            self.block(number, self.at[0]), self.items[number][1].at[0], self.local.at[number]
        )

    def away(self, number, k):
        peer = lax.rem(self.at[0] + k, self.count)
        return self.copy(number, self.block(number, peer), self.items[number][1].at[k], k - 1, peer)

    def across(self, number, way):
        near = beside(self.at[0])
        return self.copy(
            number, self.block(number, near[2], way), self.halves[number].at[way], way, near[way]
        )

    def direct(self, number, way):
        near = beside(self.at[0])
        return self.copy(
            number, self.block(number, near[way], way), self.half(number, 1 + way, way), 2 + way, near[way]
        )

    def added(self, number, way):
        peer = beside(self.at[0])[1 - way]
        return self.copy(
            number, self.block(number, peer, way), self.half(number, 2 - way, way), 4 + way, peer
        )

    def start(self, *numbers):
        for number in numbers:
            if self.plane:
                for way in range(2):
                    self.across(number, way).start()
                for way in range(2):
                    self.direct(number, way).start()
            else:
                for k in range(1, self.count):
                    self.away(number, k).start()
            self.own(number).start()

    def relay(self, *numbers):
        if self.plane:
            near = beside(self.at[0])
            for number in numbers:
                for way in range(2):
                    self.across(number, way).wait_recv()
                    part = self.block(number, near[1 - way], way)
                    part[...] = lowered(wide(part[...]) + wide(self.halves[number][way]))
                for way in range(2):
                    self.added(number, way).start()

    def wait(self, *numbers):
        for number in numbers:
            self.own(number).wait()
            if self.plane:
                for way in range(2):
                    self.across(number, way).wait_send()
                    self.direct(number, way).wait()
                    self.added(number, way).wait()
            else:
                for k in range(1, self.count):
                    self.away(number, k).wait()


def half_blocks(items, sizes):
    room = []
    for whole, axis in items:
        shape = list(whole.shape)
        shape[axis] //= sizes[0]
        room.append(pltpu.VMEM((2, shape[0] // 2, shape[1]), jnp.bfloat16))
    return room


def quarters(source, target):
    rows = source.shape[0]
    run = rows // 4
    return [(source.at[pl.ds(k * run, run)], target, 0, rows, k * run) for k in range(4)]


def pick_rows(whole, number, first, rows, bounds, shifts, begins):
    window = 2 * rows
    lane = lax.broadcasted_iota(jnp.int32, (rows, window), 1)
    slot = jnp.zeros((rows, 1), jnp.int32)
    own = first + lax.broadcasted_iota(jnp.int32, (rows, 1), 0)
    for item in range(1, SEQ_DEV):
        slot += (own >= bounds[item]).astype(jnp.int32)
    chosen, windows = [], []
    for item in range(SEQ_DEV):
        start = begins[number * SEQ_DEV + item]
        wanted = jnp.where(slot == item, own + shifts[item] - 16 * start, -1)
        chosen.append(jnp.where(lane == wanted, 1.0, 0.0).astype(jnp.bfloat16))
        windows += [whole[start + k] for k in range(window // 16)]
    return lowered(matmul(jnp.concatenate(chosen, axis=1), jnp.concatenate(windows, axis=0)))


def front_kernel(sizes, bounds, shifts, begins, tokens, cotangent, gain_rows, *refs):
    masters, refs = refs[:8], refs[8:]
    normed_out, query_out, key_out, value_out, swish_out, dy_out, *refs = refs
    weight_outs, rounded_outs, refs = refs[:4], refs[4:8], refs[8:]
    gain_one, gain_two, rows_out, unit_out, scale_out, *refs = refs
    full, *refs = refs
    gather_sems, refs = refs[:6], refs[6:]
    spread_sems, small_sems, refs = refs[:3], refs[3:6], refs[6:]
    held, rounded, weights, refs = refs[:8], refs[8:16], refs[16:20], refs[20:]
    tokens_held, dy_held, gains_held, tokens_all, dy_all, gains_all, dy_part, *refs = refs
    normed, query, keys, values, swish, load_sems, store_sems, out_sems, normed_sem = refs
    at = around(AXES)
    group, level, core = at
    place = 2 * level + core
    count, levels, _, chunk, width = full.shape
    ranks = 2 * levels
    piece = chunk // ranks
    loads = Moves(
        list(zip(masters, held)) + [(tokens, tokens_held), (gain_rows, gains_held), (cotangent, dy_held)], load_sems
    )
    loads.start(8, 9, 2, 3, 1, 0, 10, 4, 5, 6, 7)
    greet(plane_peers(at, sizes) + column_peers(at, sizes))
    loads.wait(8, 9)
    spread = Spread(
        at,
        sizes,
        quarters(tokens_held, tokens_all)
        + [(rounded[2], weights[2], 0), (rounded[3], weights[3], 0)]
        + quarters(dy_held, dy_all)
        + [(rounded[1], weights[1], 0), (rounded[0], weights[0], 0)],
        spread_sems,
    )
    small = Spread(at, sizes, [(gains_held, gains_all, 0)], small_sems, relay=False)
    spread.start(*range(4))
    small.start(0)
    gather = Gather(at, sizes, count, full, gather_sems)

    def cast(number):
        loads.wait(number)
        rows = min(32, held[number].shape[0])

        def block(k):
            held_rows = span(k, rows)
            rounded[number][held_rows, :] = lowered(held[number][held_rows, :])

        in_order(held[number].shape[0] // rows, block)

    stores = Moves(list(zip(rounded[4:], rounded_outs)), store_sems)
    cast(2)
    spread.start(4)
    for number in (3, 1, 0, 4, 5, 6, 7):
        cast(number)
    loads.wait(10)
    stores.start(*range(4))
    for number in range(4):
        spread.relay(number)
    spread.start(5, 6, 7)
    small.wait(0)
    own = gains_held.shape[0]
    for row, gain in enumerate((gain_one, gain_two)):
        gain[...] = wide(
            lowered(
                jnp.concatenate([gains_all[own * k + row : own * k + row + 1, :] for k in range(sizes[0])], axis=1)
            )
        )
    spread.wait(*range(4))
    run = chunk // 2

    def pick_chunk(whole, k, half):
        return pick_rows(whole, 2 * k + half, k * chunk + half * run, run, bounds, shifts, begins)

    def begin(k):
        for half in range(2):
            full[k, level, core, half * run : (half + 1) * run, :] = pick_chunk(tokens_all, k, half)
        gather.start(k)

    def norm(k):
        def block(number, carry):
            rows = span(number, 16)
            value = jnp.concatenate(
                [wide(full[k, q, c, rows, :]) for q in range(levels) for c in range(2)], axis=1
            )
            unit, scale = layer_norm(value, EPSILON)
            where = pl.ds(pl.multiple_of(k * chunk + number * 16, 16), 16)
            normed[where, :] = lowered(unit * gain_one[...])
            mine = wide(full[k, level, core, rows, :])
            mean = jnp.mean(value, -1, keepdims=True)
            unit_out[where, :] = (mine - mean) * scale
            scale_out[where, :] = jnp.broadcast_to(scale, (16, 128))
            return carry

        lax.fori_loop(0, chunk // 16, block, 0)
        mine = span(place, piece)
        rows_out[span(k, piece), :] = jnp.concatenate(
            [full[k, q, c, mine, :] for q in range(levels) for c in range(2)], axis=1
        )
        pltpu.make_async_copy(
            normed.at[span(k, chunk)], normed_out.at[span(k, chunk)], normed_sem.at[k]
        ).start()

    begin(0)
    outs = [(query, query_out), (keys, key_out), (values, value_out), (swish, swish_out)]
    ends = Moves(outs + list(zip(weights, weight_outs)) + [(dy_part, dy_out)], out_sems)

    def project_rows(number, k):
        where = span(k, chunk)
        target = outs[number][0]
        target[where, :] = matmul(normed[where, :], weights[number][...]).astype(target.dtype)

    def wave(number):
        @pl.when(number + 1 < count)
        def _():
            begin(number + 1)

        for hop in range(levels - 1, 0, -1):

            @pl.when(within(number - hop, count))
            def _():
                gather.hop(number - hop, hop)

        for step, relayed, started in (
            (1, (4,), (8, 9)),
            (3, (5,), (10, 11)),
            (5, (6, 7), ()),
            (6, (8, 9), ()),
            (8, (10,), ()),
        ):

            @pl.when(number == step)
            def _():
                spread.relay(*relayed)
                spread.start(*started)

        @pl.when(within(number - levels, count))
        def _():
            gather.ready(number - levels)
            norm(number - levels)

        @pl.when(number == levels + 3)
        def _():
            spread.wait(4)
            ends.start(6)
            for k in range(3):
                project_rows(2, k)

        @pl.when(number >= levels + 3)
        def _():
            project_rows(2, number - levels)

    in_order(count + levels, wave)

    def project(number, item):
        if item is not None:
            spread.wait(item)
            ends.start(4 + number)
            in_order(count, functools.partial(project_rows, number))
        ends.start(number)

    spread.relay(11)
    project(2, None)
    project(3, 5)
    spread.wait(*range(6, 10))

    def dy_chunk(k):
        for half in range(2):
            dy_part[k, half * run : (half + 1) * run, :] = pick_chunk(dy_all, k, half)

    in_order(count, dy_chunk)
    ends.start(8)
    project(1, 10)
    project(0, 11)
    small.drain(0)
    spread.drain(*range(12))
    gather.drain()
    stores.wait(*range(4))
    ends.wait(*range(9))

    def stored(k):
        pltpu.make_async_copy(
            normed.at[span(k, chunk)], normed_out.at[span(k, chunk)], normed_sem.at[k]
        ).wait()

    in_order(count, stored)


class Ring:
    def __init__(self, slots, whole, size, sems):
        self.slots, self.whole, self.size, self.sems = slots, whole, size, sems

    def load(self, k):
        return pltpu.make_async_copy(
            self.whole.at[span(k, self.size)], self.slots.at[lax.rem(k, 2)], self.sems.at[k]
        )

    def store(self, k):
        return pltpu.make_async_copy(
            self.slots.at[lax.rem(k, 2)], self.whole.at[span(k, self.size)], self.sems.at[k]
        )

    def free(self, k):
        @pl.when(k >= 2)
        def _():
            self.store(k - 2).wait()


def core_kernel(sizes, bounds, rate, gain, *refs):
    gain_first, *refs = refs
    query_src, key_src, value_src, rows_src, dy_src, swish_src, *refs = refs
    normed_src, unit_src, scale_src, *refs = refs
    project_src, refs = refs[:4], refs[4:]
    shards, refs = refs[:4], refs[4:]
    mixed_in_out, retained_out, gains_out, *refs = refs
    homes, down_dst, gate_dst, up_dst, *refs = refs
    late_dst, refs = refs[:5], refs[5:]
    query, keys, values, x_rows, out_w, gate_w, up_w, down_w, *refs = refs
    rooms, refs = refs[:4], refs[4:]
    (other_part,), refs = refs[:1], refs[1:]
    sems_one, sems_two, sems_three, sems_four, refs = refs[:6], refs[6:12], refs[12:18], refs[18:24], refs[24:]
    normed_mid, refs = refs[0], refs[1:]
    normed_sems, refs = refs[:6], refs[6:]
    dy, refs = refs[0], refs[1:]
    dy_sems, refs = refs[:6], refs[6:]
    branch, refs = refs[0], refs[1:]
    branch_sems, refs = refs[:6], refs[6:]
    spread_sems, refs = refs[:3], refs[3:]
    deal_sems, refs = refs[:3], refs[3:]
    swap_sems, late_sems, small_sems, refs = refs[:3], refs[3:6], refs[6:9], refs[9:]
    give_sems, refs = refs[:3], refs[3:]
    hidden, gate_grad, up_grad, resid, swish_slots, retained_slots, mixed_in_slots, *refs = refs
    key_acc, value_acc, query_acc, delta, down_grad, mixed, gain_acc, *refs = refs
    sums, line_one, packed, gains, gains_in, *refs = refs
    load_sems, ring_sems, late_load, unit_sems, room, sums_sent, sums_got, gain_sent, gain_got, *halves = refs
    at = around(AXES)
    group, level, core = at
    place = 2 * level + core
    count, levels, _, piece, width = normed_mid.shape
    ranks = 2 * levels
    chunk = ranks * piece
    part_width = width // ranks
    mixed_dst = homes.at[:, pl.ds(0, part_width)]
    grad_dst = homes.at[:, pl.ds(part_width, part_width)]
    loads = Moves(
        [
            (dy_src, dy.at[:, level, core]),
            (query_src, query),
            (key_src, keys),
            (value_src, values),
            (rows_src, x_rows),
        ],
        load_sems,
    )
    loads.start(*range(5))
    swish_one = Ring(swish_slots, swish_src, chunk, ring_sems.at[0])
    swish_two = Ring(swish_slots, swish_src, chunk, ring_sems.at[1])
    retained_one = Ring(retained_slots, retained_out, chunk, ring_sems.at[2])
    retained_two = Ring(retained_slots, retained_out, chunk, ring_sems.at[3])
    mixed_in_ring = Ring(mixed_in_slots, mixed_in_out, chunk, ring_sems.at[4])
    groups, v_dim = sizes[0], values.shape[1]
    late_loads = Moves(
        [(normed_src, normed_mid), (mixed_in_out, up_grad), (project_src[0], dy.at[0]), (project_src[1], dy.at[1])]
        + [
            (project_src[2 + n // 2].at[:, :, :, pl.ds(n % 2 * part_width, part_width)], dy.at[2 + n])
            for n in range(4)
        ],
        late_load,
    )
    swish_one.load(0).start()
    swish_one.load(1).start()
    greet(plane_peers(at, sizes) + column_all(at, sizes))
    spread = Spread(
        at,
        sizes,
        [(shards[0], out_w, 1), (shards[1], gate_w, 0), (shards[2], up_w, 0), (shards[3], down_w, 1)],
        spread_sems,
    )
    deal = Spread(
        at,
        sizes,
        [
            (mixed.at[pl.ds(k * chunk, chunk)], mixed_dst, 0, count * chunk, k * chunk)
            for k in range(count)
        ],
        deal_sems,
    )
    swap = Swap(
        at, sizes, [(down_grad, down_dst, 1), (gate_w, gate_dst, 0), (up_w, up_dst, 0)], swap_sems, halves[:3]
    )
    qk_dim = query.shape[1]
    late = Swap(
        at,
        sizes,
        [
            (gate_w, late_dst[0], 0),
            (out_w, late_dst[1], 1),
            (up_w, late_dst[2], 0),
            (down_grad.at[pl.ds(0, qk_dim)], late_dst[3], 1),
            (down_grad.at[pl.ds(qk_dim, qk_dim)], late_dst[4], 1),
        ],
        late_sems,
        [halves[1], halves[0], halves[2], halves[3], halves[4]],
    )
    small = Swap(at, sizes, [(gains, gains_in, 1)], small_sems)
    give = Spread(
        at,
        sizes,
        [
            (hidden.at[pl.ds(k * chunk, chunk), pl.ds(0, part_width)], grad_dst, 0, count * chunk, k * chunk)
            for k in range(count)
        ],
        give_sems,
    )
    spread.start(0)
    one = Scatter(at, sizes, count, list(rooms) + list(sems_one))
    two = Scatter(at, sizes, count, [other_part] + list(rooms[1:]) + list(sems_two))
    three = Scatter(at, sizes, count, list(rooms) + list(sems_three))
    four = Scatter(at, sizes, count, [other_part] + list(rooms[1:]) + list(sems_four))
    total = rooms[3]
    mid_gather = Gather(at, sizes, count, normed_mid, normed_sems)
    dy_gather = Gather(at, sizes, count, dy, dy_sems)
    branch_gather = Gather(at, sizes, count, branch, branch_sems)
    gain_acc[...] = jnp.zeros(gain_acc.shape, jnp.float32)
    line_one[...] = jnp.zeros(line_one.shape, jnp.float32)
    key_acc[...] = jnp.zeros(key_acc.shape, jnp.float32)
    value_acc[...] = jnp.zeros(value_acc.shape, jnp.float32)
    loads.wait(0)
    dy_gather.start(0)
    loads.wait(1, 2, 3, 4)
    tile = 512

    def first(k):
        where = span(k, chunk)
        slot = lax.rem(k, 2)
        retained_one.free(k)
        retained_slots[slot] = jnp.zeros((chunk, values.shape[1]), jnp.float32)

        def block(j, carry):
            there = span(j, chunk)
            decay = decay_tile(k, j, chunk, bounds, rate)
            weight = lowered(inner_rows(query[where, :], keys[there, :]) * decay)
            retained_slots[slot] += matmul(weight, values[there, :])
            return carry

        lax.fori_loop(0, k + 1, block, 0)
        retained_one.store(k).start()
        normed, _ = layer_norm(retained_slots[slot], GROUP_EPS)
        swish_one.load(k).wait()
        value = swish_slots[slot]
        mixed_in_ring.free(k)
        mixed_in_slots[slot] = lowered(value * jax.nn.sigmoid(value) * normed)
        mixed_in_ring.store(k).start()

        @pl.when(k + 2 < count)
        def _():
            swish_one.load(k + 2).start()

        @pl.when(k == 0)
        def _():
            spread.wait(0)

        one.free(k)
        rows = mixed_in_slots[slot]
        for column in range(0, width, tile):
            value = matmul(rows, out_w[:, column : column + tile])
            one.part[slot, :, :, :, column : column + tile] = lowered(value).reshape(levels, 2, piece, tile)
        one.start(k)

    def mid_norm(k):
        one.finish(k)

        def block(number, carry):
            sub = span(number, 16)
            where = pl.ds(pl.multiple_of(k * piece + number * 16, 16), 16)
            value = wide(x_rows[where, :]) + total[sub, :]
            resid[where, :] = value
            unit, _ = layer_norm(value, EPSILON)
            normed_mid[k, level, core, sub, :] = lowered(unit * gain[...])
            return carry

        lax.fori_loop(0, piece // 16, block, 0)
        mid_gather.start(k)

    def turn(k):
        mid_gather.ready(k)
        rows = normed_mid[k].reshape(chunk, width)
        where = span(k, chunk)
        g = matmul(rows, gate_w[...])
        u = matmul(rows, up_w[...])
        root = 0.7978845608028654
        bend = jnp.tanh(root * (g + 0.044715 * g * g * g))
        curve = 0.5 * (1.0 + bend)
        active = g * curve
        hidden[where, :] = lowered(active * u)
        slope = curve + 0.5 * g * (1.0 - bend * bend) * root * (1.0 + 0.134145 * g * g)
        dy_gather.ready(k)
        rows = jnp.concatenate([dy[k, q, c] for q in range(levels) for c in range(2)], axis=1)
        back = inner_rows(rows, down_w[...])
        gate_grad[where, :] = lowered(back * u * slope)
        up_grad[where, :] = lowered(back * active)
        two.free(k)
        for column in range(0, width, tile):
            columns = slice(column, column + tile)
            value = inner_rows(gate_grad[where, :], gate_w[columns, :])
            value += inner_rows(up_grad[where, :], up_w[columns, :])
            two.part[lax.rem(k, 2), :, :, :, columns] = lowered(value).reshape(levels, 2, piece, tile)
        two.start(k)

    def branch_norm(k):
        two.finish(k)

        def block(number, carry):
            sub = span(number, 16)
            where = pl.ds(pl.multiple_of(k * piece + number * 16, 16), 16)
            unit, scale = layer_norm(resid[where, :], EPSILON)
            grad = total[sub, :]
            outer = grad * unit
            gain_acc[...] += outer[:8] + outer[8:]
            mine = pl.ds(pl.multiple_of(place * piece + number * 16, 16), 16)
            upstream = jnp.concatenate(
                [dy[k, q, c, mine, :] for q in range(levels) for c in range(2)], axis=1
            )
            value = wide(upstream) + norm_back(grad * gain[...], unit, scale)
            branch[k, level, core, sub, :] = lowered(value)
            return carry

        lax.fori_loop(0, piece // 16, block, 0)
        branch_gather.start(k)

    def last(k):
        branch_gather.ready(k)
        rows = branch[k].reshape(chunk, width)
        where = span(k, chunk)
        slot = lax.rem(k, 2)
        grad = inner_rows(rows, out_w[...])
        retained_two.load(k).wait()
        swish_two.load(k).wait()
        normed, scale = layer_norm(retained_slots[slot], GROUP_EPS)
        value = swish_slots[slot]
        gated = jax.nn.sigmoid(value)
        gate_grad[where, :] = lowered(grad * normed * gated * (1.0 + value * (1.0 - gated)))
        delta[...] = lowered(norm_back(grad * value * gated, normed, scale))

        @pl.when(k + 2 < count)
        def _():
            retained_two.load(k + 2).start()
            swish_two.load(k + 2).start()

        query_acc[...] = jnp.zeros(query_acc.shape, jnp.float32)

        def block(j, carry):
            there = span(j, chunk)
            decay = decay_tile(k, j, chunk, bounds, rate)
            weight = lowered(inner_rows(query[where, :], keys[there, :]) * decay)
            score = lowered(inner_rows(delta[...], values[there, :]) * decay)
            query_acc[...] += matmul(score, keys[there, :])
            key_acc[there, :] += inner_cols(score, query[where, :])
            value_acc[there, :] += inner_cols(weight, delta[...])
            return carry

        lax.fori_loop(0, k + 1, block, 0)
        query[where, :] = lowered(query_acc[...])

    def out_part(k):
        three.free(k, one)
        rows = hidden[span(k, chunk), :]
        mine = pl.ds(pl.multiple_of(k * piece, piece), piece)
        for rank in range(ranks):
            columns = slice(rank * part_width, (rank + 1) * part_width)
            value = matmul(rows, down_w[:, columns])
            for run in range(ranks):
                held = jnp.where(place == run, resid[mine, columns], 0.0)
                three.part[
                    lax.rem(k, 2), rank // 2, rank % 2, :, run * part_width : (run + 1) * part_width
                ] = lowered(value[run * piece : (run + 1) * piece, :] + held)
        pl.semaphore_wait(room.at[0, 0], 1)
        three.start(k)

    def out_finish(k):
        three.finish(k)
        for run in range(ranks):
            where = pl.ds(pl.multiple_of(k * chunk + run * piece, piece), piece)
            mixed[where, :] = lowered(total[:, run * part_width : (run + 1) * part_width])

    def runs_of(ref, columns):
        return jnp.concatenate(
            [ref[j, q, c, :, columns] for j in range(count) for q in range(levels) for c in range(2)], axis=0
        )

    def weigh(which):
        def part(k):
            columns = span(k, chunk)
            if which == 0:
                down = jnp.zeros((hidden.shape[1], part_width), jnp.float32)
                for j in range(count):
                    down += inner_cols(hidden[j * chunk : (j + 1) * chunk, :], dy[j, k // 2, lax.rem(k, 2)])
                there = pl.ds(pl.multiple_of(k * part_width, part_width), part_width)
                down_grad[:, there] = lowered(down)
            else:
                target, source = ((gate_w, gate_grad), (up_w, up_grad))[which - 1]
                target[columns, :] = lowered(inner_cols(runs_of(normed_mid, columns), source[...]))

        in_order(width // chunk, part)
        swap.start(which)

    def weigh_late(which):
        def part(k):
            columns = span(k, chunk)
            if which == 0:
                gate_w[columns, :] = lowered(inner_cols(runs_of(normed_mid, columns), gate_grad[...]))
            elif which == 1:
                out_w[:, columns] = lowered(inner_cols(up_grad[...], runs_of(branch, columns)))
            elif which == 2:
                up_w[columns, :] = lowered(inner_cols(runs_of(normed_mid, columns), values[...]))
            else:
                rows = runs_of(normed_mid, columns)
                down_grad[:qk_dim, columns] = lowered(inner_cols(query[...], rows))
                down_grad[qk_dim:, columns] = lowered(inner_cols(keys[...], rows))

        in_order(width // chunk, part)
        late.start(*((which,) if which < 3 else (3, 4)))

    def units(k):
        slot = lax.rem(k, 2)
        return [
            pltpu.make_async_copy(
                unit_src.at[span(k, chunk)], swish_slots.at[slot, :, pl.ds(0, part_width)], unit_sems.at[0, k]
            ),
            pltpu.make_async_copy(
                scale_src.at[span(k, chunk)], retained_slots.at[slot, :, pl.ds(0, 128)], unit_sems.at[1, k]
            ),
        ]

    def peer_of(j):
        peer = lax.rem(place + j, ranks)
        return (group, peer // 2, lax.rem(peer, 2))

    def sender(j):
        return lax.rem(place + ranks - j, ranks)

    def sums_copy(k, j, owner):
        return pltpu.make_async_remote_copy(
            src_ref=sums.at[owner, k],
            dst_ref=sums.at[owner, k],
            send_sem=sums_sent.at[j - 1, k],
            recv_sem=sums_got.at[j - 1, k],
            device_id=peer_of(j),
            device_id_type=MESH,
        )

    def pack_copy(j, owner):
        return pltpu.make_async_remote_copy(
            src_ref=packed.at[owner],
            dst_ref=packed.at[owner],
            send_sem=gain_sent.at[j - 1],
            recv_sem=gain_got.at[j - 1],
            device_id=peer_of(j),
            device_id_type=MESH,
        )

    def make_room(scatter, turn_of, k):
        scatter.sent(k)
        where = room.at[turn_of]
        pl.semaphore_signal(where.at[0], inc=1, device_id=(group, level, 1 - core), device_id_type=MESH)

        @pl.when(level > 0)
        def _():
            pl.semaphore_signal(where.at[1], inc=1, device_id=(group, level - 1, core), device_id_type=MESH)

        @pl.when(level < levels - 1)
        def _():
            pl.semaphore_signal(where.at[2], inc=1, device_id=(group, level + 1, core), device_id_type=MESH)

    def in_part(k):
        four.free(k, two)
        where = span(k, chunk)
        slot = lax.rem(k, 2)
        rows = [query[where, :], keys[where, :]]
        for source in (values, gate_grad):
            rows += [source[where, n : n + part_width] for n in range(0, v_dim, part_width)]
        first_sum = jnp.zeros((chunk, part_width), jnp.float32)
        second_sum = jnp.zeros((chunk, part_width), jnp.float32)
        for rank in range(ranks):
            columns = slice(rank * part_width, (rank + 1) * part_width)
            value = inner_rows(rows[0], dy[0, rank // 2, rank % 2])
            for n in range(1, len(rows)):
                value += inner_rows(rows[n], dy[n, rank // 2, rank % 2])
            for run in range(ranks):
                four.part[
                    slot, rank // 2, rank % 2, :, run * part_width : (run + 1) * part_width
                ] = lowered(value[run * piece : (run + 1) * piece, :])
            first_sum += value * gain_first[:, columns]
            second_sum += value * wide(normed_mid[k, :, :, :, columns].reshape(chunk, part_width))
        pl.semaphore_wait(room.at[1, 0], 1)
        four.start(k)
        ones = jnp.ones((8, part_width), jnp.float32)
        flat = [
            lax.dot_general(
                ones,
                item,
                (((1,), (1,)), ((), ())),
                precision=lax.Precision.HIGHEST,
                preferred_element_type=jnp.float32,
            )
            for item in (first_sum, second_sum)
        ]
        line = lax.broadcasted_iota(jnp.int32, (8, chunk), 0)
        sums[place, k] = jnp.where(line == 0, flat[0], flat[1])
        for j in range(1, ranks):
            sums_copy(k, j, place).start()

    def in_room(turn_of, wave):
        @pl.when(within(wave - level, count) & (level < levels - 1))
        def _():
            pl.semaphore_wait(room.at[turn_of, 1], 1)

        @pl.when(within(wave - (levels - 1 - level), count) & (level > 0))
        def _():
            pl.semaphore_wait(room.at[turn_of, 2], 1)

    def in_finish(k):
        four.finish(k)
        for j in range(1, ranks):
            sums_copy(k, j, sender(j)).wait_recv()
        line = lax.broadcasted_iota(jnp.int32, (8, 128), 0)
        lane = lax.broadcasted_iota(jnp.int32, (8, 128), 1)
        means = lax.dot_general(
            jnp.sum(sums[:, k], 0),
            jnp.where(line == lane, 1.0 / width, 0.0),
            (((0,), (0,)), ((), ())),
            precision=lax.Precision.HIGHEST,
            preferred_element_type=jnp.float32,
        )
        slot = lax.rem(k, 2)
        for copy in units(k):
            copy.wait()
        mine = pl.ds(pl.multiple_of(place * part_width, part_width), part_width)
        value = jnp.concatenate(
            [total[:, run * part_width : (run + 1) * part_width] for run in range(ranks)], axis=0
        )
        normed = swish_slots[slot, :, :part_width]
        outer = value * normed
        line_one[...] += jnp.sum(outer.reshape(chunk // 8, 8, part_width), 0)
        back = value * gain_first[:, mine] - means[:, :1] - normed * means[:, 1:2]
        upstream = wide(branch[k, :, :, :, mine].reshape(chunk, part_width))
        hidden[span(k, chunk), :part_width] = lowered(upstream + retained_slots[slot, :, :1] * back)

        @pl.when(k + 2 < count)
        def _():
            for copy in units(k + 2):
                copy.start()

    lead = 3
    mid_lag = lead + levels
    turn_lag = mid_lag + levels - 1
    branch_lag = turn_lag + levels
    last_lag = branch_lag + levels - 1
    turned = turn_lag + count
    close_lag = last_lag + count
    out_lag = last_lag - 2

    def at_wave(number, lag, step):
        @pl.when(within(number - lag, count))
        def _():
            step(number - lag)

    def wave(number):
        at_wave(number, lead, first)
        for gather, lag, sent in (
            (branch_gather, branch_lag, functools.partial(make_room, two, 0)),
            (mid_gather, mid_lag, one.sent),
        ):
            at_wave(number, lag + 1, sent)
            for hop in range(levels - 1, 0, -1):
                at_wave(number, lag + hop, functools.partial(hop_on, gather, hop))
        at_wave(number, branch_lag, branch_norm)
        at_wave(number, mid_lag, mid_norm)
        at_wave(number, -1, next_dy)
        for hop in range(levels - 1, 0, -1):
            at_wave(number, hop, functools.partial(hop_on, dy_gather, hop))
        for scatter, lag in ((two, turn_lag), (one, lead)):
            at_wave(number, lag + 1, scatter.join)
            scatter.steps(number - lag - 1)
        for step, relayed, started in ((1, (0,), (1, 2)), (4, (1,), (3,)), (6, (2,), ()), (8, (3,), ())):

            @pl.when(number == step)
            def _():
                spread.relay(*relayed)
                spread.start(*started)

        @pl.when(number == turn_lag)
        def _():
            spread.wait(1, 2, 3)

        at_wave(number, turn_lag, turn)

        @pl.when(number == turn_lag + 1)
        def _():
            retained_one.store(count - 2).wait()
            retained_one.store(count - 1).wait()
            for k in range(2):
                retained_two.load(k).start()
                swish_two.load(k).start()

        @pl.when(number == turned)
        def _():
            spread.drain(*range(4))

        for step, which in ((0, 1), (1, 2), (2, 0)):

            @pl.when(number == turned + step)
            def _():
                weigh(which)

        for step, which in ((2, 1), (4, 2), (6, 0)):

            @pl.when(number == turned + step)
            def _():
                swap.relay(which)

        @pl.when(number == turned + 2)
        def _():
            mid_gather.drain()
            mixed_in_ring.store(count - 2).wait()
            mixed_in_ring.store(count - 1).wait()
            late_loads.start(0, 1)

        @pl.when(number == branch_lag + count)
        def _():
            dy_gather.drain()
            late_loads.start(*range(2, 8))

        at_wave(number, last_lag, last)
        at_wave(number, out_lag, out_part)
        at_wave(number, out_lag + 1, three.join)
        in_room(0, number - out_lag - 1)
        three.steps(number - out_lag - 1)
        at_wave(number, out_lag + levels, out_finish)
        for k in range(count):

            @pl.when(number == out_lag + levels + k)
            def _():
                deal.start(k)

            @pl.when(number == out_lag + levels + k + 2)
            def _():
                deal.relay(k)

        at_wave(number, out_lag + levels + 1, functools.partial(make_room, three, 1))

        @pl.when(number == close_lag)
        def _():
            keys[...] = lowered(key_acc[...])
            values[...] = lowered(value_acc[...])
            for k in range(2):
                for copy in units(k):
                    copy.start()
            late_loads.wait(*range(8))

        for step, before, which in ((0, 1, 0), (1, 0, 1), (2, 2, 2), (3, None, 3)):

            @pl.when(number == close_lag + step)
            def _():
                if before is not None:
                    swap.wait(before)
                weigh_late(which)

        at_wave(number, close_lag, in_part)
        at_wave(number, close_lag + 1, four.join)
        in_room(1, number - close_lag - 1)
        four.steps(number - close_lag - 1)
        at_wave(number, close_lag + levels, in_finish)
        for step, which in ((3, (0,)), (4, (1,)), (5, (2,)), (7, (3, 4))):

            @pl.when(number == close_lag + step)
            def _():
                late.relay(*which)

        for k in range(count):

            @pl.when(number == close_lag + levels + k)
            def _():
                give.start(k)

            @pl.when(number == close_lag + levels + k + 2)
            def _():
                give.relay(k)

    def hop_on(gather, hop, k):
        gather.hop(k, hop)

    def next_dy(k):
        @pl.when(k > 0)
        def _():
            dy_gather.start(k)

    in_order(close_lag + levels + count, wave)
    give.relay(count - 2, count - 1)
    packed[place] = jnp.concatenate(
        [jnp.sum(gain_acc[...], 0, keepdims=True), jnp.sum(line_one[...], 0, keepdims=True)], axis=1
    )
    for j in range(1, ranks):
        pack_copy(j, place).start()
    for j in range(1, ranks):
        pack_copy(j, sender(j)).wait_recv()
    line = lax.broadcasted_iota(jnp.int32, (8, width), 0)
    two_sum = sum(packed[rank, :, :width] for rank in range(ranks))
    one_sum = jnp.concatenate([packed[rank, :, width:] for rank in range(ranks)], axis=1)
    gains[...] = jnp.where(line == 0, one_sum, two_sum)
    small.start(0)
    small.wait(0)
    gains_out[...] = jnp.sum(gains_in[...], 0)
    late.wait(*range(5))
    give.wait(*range(count))
    give.drain(*range(count))
    deal.wait(*range(count))
    deal.drain(*range(count))
    four.drain()
    three.across(count - 2).wait_send()
    three.across(count - 1).wait_send()
    branch_gather.drain()
    for j in range(1, ranks):
        pack_copy(j, place).wait_send()

    def drain(k):
        for j in range(1, ranks):
            sums_copy(k, j, place).wait_send()

    in_order(count, drain)


def finish_kernel(first_seq, last_seq, starts, bases, begins, home, homes, *refs):
    parts, refs = refs[:8], refs[8:]
    mixed_out, grad_out, *refs = refs
    outs, refs = refs[:8], refs[8:]
    homes_held, *refs = refs
    held, sums, refs = refs[:8], refs[8:16], refs[16:]
    picked, load_sems, store_sems = refs
    loads = Moves(list(zip(parts, held)) + [(homes, homes_held)], load_sems)
    stores = Moves(
        list(zip(sums, outs)) + [(picked.at[0], mixed_out), (picked.at[1], grad_out)], store_sems
    )
    loads.start(*range(9))
    for number in range(8):
        loads.wait(number)
        ways, rows, columns = held[number].shape
        run = min(64, rows)
        turned = number < 2

        def block(k):
            where = span(k, run)
            total = wide(held[number][0, where, :])
            for way in range(1, ways):
                total += wide(held[number][way, where, :])
            sums[number][where, :] = total

        def turn(k):
            where = span(k, 128)
            total = wide(held[number][0, :, where])
            for way in range(1, ways):
                total += wide(held[number][way, :, where])
            sums[number][where, :] = total.T

        if turned:
            in_order(columns // 128, turn)
        else:
            in_order(rows // run, block)
        stores.start(number)
    loads.wait(8)
    width = picked.shape[2]
    rows = 128
    window = rows + 16
    lane = lax.broadcasted_iota(jnp.int32, (rows, window), 1)

    def pick_block(k):
        own = home[0] + k * rows + lax.broadcasted_iota(jnp.int32, (rows, 1), 0)

        def one(seq, total):
            start = begins[k, seq]
            inside = (own >= starts[seq]) & (own < starts[seq + 1])
            wanted = jnp.where(inside, own + bases[seq] - 16 * start, -1)
            chosen = jnp.where(lane == wanted, 1.0, 0.0).astype(jnp.bfloat16)
            there = jnp.concatenate([homes_held[start + n] for n in range(window // 16)], axis=0)
            return total + matmul(chosen, there)

        total = lax.fori_loop(
            first_seq[k], last_seq[k] + 1, one, jnp.zeros((rows, 2 * width), jnp.float32)
        )
        where = span(k, rows)
        picked[0, where, :] = lowered(total[:, :width])
        picked[1, where, :] = lowered(total[:, width:])

    in_order(picked.shape[1] // rows, pick_block)
    stores.start(8, 9)
    stores.wait(*range(10))


def column_all(at, sizes):
    group, level, core = at
    return column_peers(at, sizes) + [
        (group, lax.rem(level + k, sizes[1]), 1 - core) for k in range(1, sizes[1])
    ]


def struct(shape, kind=jnp.bfloat16):
    return jax.ShapeDtypeStruct(shape, kind)


VMEM = pltpu.VMEM
DMA = pltpu.SemaphoreType.DMA


def kernel_call(body, number, ins, outs, scratch):
    places = {
        "vmem": pl.BlockSpec(memory_space=pltpu.VMEM),
        "smem": pl.BlockSpec(memory_space=pltpu.SMEM),
        "any": pl.BlockSpec(memory_space=pl.ANY),
    }
    return pl.pallas_call(
        body,
        out_shape=[shape for _, shape in outs],
        in_specs=[places[inside] for inside, _ in ins],
        out_specs=[places[inside] for inside, _ in outs],
        scratch_shapes=scratch,
        compiler_params=pltpu.CompilerParams(
            collective_id=number, has_side_effects=True, vmem_limit_bytes=63 * 2**20
        ),
    )(*[array for _, array in ins])


def spread_shape(shard, axis, sizes):
    shape = list(shard.shape)
    shape[axis] *= sizes[0]
    return struct(tuple(shape), shard.dtype)


def swap_shape(whole, axis, sizes):
    shape = list(whole.shape)
    shape[axis] //= sizes[0]
    return struct((3 if sizes[0] == 4 else sizes[0],) + tuple(shape), whole.dtype)


def anywhere(items):
    return [("any", item) for item in items]


def held_like(arrays):
    return [VMEM(a.shape, a.dtype) for a in arrays]


def pick(rows, whole):
    return whole.at[rows].get(mode="promise_in_bounds")


def shards(
    tokens,
    cotangent,
    lengths,
    dealing,
    w_query,
    w_key,
    w_value,
    w_swish,
    w_out,
    w_gate,
    w_up,
    w_down,
    gain_attn,
    gain_mlp,
):
    group = lax.axis_index("dp")
    place = lax.axis_index(("heads", "tensor"))
    rows_dev = tokens.shape[0]
    slice_width = tokens.shape[1]
    seq_count = lengths.shape[0]
    ident = jnp.arange(seq_count, dtype=jnp.int32)
    starts = jnp.cumsum(lengths) - lengths
    picked = lax.dynamic_slice_in_dim(dealing, group * SEQ_DEV, SEQ_DEV)
    match = picked[:, None] == ident[None, :]
    dealt_len = jnp.sum(jnp.where(match, lengths[None, :], 0), 1)
    home_start = jnp.sum(jnp.where(match, starts[None, :], 0), 1)
    dealt_start = jnp.cumsum(dealt_len) - dealt_len
    rows = jnp.arange(rows_dev, dtype=jnp.int32)
    seq_ids = jnp.sum((rows[:, None] >= dealt_start[None, :]).astype(jnp.int32), 1) - 1
    sizes = (lax.axis_size("dp"), lax.axis_size("heads"))
    ranks = sizes[1] * lax.axis_size("tensor")
    chunk = ranks * PIECE
    count = rows_dev // chunk
    width = slice_width * ranks
    own = rows_dev // ranks
    qk_dim, v_dim, ff_dim = w_query.shape[1], w_value.shape[1], w_gate.shape[1]
    f32 = jnp.float32
    masters = (w_query, w_key, w_value, w_swish, w_out, w_gate, w_up, w_down)
    axes = (0, 0, 0, 0, 1, 0, 0, 1)
    gain_rows = jnp.pad(jnp.stack([gain_attn, gain_mlp]), ((0, 6), (0, 0)))
    shifts = home_start - dealt_start
    firsts = jnp.arange(2 * count, dtype=jnp.int32) * (chunk // 2)
    begins = jnp.clip(firsts[:, None] + shifts[None, :], 0, sizes[0] * rows_dev - chunk) // 16
    bf16 = jnp.bfloat16
    rounded = [struct(w.shape) for w in masters]
    full_w = [spread_shape(w, a, sizes) for w, a in zip(rounded, axes)]
    by_runs = struct((rows_dev // 16, 16, slice_width))
    every = spread_shape(by_runs, 0, sizes)
    gains_all = struct((sizes[0] * 8, gain_rows.shape[1]), f32)
    (
        normed_in,
        query,
        keys,
        values,
        swish_in,
        dy_part,
        query_w,
        key_w,
        value_w,
        swish_w,
        *low,
        wide_one,
        wide_two,
        x_rows,
        unit_share,
        scale_one,
    ) = kernel_call(
        functools.partial(front_kernel, sizes),
        0,
        [("smem", dealt_start), ("smem", shifts), ("smem", begins.reshape(-1))]
        + anywhere((tokens.reshape(by_runs.shape), cotangent.reshape(by_runs.shape), gain_rows) + masters),
        anywhere(
            [
                struct((rows_dev, width)),
                struct((rows_dev, qk_dim)),
                struct((rows_dev, qk_dim)),
                struct((rows_dev, v_dim)),
                struct((rows_dev, v_dim), f32),
                struct((count, chunk, slice_width)),
            ]
            + full_w[:4]
            + rounded[4:]
        )
        + [
            ("vmem", struct((1, width), f32)),
            ("vmem", struct((1, width), f32)),
            ("vmem", struct((own, width))),
            ("vmem", struct((rows_dev, slice_width), f32)),
            ("vmem", struct((rows_dev, 128), f32)),
        ],
        Gather.scratch(count, sizes, (chunk, slice_width))
        + Spread.scratch(12, sizes)
        + Spread.scratch(1, sizes)
        + held_like(masters)
        + held_like(rounded)
        + held_like(full_w[:4])
        + held_like((by_runs, by_runs, gain_rows, every, every, gains_all))
        + [
            VMEM((count, chunk, slice_width), bf16),
            VMEM((rows_dev, width), bf16),
            VMEM((rows_dev, qk_dim), bf16),
            VMEM((rows_dev, qk_dim), bf16),
            VMEM((rows_dev, v_dim), bf16),
            VMEM((rows_dev, v_dim), f32),
            DMA((11,)),
            DMA((4,)),
            DMA((9,)),
            DMA((count,)),
        ],
    )
    rate = jnp.log1p(-jnp.exp2(-5.0 - place.astype(f32))).reshape(1)
    by_rows = (PIECE, width)
    pieces = (count, sizes[1], 2) + by_rows
    blocks = (sizes[1], 2, slice_width)
    late_w = [struct(shape) for shape in ((width, v_dim), (v_dim, width), (width, v_dim), (qk_dim, width))]
    late_w.append(late_w[3])
    late_axes = (0, 1, 0, 1, 1)
    core_outs = kernel_call(
        functools.partial(core_kernel, sizes),
        1,
        [("smem", dealt_start), ("smem", rate), ("vmem", wide_two), ("vmem", wide_one)]
        + anywhere((query, keys, values, x_rows, dy_part, swish_in))
        + anywhere((normed_in.reshape(pieces), unit_share, scale_one))
        + anywhere([w.reshape(blocks + w.shape[1:]) for w in (query_w, key_w, value_w, swish_w)])
        + anywhere(low),
        anywhere([struct((rows_dev, v_dim)), struct((rows_dev, v_dim), f32)])
        + [("vmem", struct((8, gain_attn.shape[0]), f32))]
        + anywhere(
            [
                struct((sizes[0] * rows_dev, 2 * slice_width)),
                swap_shape(full_w[7], 1, sizes),
                swap_shape(full_w[5], 0, sizes),
                swap_shape(full_w[6], 0, sizes),
            ]
            + [swap_shape(w, a, sizes) for w, a in zip(late_w, late_axes)]
        ),
        held_like((query, keys, values, x_rows))
        + held_like(full_w[4:])
        + Scatter.rooms(count, sizes, by_rows)
        + Scatter.rooms(count, sizes, by_rows)[:1]
        + Scatter.sems(count, sizes) * 4
        + Gather.scratch(count, sizes, by_rows)
        + Gather.scratch(count, sizes, (chunk, slice_width))
        + Gather.scratch(count, sizes, by_rows)
        + Spread.scratch(4, sizes)
        + Spread.scratch(count, sizes)
        + Swap.scratch(3, sizes)
        + Swap.scratch(5, sizes)
        + Swap.scratch(1, sizes)
        + Spread.scratch(count, sizes)
        + [
            VMEM((rows_dev, ff_dim), bf16),
            VMEM((rows_dev, ff_dim), bf16),
            VMEM((rows_dev, ff_dim), bf16),
            VMEM((own, width), f32),
            VMEM((2, chunk, v_dim), f32),
            VMEM((2, chunk, v_dim), f32),
            VMEM((2, chunk, v_dim), bf16),
            VMEM((rows_dev, qk_dim), f32),
            VMEM((rows_dev, v_dim), f32),
            VMEM((chunk, qk_dim), f32),
            VMEM((chunk, v_dim), bf16),
            VMEM((ff_dim, width), bf16),
            VMEM((rows_dev, slice_width), bf16),
            VMEM((8, width), f32),
            VMEM((ranks, count, 8, chunk), f32),
            VMEM((8, slice_width), f32),
            VMEM((ranks, 1, width + slice_width), f32),
            VMEM((8, width), f32),
            VMEM((sizes[0], 8, gain_attn.shape[0]), f32),
            DMA((5,)),
            DMA((5, count)),
            DMA((8,)),
            DMA((2, count)),
            pltpu.SemaphoreType.REGULAR((2, 3)),
            DMA((ranks - 1, count)),
            DMA((ranks - 1, count)),
            DMA((ranks - 1,)),
            DMA((ranks - 1,)),
        ]
        + half_blocks([(full_w[7], 1), (full_w[5], 0), (full_w[6], 0)], sizes)
        + half_blocks(list(zip(late_w, late_axes))[3:], sizes),
    )
    _, _, gains, homes, *parts = core_outs
    slot_match = dealing[:, None] == ident[None, :]
    slot_len = jnp.sum(jnp.where(slot_match, lengths[None, :], 0), 1)
    slot_home = jnp.sum(jnp.where(slot_match, starts[None, :], 0), 1)
    per_group = slot_len.reshape(-1, SEQ_DEV)
    slot_start = (jnp.cumsum(per_group, 1) - per_group).reshape(-1)
    slot_base = ident // SEQ_DEV * rows_dev + slot_start - slot_home
    owner_base = jnp.sum(jnp.where(dealing[None, :] == ident[:, None], slot_base[None, :], 0), 1)
    blocks_at = group * rows_dev + jnp.arange(rows_dev // 128, dtype=jnp.int32) * 128
    first_seq = jnp.sum((blocks_at[:, None] >= starts[None, :]).astype(jnp.int32), 1) - 1
    last_seq = jnp.sum((blocks_at[:, None] + 127 >= starts[None, :]).astype(jnp.int32), 1) - 1
    total_rows = sizes[0] * rows_dev
    home_begins = jnp.clip(blocks_at[:, None] + owner_base[None, :], 0, total_rows - 144) // 16
    all_starts = jnp.concatenate([starts, jnp.full((1,), total_rows, jnp.int32)])
    homes = homes.reshape(total_rows // 16, 16, 2 * slice_width)
    order = [parts[n] for n in (6, 7, 5, 3, 4, 1, 2, 0)]
    owners = (w_query, w_key, w_value, w_swish, w_out, w_gate, w_up, w_down)
    finals = [struct(w.shape, f32) for w in owners]
    picks = struct((2, rows_dev, slice_width))
    one_place = {"smem": pl.BlockSpec(memory_space=pltpu.SMEM), "any": pl.BlockSpec(memory_space=pl.ANY)}
    mixed_rows, grad_rows, *grads = pl.pallas_call(
        finish_kernel,
        out_shape=[struct((rows_dev, slice_width))] * 2 + finals,
        in_specs=[one_place["smem"]] * 6 + [one_place["any"]] * 9,
        out_specs=[one_place["any"]] * 10,
        scratch_shapes=held_like([homes] + order + finals + [picks]) + [DMA((9,)), DMA((10,))],
        compiler_params=pltpu.CompilerParams(vmem_limit_bytes=60 * 2**20),
    )(first_seq, last_seq, all_starts, owner_base, home_begins, blocks_at[:1], homes, *order)
    return (
        mixed_rows,
        grad_rows,
        grads[0],
        grads[1],
        grads[2],
        grads[3],
        grads[4],
        grads[5],
        grads[6],
        grads[7],
        gains[0],
        gains[1],
    )


def solution(mesh):
    in_specs = (
        P("dp", ("heads", "tensor")),
        P("dp", ("heads", "tensor")),
        P(),
        P(),
        P("dp", ("heads", "tensor")),
        P("dp", ("heads", "tensor")),
        P("dp", ("heads", "tensor")),
        P("dp", ("heads", "tensor")),
        P(("heads", "tensor"), "dp"),
        P("dp", ("heads", "tensor")),
        P("dp", ("heads", "tensor")),
        P(("heads", "tensor"), "dp"),
        P("dp"),
        P("dp"),
    )
    out_specs = (
        P("dp", ("heads", "tensor")),
        P("dp", ("heads", "tensor")),
        P("dp", ("heads", "tensor")),
        P("dp", ("heads", "tensor")),
        P("dp", ("heads", "tensor")),
        P("dp", ("heads", "tensor")),
        P(("heads", "tensor"), "dp"),
        P("dp", ("heads", "tensor")),
        P("dp", ("heads", "tensor")),
        P(("heads", "tensor"), "dp"),
        P("dp"),
        P("dp"),
    )
    return jax.shard_map(shards, mesh=mesh, in_specs=in_specs, out_specs=out_specs, check_vma=False)
```

```python
import functools

import jax
import jax.numpy as jnp
from jax import lax
from jax.experimental import pallas as pl
from jax.experimental.pallas import tpu as pltpu
from jax.sharding import PartitionSpec as P

QK_DIM = 256
SEQ_DEV = 3
PIECE = 32
AXES = ("dp", "heads", "tensor")
MESH = pl.DeviceIdType.MESH


EPSILON = 1e-05
GROUP_EPS = 1.0


def layer_norm(values, epsilon):
    center = values - jnp.mean(values, -1, keepdims=True)
    scale = lax.rsqrt(jnp.mean(center * center, -1, keepdims=True) + epsilon)
    return (center * scale, scale)


def norm_back(grad, normed, scale):
    return scale * (
        grad
        - jnp.mean(grad, -1, keepdims=True)
        - normed * jnp.mean(grad * normed, -1, keepdims=True)
    )


def product(left, right):
    return jnp.dot(left, right, preferred_element_type=jnp.float32)


def inner_rows(left, right):
    return lax.dot_general(
        left, right, (((1,), (1,)), ((), ())), preferred_element_type=jnp.float32
    )


def inner_cols(left, right):
    return lax.dot_general(
        left, right, (((0,), (0,)), ((), ())), preferred_element_type=jnp.float32
    )


def lowered(value):
    return value.astype(jnp.bfloat16)


def around(axes):
    return tuple(lax.axis_index(name) for name in axes)


def wide(value):
    return value.astype(jnp.float32)


def within(number, count):
    return (number >= 0) & (number < count)


def greet(others):
    barrier = pltpu.get_barrier_semaphore()
    for other in others:
        pl.semaphore_signal(barrier, inc=1, device_id=other, device_id_type=MESH)
    pl.semaphore_wait(barrier, len(others))


def plane_peers(at, sizes):
    group, level, core = at
    return [(lax.rem(group + k, sizes[0]), level, core) for k in range(1, sizes[0])]


def column_peers(at, sizes):
    group, level, core = at
    return [(group, lax.rem(level + k, sizes[1]), core) for k in range(1, sizes[1])] + [
        (group, level, 1 - core)
    ]


def beside(group):
    return group + 1 - 2 * lax.rem(group, 2), lax.rem(group + 2, 4), 3 - group


class Spread:
    def __init__(self, at, sizes, items, sems, relay=True):
        self.at, self.count, self.items = at, sizes[0], items
        self.local, self.sent, self.got = sems
        self.plane = relay and sizes[0] == 4

    @staticmethod
    def scratch(items, sizes):
        ways = max(4, sizes[0] - 1)
        return [
            pltpu.SemaphoreType.DMA((items,)),
            pltpu.SemaphoreType.DMA((items, ways)),
            pltpu.SemaphoreType.DMA((items, ways)),
        ]

    def place(self, number, owner, half=None):
        source, target, axis, *where = self.items[number]
        rows = source.shape[0]
        size = source.shape[axis]
        step, offset = where or (size, 0)
        start = owner * step + offset
        if half is None:
            begin, height = 0, rows
        else:
            begin, height = half * (rows // 2), rows // 2
        if axis == 0:
            return target.at[pl.ds(pl.multiple_of(start + begin, height), height)]
        return target.at[pl.ds(begin, height), pl.ds(pl.multiple_of(start, size), size)]

    def own(self, number):
        return pltpu.make_async_copy(
            self.items[number][0], self.place(number, self.at[0]), self.local.at[number]
        )

    def copy(self, number, source, place, way, peer):
        return pltpu.make_async_remote_copy(
            src_ref=source,
            dst_ref=place,
            send_sem=self.sent.at[number, way],
            recv_sem=self.got.at[number, way],
            device_id=(peer,) + self.at[1:],
            device_id_type=MESH,
        )

    def away(self, number, k):
        peer = lax.rem(self.at[0] + k, self.count)
        return self.copy(number, self.items[number][0], self.place(number, self.at[0]), k - 1, peer)

    def landed(self, number, k):
        owner = lax.rem(self.at[0] + self.count - k, self.count)
        return self.copy(number, self.items[number][0], self.place(number, owner), k - 1, owner)

    def to(self, number, way):
        peer = beside(self.at[0])[way]
        return self.copy(number, self.items[number][0], self.place(number, self.at[0]), way, peer)

    def of(self, number, way):
        peer = beside(self.at[0])[way]
        return self.copy(number, self.items[number][0], self.place(number, peer), way, peer)

    def on(self, number, way):
        near = beside(self.at[0])
        ref = self.place(number, near[way], way)
        return self.copy(number, ref, ref, 2 + way, near[1 - way])

    def last(self, number, way):
        near = beside(self.at[0])
        ref = self.place(number, near[2], way)
        return self.copy(number, ref, ref, 2 + way, near[1 - way])

    def start(self, *numbers):
        for number in numbers:
            if self.plane:
                self.to(number, 0).start()
                self.to(number, 1).start()
            else:
                for k in range(1, self.count):
                    self.away(number, k).start()
            self.own(number).start()

    def relay(self, *numbers):
        if self.plane:
            for number in numbers:
                for way in range(2):
                    self.of(number, way).wait_recv()
                    self.on(number, way).start()

    def wait(self, *numbers):
        for number in numbers:
            self.own(number).wait()
            if self.plane:
                self.last(number, 0).wait_recv()
                self.last(number, 1).wait_recv()
            else:
                for k in range(1, self.count):
                    self.landed(number, k).wait_recv()

    def drain(self, *numbers):
        for number in numbers:
            if self.plane:
                for way in range(2):
                    self.to(number, way).wait_send()
                    self.on(number, way).wait_send()
            else:
                for k in range(1, self.count):
                    self.away(number, k).wait_send()


class Gather:
    def __init__(self, at, sizes, count, full, sems):
        self.at, self.levels, self.count, self.full = at, sizes[1], count, full
        self.sent_up, self.got_up, self.sent_down, self.got_down, self.sent_core, self.got_core = sems

    @staticmethod
    def scratch(count, sizes, piece):
        levels = sizes[1]
        dma = pltpu.SemaphoreType.DMA
        return [pltpu.VMEM((count, levels, 2) + piece, jnp.bfloat16)] + [
            dma((levels - 1, count)) for _ in range(4)
        ] + [dma((2 * levels - 1, count)) for _ in range(2)]

    def copy(self, ref, sent, got, target):
        return pltpu.make_async_remote_copy(
            src_ref=ref, dst_ref=ref, send_sem=sent, recv_sem=got, device_id=target, device_id_type=MESH
        )

    def up(self, k, hop, origin, sem):
        group, level, core = self.at
        target = (group, lax.rem(level + 1, self.levels), core)
        return self.copy(self.full.at[k, origin, core], self.sent_up.at[sem, k], self.got_up.at[sem, k], target)

    def down(self, k, hop, origin, sem):
        group, level, core = self.at
        target = (group, lax.rem(level + self.levels - 1, self.levels), core)
        return self.copy(
            self.full.at[k, origin, core], self.sent_down.at[sem, k], self.got_down.at[sem, k], target
        )

    def across(self, k, origin, side, sem):
        group, level, core = self.at
        return self.copy(
            self.full.at[k, origin, side], self.sent_core.at[sem, k], self.got_core.at[sem, k], (group, level, 1 - core)
        )

    def start(self, k):
        group, level, core = self.at

        @pl.when(level < self.levels - 1)
        def _():
            self.up(k, 0, level, 0).start()

        @pl.when(level > 0)
        def _():
            self.down(k, 0, level, 0).start()

        self.across(k, level, core, 0).start()

    def hop(self, k, hop):
        group, level, core = self.at
        last = self.levels - 1

        @pl.when(level >= hop)
        def _():
            origin = level - hop
            self.up(k, hop, origin, hop - 1).wait_recv()
            if hop < last:

                @pl.when(level < last)
                def _():
                    self.up(k, hop, origin, hop).start()

            self.across(k, origin, core, hop).start()

        @pl.when(level + hop <= last)
        def _():
            origin = level + hop
            self.down(k, hop, origin, hop - 1).wait_recv()
            if hop < last:

                @pl.when(level > 0)
                def _():
                    self.down(k, hop, origin, hop).start()

            self.across(k, origin, core, last + hop).start()

    def ready(self, k):
        group, level, core = self.at
        last = self.levels - 1
        self.across(k, level, 1 - core, 0).wait_recv()
        for hop in range(1, self.levels):

            @pl.when(level >= hop)
            def _():
                self.across(k, level - hop, 1 - core, hop).wait_recv()

            @pl.when(level + hop <= last)
            def _():
                self.across(k, level + hop, 1 - core, last + hop).wait_recv()

    def drain(self):
        group, level, core = self.at
        last = self.levels - 1

        def one(k, _):
            self.across(k, level, core, 0).wait_send()
            for hop in range(self.levels):
                if hop < last:

                    @pl.when((level >= hop) & (level < last))
                    def _():
                        self.up(k, hop, level - hop, hop).wait_send()

                    @pl.when((level + hop <= last) & (level > 0))
                    def _():
                        self.down(k, hop, level + hop, hop).wait_send()

                if hop > 0:

                    @pl.when(level >= hop)
                    def _():
                        self.across(k, level - hop, core, hop).wait_send()

                    @pl.when(level + hop <= last)
                    def _():
                        self.across(k, level + hop, core, last + hop).wait_send()

            return 0

        lax.fori_loop(0, self.count, one, 0)


class Scatter:
    REFS = 4

    def __init__(self, at, sizes, count, refs):
        self.at, self.levels, self.count = at, sizes[1], count
        self.part, self.cross, self.inbox, self.total = refs[:4]
        self.sent_core, self.got_core, self.sent_up, self.got_up, self.sent_down, self.got_down = refs[4:]

    @staticmethod
    def rooms(count, sizes, piece):
        levels = sizes[1]
        return [
            pltpu.VMEM((2, levels, 2) + piece, jnp.bfloat16),
            pltpu.VMEM((count, levels) + piece, jnp.bfloat16),
            pltpu.VMEM((count, levels + 1) + piece, jnp.bfloat16),
            pltpu.VMEM(piece, jnp.float32),
        ]

    @staticmethod
    def sems(count, sizes):
        dma = pltpu.SemaphoreType.DMA
        return [dma((count,)) for _ in range(2)] + [dma((sizes[1], count)) for _ in range(4)]

    @staticmethod
    def scratch(count, sizes, piece):
        return Scatter.rooms(count, sizes, piece) + Scatter.sems(count, sizes)

    def across(self, k):
        group, level, core = self.at
        return pltpu.make_async_remote_copy(
            src_ref=self.part.at[lax.rem(k, 2), :, 1 - core],
            dst_ref=self.cross.at[k],
            send_sem=self.sent_core.at[k],
            recv_sem=self.got_core.at[k],
            device_id=(group, level, 1 - core),
            device_id_type=MESH,
        )

    def up(self, k, owner):
        group, level, core = self.at
        return pltpu.make_async_remote_copy(
            src_ref=self.cross.at[k, owner],
            dst_ref=self.inbox.at[k, owner + 1],
            send_sem=self.sent_up.at[owner, k],
            recv_sem=self.got_up.at[owner, k],
            device_id=(group, lax.rem(level + 1, self.levels), core),
            device_id_type=MESH,
        )

    def down(self, k, owner):
        group, level, core = self.at
        return pltpu.make_async_remote_copy(
            src_ref=self.cross.at[k, owner],
            dst_ref=self.inbox.at[k, owner],
            send_sem=self.sent_down.at[owner, k],
            recv_sem=self.got_down.at[owner, k],
            device_id=(group, lax.rem(level + self.levels - 1, self.levels), core),
            device_id_type=MESH,
        )

    def free(self, k, before=None):
        @pl.when(k >= 2)
        def _():
            self.across(k - 2).wait_send()

        if before is not None:

            @pl.when(k < 2)
            def _():
                before.across(self.count - 2 + k).wait_send()

    def start(self, k):
        self.across(k).start()

    def join(self, k):
        core = self.at[2]
        self.across(k).wait_recv()
        for owner in range(self.levels):
            self.cross[k, owner] = lowered(
                wide(self.part[lax.rem(k, 2), owner, core]) + wide(self.cross[k, owner])
            )

    def step_up(self, k):
        level = self.at[1]
        for owner in range(self.levels - 1, 0, -1):

            @pl.when(level < owner)
            def _():
                @pl.when(level > 0)
                def _():
                    self.up(k, owner).wait_recv()
                    self.cross[k, owner] = lowered(wide(self.cross[k, owner]) + wide(self.inbox[k, owner + 1]))

                self.up(k, owner).start()

    def step_down(self, k):
        level = self.at[1]
        for owner in range(self.levels - 1):

            @pl.when(level > owner)
            def _():
                @pl.when(level < self.levels - 1)
                def _():
                    self.down(k, owner).wait_recv()
                    self.cross[k, owner] = lowered(wide(self.cross[k, owner]) + wide(self.inbox[k, owner]))

                self.down(k, owner).start()

    def steps(self, wave):
        level = self.at[1]
        above = wave - level
        below = wave - (self.levels - 1 - level)

        @pl.when(within(above, self.count) & (level < self.levels // 2))
        def _():
            self.step_up(above)

        @pl.when(within(below, self.count))
        def _():
            self.step_down(below)

        @pl.when(within(above, self.count) & (level >= self.levels // 2))
        def _():
            self.step_up(above)

    def finish(self, k):
        level = self.at[1]
        self.total[...] = wide(self.cross[k, level])

        @pl.when(level > 0)
        def _():
            self.up(k, level).wait_recv()
            self.total[...] += wide(self.inbox[k, level + 1])

        @pl.when(level < self.levels - 1)
        def _():
            self.down(k, level).wait_recv()
            self.total[...] += wide(self.inbox[k, level])

    def sent(self, k):
        level = self.at[1]
        for owner in range(self.levels):

            @pl.when(level < owner)
            def _():
                self.up(k, owner).wait_send()

            @pl.when(level > owner)
            def _():
                self.down(k, owner).wait_send()

    def drain(self):
        self.across(self.count - 2).wait_send()
        self.across(self.count - 1).wait_send()
        in_order(self.count, self.sent)


def in_order(count, step):
    def body(number, carry):
        step(number)
        return carry

    lax.fori_loop(0, count, body, 0)


def span(number, size):
    return pl.ds(pl.multiple_of(number * size, size), size)


class Moves:
    def __init__(self, pairs, sems):
        self.pairs, self.sems = pairs, sems

    def copy(self, number):
        return pltpu.make_async_copy(*self.pairs[number], self.sems.at[number])

    def start(self, *numbers):
        for number in numbers:
            self.copy(number).start()

    def wait(self, *numbers):
        for number in numbers:
            self.copy(number).wait()


class Chunks:
    def __init__(self, pairs, size, sems):
        self.pairs, self.size, self.sems = pairs, size, sems

    def start(self, k):
        for number, (source, target) in enumerate(self.pairs):
            rows = span(k, self.size)
            pltpu.make_async_copy(source.at[rows], target.at[rows], self.sems.at[number, k]).start()

    def wait(self, count):
        def one(k, carry):
            for number, (source, target) in enumerate(self.pairs):
                rows = span(k, self.size)
                pltpu.make_async_copy(source.at[rows], target.at[rows], self.sems.at[number, k]).wait()
            return carry

        lax.fori_loop(0, count, one, 0)


def matmul(left, right):
    return jnp.dot(left, right, preferred_element_type=jnp.float32)


def decay_tile(near, far, size, bounds, rate):
    rows = near * size + lax.broadcasted_iota(jnp.int32, (size, 1), 0)
    columns = far * size + lax.broadcasted_iota(jnp.int32, (1, size), 1)
    row_seq, column_seq = jnp.zeros((size, 1), jnp.int32), jnp.zeros((1, size), jnp.int32)
    for number in range(1, SEQ_DEV):
        row_seq += (rows >= bounds[number]).astype(jnp.int32)
        column_seq += (columns >= bounds[number]).astype(jnp.int32)
    distance = rows - columns
    valid = (distance >= 0) & (row_seq == column_seq)
    return (
        jnp.where(valid, jnp.exp(jnp.maximum(distance, 0).astype(jnp.float32) * rate[0]), 0.0)
        * QK_DIM ** (-0.5)
    )


class Swap:
    def __init__(self, at, sizes, items, sems, halves=None):
        self.at, self.count, self.items = at, sizes[0], items
        self.local, self.sent, self.got = sems
        self.halves = halves
        self.plane = halves is not None and sizes[0] == 4

    @staticmethod
    def scratch(items, sizes):
        ways = max(6, sizes[0] - 1)
        return [
            pltpu.SemaphoreType.DMA((items,)),
            pltpu.SemaphoreType.DMA((items, ways)),
            pltpu.SemaphoreType.DMA((items, ways)),
        ]

    def block(self, number, owner, half=None):
        source, target, axis = self.items[number]
        rows = source.shape[0]
        size = source.shape[axis] // self.count
        height = size if axis == 0 else rows
        begin = 0
        if half is not None:
            height //= 2
            begin = half * height
        if axis == 0:
            return source.at[pl.ds(pl.multiple_of(owner * size + begin, height), height)]
        return source.at[pl.ds(begin, height), pl.ds(pl.multiple_of(owner * size, size), size)]

    def half(self, number, slot, half):
        target = self.items[number][1]
        height = target.shape[1] // 2
        return target.at[slot, pl.ds(half * height, height)]

    def copy(self, number, source, place, way, peer):
        return pltpu.make_async_remote_copy(
            src_ref=source,
            dst_ref=place,
            send_sem=self.sent.at[number, way],
            recv_sem=self.got.at[number, way],
            device_id=(peer,) + self.at[1:],
            device_id_type=MESH,
        )

    def own(self, number):
        return pltpu.make_async_copy(
            self.block(number, self.at[0]), self.items[number][1].at[0], self.local.at[number]
        )

    def away(self, number, k):
        peer = lax.rem(self.at[0] + k, self.count)
        return self.copy(number, self.block(number, peer), self.items[number][1].at[k], k - 1, peer)

    def across(self, number, way):
        near = beside(self.at[0])
        return self.copy(
            number, self.block(number, near[2], way), self.halves[number].at[way], way, near[way]
        )

    def direct(self, number, way):
        near = beside(self.at[0])
        return self.copy(
            number, self.block(number, near[way], way), self.half(number, 1 + way, way), 2 + way, near[way]
        )

    def added(self, number, way):
        peer = beside(self.at[0])[1 - way]
        return self.copy(
            number, self.block(number, peer, way), self.half(number, 2 - way, way), 4 + way, peer
        )

    def start(self, *numbers):
        for number in numbers:
            if self.plane:
                for way in range(2):
                    self.across(number, way).start()
                for way in range(2):
                    self.direct(number, way).start()
            else:
                for k in range(1, self.count):
                    self.away(number, k).start()
            self.own(number).start()

    def relay(self, *numbers):
        if self.plane:
            near = beside(self.at[0])
            for number in numbers:
                for way in range(2):
                    self.across(number, way).wait_recv()
                    part = self.block(number, near[1 - way], way)
                    part[...] = lowered(wide(part[...]) + wide(self.halves[number][way]))
                for way in range(2):
                    self.added(number, way).start()

    def wait(self, *numbers):
        for number in numbers:
            self.own(number).wait()
            if self.plane:
                for way in range(2):
                    self.across(number, way).wait_send()
                    self.direct(number, way).wait()
                    self.added(number, way).wait()
            else:
                for k in range(1, self.count):
                    self.away(number, k).wait()


def half_blocks(items, sizes):
    room = []
    for whole, axis in items:
        shape = list(whole.shape)
        shape[axis] //= sizes[0]
        room.append(pltpu.VMEM((2, shape[0] // 2, shape[1]), jnp.bfloat16))
    return room


def quarters(source, target):
    rows = source.shape[0]
    run = rows // 4
    return [(source.at[pl.ds(k * run, run)], target, 0, rows, k * run) for k in range(4)]


def pick_rows(whole, number, first, rows, bounds, shifts, begins):
    window = 2 * rows
    lane = lax.broadcasted_iota(jnp.int32, (rows, window), 1)
    slot = jnp.zeros((rows, 1), jnp.int32)
    own = first + lax.broadcasted_iota(jnp.int32, (rows, 1), 0)
    for item in range(1, SEQ_DEV):
        slot += (own >= bounds[item]).astype(jnp.int32)
    chosen, windows = [], []
    for item in range(SEQ_DEV):
        start = begins[number * SEQ_DEV + item]
        wanted = jnp.where(slot == item, own + shifts[item] - 16 * start, -1)
        chosen.append(jnp.where(lane == wanted, 1.0, 0.0).astype(jnp.bfloat16))
        windows += [whole[start + k] for k in range(window // 16)]
    return lowered(matmul(jnp.concatenate(chosen, axis=1), jnp.concatenate(windows, axis=0)))


def front_kernel(sizes, bounds, shifts, begins, tokens, cotangent, gain_attn, gain_mlp, *refs):
    masters, refs = refs[:8], refs[8:]
    normed_out, query_out, key_out, value_out, swish_out, dy_out, *refs = refs
    weight_outs, rounded_outs, refs = refs[:4], refs[4:8], refs[8:]
    gain_one, gain_two, rows_out, unit_out, scale_out, *refs = refs
    full, *refs = refs
    gather_sems, refs = refs[:6], refs[6:]
    spread_sems, small_sems, refs = refs[:3], refs[3:6], refs[6:]
    held, rounded, weights, refs = refs[:8], refs[8:16], refs[16:20], refs[20:]
    tokens_held, dy_held, gains_held, tokens_all, dy_all, gains_all, dy_part, *refs = refs
    normed, query, keys, values, swish, load_sems, store_sems, out_sems, normed_sem = refs
    at = around(AXES)
    group, level, core = at
    place = 2 * level + core
    count, levels, _, chunk, width = full.shape
    ranks = 2 * levels
    piece = chunk // ranks
    loads = Moves(
        list(zip(masters, held)) + [(tokens, tokens_held), (cotangent, dy_held)], load_sems
    )
    loads.start(8, 2, 3, 1, 0, 9, 4, 5, 6, 7)
    gains_held[...] = jnp.zeros(gains_held.shape, jnp.float32)
    gains_held[0:1, :] = gain_attn[...]
    gains_held[1:2, :] = gain_mlp[...]
    greet(plane_peers(at, sizes) + column_peers(at, sizes))
    loads.wait(8)
    spread = Spread(
        at,
        sizes,
        quarters(tokens_held, tokens_all)
        + [(rounded[number], weights[number], 0) for number in (2, 3, 1, 0)]
        + quarters(dy_held, dy_all),
        spread_sems,
    )
    small = Spread(at, sizes, [(gains_held, gains_all, 0)], small_sems, relay=False)
    spread.start(*range(4))
    small.start(0)
    gather = Gather(at, sizes, count, full, gather_sems)

    def cast(number):
        loads.wait(number)
        rows = min(32, held[number].shape[0])

        def block(k):
            held_rows = span(k, rows)
            rounded[number][held_rows, :] = lowered(held[number][held_rows, :])

        in_order(held[number].shape[0] // rows, block)

    stores = Moves(list(zip(rounded[4:], rounded_outs)), store_sems)
    cast(2)
    spread.start(4)
    for number in (3, 1, 0, 4, 5, 6, 7):
        cast(number)
    loads.wait(9)
    stores.start(*range(4))
    for number in range(4):
        spread.relay(number)
    spread.start(5, 6, 7)
    small.wait(0)
    own = gains_held.shape[0]
    for row, gain in enumerate((gain_one, gain_two)):
        gain[...] = wide(
            lowered(
                jnp.concatenate([gains_all[own * k + row : own * k + row + 1, :] for k in range(sizes[0])], axis=1)
            )
        )
    spread.wait(*range(4))
    run = chunk // 2

    def pick_chunk(whole, k, half):
        return pick_rows(whole, 2 * k + half, k * chunk + half * run, run, bounds, shifts, begins)

    def begin(k):
        for half in range(2):
            full[k, level, core, half * run : (half + 1) * run, :] = pick_chunk(tokens_all, k, half)
        gather.start(k)

    def norm(k):
        def block(number, carry):
            rows = span(number, 16)
            value = jnp.concatenate(
                [wide(full[k, q, c, rows, :]) for q in range(levels) for c in range(2)], axis=1
            )
            unit, scale = layer_norm(value, EPSILON)
            where = pl.ds(pl.multiple_of(k * chunk + number * 16, 16), 16)
            normed[where, :] = lowered(unit * gain_one[...])
            mine = wide(full[k, level, core, rows, :])
            mean = jnp.mean(value, -1, keepdims=True)
            unit_out[where, :] = (mine - mean) * scale
            scale_out[where, :] = jnp.broadcast_to(scale, (16, 128))
            return carry

        lax.fori_loop(0, chunk // 16, block, 0)
        mine = span(place, piece)
        rows_out[span(k, piece), :] = jnp.concatenate(
            [full[k, q, c, mine, :] for q in range(levels) for c in range(2)], axis=1
        )
        pltpu.make_async_copy(
            normed.at[span(k, chunk)], normed_out.at[span(k, chunk)], normed_sem.at[k]
        ).start()

    begin(0)
    outs = [(query, query_out), (keys, key_out), (values, value_out), (swish, swish_out)]
    ends = Moves(outs + list(zip(weights, weight_outs)) + [(dy_part, dy_out)], out_sems)

    def project_rows(number, k):
        where = span(k, chunk)
        target = outs[number][0]
        target[where, :] = matmul(normed[where, :], weights[number][...]).astype(target.dtype)

    def wave(number):
        @pl.when(number + 1 < count)
        def _():
            begin(number + 1)

        for hop in range(levels - 1, 0, -1):

            @pl.when(within(number - hop, count))
            def _():
                gather.hop(number - hop, hop)

        for step, relayed, started in (
            (1, (4,), (8, 9)),
            (3, (5,), (10, 11)),
            (4, (6,), ()),
            (5, (7,), ()),
            (7, (8, 9), ()),
            (9, (10,), ()),
        ):

            @pl.when(number == step)
            def _():
                spread.relay(*relayed)
                spread.start(*started)

        @pl.when(within(number - levels, count))
        def _():
            gather.ready(number - levels)
            norm(number - levels)

        @pl.when(number == levels + 3)
        def _():
            spread.wait(4)
            ends.start(6)
            for k in range(3):
                project_rows(2, k)

        @pl.when(number >= levels + 3)
        def _():
            project_rows(2, number - levels)

    in_order(count + levels, wave)

    def project(number, item):
        if item is not None:
            spread.wait(item)
            ends.start(4 + number)
            in_order(count, functools.partial(project_rows, number))
        ends.start(number)

    spread.relay(11)
    project(2, None)
    project(3, 5)
    project(1, 6)
    project(0, 7)
    spread.wait(*range(8, 12))

    def dy_chunk(k):
        for half in range(2):
            dy_part[k, half * run : (half + 1) * run, :] = pick_chunk(dy_all, k, half)

    in_order(count, dy_chunk)
    ends.start(8)
    small.drain(0)
    spread.drain(*range(12))
    gather.drain()
    stores.wait(*range(4))
    ends.wait(*range(9))

    def stored(k):
        pltpu.make_async_copy(
            normed.at[span(k, chunk)], normed_out.at[span(k, chunk)], normed_sem.at[k]
        ).wait()

    in_order(count, stored)


class Ring:
    def __init__(self, slots, whole, size, sems):
        self.slots, self.whole, self.size, self.sems = slots, whole, size, sems

    def load(self, k):
        return pltpu.make_async_copy(
            self.whole.at[span(k, self.size)], self.slots.at[lax.rem(k, 2)], self.sems.at[k]
        )

    def store(self, k):
        return pltpu.make_async_copy(
            self.slots.at[lax.rem(k, 2)], self.whole.at[span(k, self.size)], self.sems.at[k]
        )

    def free(self, k):
        @pl.when(k >= 2)
        def _():
            self.store(k - 2).wait()


def core_kernel(sizes, bounds, rate, gain, *refs):
    gain_first, *refs = refs
    query_src, key_src, value_src, rows_src, dy_src, swish_src, *refs = refs
    normed_src, unit_src, scale_src, *refs = refs
    project_src, refs = refs[:4], refs[4:]
    shards, refs = refs[:4], refs[4:]
    mixed_in_out, retained_out, gains_out, *refs = refs
    homes, down_dst, gate_dst, up_dst, *refs = refs
    late_dst, refs = refs[:5], refs[5:]
    query, keys, values, x_rows, out_w, gate_w, up_w, down_w, *refs = refs
    rooms, refs = refs[:4], refs[4:]
    (other_part,), refs = refs[:1], refs[1:]
    sems_one, sems_two, sems_three, sems_four, refs = refs[:6], refs[6:12], refs[12:18], refs[18:24], refs[24:]
    normed_mid, refs = refs[0], refs[1:]
    normed_sems, refs = refs[:6], refs[6:]
    dy, refs = refs[0], refs[1:]
    dy_sems, refs = refs[:6], refs[6:]
    branch, refs = refs[0], refs[1:]
    branch_sems, refs = refs[:6], refs[6:]
    spread_sems, refs = refs[:3], refs[3:]
    deal_sems, refs = refs[:3], refs[3:]
    swap_sems, late_sems, small_sems, refs = refs[:3], refs[3:6], refs[6:9], refs[9:]
    give_sems, refs = refs[:3], refs[3:]
    hidden, gate_grad, up_grad, resid, swish_slots, retained_slots, mixed_in_slots, *refs = refs
    key_acc, value_acc, query_acc, delta, down_grad, mixed, gain_acc, *refs = refs
    sums, line_one, packed, gains, gains_in, *refs = refs
    load_sems, ring_sems, late_load, unit_sems, room, sums_sent, sums_got, gain_sent, gain_got, *halves = refs
    at = around(AXES)
    group, level, core = at
    place = 2 * level + core
    count, levels, _, piece, width = normed_mid.shape
    ranks = 2 * levels
    chunk = ranks * piece
    part_width = width // ranks
    mixed_dst = homes.at[:, pl.ds(0, part_width)]
    grad_dst = homes.at[:, pl.ds(part_width, part_width)]
    loads = Moves(
        [
            (dy_src, dy.at[:, level, core]),
            (query_src, query),
            (key_src, keys),
            (value_src, values),
            (rows_src, x_rows),
        ],
        load_sems,
    )
    loads.start(*range(5))
    swish_one = Ring(swish_slots, swish_src, chunk, ring_sems.at[0])
    swish_two = Ring(swish_slots, swish_src, chunk, ring_sems.at[1])
    retained_one = Ring(retained_slots, retained_out, chunk, ring_sems.at[2])
    retained_two = Ring(retained_slots, retained_out, chunk, ring_sems.at[3])
    mixed_in_ring = Ring(mixed_in_slots, mixed_in_out, chunk, ring_sems.at[4])
    groups, v_dim = sizes[0], values.shape[1]
    late_loads = Moves(
        [(normed_src, normed_mid), (mixed_in_out, up_grad), (project_src[0], dy.at[0]), (project_src[1], dy.at[1])]
        + [
            (project_src[2 + n // 2].at[:, :, :, pl.ds(n % 2 * part_width, part_width)], dy.at[2 + n])
            for n in range(4)
        ],
        late_load,
    )
    swish_one.load(0).start()
    swish_one.load(1).start()
    greet(plane_peers(at, sizes) + column_all(at, sizes))
    spread = Spread(
        at,
        sizes,
        [(shards[0], out_w, 1), (shards[1], gate_w, 0), (shards[2], up_w, 0), (shards[3], down_w, 1)],
        spread_sems,
    )
    deal = Spread(
        at,
        sizes,
        [
            (mixed.at[pl.ds(k * chunk, chunk)], mixed_dst, 0, count * chunk, k * chunk)
            for k in range(count)
        ],
        deal_sems,
    )
    swap = Swap(
        at, sizes, [(down_grad, down_dst, 1), (gate_w, gate_dst, 0), (up_w, up_dst, 0)], swap_sems, halves[:3]
    )
    qk_dim = query.shape[1]
    late = Swap(
        at,
        sizes,
        [
            (gate_w, late_dst[0], 0),
            (out_w, late_dst[1], 1),
            (up_w, late_dst[2], 0),
            (down_grad.at[pl.ds(0, qk_dim)], late_dst[3], 1),
            (down_grad.at[pl.ds(qk_dim, qk_dim)], late_dst[4], 1),
        ],
        late_sems,
        [halves[1], halves[0], halves[2], halves[3], halves[4]],
    )
    small = Swap(at, sizes, [(gains, gains_in, 1)], small_sems)
    give = Spread(
        at,
        sizes,
        [
            (hidden.at[pl.ds(k * chunk, chunk), pl.ds(0, part_width)], grad_dst, 0, count * chunk, k * chunk)
            for k in range(count)
        ],
        give_sems,
    )
    spread.start(0)
    one = Scatter(at, sizes, count, list(rooms) + list(sems_one))
    two = Scatter(at, sizes, count, [other_part] + list(rooms[1:]) + list(sems_two))
    three = Scatter(at, sizes, count, list(rooms) + list(sems_three))
    four = Scatter(at, sizes, count, [other_part] + list(rooms[1:]) + list(sems_four))
    total = rooms[3]
    mid_gather = Gather(at, sizes, count, normed_mid, normed_sems)
    dy_gather = Gather(at, sizes, count, dy, dy_sems)
    branch_gather = Gather(at, sizes, count, branch, branch_sems)
    gain_acc[...] = jnp.zeros(gain_acc.shape, jnp.float32)
    line_one[...] = jnp.zeros(line_one.shape, jnp.float32)
    key_acc[...] = jnp.zeros(key_acc.shape, jnp.float32)
    value_acc[...] = jnp.zeros(value_acc.shape, jnp.float32)
    loads.wait(0)
    dy_gather.start(0)
    loads.wait(1, 2, 3, 4)
    tile = 512

    def first(k):
        where = span(k, chunk)
        slot = lax.rem(k, 2)
        retained_one.free(k)
        retained_slots[slot] = jnp.zeros((chunk, values.shape[1]), jnp.float32)

        def block(j, carry):
            there = span(j, chunk)
            decay = decay_tile(k, j, chunk, bounds, rate)
            weight = lowered(inner_rows(query[where, :], keys[there, :]) * decay)
            retained_slots[slot] += matmul(weight, values[there, :])
            return carry

        lax.fori_loop(0, k + 1, block, 0)
        retained_one.store(k).start()
        normed, _ = layer_norm(retained_slots[slot], GROUP_EPS)
        swish_one.load(k).wait()
        value = swish_slots[slot]
        mixed_in_ring.free(k)
        mixed_in_slots[slot] = lowered(value * jax.nn.sigmoid(value) * normed)
        mixed_in_ring.store(k).start()

        @pl.when(k + 2 < count)
        def _():
            swish_one.load(k + 2).start()

        @pl.when(k == 0)
        def _():
            spread.wait(0)

        one.free(k)
        rows = mixed_in_slots[slot]
        for column in range(0, width, tile):
            value = matmul(rows, out_w[:, column : column + tile])
            one.part[slot, :, :, :, column : column + tile] = lowered(value).reshape(levels, 2, piece, tile)
        one.start(k)

    def mid_norm(k):
        one.finish(k)

        def block(number, carry):
            sub = span(number, 16)
            where = pl.ds(pl.multiple_of(k * piece + number * 16, 16), 16)
            value = wide(x_rows[where, :]) + total[sub, :]
            resid[where, :] = value
            unit, _ = layer_norm(value, EPSILON)
            normed_mid[k, level, core, sub, :] = lowered(unit * gain[...])
            return carry

        lax.fori_loop(0, piece // 16, block, 0)
        mid_gather.start(k)

    def turn(k):
        mid_gather.ready(k)
        rows = normed_mid[k].reshape(chunk, width)
        where = span(k, chunk)
        g = matmul(rows, gate_w[...])
        u = matmul(rows, up_w[...])
        root = 0.7978845608028654
        bend = jnp.tanh(root * (g + 0.044715 * g * g * g))
        curve = 0.5 * (1.0 + bend)
        active = g * curve
        hidden[where, :] = lowered(active * u)
        slope = curve + 0.5 * g * (1.0 - bend * bend) * root * (1.0 + 0.134145 * g * g)
        dy_gather.ready(k)
        rows = jnp.concatenate([dy[k, q, c] for q in range(levels) for c in range(2)], axis=1)
        back = inner_rows(rows, down_w[...])
        gate_grad[where, :] = lowered(back * u * slope)
        up_grad[where, :] = lowered(back * active)
        two.free(k)
        for column in range(0, width, tile):
            columns = slice(column, column + tile)
            value = inner_rows(gate_grad[where, :], gate_w[columns, :])
            value += inner_rows(up_grad[where, :], up_w[columns, :])
            two.part[lax.rem(k, 2), :, :, :, columns] = lowered(value).reshape(levels, 2, piece, tile)
        two.start(k)

    def branch_norm(k):
        two.finish(k)

        def block(number, carry):
            sub = span(number, 16)
            where = pl.ds(pl.multiple_of(k * piece + number * 16, 16), 16)
            unit, scale = layer_norm(resid[where, :], EPSILON)
            grad = total[sub, :]
            outer = grad * unit
            gain_acc[...] += outer[:8] + outer[8:]
            mine = pl.ds(pl.multiple_of(place * piece + number * 16, 16), 16)
            upstream = jnp.concatenate(
                [dy[k, q, c, mine, :] for q in range(levels) for c in range(2)], axis=1
            )
            value = wide(upstream) + norm_back(grad * gain[...], unit, scale)
            branch[k, level, core, sub, :] = lowered(value)
            return carry

        lax.fori_loop(0, piece // 16, block, 0)
        branch_gather.start(k)

    def last(k):
        branch_gather.ready(k)
        rows = branch[k].reshape(chunk, width)
        where = span(k, chunk)
        slot = lax.rem(k, 2)
        grad = inner_rows(rows, out_w[...])
        retained_two.load(k).wait()
        swish_two.load(k).wait()
        normed, scale = layer_norm(retained_slots[slot], GROUP_EPS)
        value = swish_slots[slot]
        gated = jax.nn.sigmoid(value)
        gate_grad[where, :] = lowered(grad * normed * gated * (1.0 + value * (1.0 - gated)))
        delta[...] = lowered(norm_back(grad * value * gated, normed, scale))

        @pl.when(k + 2 < count)
        def _():
            retained_two.load(k + 2).start()
            swish_two.load(k + 2).start()

        query_acc[...] = jnp.zeros(query_acc.shape, jnp.float32)

        def block(j, carry):
            there = span(j, chunk)
            decay = decay_tile(k, j, chunk, bounds, rate)
            weight = lowered(inner_rows(query[where, :], keys[there, :]) * decay)
            score = lowered(inner_rows(delta[...], values[there, :]) * decay)
            query_acc[...] += matmul(score, keys[there, :])
            key_acc[there, :] += inner_cols(score, query[where, :])
            value_acc[there, :] += inner_cols(weight, delta[...])
            return carry

        lax.fori_loop(0, k + 1, block, 0)
        query[where, :] = lowered(query_acc[...])

    def out_part(k):
        three.free(k, one)
        rows = hidden[span(k, chunk), :]
        mine = pl.ds(pl.multiple_of(k * piece, piece), piece)
        for rank in range(ranks):
            columns = slice(rank * part_width, (rank + 1) * part_width)
            value = matmul(rows, down_w[:, columns])
            for run in range(ranks):
                held = jnp.where(place == run, resid[mine, columns], 0.0)
                three.part[
                    lax.rem(k, 2), rank // 2, rank % 2, :, run * part_width : (run + 1) * part_width
                ] = lowered(value[run * piece : (run + 1) * piece, :] + held)
        pl.semaphore_wait(room.at[0, 0], 1)
        three.start(k)

    def out_finish(k):
        three.finish(k)
        for run in range(ranks):
            where = pl.ds(pl.multiple_of(k * chunk + run * piece, piece), piece)
            mixed[where, :] = lowered(total[:, run * part_width : (run + 1) * part_width])

    def runs_of(ref, columns):
        return jnp.concatenate(
            [ref[j, q, c, :, columns] for j in range(count) for q in range(levels) for c in range(2)], axis=0
        )

    def weigh(which):
        def part(k):
            columns = span(k, chunk)
            if which == 0:
                down = jnp.zeros((hidden.shape[1], part_width), jnp.float32)
                for j in range(count):
                    down += inner_cols(hidden[j * chunk : (j + 1) * chunk, :], dy[j, k // 2, lax.rem(k, 2)])
                there = pl.ds(pl.multiple_of(k * part_width, part_width), part_width)
                down_grad[:, there] = lowered(down)
            else:
                target, source = ((gate_w, gate_grad), (up_w, up_grad))[which - 1]
                target[columns, :] = lowered(inner_cols(runs_of(normed_mid, columns), source[...]))

        in_order(width // chunk, part)
        swap.start(which)

    def weigh_late(which):
        def part(k):
            columns = span(k, chunk)
            if which == 0:
                gate_w[columns, :] = lowered(inner_cols(runs_of(normed_mid, columns), gate_grad[...]))
            elif which == 1:
                out_w[:, columns] = lowered(inner_cols(up_grad[...], runs_of(branch, columns)))
            elif which == 2:
                up_w[columns, :] = lowered(inner_cols(runs_of(normed_mid, columns), values[...]))
            else:
                rows = runs_of(normed_mid, columns)
                down_grad[:qk_dim, columns] = lowered(inner_cols(query[...], rows))
                down_grad[qk_dim:, columns] = lowered(inner_cols(keys[...], rows))

        in_order(width // chunk, part)
        late.start(*((which,) if which < 3 else (3, 4)))

    def units(k):
        slot = lax.rem(k, 2)
        return [
            pltpu.make_async_copy(
                unit_src.at[span(k, chunk)], swish_slots.at[slot, :, pl.ds(0, part_width)], unit_sems.at[0, k]
            ),
            pltpu.make_async_copy(
                scale_src.at[span(k, chunk)], retained_slots.at[slot, :, pl.ds(0, 128)], unit_sems.at[1, k]
            ),
        ]

    def peer_of(j):
        peer = lax.rem(place + j, ranks)
        return (group, peer // 2, lax.rem(peer, 2))

    def sender(j):
        return lax.rem(place + ranks - j, ranks)

    def sums_copy(k, j, owner):
        return pltpu.make_async_remote_copy(
            src_ref=sums.at[owner, k],
            dst_ref=sums.at[owner, k],
            send_sem=sums_sent.at[j - 1, k],
            recv_sem=sums_got.at[j - 1, k],
            device_id=peer_of(j),
            device_id_type=MESH,
        )

    def pack_copy(j, owner):
        return pltpu.make_async_remote_copy(
            src_ref=packed.at[owner],
            dst_ref=packed.at[owner],
            send_sem=gain_sent.at[j - 1],
            recv_sem=gain_got.at[j - 1],
            device_id=peer_of(j),
            device_id_type=MESH,
        )

    def make_room(scatter, turn_of, k):
        scatter.sent(k)
        where = room.at[turn_of]
        pl.semaphore_signal(where.at[0], inc=1, device_id=(group, level, 1 - core), device_id_type=MESH)

        @pl.when(level > 0)
        def _():
            pl.semaphore_signal(where.at[1], inc=1, device_id=(group, level - 1, core), device_id_type=MESH)

        @pl.when(level < levels - 1)
        def _():
            pl.semaphore_signal(where.at[2], inc=1, device_id=(group, level + 1, core), device_id_type=MESH)

    def in_part(k):
        four.free(k, two)
        where = span(k, chunk)
        slot = lax.rem(k, 2)
        rows = [query[where, :], keys[where, :]]
        for source in (values, gate_grad):
            rows += [source[where, n : n + part_width] for n in range(0, v_dim, part_width)]
        first_sum = jnp.zeros((chunk, part_width), jnp.float32)
        second_sum = jnp.zeros((chunk, part_width), jnp.float32)
        for rank in range(ranks):
            columns = slice(rank * part_width, (rank + 1) * part_width)
            value = inner_rows(rows[0], dy[0, rank // 2, rank % 2])
            for n in range(1, len(rows)):
                value += inner_rows(rows[n], dy[n, rank // 2, rank % 2])
            for run in range(ranks):
                four.part[
                    slot, rank // 2, rank % 2, :, run * part_width : (run + 1) * part_width
                ] = lowered(value[run * piece : (run + 1) * piece, :])
            first_sum += value * gain_first[:, columns]
            second_sum += value * wide(normed_mid[k, :, :, :, columns].reshape(chunk, part_width))
        pl.semaphore_wait(room.at[1, 0], 1)
        four.start(k)
        ones = jnp.ones((8, part_width), jnp.float32)
        flat = [
            lax.dot_general(
                ones,
                item,
                (((1,), (1,)), ((), ())),
                precision=lax.Precision.HIGHEST,
                preferred_element_type=jnp.float32,
            )
            for item in (first_sum, second_sum)
        ]
        line = lax.broadcasted_iota(jnp.int32, (8, chunk), 0)
        sums[place, k] = jnp.where(line == 0, flat[0], flat[1])
        for j in range(1, ranks):
            sums_copy(k, j, place).start()

    def in_room(turn_of, wave):
        @pl.when(within(wave - level, count) & (level < levels - 1))
        def _():
            pl.semaphore_wait(room.at[turn_of, 1], 1)

        @pl.when(within(wave - (levels - 1 - level), count) & (level > 0))
        def _():
            pl.semaphore_wait(room.at[turn_of, 2], 1)

    def in_finish(k):
        four.finish(k)
        for j in range(1, ranks):
            sums_copy(k, j, sender(j)).wait_recv()
        line = lax.broadcasted_iota(jnp.int32, (8, 128), 0)
        lane = lax.broadcasted_iota(jnp.int32, (8, 128), 1)
        means = lax.dot_general(
            jnp.sum(sums[:, k], 0),
            jnp.where(line == lane, 1.0 / width, 0.0),
            (((0,), (0,)), ((), ())),
            precision=lax.Precision.HIGHEST,
            preferred_element_type=jnp.float32,
        )
        slot = lax.rem(k, 2)
        for copy in units(k):
            copy.wait()
        mine = pl.ds(pl.multiple_of(place * part_width, part_width), part_width)
        value = jnp.concatenate(
            [total[:, run * part_width : (run + 1) * part_width] for run in range(ranks)], axis=0
        )
        normed = swish_slots[slot, :, :part_width]
        outer = value * normed
        line_one[...] += jnp.sum(outer.reshape(chunk // 8, 8, part_width), 0)
        back = value * gain_first[:, mine] - means[:, :1] - normed * means[:, 1:2]
        upstream = wide(branch[k, :, :, :, mine].reshape(chunk, part_width))
        hidden[span(k, chunk), :part_width] = lowered(upstream + retained_slots[slot, :, :1] * back)

        @pl.when(k + 2 < count)
        def _():
            for copy in units(k + 2):
                copy.start()

    lead = 3
    mid_lag = lead + levels
    turn_lag = mid_lag + levels - 1
    branch_lag = turn_lag + levels
    last_lag = branch_lag + levels - 1
    turned = turn_lag + count
    close_lag = last_lag + count
    out_lag = last_lag - 2

    def at_wave(number, lag, step):
        @pl.when(within(number - lag, count))
        def _():
            step(number - lag)

    def wave(number):
        at_wave(number, lead, first)
        for gather, lag, sent in (
            (branch_gather, branch_lag, functools.partial(make_room, two, 0)),
            (mid_gather, mid_lag, one.sent),
        ):
            at_wave(number, lag + 1, sent)
            for hop in range(levels - 1, 0, -1):
                at_wave(number, lag + hop, functools.partial(hop_on, gather, hop))
        at_wave(number, branch_lag, branch_norm)
        at_wave(number, mid_lag, mid_norm)
        at_wave(number, -1, next_dy)
        for hop in range(levels - 1, 0, -1):
            at_wave(number, hop, functools.partial(hop_on, dy_gather, hop))
        for scatter, lag in ((two, turn_lag), (one, lead)):
            at_wave(number, lag + 1, scatter.join)
            scatter.steps(number - lag - 1)
        for step, relayed, started in ((1, (0,), (1, 2)), (4, (1,), (3,)), (6, (2,), ()), (8, (3,), ())):

            @pl.when(number == step)
            def _():
                spread.relay(*relayed)
                spread.start(*started)

        @pl.when(number == turn_lag)
        def _():
            spread.wait(1, 2, 3)

        at_wave(number, turn_lag, turn)

        @pl.when(number == turn_lag + 1)
        def _():
            retained_one.store(count - 2).wait()
            retained_one.store(count - 1).wait()
            for k in range(2):
                retained_two.load(k).start()
                swish_two.load(k).start()

        @pl.when(number == turned)
        def _():
            spread.drain(*range(4))

        for step, which in ((0, 1), (1, 2), (2, 0)):

            @pl.when(number == turned + step)
            def _():
                weigh(which)

        for step, which in ((2, 1), (4, 2), (6, 0)):

            @pl.when(number == turned + step)
            def _():
                swap.relay(which)

        @pl.when(number == turned + 2)
        def _():
            mid_gather.drain()
            mixed_in_ring.store(count - 2).wait()
            mixed_in_ring.store(count - 1).wait()
            late_loads.start(0, 1)

        @pl.when(number == branch_lag + count)
        def _():
            dy_gather.drain()
            late_loads.start(*range(2, 8))

        at_wave(number, last_lag, last)
        at_wave(number, out_lag, out_part)
        at_wave(number, out_lag + 1, three.join)
        in_room(0, number - out_lag - 1)
        three.steps(number - out_lag - 1)
        at_wave(number, out_lag + levels, out_finish)
        for k in range(count):

            @pl.when(number == out_lag + levels + k)
            def _():
                deal.start(k)

            @pl.when(number == out_lag + levels + k + 2)
            def _():
                deal.relay(k)

        at_wave(number, out_lag + levels + 1, functools.partial(make_room, three, 1))

        @pl.when(number == close_lag)
        def _():
            keys[...] = lowered(key_acc[...])
            values[...] = lowered(value_acc[...])
            for k in range(2):
                for copy in units(k):
                    copy.start()
            late_loads.wait(*range(8))

        for step, before, which in ((0, 1, 0), (1, 0, 1), (2, 2, 2), (3, None, 3)):

            @pl.when(number == close_lag + step)
            def _():
                if before is not None:
                    swap.wait(before)
                weigh_late(which)

        at_wave(number, close_lag, in_part)
        at_wave(number, close_lag + 1, four.join)
        in_room(1, number - close_lag - 1)
        four.steps(number - close_lag - 1)
        at_wave(number, close_lag + levels, in_finish)
        for step, which in ((3, (0,)), (4, (1,)), (5, (2,)), (7, (3, 4))):

            @pl.when(number == close_lag + step)
            def _():
                late.relay(*which)

        for k in range(count):

            @pl.when(number == close_lag + levels + k)
            def _():
                give.start(k)

            @pl.when(number == close_lag + levels + k + 2)
            def _():
                give.relay(k)

    def hop_on(gather, hop, k):
        gather.hop(k, hop)

    def next_dy(k):
        @pl.when(k > 0)
        def _():
            dy_gather.start(k)

    in_order(close_lag + levels + count, wave)
    give.relay(count - 2, count - 1)
    packed[place] = jnp.concatenate(
        [jnp.sum(gain_acc[...], 0, keepdims=True), jnp.sum(line_one[...], 0, keepdims=True)], axis=1
    )
    for j in range(1, ranks):
        pack_copy(j, place).start()
    for j in range(1, ranks):
        pack_copy(j, sender(j)).wait_recv()
    line = lax.broadcasted_iota(jnp.int32, (8, width), 0)
    two_sum = sum(packed[rank, :, :width] for rank in range(ranks))
    one_sum = jnp.concatenate([packed[rank, :, width:] for rank in range(ranks)], axis=1)
    gains[...] = jnp.where(line == 0, one_sum, two_sum)
    small.start(0)
    small.wait(0)
    gains_out[...] = jnp.sum(gains_in[...], 0)
    late.wait(*range(5))
    give.wait(*range(count))
    give.drain(*range(count))
    deal.wait(*range(count))
    deal.drain(*range(count))
    four.drain()
    three.across(count - 2).wait_send()
    three.across(count - 1).wait_send()
    branch_gather.drain()
    for j in range(1, ranks):
        pack_copy(j, place).wait_send()

    def drain(k):
        for j in range(1, ranks):
            sums_copy(k, j, place).wait_send()

    in_order(count, drain)


def finish_kernel(first_seq, last_seq, starts, bases, begins, home, homes, *refs):
    parts, refs = refs[:8], refs[8:]
    mixed_out, grad_out, *refs = refs
    outs, refs = refs[:8], refs[8:]
    homes_held, *refs = refs
    held, sums, refs = refs[:8], refs[8:16], refs[16:]
    picked, load_sems, store_sems = refs
    loads = Moves(list(zip(parts, held)) + [(homes, homes_held)], load_sems)
    stores = Moves(
        list(zip(sums, outs)) + [(picked.at[0], mixed_out), (picked.at[1], grad_out)], store_sems
    )
    loads.start(*range(9))
    for number in range(8):
        loads.wait(number)
        ways, rows, columns = held[number].shape
        run = min(64, rows)
        turned = number < 2

        def block(k):
            where = span(k, run)
            total = wide(held[number][0, where, :])
            for way in range(1, ways):
                total += wide(held[number][way, where, :])
            sums[number][where, :] = total

        def turn(k):
            where = span(k, 128)
            total = wide(held[number][0, :, where])
            for way in range(1, ways):
                total += wide(held[number][way, :, where])
            sums[number][where, :] = total.T

        if turned:
            in_order(columns // 128, turn)
        else:
            in_order(rows // run, block)
        stores.start(number)
    loads.wait(8)
    width = picked.shape[2]
    rows = 128
    window = rows + 16
    lane = lax.broadcasted_iota(jnp.int32, (rows, window), 1)

    def pick_block(k):
        own = home[0] + k * rows + lax.broadcasted_iota(jnp.int32, (rows, 1), 0)

        def one(seq, total):
            start = begins[k, seq]
            inside = (own >= starts[seq]) & (own < starts[seq + 1])
            wanted = jnp.where(inside, own + bases[seq] - 16 * start, -1)
            chosen = jnp.where(lane == wanted, 1.0, 0.0).astype(jnp.bfloat16)
            there = jnp.concatenate([homes_held[start + n] for n in range(window // 16)], axis=0)
            return total + matmul(chosen, there)

        total = lax.fori_loop(
            first_seq[k], last_seq[k] + 1, one, jnp.zeros((rows, 2 * width), jnp.float32)
        )
        where = span(k, rows)
        picked[0, where, :] = lowered(total[:, :width])
        picked[1, where, :] = lowered(total[:, width:])

    in_order(picked.shape[1] // rows, pick_block)
    stores.start(8, 9)
    stores.wait(*range(10))


def column_all(at, sizes):
    group, level, core = at
    return column_peers(at, sizes) + [
        (group, lax.rem(level + k, sizes[1]), 1 - core) for k in range(1, sizes[1])
    ]


def struct(shape, kind=jnp.bfloat16):
    return jax.ShapeDtypeStruct(shape, kind)


VMEM = pltpu.VMEM
DMA = pltpu.SemaphoreType.DMA


def kernel_call(body, number, ins, outs, scratch):
    places = {
        "vmem": pl.BlockSpec(memory_space=pltpu.VMEM),
        "smem": pl.BlockSpec(memory_space=pltpu.SMEM),
        "any": pl.BlockSpec(memory_space=pl.ANY),
    }
    return pl.pallas_call(
        body,
        out_shape=[shape for _, shape in outs],
        in_specs=[places[inside] for inside, _ in ins],
        out_specs=[places[inside] for inside, _ in outs],
        scratch_shapes=scratch,
        compiler_params=pltpu.CompilerParams(
            collective_id=number, has_side_effects=True, vmem_limit_bytes=63 * 2**20
        ),
    )(*[array for _, array in ins])


def spread_shape(shard, axis, sizes):
    shape = list(shard.shape)
    shape[axis] *= sizes[0]
    return struct(tuple(shape), shard.dtype)


def swap_shape(whole, axis, sizes):
    shape = list(whole.shape)
    shape[axis] //= sizes[0]
    return struct((3 if sizes[0] == 4 else sizes[0],) + tuple(shape), whole.dtype)


def anywhere(items):
    return [("any", item) for item in items]


def held_like(arrays):
    return [VMEM(a.shape, a.dtype) for a in arrays]


def pick(rows, whole):
    return whole.at[rows].get(mode="promise_in_bounds")


def shards(
    tokens,
    cotangent,
    lengths,
    dealing,
    w_query,
    w_key,
    w_value,
    w_swish,
    w_out,
    w_gate,
    w_up,
    w_down,
    gain_attn,
    gain_mlp,
):
    group = lax.axis_index("dp")
    place = lax.axis_index(("heads", "tensor"))
    rows_dev = tokens.shape[0]
    slice_width = tokens.shape[1]
    seq_count = lengths.shape[0]
    ident = jnp.arange(seq_count, dtype=jnp.int32)
    starts = jnp.sum(jnp.where(ident[:, None] > ident[None, :], lengths[None, :], 0), 1)
    picked = lax.dynamic_slice_in_dim(dealing, group * SEQ_DEV, SEQ_DEV)
    match = picked[:, None] == ident[None, :]
    dealt_len = jnp.sum(jnp.where(match, lengths[None, :], 0), 1)
    home_start = jnp.sum(jnp.where(match, starts[None, :], 0), 1)
    slots = jnp.arange(SEQ_DEV, dtype=jnp.int32)
    dealt_start = jnp.sum(jnp.where(slots[:, None] > slots[None, :], dealt_len[None, :], 0), 1)
    rows = jnp.arange(rows_dev, dtype=jnp.int32)
    seq_ids = jnp.sum((rows[:, None] >= dealt_start[None, :]).astype(jnp.int32), 1) - 1
    sizes = (lax.axis_size("dp"), lax.axis_size("heads"))
    ranks = sizes[1] * lax.axis_size("tensor")
    chunk = ranks * PIECE
    count = rows_dev // chunk
    width = slice_width * ranks
    own = rows_dev // ranks
    qk_dim, v_dim, ff_dim = w_query.shape[1], w_value.shape[1], w_gate.shape[1]
    f32 = jnp.float32
    masters = (w_query, w_key, w_value, w_swish, w_out, w_gate, w_up, w_down)
    axes = (0, 0, 0, 0, 1, 0, 0, 1)
    gain_rows = struct((8, gain_attn.shape[0]), f32)
    shifts = home_start - dealt_start
    firsts = jnp.arange(2 * count, dtype=jnp.int32) * (chunk // 2)
    begins = jnp.clip(firsts[:, None] + shifts[None, :], 0, sizes[0] * rows_dev - chunk) // 16
    bf16 = jnp.bfloat16
    rounded = [struct(w.shape) for w in masters]
    full_w = [spread_shape(w, a, sizes) for w, a in zip(rounded, axes)]
    by_runs = struct((rows_dev // 16, 16, slice_width))
    every = spread_shape(by_runs, 0, sizes)
    gains_all = struct((sizes[0] * 8, gain_rows.shape[1]), f32)
    (
        normed_in,
        query,
        keys,
        values,
        swish_in,
        dy_part,
        query_w,
        key_w,
        value_w,
        swish_w,
        *low,
        wide_one,
        wide_two,
        x_rows,
        unit_share,
        scale_one,
    ) = kernel_call(
        functools.partial(front_kernel, sizes),
        0,
        [("smem", dealt_start), ("smem", shifts), ("smem", begins.reshape(-1))]
        + anywhere((tokens.reshape(by_runs.shape), cotangent.reshape(by_runs.shape)))
        + [("vmem", gain_attn.reshape(1, -1)), ("vmem", gain_mlp.reshape(1, -1))]
        + anywhere(masters),
        anywhere(
            [
                struct((rows_dev, width)),
                struct((rows_dev, qk_dim)),
                struct((rows_dev, qk_dim)),
                struct((rows_dev, v_dim)),
                struct((rows_dev, v_dim), f32),
                struct((count, chunk, slice_width)),
            ]
            + full_w[:4]
            + rounded[4:]
        )
        + [
            ("vmem", struct((1, width), f32)),
            ("vmem", struct((1, width), f32)),
            ("vmem", struct((own, width))),
            ("vmem", struct((rows_dev, slice_width), f32)),
            ("vmem", struct((rows_dev, 128), f32)),
        ],
        Gather.scratch(count, sizes, (chunk, slice_width))
        + Spread.scratch(12, sizes)
        + Spread.scratch(1, sizes)
        + held_like(masters)
        + held_like(rounded)
        + held_like(full_w[:4])
        + held_like((by_runs, by_runs, gain_rows, every, every, gains_all))
        + [
            VMEM((count, chunk, slice_width), bf16),
            VMEM((rows_dev, width), bf16),
            VMEM((rows_dev, qk_dim), bf16),
            VMEM((rows_dev, qk_dim), bf16),
            VMEM((rows_dev, v_dim), bf16),
            VMEM((rows_dev, v_dim), f32),
            DMA((10,)),
            DMA((4,)),
            DMA((9,)),
            DMA((count,)),
        ],
    )
    rate = jnp.log1p(-jnp.exp2(-5.0 - place.astype(f32))).reshape(1)
    by_rows = (PIECE, width)
    pieces = (count, sizes[1], 2) + by_rows
    blocks = (sizes[1], 2, slice_width)
    late_w = [struct(shape) for shape in ((width, v_dim), (v_dim, width), (width, v_dim), (qk_dim, width))]
    late_w.append(late_w[3])
    late_axes = (0, 1, 0, 1, 1)
    core_outs = kernel_call(
        functools.partial(core_kernel, sizes),
        1,
        [("smem", dealt_start), ("smem", rate), ("vmem", wide_two), ("vmem", wide_one)]
        + anywhere((query, keys, values, x_rows, dy_part, swish_in))
        + anywhere((normed_in.reshape(pieces), unit_share, scale_one))
        + anywhere([w.reshape(blocks + w.shape[1:]) for w in (query_w, key_w, value_w, swish_w)])
        + anywhere(low),
        anywhere([struct((rows_dev, v_dim)), struct((rows_dev, v_dim), f32)])
        + [("vmem", struct((8, gain_attn.shape[0]), f32))]
        + anywhere(
            [
                struct((sizes[0] * rows_dev, 2 * slice_width)),
                swap_shape(full_w[7], 1, sizes),
                swap_shape(full_w[5], 0, sizes),
                swap_shape(full_w[6], 0, sizes),
            ]
            + [swap_shape(w, a, sizes) for w, a in zip(late_w, late_axes)]
        ),
        held_like((query, keys, values, x_rows))
        + held_like(full_w[4:])
        + Scatter.rooms(count, sizes, by_rows)
        + Scatter.rooms(count, sizes, by_rows)[:1]
        + Scatter.sems(count, sizes) * 4
        + Gather.scratch(count, sizes, by_rows)
        + Gather.scratch(count, sizes, (chunk, slice_width))
        + Gather.scratch(count, sizes, by_rows)
        + Spread.scratch(4, sizes)
        + Spread.scratch(count, sizes)
        + Swap.scratch(3, sizes)
        + Swap.scratch(5, sizes)
        + Swap.scratch(1, sizes)
        + Spread.scratch(count, sizes)
        + [
            VMEM((rows_dev, ff_dim), bf16),
            VMEM((rows_dev, ff_dim), bf16),
            VMEM((rows_dev, ff_dim), bf16),
            VMEM((own, width), f32),
            VMEM((2, chunk, v_dim), f32),
            VMEM((2, chunk, v_dim), f32),
            VMEM((2, chunk, v_dim), bf16),
            VMEM((rows_dev, qk_dim), f32),
            VMEM((rows_dev, v_dim), f32),
            VMEM((chunk, qk_dim), f32),
            VMEM((chunk, v_dim), bf16),
            VMEM((ff_dim, width), bf16),
            VMEM((rows_dev, slice_width), bf16),
            VMEM((8, width), f32),
            VMEM((ranks, count, 8, chunk), f32),
            VMEM((8, slice_width), f32),
            VMEM((ranks, 1, width + slice_width), f32),
            VMEM((8, width), f32),
            VMEM((sizes[0], 8, gain_attn.shape[0]), f32),
            DMA((5,)),
            DMA((5, count)),
            DMA((8,)),
            DMA((2, count)),
            pltpu.SemaphoreType.REGULAR((2, 3)),
            DMA((ranks - 1, count)),
            DMA((ranks - 1, count)),
            DMA((ranks - 1,)),
            DMA((ranks - 1,)),
        ]
        + half_blocks([(full_w[7], 1), (full_w[5], 0), (full_w[6], 0)], sizes)
        + half_blocks(list(zip(late_w, late_axes))[3:], sizes),
    )
    _, _, gains, homes, *parts = core_outs
    slot_match = dealing[:, None] == ident[None, :]
    slot_len = jnp.sum(jnp.where(slot_match, lengths[None, :], 0), 1)
    slot_home = jnp.sum(jnp.where(slot_match, starts[None, :], 0), 1)
    per_group = slot_len.reshape(-1, SEQ_DEV)
    slot_start = (jnp.cumsum(per_group, 1) - per_group).reshape(-1)
    slot_base = ident // SEQ_DEV * rows_dev + slot_start - slot_home
    owner_base = jnp.sum(jnp.where(dealing[None, :] == ident[:, None], slot_base[None, :], 0), 1)
    blocks_at = group * rows_dev + jnp.arange(rows_dev // 128, dtype=jnp.int32) * 128
    first_seq = jnp.sum((blocks_at[:, None] >= starts[None, :]).astype(jnp.int32), 1) - 1
    last_seq = jnp.sum((blocks_at[:, None] + 127 >= starts[None, :]).astype(jnp.int32), 1) - 1
    total_rows = sizes[0] * rows_dev
    home_begins = jnp.clip(blocks_at[:, None] + owner_base[None, :], 0, total_rows - 144) // 16
    all_starts = jnp.concatenate([starts, jnp.full((1,), total_rows, jnp.int32)])
    homes = homes.reshape(total_rows // 16, 16, 2 * slice_width)
    order = [parts[n] for n in (6, 7, 5, 3, 4, 1, 2, 0)]
    owners = (w_query, w_key, w_value, w_swish, w_out, w_gate, w_up, w_down)
    finals = [struct(w.shape, f32) for w in owners]
    picks = struct((2, rows_dev, slice_width))
    one_place = {"smem": pl.BlockSpec(memory_space=pltpu.SMEM), "any": pl.BlockSpec(memory_space=pl.ANY)}
    mixed_rows, grad_rows, *grads = pl.pallas_call(
        finish_kernel,
        out_shape=[struct((rows_dev, slice_width))] * 2 + finals,
        in_specs=[one_place["smem"]] * 6 + [one_place["any"]] * 9,
        out_specs=[one_place["any"]] * 10,
        scratch_shapes=held_like([homes] + order + finals + [picks]) + [DMA((9,)), DMA((10,))],
        compiler_params=pltpu.CompilerParams(vmem_limit_bytes=60 * 2**20),
    )(first_seq, last_seq, all_starts, owner_base, home_begins, blocks_at[:1], homes, *order)
    return (
        mixed_rows,
        grad_rows,
        grads[0],
        grads[1],
        grads[2],
        grads[3],
        grads[4],
        grads[5],
        grads[6],
        grads[7],
        gains[0],
        gains[1],
    )


def solution(mesh):
    in_specs = (
        P("dp", ("heads", "tensor")),
        P("dp", ("heads", "tensor")),
        P(),
        P(),
        P("dp", ("heads", "tensor")),
        P("dp", ("heads", "tensor")),
        P("dp", ("heads", "tensor")),
        P("dp", ("heads", "tensor")),
        P(("heads", "tensor"), "dp"),
        P("dp", ("heads", "tensor")),
        P("dp", ("heads", "tensor")),
        P(("heads", "tensor"), "dp"),
        P("dp"),
        P("dp"),
    )
    out_specs = (
        P("dp", ("heads", "tensor")),
        P("dp", ("heads", "tensor")),
        P("dp", ("heads", "tensor")),
        P("dp", ("heads", "tensor")),
        P("dp", ("heads", "tensor")),
        P("dp", ("heads", "tensor")),
        P(("heads", "tensor"), "dp"),
        P("dp", ("heads", "tensor")),
        P("dp", ("heads", "tensor")),
        P(("heads", "tensor"), "dp"),
        P("dp"),
        P("dp"),
    )
    return jax.shard_map(shards, mesh=mesh, in_specs=in_specs, out_specs=out_specs, check_vma=False)
```

```python
import functools

import jax
import jax.numpy as jnp
from jax import lax
from jax.experimental import pallas as pl
from jax.experimental.pallas import tpu as pltpu
from jax.sharding import PartitionSpec as P

QK_DIM = 256
SEQ_DEV = 3
PIECE = 32
AXES = ("dp", "heads", "tensor")
MESH = pl.DeviceIdType.MESH


EPSILON = 1e-05
GROUP_EPS = 1.0


def layer_norm(values, epsilon):
    center = values - jnp.mean(values, -1, keepdims=True)
    scale = lax.rsqrt(jnp.mean(center * center, -1, keepdims=True) + epsilon)
    return (center * scale, scale)


def norm_back(grad, normed, scale):
    return scale * (
        grad
        - jnp.mean(grad, -1, keepdims=True)
        - normed * jnp.mean(grad * normed, -1, keepdims=True)
    )


def product(left, right):
    return jnp.dot(left, right, preferred_element_type=jnp.float32)


def inner_rows(left, right):
    return lax.dot_general(
        left, right, (((1,), (1,)), ((), ())), preferred_element_type=jnp.float32
    )


def inner_cols(left, right):
    return lax.dot_general(
        left, right, (((0,), (0,)), ((), ())), preferred_element_type=jnp.float32
    )


def lowered(value):
    return value.astype(jnp.bfloat16)


def around(axes):
    return tuple(lax.axis_index(name) for name in axes)


def wide(value):
    return value.astype(jnp.float32)


def within(number, count):
    return (number >= 0) & (number < count)


def greet(others):
    barrier = pltpu.get_barrier_semaphore()
    for other in others:
        pl.semaphore_signal(barrier, inc=1, device_id=other, device_id_type=MESH)
    pl.semaphore_wait(barrier, len(others))


def plane_peers(at, sizes):
    group, level, core = at
    return [(lax.rem(group + k, sizes[0]), level, core) for k in range(1, sizes[0])]


def column_peers(at, sizes):
    group, level, core = at
    return [(group, lax.rem(level + k, sizes[1]), core) for k in range(1, sizes[1])] + [
        (group, level, 1 - core)
    ]


def beside(group):
    return group + 1 - 2 * lax.rem(group, 2), lax.rem(group + 2, 4), 3 - group


class Spread:
    def __init__(self, at, sizes, items, sems, relay=True):
        self.at, self.count, self.items = at, sizes[0], items
        self.local, self.sent, self.got = sems
        self.plane = relay and sizes[0] == 4

    @staticmethod
    def scratch(items, sizes):
        ways = max(4, sizes[0] - 1)
        return [
            pltpu.SemaphoreType.DMA((items,)),
            pltpu.SemaphoreType.DMA((items, ways)),
            pltpu.SemaphoreType.DMA((items, ways)),
        ]

    def place(self, number, owner, half=None):
        source, target, axis, *where = self.items[number]
        rows = source.shape[0]
        size = source.shape[axis]
        step, offset = where or (size, 0)
        start = owner * step + offset
        if half is None:
            begin, height = 0, rows
        else:
            begin, height = half * (rows // 2), rows // 2
        if axis == 0:
            return target.at[pl.ds(pl.multiple_of(start + begin, height), height)]
        return target.at[pl.ds(begin, height), pl.ds(pl.multiple_of(start, size), size)]

    def own(self, number):
        return pltpu.make_async_copy(
            self.items[number][0], self.place(number, self.at[0]), self.local.at[number]
        )

    def copy(self, number, source, place, way, peer):
        return pltpu.make_async_remote_copy(
            src_ref=source,
            dst_ref=place,
            send_sem=self.sent.at[number, way],
            recv_sem=self.got.at[number, way],
            device_id=(peer,) + self.at[1:],
            device_id_type=MESH,
        )

    def away(self, number, k):
        peer = lax.rem(self.at[0] + k, self.count)
        return self.copy(number, self.items[number][0], self.place(number, self.at[0]), k - 1, peer)

    def landed(self, number, k):
        owner = lax.rem(self.at[0] + self.count - k, self.count)
        return self.copy(number, self.items[number][0], self.place(number, owner), k - 1, owner)

    def to(self, number, way):
        peer = beside(self.at[0])[way]
        return self.copy(number, self.items[number][0], self.place(number, self.at[0]), way, peer)

    def of(self, number, way):
        peer = beside(self.at[0])[way]
        return self.copy(number, self.items[number][0], self.place(number, peer), way, peer)

    def on(self, number, way):
        near = beside(self.at[0])
        ref = self.place(number, near[way], way)
        return self.copy(number, ref, ref, 2 + way, near[1 - way])

    def last(self, number, way):
        near = beside(self.at[0])
        ref = self.place(number, near[2], way)
        return self.copy(number, ref, ref, 2 + way, near[1 - way])

    def start(self, *numbers):
        for number in numbers:
            if self.plane:
                self.to(number, 0).start()
                self.to(number, 1).start()
            else:
                for k in range(1, self.count):
                    self.away(number, k).start()
            self.own(number).start()

    def relay(self, *numbers):
        if self.plane:
            for number in numbers:
                for way in range(2):
                    self.of(number, way).wait_recv()
                    self.on(number, way).start()

    def wait(self, *numbers):
        for number in numbers:
            self.own(number).wait()
            if self.plane:
                self.last(number, 0).wait_recv()
                self.last(number, 1).wait_recv()
            else:
                for k in range(1, self.count):
                    self.landed(number, k).wait_recv()

    def drain(self, *numbers):
        for number in numbers:
            if self.plane:
                for way in range(2):
                    self.to(number, way).wait_send()
                    self.on(number, way).wait_send()
            else:
                for k in range(1, self.count):
                    self.away(number, k).wait_send()


class Gather:
    def __init__(self, at, sizes, count, full, sems):
        self.at, self.levels, self.count, self.full = at, sizes[1], count, full
        self.sent_up, self.got_up, self.sent_down, self.got_down, self.sent_core, self.got_core = sems

    @staticmethod
    def scratch(count, sizes, piece):
        levels = sizes[1]
        dma = pltpu.SemaphoreType.DMA
        return [pltpu.VMEM((count, levels, 2) + piece, jnp.bfloat16)] + [
            dma((levels - 1, count)) for _ in range(4)
        ] + [dma((2 * levels - 1, count)) for _ in range(2)]

    def copy(self, ref, sent, got, target):
        return pltpu.make_async_remote_copy(
            src_ref=ref, dst_ref=ref, send_sem=sent, recv_sem=got, device_id=target, device_id_type=MESH
        )

    def up(self, k, hop, origin, sem):
        group, level, core = self.at
        target = (group, lax.rem(level + 1, self.levels), core)
        return self.copy(self.full.at[k, origin, core], self.sent_up.at[sem, k], self.got_up.at[sem, k], target)

    def down(self, k, hop, origin, sem):
        group, level, core = self.at
        target = (group, lax.rem(level + self.levels - 1, self.levels), core)
        return self.copy(
            self.full.at[k, origin, core], self.sent_down.at[sem, k], self.got_down.at[sem, k], target
        )

    def across(self, k, origin, side, sem):
        group, level, core = self.at
        return self.copy(
            self.full.at[k, origin, side], self.sent_core.at[sem, k], self.got_core.at[sem, k], (group, level, 1 - core)
        )

    def start(self, k):
        group, level, core = self.at

        @pl.when(level < self.levels - 1)
        def _():
            self.up(k, 0, level, 0).start()

        @pl.when(level > 0)
        def _():
            self.down(k, 0, level, 0).start()

        self.across(k, level, core, 0).start()

    def hop(self, k, hop):
        group, level, core = self.at
        last = self.levels - 1

        @pl.when(level >= hop)
        def _():
            origin = level - hop
            self.up(k, hop, origin, hop - 1).wait_recv()
            if hop < last:

                @pl.when(level < last)
                def _():
                    self.up(k, hop, origin, hop).start()

            self.across(k, origin, core, hop).start()

        @pl.when(level + hop <= last)
        def _():
            origin = level + hop
            self.down(k, hop, origin, hop - 1).wait_recv()
            if hop < last:

                @pl.when(level > 0)
                def _():
                    self.down(k, hop, origin, hop).start()

            self.across(k, origin, core, last + hop).start()

    def ready(self, k):
        group, level, core = self.at
        last = self.levels - 1
        self.across(k, level, 1 - core, 0).wait_recv()
        for hop in range(1, self.levels):

            @pl.when(level >= hop)
            def _():
                self.across(k, level - hop, 1 - core, hop).wait_recv()

            @pl.when(level + hop <= last)
            def _():
                self.across(k, level + hop, 1 - core, last + hop).wait_recv()

    def drain(self):
        group, level, core = self.at
        last = self.levels - 1

        def one(k, _):
            self.across(k, level, core, 0).wait_send()
            for hop in range(self.levels):
                if hop < last:

                    @pl.when((level >= hop) & (level < last))
                    def _():
                        self.up(k, hop, level - hop, hop).wait_send()

                    @pl.when((level + hop <= last) & (level > 0))
                    def _():
                        self.down(k, hop, level + hop, hop).wait_send()

                if hop > 0:

                    @pl.when(level >= hop)
                    def _():
                        self.across(k, level - hop, core, hop).wait_send()

                    @pl.when(level + hop <= last)
                    def _():
                        self.across(k, level + hop, core, last + hop).wait_send()

            return 0

        lax.fori_loop(0, self.count, one, 0)


class Scatter:
    REFS = 4

    def __init__(self, at, sizes, count, refs):
        self.at, self.levels, self.count = at, sizes[1], count
        self.part, self.cross, self.inbox, self.total = refs[:4]
        self.sent_core, self.got_core, self.sent_up, self.got_up, self.sent_down, self.got_down = refs[4:]

    @staticmethod
    def rooms(count, sizes, piece):
        levels = sizes[1]
        return [
            pltpu.VMEM((2, levels, 2) + piece, jnp.bfloat16),
            pltpu.VMEM((count, levels) + piece, jnp.bfloat16),
            pltpu.VMEM((count, levels + 1) + piece, jnp.bfloat16),
            pltpu.VMEM(piece, jnp.float32),
        ]

    @staticmethod
    def sems(count, sizes):
        dma = pltpu.SemaphoreType.DMA
        return [dma((count,)) for _ in range(2)] + [dma((sizes[1], count)) for _ in range(4)]

    @staticmethod
    def scratch(count, sizes, piece):
        return Scatter.rooms(count, sizes, piece) + Scatter.sems(count, sizes)

    def across(self, k):
        group, level, core = self.at
        return pltpu.make_async_remote_copy(
            src_ref=self.part.at[lax.rem(k, 2), :, 1 - core],
            dst_ref=self.cross.at[k],
            send_sem=self.sent_core.at[k],
            recv_sem=self.got_core.at[k],
            device_id=(group, level, 1 - core),
            device_id_type=MESH,
        )

    def up(self, k, owner):
        group, level, core = self.at
        return pltpu.make_async_remote_copy(
            src_ref=self.cross.at[k, owner],
            dst_ref=self.inbox.at[k, owner + 1],
            send_sem=self.sent_up.at[owner, k],
            recv_sem=self.got_up.at[owner, k],
            device_id=(group, lax.rem(level + 1, self.levels), core),
            device_id_type=MESH,
        )

    def down(self, k, owner):
        group, level, core = self.at
        return pltpu.make_async_remote_copy(
            src_ref=self.cross.at[k, owner],
            dst_ref=self.inbox.at[k, owner],
            send_sem=self.sent_down.at[owner, k],
            recv_sem=self.got_down.at[owner, k],
            device_id=(group, lax.rem(level + self.levels - 1, self.levels), core),
            device_id_type=MESH,
        )

    def free(self, k, before=None):
        @pl.when(k >= 2)
        def _():
            self.across(k - 2).wait_send()

        if before is not None:

            @pl.when(k < 2)
            def _():
                before.across(self.count - 2 + k).wait_send()

    def start(self, k):
        self.across(k).start()

    def join(self, k):
        core = self.at[2]
        self.across(k).wait_recv()
        for owner in range(self.levels):
            self.cross[k, owner] = lowered(
                wide(self.part[lax.rem(k, 2), owner, core]) + wide(self.cross[k, owner])
            )

    def step_up(self, k):
        level = self.at[1]
        for owner in range(self.levels - 1, 0, -1):

            @pl.when(level < owner)
            def _():
                @pl.when(level > 0)
                def _():
                    self.up(k, owner).wait_recv()
                    self.cross[k, owner] = lowered(wide(self.cross[k, owner]) + wide(self.inbox[k, owner + 1]))

                self.up(k, owner).start()

    def step_down(self, k):
        level = self.at[1]
        for owner in range(self.levels - 1):

            @pl.when(level > owner)
            def _():
                @pl.when(level < self.levels - 1)
                def _():
                    self.down(k, owner).wait_recv()
                    self.cross[k, owner] = lowered(wide(self.cross[k, owner]) + wide(self.inbox[k, owner]))

                self.down(k, owner).start()

    def steps(self, wave):
        level = self.at[1]
        above = wave - level
        below = wave - (self.levels - 1 - level)

        @pl.when(within(above, self.count) & (level < self.levels // 2))
        def _():
            self.step_up(above)

        @pl.when(within(below, self.count))
        def _():
            self.step_down(below)

        @pl.when(within(above, self.count) & (level >= self.levels // 2))
        def _():
            self.step_up(above)

    def finish(self, k):
        level = self.at[1]
        self.total[...] = wide(self.cross[k, level])

        @pl.when(level > 0)
        def _():
            self.up(k, level).wait_recv()
            self.total[...] += wide(self.inbox[k, level + 1])

        @pl.when(level < self.levels - 1)
        def _():
            self.down(k, level).wait_recv()
            self.total[...] += wide(self.inbox[k, level])

    def sent(self, k):
        level = self.at[1]
        for owner in range(self.levels):

            @pl.when(level < owner)
            def _():
                self.up(k, owner).wait_send()

            @pl.when(level > owner)
            def _():
                self.down(k, owner).wait_send()

    def drain(self):
        self.across(self.count - 2).wait_send()
        self.across(self.count - 1).wait_send()
        in_order(self.count, self.sent)


def in_order(count, step):
    def body(number, carry):
        step(number)
        return carry

    lax.fori_loop(0, count, body, 0)


def span(number, size):
    return pl.ds(pl.multiple_of(number * size, size), size)


class Moves:
    def __init__(self, pairs, sems):
        self.pairs, self.sems = pairs, sems

    def copy(self, number):
        return pltpu.make_async_copy(*self.pairs[number], self.sems.at[number])

    def start(self, *numbers):
        for number in numbers:
            self.copy(number).start()

    def wait(self, *numbers):
        for number in numbers:
            self.copy(number).wait()


class Chunks:
    def __init__(self, pairs, size, sems):
        self.pairs, self.size, self.sems = pairs, size, sems

    def start(self, k):
        for number, (source, target) in enumerate(self.pairs):
            rows = span(k, self.size)
            pltpu.make_async_copy(source.at[rows], target.at[rows], self.sems.at[number, k]).start()

    def wait(self, count):
        def one(k, carry):
            for number, (source, target) in enumerate(self.pairs):
                rows = span(k, self.size)
                pltpu.make_async_copy(source.at[rows], target.at[rows], self.sems.at[number, k]).wait()
            return carry

        lax.fori_loop(0, count, one, 0)


def matmul(left, right):
    return jnp.dot(left, right, preferred_element_type=jnp.float32)


def decay_tile(near, far, size, bounds, rate):
    rows = near * size + lax.broadcasted_iota(jnp.int32, (size, 1), 0)
    columns = far * size + lax.broadcasted_iota(jnp.int32, (1, size), 1)
    row_seq, column_seq = jnp.zeros((size, 1), jnp.int32), jnp.zeros((1, size), jnp.int32)
    for number in range(1, SEQ_DEV):
        row_seq += (rows >= bounds[number]).astype(jnp.int32)
        column_seq += (columns >= bounds[number]).astype(jnp.int32)
    distance = rows - columns
    valid = (distance >= 0) & (row_seq == column_seq)
    return (
        jnp.where(valid, jnp.exp(jnp.maximum(distance, 0).astype(jnp.float32) * rate[0]), 0.0)
        * QK_DIM ** (-0.5)
    )


class Swap:
    def __init__(self, at, sizes, items, sems, halves=None):
        self.at, self.count, self.items = at, sizes[0], items
        self.local, self.sent, self.got = sems
        self.halves = halves
        self.plane = halves is not None and sizes[0] == 4

    @staticmethod
    def scratch(items, sizes):
        ways = max(6, sizes[0] - 1)
        return [
            pltpu.SemaphoreType.DMA((items,)),
            pltpu.SemaphoreType.DMA((items, ways)),
            pltpu.SemaphoreType.DMA((items, ways)),
        ]

    def block(self, number, owner, half=None):
        source, target, axis = self.items[number]
        rows = source.shape[0]
        size = source.shape[axis] // self.count
        height = size if axis == 0 else rows
        begin = 0
        if half is not None:
            height //= 2
            begin = half * height
        if axis == 0:
            return source.at[pl.ds(pl.multiple_of(owner * size + begin, height), height)]
        return source.at[pl.ds(begin, height), pl.ds(pl.multiple_of(owner * size, size), size)]

    def half(self, number, slot, half):
        target = self.items[number][1]
        height = target.shape[1] // 2
        return target.at[slot, pl.ds(half * height, height)]

    def copy(self, number, source, place, way, peer):
        return pltpu.make_async_remote_copy(
            src_ref=source,
            dst_ref=place,
            send_sem=self.sent.at[number, way],
            recv_sem=self.got.at[number, way],
            device_id=(peer,) + self.at[1:],
            device_id_type=MESH,
        )

    def own(self, number):
        return pltpu.make_async_copy(
            self.block(number, self.at[0]), self.items[number][1].at[0], self.local.at[number]
        )

    def away(self, number, k):
        peer = lax.rem(self.at[0] + k, self.count)
        return self.copy(number, self.block(number, peer), self.items[number][1].at[k], k - 1, peer)

    def across(self, number, way):
        near = beside(self.at[0])
        return self.copy(
            number, self.block(number, near[2], way), self.halves[number].at[way], way, near[way]
        )

    def direct(self, number, way):
        near = beside(self.at[0])
        return self.copy(
            number, self.block(number, near[way], way), self.half(number, 1 + way, way), 2 + way, near[way]
        )

    def added(self, number, way):
        peer = beside(self.at[0])[1 - way]
        return self.copy(
            number, self.block(number, peer, way), self.half(number, 2 - way, way), 4 + way, peer
        )

    def start(self, *numbers):
        for number in numbers:
            if self.plane:
                for way in range(2):
                    self.across(number, way).start()
                for way in range(2):
                    self.direct(number, way).start()
            else:
                for k in range(1, self.count):
                    self.away(number, k).start()
            self.own(number).start()

    def relay(self, *numbers):
        if self.plane:
            near = beside(self.at[0])
            for number in numbers:
                for way in range(2):
                    self.across(number, way).wait_recv()
                    part = self.block(number, near[1 - way], way)
                    part[...] = lowered(wide(part[...]) + wide(self.halves[number][way]))
                for way in range(2):
                    self.added(number, way).start()

    def wait(self, *numbers):
        for number in numbers:
            self.own(number).wait()
            if self.plane:
                for way in range(2):
                    self.across(number, way).wait_send()
                    self.direct(number, way).wait()
                    self.added(number, way).wait()
            else:
                for k in range(1, self.count):
                    self.away(number, k).wait()


def half_blocks(items, sizes):
    room = []
    for whole, axis in items:
        shape = list(whole.shape)
        shape[axis] //= sizes[0]
        room.append(pltpu.VMEM((2, shape[0] // 2, shape[1]), jnp.bfloat16))
    return room


def quarters(source, target):
    rows = source.shape[0]
    run = rows // 4
    return [(source.at[pl.ds(k * run, run)], target, 0, rows, k * run) for k in range(4)]


def pick_rows(whole, number, first, rows, bounds, shifts, begins):
    window = 2 * rows
    lane = lax.broadcasted_iota(jnp.int32, (rows, window), 1)
    slot = jnp.zeros((rows, 1), jnp.int32)
    own = first + lax.broadcasted_iota(jnp.int32, (rows, 1), 0)
    for item in range(1, SEQ_DEV):
        slot += (own >= bounds[item]).astype(jnp.int32)
    chosen, windows = [], []
    for item in range(SEQ_DEV):
        start = begins[number * SEQ_DEV + item]
        wanted = jnp.where(slot == item, own + shifts[item] - 16 * start, -1)
        chosen.append(jnp.where(lane == wanted, 1.0, 0.0).astype(jnp.bfloat16))
        windows += [whole[start + k] for k in range(window // 16)]
    return lowered(matmul(jnp.concatenate(chosen, axis=1), jnp.concatenate(windows, axis=0)))


def front_kernel(sizes, bounds, shifts, begins, tokens, cotangent, gain_attn, gain_mlp, *refs):
    masters, refs = refs[:8], refs[8:]
    normed_out, query_out, key_out, value_out, swish_out, dy_out, *refs = refs
    weight_outs, rounded_outs, refs = refs[:4], refs[4:8], refs[8:]
    gain_one, gain_two, rows_out, unit_out, scale_out, *refs = refs
    full, *refs = refs
    gather_sems, refs = refs[:6], refs[6:]
    spread_sems, small_sems, refs = refs[:3], refs[3:6], refs[6:]
    held, rounded, weights, refs = refs[:8], refs[8:16], refs[16:20], refs[20:]
    tokens_held, dy_held, gains_held, tokens_all, dy_all, gains_all, dy_part, *refs = refs
    normed, query, keys, values, swish, load_sems, store_sems, out_sems, normed_sem = refs
    at = around(AXES)
    group, level, core = at
    place = 2 * level + core
    count, levels, _, chunk, width = full.shape
    ranks = 2 * levels
    piece = chunk // ranks
    loads = Moves(
        list(zip(masters, held)) + [(tokens, tokens_held), (cotangent, dy_held)], load_sems
    )
    loads.start(8, 2, 3, 1, 0, 9, 4, 5, 6, 7)
    gains_held[...] = jnp.zeros(gains_held.shape, jnp.float32)
    gains_held[0:1, :] = gain_attn[...]
    gains_held[1:2, :] = gain_mlp[...]
    greet(plane_peers(at, sizes) + column_peers(at, sizes))
    loads.wait(8)
    spread = Spread(
        at,
        sizes,
        quarters(tokens_held, tokens_all)
        + [(rounded[number], weights[number], 0) for number in (2, 3, 1, 0)]
        + quarters(dy_held, dy_all),
        spread_sems,
    )
    small = Spread(at, sizes, [(gains_held, gains_all, 0)], small_sems, relay=False)
    spread.start(*range(4))
    small.start(0)
    gather = Gather(at, sizes, count, full, gather_sems)

    def cast(number):
        loads.wait(number)
        rows = min(32, held[number].shape[0])

        def block(k):
            held_rows = span(k, rows)
            rounded[number][held_rows, :] = lowered(held[number][held_rows, :])

        in_order(held[number].shape[0] // rows, block)

    stores = Moves(list(zip(rounded[4:], rounded_outs)), store_sems)
    cast(2)
    spread.start(4)
    for number in (3, 1, 0, 4, 5, 6, 7):
        cast(number)
    loads.wait(9)
    stores.start(*range(4))
    for number in range(4):
        spread.relay(number)
    spread.start(5, 6, 7)
    small.wait(0)
    own = gains_held.shape[0]
    for row, gain in enumerate((gain_one, gain_two)):
        gain[...] = wide(
            lowered(
                jnp.concatenate([gains_all[own * k + row : own * k + row + 1, :] for k in range(sizes[0])], axis=1)
            )
        )
    spread.wait(*range(4))
    run = chunk // 2

    def pick_chunk(whole, k, half):
        return pick_rows(whole, 2 * k + half, k * chunk + half * run, run, bounds, shifts, begins)

    def begin(k):
        for half in range(2):
            full[k, level, core, half * run : (half + 1) * run, :] = pick_chunk(tokens_all, k, half)
        gather.start(k)

    def norm(k):
        def block(number, carry):
            rows = span(number, 16)
            value = jnp.concatenate(
                [wide(full[k, q, c, rows, :]) for q in range(levels) for c in range(2)], axis=1
            )
            unit, scale = layer_norm(value, EPSILON)
            where = pl.ds(pl.multiple_of(k * chunk + number * 16, 16), 16)
            normed[where, :] = lowered(unit * gain_one[...])
            mine = wide(full[k, level, core, rows, :])
            mean = jnp.mean(value, -1, keepdims=True)
            unit_out[where, :] = (mine - mean) * scale
            scale_out[where, :] = jnp.broadcast_to(scale, (16, 128))
            return carry

        lax.fori_loop(0, chunk // 16, block, 0)
        mine = span(place, piece)
        rows_out[span(k, piece), :] = jnp.concatenate(
            [full[k, q, c, mine, :] for q in range(levels) for c in range(2)], axis=1
        )
        pltpu.make_async_copy(
            normed.at[span(k, chunk)], normed_out.at[span(k, chunk)], normed_sem.at[k]
        ).start()

    begin(0)
    outs = [(query, query_out), (keys, key_out), (values, value_out), (swish, swish_out)]
    ends = Moves(outs + list(zip(weights, weight_outs)) + [(dy_part, dy_out)], out_sems)

    def project_rows(number, k):
        where = span(k, chunk)
        target = outs[number][0]
        target[where, :] = matmul(normed[where, :], weights[number][...]).astype(target.dtype)

    def wave(number):
        @pl.when(number + 1 < count)
        def _():
            begin(number + 1)

        for hop in range(levels - 1, 0, -1):

            @pl.when(within(number - hop, count))
            def _():
                gather.hop(number - hop, hop)

        for step, relayed, started in (
            (1, (4,), (8, 9)),
            (3, (5,), (10, 11)),
            (4, (6,), ()),
            (5, (7,), ()),
            (7, (8, 9), ()),
            (9, (10,), ()),
        ):

            @pl.when(number == step)
            def _():
                spread.relay(*relayed)
                spread.start(*started)

        @pl.when(within(number - levels, count))
        def _():
            gather.ready(number - levels)
            norm(number - levels)

        @pl.when(number == levels + 3)
        def _():
            spread.wait(4)
            ends.start(6)
            for k in range(3):
                project_rows(2, k)

        @pl.when(number >= levels + 3)
        def _():
            project_rows(2, number - levels)

    in_order(count + levels, wave)

    def project(number, item):
        if item is not None:
            spread.wait(item)
            ends.start(4 + number)
            in_order(count, functools.partial(project_rows, number))
        ends.start(number)

    spread.relay(11)
    project(2, None)
    project(3, 5)
    project(1, 6)
    project(0, 7)
    spread.wait(*range(8, 12))

    def dy_chunk(k):
        for half in range(2):
            dy_part[k, half * run : (half + 1) * run, :] = pick_chunk(dy_all, k, half)

    in_order(count, dy_chunk)
    ends.start(8)
    small.drain(0)
    spread.drain(*range(12))
    gather.drain()
    stores.wait(*range(4))
    ends.wait(*range(9))

    def stored(k):
        pltpu.make_async_copy(
            normed.at[span(k, chunk)], normed_out.at[span(k, chunk)], normed_sem.at[k]
        ).wait()

    in_order(count, stored)


class Ring:
    def __init__(self, slots, whole, size, sems):
        self.slots, self.whole, self.size, self.sems = slots, whole, size, sems

    def load(self, k):
        return pltpu.make_async_copy(
            self.whole.at[span(k, self.size)], self.slots.at[lax.rem(k, 2)], self.sems.at[k]
        )

    def store(self, k):
        return pltpu.make_async_copy(
            self.slots.at[lax.rem(k, 2)], self.whole.at[span(k, self.size)], self.sems.at[k]
        )

    def free(self, k):
        @pl.when(k >= 2)
        def _():
            self.store(k - 2).wait()


def core_kernel(sizes, bounds, rate, gain, *refs):
    gain_first, *refs = refs
    query_src, key_src, value_src, rows_src, dy_src, swish_src, *refs = refs
    normed_src, unit_src, scale_src, *refs = refs
    project_src, refs = refs[:4], refs[4:]
    shards, refs = refs[:4], refs[4:]
    mixed_in_out, retained_out, gains_out, *refs = refs
    homes, down_dst, gate_dst, up_dst, *refs = refs
    late_dst, refs = refs[:5], refs[5:]
    query, keys, values, x_rows, out_w, gate_w, up_w, down_w, *refs = refs
    rooms, refs = refs[:4], refs[4:]
    (other_part,), refs = refs[:1], refs[1:]
    sems_one, sems_two, sems_three, sems_four, refs = refs[:6], refs[6:12], refs[12:18], refs[18:24], refs[24:]
    normed_mid, refs = refs[0], refs[1:]
    normed_sems, refs = refs[:6], refs[6:]
    dy, refs = refs[0], refs[1:]
    dy_sems, refs = refs[:6], refs[6:]
    branch, refs = refs[0], refs[1:]
    branch_sems, refs = refs[:6], refs[6:]
    spread_sems, refs = refs[:3], refs[3:]
    deal_sems, refs = refs[:3], refs[3:]
    swap_sems, late_sems, small_sems, refs = refs[:3], refs[3:6], refs[6:9], refs[9:]
    give_sems, refs = refs[:3], refs[3:]
    hidden, gate_grad, up_grad, resid, swish_slots, retained_slots, mixed_in_slots, *refs = refs
    key_acc, value_acc, query_acc, delta, down_grad, mixed, gain_acc, *refs = refs
    sums, line_one, packed, gains, gains_in, *refs = refs
    load_sems, ring_sems, late_load, unit_sems, room, sums_sent, sums_got, gain_sent, gain_got, *halves = refs
    at = around(AXES)
    group, level, core = at
    place = 2 * level + core
    count, levels, _, piece, width = normed_mid.shape
    ranks = 2 * levels
    chunk = ranks * piece
    part_width = width // ranks
    mixed_dst = homes.at[:, pl.ds(0, part_width)]
    grad_dst = homes.at[:, pl.ds(part_width, part_width)]
    loads = Moves(
        [
            (dy_src, dy.at[:, level, core]),
            (query_src, query),
            (key_src, keys),
            (value_src, values),
            (rows_src, x_rows),
        ],
        load_sems,
    )
    loads.start(*range(5))
    swish_one = Ring(swish_slots, swish_src, chunk, ring_sems.at[0])
    swish_two = Ring(swish_slots, swish_src, chunk, ring_sems.at[1])
    retained_one = Ring(retained_slots, retained_out, chunk, ring_sems.at[2])
    retained_two = Ring(retained_slots, retained_out, chunk, ring_sems.at[3])
    mixed_in_ring = Ring(mixed_in_slots, mixed_in_out, chunk, ring_sems.at[4])
    groups, v_dim = sizes[0], values.shape[1]
    late_loads = Moves(
        [(normed_src, normed_mid), (mixed_in_out, up_grad), (project_src[0], dy.at[0]), (project_src[1], dy.at[1])]
        + [
            (project_src[2 + n // 2].at[:, :, :, pl.ds(n % 2 * part_width, part_width)], dy.at[2 + n])
            for n in range(4)
        ],
        late_load,
    )
    swish_one.load(0).start()
    swish_one.load(1).start()
    greet(plane_peers(at, sizes) + column_all(at, sizes))
    spread = Spread(
        at,
        sizes,
        [(shards[0], out_w, 1), (shards[1], gate_w, 0), (shards[2], up_w, 0), (shards[3], down_w, 1)],
        spread_sems,
    )
    deal = Spread(
        at,
        sizes,
        [
            (mixed.at[pl.ds(k * chunk, chunk)], mixed_dst, 0, count * chunk, k * chunk)
            for k in range(count)
        ],
        deal_sems,
    )
    swap = Swap(
        at, sizes, [(down_grad, down_dst, 1), (gate_w, gate_dst, 0), (up_w, up_dst, 0)], swap_sems, halves[:3]
    )
    qk_dim = query.shape[1]
    late = Swap(
        at,
        sizes,
        [
            (gate_w, late_dst[0], 0),
            (out_w, late_dst[1], 1),
            (up_w, late_dst[2], 0),
            (down_grad.at[pl.ds(0, qk_dim)], late_dst[3], 1),
            (down_grad.at[pl.ds(qk_dim, qk_dim)], late_dst[4], 1),
        ],
        late_sems,
        [halves[1], halves[0], halves[2], halves[3], halves[4]],
    )
    small = Swap(at, sizes, [(gains, gains_in, 1)], small_sems)
    give = Spread(
        at,
        sizes,
        [
            (hidden.at[pl.ds(k * chunk, chunk), pl.ds(0, part_width)], grad_dst, 0, count * chunk, k * chunk)
            for k in range(count)
        ],
        give_sems,
    )
    spread.start(0)
    one = Scatter(at, sizes, count, list(rooms) + list(sems_one))
    two = Scatter(at, sizes, count, [other_part] + list(rooms[1:]) + list(sems_two))
    three = Scatter(at, sizes, count, list(rooms) + list(sems_three))
    four = Scatter(at, sizes, count, [other_part] + list(rooms[1:]) + list(sems_four))
    total = rooms[3]
    mid_gather = Gather(at, sizes, count, normed_mid, normed_sems)
    dy_gather = Gather(at, sizes, count, dy, dy_sems)
    branch_gather = Gather(at, sizes, count, branch, branch_sems)
    gain_acc[...] = jnp.zeros(gain_acc.shape, jnp.float32)
    line_one[...] = jnp.zeros(line_one.shape, jnp.float32)
    key_acc[...] = jnp.zeros(key_acc.shape, jnp.float32)
    value_acc[...] = jnp.zeros(value_acc.shape, jnp.float32)
    loads.wait(0)
    dy_gather.start(0)
    loads.wait(1, 2, 3, 4)
    tile = 512

    def first(k):
        where = span(k, chunk)
        slot = lax.rem(k, 2)
        retained_one.free(k)
        retained_slots[slot] = jnp.zeros((chunk, values.shape[1]), jnp.float32)

        def block(j, carry):
            there = span(j, chunk)
            decay = decay_tile(k, j, chunk, bounds, rate)
            weight = lowered(inner_rows(query[where, :], keys[there, :]) * decay)
            retained_slots[slot] += matmul(weight, values[there, :])
            return carry

        lax.fori_loop(0, k + 1, block, 0)
        retained_one.store(k).start()
        normed, _ = layer_norm(retained_slots[slot], GROUP_EPS)
        swish_one.load(k).wait()
        value = swish_slots[slot]
        mixed_in_ring.free(k)
        mixed_in_slots[slot] = lowered(value * jax.nn.sigmoid(value) * normed)
        mixed_in_ring.store(k).start()

        @pl.when(k + 2 < count)
        def _():
            swish_one.load(k + 2).start()

        @pl.when(k == 0)
        def _():
            spread.wait(0)

        one.free(k)
        rows = mixed_in_slots[slot]
        for column in range(0, width, tile):
            value = matmul(rows, out_w[:, column : column + tile])
            one.part[slot, :, :, :, column : column + tile] = lowered(value).reshape(levels, 2, piece, tile)
        one.start(k)

    def mid_norm(k):
        one.finish(k)

        def block(number, carry):
            sub = span(number, 16)
            where = pl.ds(pl.multiple_of(k * piece + number * 16, 16), 16)
            value = wide(x_rows[where, :]) + total[sub, :]
            resid[where, :] = value
            unit, _ = layer_norm(value, EPSILON)
            normed_mid[k, level, core, sub, :] = lowered(unit * gain[...])
            return carry

        lax.fori_loop(0, piece // 16, block, 0)
        mid_gather.start(k)

    def turn(k):
        mid_gather.ready(k)
        rows = normed_mid[k].reshape(chunk, width)
        where = span(k, chunk)
        g = matmul(rows, gate_w[...])
        u = matmul(rows, up_w[...])
        root = 0.7978845608028654
        bend = jnp.tanh(root * (g + 0.044715 * g * g * g))
        curve = 0.5 * (1.0 + bend)
        active = g * curve
        hidden[where, :] = lowered(active * u)
        slope = curve + 0.5 * g * (1.0 - bend * bend) * root * (1.0 + 0.134145 * g * g)
        dy_gather.ready(k)
        rows = jnp.concatenate([dy[k, q, c] for q in range(levels) for c in range(2)], axis=1)
        back = inner_rows(rows, down_w[...])
        gate_grad[where, :] = lowered(back * u * slope)
        up_grad[where, :] = lowered(back * active)
        two.free(k)
        for column in range(0, width, tile):
            columns = slice(column, column + tile)
            value = inner_rows(gate_grad[where, :], gate_w[columns, :])
            value += inner_rows(up_grad[where, :], up_w[columns, :])
            two.part[lax.rem(k, 2), :, :, :, columns] = lowered(value).reshape(levels, 2, piece, tile)
        two.start(k)

    def branch_norm(k):
        two.finish(k)

        def block(number, carry):
            sub = span(number, 16)
            where = pl.ds(pl.multiple_of(k * piece + number * 16, 16), 16)
            unit, scale = layer_norm(resid[where, :], EPSILON)
            grad = total[sub, :]
            outer = grad * unit
            gain_acc[...] += outer[:8] + outer[8:]
            mine = pl.ds(pl.multiple_of(place * piece + number * 16, 16), 16)
            upstream = jnp.concatenate(
                [dy[k, q, c, mine, :] for q in range(levels) for c in range(2)], axis=1
            )
            value = wide(upstream) + norm_back(grad * gain[...], unit, scale)
            branch[k, level, core, sub, :] = lowered(value)
            return carry

        lax.fori_loop(0, piece // 16, block, 0)
        branch_gather.start(k)

    def last(k):
        branch_gather.ready(k)
        rows = branch[k].reshape(chunk, width)
        where = span(k, chunk)
        slot = lax.rem(k, 2)
        grad = inner_rows(rows, out_w[...])
        retained_two.load(k).wait()
        swish_two.load(k).wait()
        normed, scale = layer_norm(retained_slots[slot], GROUP_EPS)
        value = swish_slots[slot]
        gated = jax.nn.sigmoid(value)
        gate_grad[where, :] = lowered(grad * normed * gated * (1.0 + value * (1.0 - gated)))
        delta[...] = lowered(norm_back(grad * value * gated, normed, scale))

        @pl.when(k + 2 < count)
        def _():
            retained_two.load(k + 2).start()
            swish_two.load(k + 2).start()

        query_acc[...] = jnp.zeros(query_acc.shape, jnp.float32)

        def block(j, carry):
            there = span(j, chunk)
            decay = decay_tile(k, j, chunk, bounds, rate)
            weight = lowered(inner_rows(query[where, :], keys[there, :]) * decay)
            score = lowered(inner_rows(delta[...], values[there, :]) * decay)
            query_acc[...] += matmul(score, keys[there, :])
            key_acc[there, :] += inner_cols(score, query[where, :])
            value_acc[there, :] += inner_cols(weight, delta[...])
            return carry

        lax.fori_loop(0, k + 1, block, 0)
        query[where, :] = lowered(query_acc[...])

    def out_part(k):
        three.free(k, one)
        rows = hidden[span(k, chunk), :]
        mine = pl.ds(pl.multiple_of(k * piece, piece), piece)
        for rank in range(ranks):
            columns = slice(rank * part_width, (rank + 1) * part_width)
            value = matmul(rows, down_w[:, columns])
            for run in range(ranks):
                held = jnp.where(place == run, resid[mine, columns], 0.0)
                three.part[
                    lax.rem(k, 2), rank // 2, rank % 2, :, run * part_width : (run + 1) * part_width
                ] = lowered(value[run * piece : (run + 1) * piece, :] + held)
        pl.semaphore_wait(room.at[0, 0], 1)
        three.start(k)

    def out_finish(k):
        three.finish(k)
        for run in range(ranks):
            where = pl.ds(pl.multiple_of(k * chunk + run * piece, piece), piece)
            mixed[where, :] = lowered(total[:, run * part_width : (run + 1) * part_width])

    def runs_of(ref, columns):
        return jnp.concatenate(
            [ref[j, q, c, :, columns] for j in range(count) for q in range(levels) for c in range(2)], axis=0
        )

    def weigh(which):
        def part(k):
            columns = span(k, chunk)
            if which == 0:
                down = jnp.zeros((hidden.shape[1], part_width), jnp.float32)
                for j in range(count):
                    down += inner_cols(hidden[j * chunk : (j + 1) * chunk, :], dy[j, k // 2, lax.rem(k, 2)])
                there = pl.ds(pl.multiple_of(k * part_width, part_width), part_width)
                down_grad[:, there] = lowered(down)
            else:
                target, source = ((gate_w, gate_grad), (up_w, up_grad))[which - 1]
                target[columns, :] = lowered(inner_cols(runs_of(normed_mid, columns), source[...]))

        in_order(width // chunk, part)
        swap.start(which)

    def weigh_late(which):
        def part(k):
            columns = span(k, chunk)
            if which == 0:
                gate_w[columns, :] = lowered(inner_cols(runs_of(normed_mid, columns), gate_grad[...]))
            elif which == 1:
                out_w[:, columns] = lowered(inner_cols(up_grad[...], runs_of(branch, columns)))
            elif which == 2:
                up_w[columns, :] = lowered(inner_cols(runs_of(normed_mid, columns), values[...]))
            else:
                rows = runs_of(normed_mid, columns)
                down_grad[:qk_dim, columns] = lowered(inner_cols(query[...], rows))
                down_grad[qk_dim:, columns] = lowered(inner_cols(keys[...], rows))

        in_order(width // chunk, part)
        late.start(*((which,) if which < 3 else (3, 4)))

    def units(k):
        slot = lax.rem(k, 2)
        return [
            pltpu.make_async_copy(
                unit_src.at[span(k, chunk)], swish_slots.at[slot, :, pl.ds(0, part_width)], unit_sems.at[0, k]
            ),
            pltpu.make_async_copy(
                scale_src.at[span(k, chunk)], retained_slots.at[slot, :, pl.ds(0, 128)], unit_sems.at[1, k]
            ),
        ]

    def peer_of(j):
        peer = lax.rem(place + j, ranks)
        return (group, peer // 2, lax.rem(peer, 2))

    def sender(j):
        return lax.rem(place + ranks - j, ranks)

    def sums_copy(k, j, owner):
        return pltpu.make_async_remote_copy(
            src_ref=sums.at[owner, k],
            dst_ref=sums.at[owner, k],
            send_sem=sums_sent.at[j - 1, k],
            recv_sem=sums_got.at[j - 1, k],
            device_id=peer_of(j),
            device_id_type=MESH,
        )

    def pack_copy(j, owner):
        return pltpu.make_async_remote_copy(
            src_ref=packed.at[owner],
            dst_ref=packed.at[owner],
            send_sem=gain_sent.at[j - 1],
            recv_sem=gain_got.at[j - 1],
            device_id=peer_of(j),
            device_id_type=MESH,
        )

    def make_room(scatter, turn_of, k):
        scatter.sent(k)
        where = room.at[turn_of]
        pl.semaphore_signal(where.at[0], inc=1, device_id=(group, level, 1 - core), device_id_type=MESH)

        @pl.when(level > 0)
        def _():
            pl.semaphore_signal(where.at[1], inc=1, device_id=(group, level - 1, core), device_id_type=MESH)

        @pl.when(level < levels - 1)
        def _():
            pl.semaphore_signal(where.at[2], inc=1, device_id=(group, level + 1, core), device_id_type=MESH)

    def in_part(k):
        four.free(k, two)
        where = span(k, chunk)
        slot = lax.rem(k, 2)
        rows = [query[where, :], keys[where, :]]
        for source in (values, gate_grad):
            rows += [source[where, n : n + part_width] for n in range(0, v_dim, part_width)]
        first_sum = jnp.zeros((chunk, part_width), jnp.float32)
        second_sum = jnp.zeros((chunk, part_width), jnp.float32)
        for rank in range(ranks):
            columns = slice(rank * part_width, (rank + 1) * part_width)
            value = inner_rows(rows[0], dy[0, rank // 2, rank % 2])
            for n in range(1, len(rows)):
                value += inner_rows(rows[n], dy[n, rank // 2, rank % 2])
            for run in range(ranks):
                four.part[
                    slot, rank // 2, rank % 2, :, run * part_width : (run + 1) * part_width
                ] = lowered(value[run * piece : (run + 1) * piece, :])
            first_sum += value * gain_first[:, columns]
            second_sum += value * wide(normed_mid[k, :, :, :, columns].reshape(chunk, part_width))
        pl.semaphore_wait(room.at[1, 0], 1)
        four.start(k)
        ones = jnp.ones((8, part_width), jnp.float32)
        flat = [
            lax.dot_general(
                ones,
                item,
                (((1,), (1,)), ((), ())),
                precision=lax.Precision.HIGHEST,
                preferred_element_type=jnp.float32,
            )
            for item in (first_sum, second_sum)
        ]
        line = lax.broadcasted_iota(jnp.int32, (8, chunk), 0)
        sums[place, k] = jnp.where(line == 0, flat[0], flat[1])
        for j in range(1, ranks):
            sums_copy(k, j, place).start()

    def in_room(turn_of, wave):
        @pl.when(within(wave - level, count) & (level < levels - 1))
        def _():
            pl.semaphore_wait(room.at[turn_of, 1], 1)

        @pl.when(within(wave - (levels - 1 - level), count) & (level > 0))
        def _():
            pl.semaphore_wait(room.at[turn_of, 2], 1)

    def in_finish(k):
        four.finish(k)
        for j in range(1, ranks):
            sums_copy(k, j, sender(j)).wait_recv()
        line = lax.broadcasted_iota(jnp.int32, (8, 128), 0)
        lane = lax.broadcasted_iota(jnp.int32, (8, 128), 1)
        means = lax.dot_general(
            jnp.sum(sums[:, k], 0),
            jnp.where(line == lane, 1.0 / width, 0.0),
            (((0,), (0,)), ((), ())),
            precision=lax.Precision.HIGHEST,
            preferred_element_type=jnp.float32,
        )
        slot = lax.rem(k, 2)
        for copy in units(k):
            copy.wait()
        mine = pl.ds(pl.multiple_of(place * part_width, part_width), part_width)
        value = jnp.concatenate(
            [total[:, run * part_width : (run + 1) * part_width] for run in range(ranks)], axis=0
        )
        normed = swish_slots[slot, :, :part_width]
        outer = value * normed
        line_one[...] += jnp.sum(outer.reshape(chunk // 8, 8, part_width), 0)
        back = value * gain_first[:, mine] - means[:, :1] - normed * means[:, 1:2]
        upstream = wide(branch[k, :, :, :, mine].reshape(chunk, part_width))
        hidden[span(k, chunk), :part_width] = lowered(upstream + retained_slots[slot, :, :1] * back)

        @pl.when(k + 2 < count)
        def _():
            for copy in units(k + 2):
                copy.start()

    lead = 3
    mid_lag = lead + levels
    turn_lag = mid_lag + levels - 1
    branch_lag = turn_lag + levels
    last_lag = branch_lag + levels - 1
    turned = turn_lag + count
    close_lag = last_lag + count
    out_lag = last_lag - 2

    def at_wave(number, lag, step):
        @pl.when(within(number - lag, count))
        def _():
            step(number - lag)

    def wave(number):
        at_wave(number, lead, first)
        for gather, lag, sent in (
            (branch_gather, branch_lag, functools.partial(make_room, two, 0)),
            (mid_gather, mid_lag, one.sent),
        ):
            at_wave(number, lag + 1, sent)
            for hop in range(levels - 1, 0, -1):
                at_wave(number, lag + hop, functools.partial(hop_on, gather, hop))
        at_wave(number, branch_lag, branch_norm)
        at_wave(number, mid_lag, mid_norm)
        at_wave(number, -1, next_dy)
        for hop in range(levels - 1, 0, -1):
            at_wave(number, hop, functools.partial(hop_on, dy_gather, hop))
        for scatter, lag in ((two, turn_lag), (one, lead)):
            at_wave(number, lag + 1, scatter.join)
            scatter.steps(number - lag - 1)
        for step, relayed, started in ((1, (0,), (1, 2)), (4, (1,), (3,)), (6, (2,), ()), (8, (3,), ())):

            @pl.when(number == step)
            def _():
                spread.relay(*relayed)
                spread.start(*started)

        @pl.when(number == turn_lag)
        def _():
            spread.wait(1, 2, 3)

        at_wave(number, turn_lag, turn)

        @pl.when(number == turn_lag + 1)
        def _():
            retained_one.store(count - 2).wait()
            retained_one.store(count - 1).wait()
            for k in range(2):
                retained_two.load(k).start()
                swish_two.load(k).start()

        @pl.when(number == turned)
        def _():
            spread.drain(*range(4))

        for step, which in ((0, 1), (1, 2), (2, 0)):

            @pl.when(number == turned + step)
            def _():
                weigh(which)

        for step, which in ((2, 1), (4, 2), (6, 0)):

            @pl.when(number == turned + step)
            def _():
                swap.relay(which)

        @pl.when(number == turned + 2)
        def _():
            mid_gather.drain()
            mixed_in_ring.store(count - 2).wait()
            mixed_in_ring.store(count - 1).wait()
            late_loads.start(0, 1)

        @pl.when(number == branch_lag + count)
        def _():
            dy_gather.drain()
            late_loads.start(*range(2, 8))

        at_wave(number, last_lag, last)
        at_wave(number, out_lag, out_part)
        at_wave(number, out_lag + 1, three.join)
        in_room(0, number - out_lag - 1)
        three.steps(number - out_lag - 1)
        at_wave(number, out_lag + levels, out_finish)
        for k in range(count):

            @pl.when(number == out_lag + levels + k)
            def _():
                deal.start(k)

            @pl.when(number == out_lag + levels + k + 2)
            def _():
                deal.relay(k)

        at_wave(number, out_lag + levels + 1, functools.partial(make_room, three, 1))

        @pl.when(number == close_lag)
        def _():
            keys[...] = lowered(key_acc[...])
            values[...] = lowered(value_acc[...])
            for k in range(2):
                for copy in units(k):
                    copy.start()
            late_loads.wait(*range(8))

        for step, before, which in ((0, 1, 0), (1, 0, 1), (2, 2, 2), (3, None, 3)):

            @pl.when(number == close_lag + step)
            def _():
                if before is not None:
                    swap.wait(before)
                weigh_late(which)

        at_wave(number, close_lag, in_part)
        at_wave(number, close_lag + 1, four.join)
        in_room(1, number - close_lag - 1)
        four.steps(number - close_lag - 1)
        at_wave(number, close_lag + levels, in_finish)
        for step, which in ((3, (0,)), (4, (1,)), (5, (2,)), (7, (3, 4))):

            @pl.when(number == close_lag + step)
            def _():
                late.relay(*which)

        for k in range(count):

            @pl.when(number == close_lag + levels + k)
            def _():
                give.start(k)

            @pl.when(number == close_lag + levels + k + 2)
            def _():
                give.relay(k)

    def hop_on(gather, hop, k):
        gather.hop(k, hop)

    def next_dy(k):
        @pl.when(k > 0)
        def _():
            dy_gather.start(k)

    in_order(close_lag + levels + count, wave)
    give.relay(count - 2, count - 1)
    packed[place] = jnp.concatenate(
        [jnp.sum(gain_acc[...], 0, keepdims=True), jnp.sum(line_one[...], 0, keepdims=True)], axis=1
    )
    for j in range(1, ranks):
        pack_copy(j, place).start()
    for j in range(1, ranks):
        pack_copy(j, sender(j)).wait_recv()
    line = lax.broadcasted_iota(jnp.int32, (8, width), 0)
    two_sum = sum(packed[rank, :, :width] for rank in range(ranks))
    one_sum = jnp.concatenate([packed[rank, :, width:] for rank in range(ranks)], axis=1)
    gains[...] = jnp.where(line == 0, one_sum, two_sum)
    small.start(0)
    small.wait(0)
    gains_out[...] = jnp.sum(gains_in[...], 0)
    late.wait(*range(5))
    give.wait(*range(count))
    give.drain(*range(count))
    deal.wait(*range(count))
    deal.drain(*range(count))
    four.drain()
    three.across(count - 2).wait_send()
    three.across(count - 1).wait_send()
    branch_gather.drain()
    for j in range(1, ranks):
        pack_copy(j, place).wait_send()

    def drain(k):
        for j in range(1, ranks):
            sums_copy(k, j, place).wait_send()

    in_order(count, drain)


def finish_kernel(first_seq, last_seq, starts, bases, begins, home, gains, homes, *refs):
    parts, refs = refs[:8], refs[8:]
    mixed_out, grad_out, *refs = refs
    outs, refs = refs[:8], refs[8:]
    gain_one, gain_two, *refs = refs
    homes_held, *refs = refs
    held, sums, refs = refs[:8], refs[8:16], refs[16:]
    picked, load_sems, store_sems = refs
    loads = Moves(list(zip(parts, held)) + [(homes, homes_held)], load_sems)
    stores = Moves(
        list(zip(sums, outs)) + [(picked.at[0], mixed_out), (picked.at[1], grad_out)], store_sems
    )
    loads.start(*range(9))
    gain_one[...] = gains[0:1, :]
    gain_two[...] = gains[1:2, :]
    for number in range(8):
        loads.wait(number)
        ways, rows, columns = held[number].shape
        run = min(64, rows)
        turned = number < 2

        def block(k):
            where = span(k, run)
            total = wide(held[number][0, where, :])
            for way in range(1, ways):
                total += wide(held[number][way, where, :])
            sums[number][where, :] = total

        def turn(k):
            where = span(k, 128)
            total = wide(held[number][0, :, where])
            for way in range(1, ways):
                total += wide(held[number][way, :, where])
            sums[number][where, :] = total.T

        if turned:
            in_order(columns // 128, turn)
        else:
            in_order(rows // run, block)
        stores.start(number)
    loads.wait(8)
    width = picked.shape[2]
    rows = 128
    window = rows + 16
    lane = lax.broadcasted_iota(jnp.int32, (rows, window), 1)

    def pick_block(k):
        own = home[0] + k * rows + lax.broadcasted_iota(jnp.int32, (rows, 1), 0)

        def one(seq, total):
            start = begins[k, seq]
            inside = (own >= starts[seq]) & (own < starts[seq + 1])
            wanted = jnp.where(inside, own + bases[seq] - 16 * start, -1)
            chosen = jnp.where(lane == wanted, 1.0, 0.0).astype(jnp.bfloat16)
            there = jnp.concatenate([homes_held[start + n] for n in range(window // 16)], axis=0)
            return total + matmul(chosen, there)

        total = lax.fori_loop(
            first_seq[k], last_seq[k] + 1, one, jnp.zeros((rows, 2 * width), jnp.float32)
        )
        where = span(k, rows)
        picked[0, where, :] = lowered(total[:, :width])
        picked[1, where, :] = lowered(total[:, width:])

    in_order(picked.shape[1] // rows, pick_block)
    stores.start(8, 9)
    stores.wait(*range(10))


def column_all(at, sizes):
    group, level, core = at
    return column_peers(at, sizes) + [
        (group, lax.rem(level + k, sizes[1]), 1 - core) for k in range(1, sizes[1])
    ]


def struct(shape, kind=jnp.bfloat16):
    return jax.ShapeDtypeStruct(shape, kind)


VMEM = pltpu.VMEM
DMA = pltpu.SemaphoreType.DMA


def kernel_call(body, number, ins, outs, scratch):
    places = {
        "vmem": pl.BlockSpec(memory_space=pltpu.VMEM),
        "smem": pl.BlockSpec(memory_space=pltpu.SMEM),
        "any": pl.BlockSpec(memory_space=pl.ANY),
    }
    return pl.pallas_call(
        body,
        out_shape=[shape for _, shape in outs],
        in_specs=[places[inside] for inside, _ in ins],
        out_specs=[places[inside] for inside, _ in outs],
        scratch_shapes=scratch,
        compiler_params=pltpu.CompilerParams(
            collective_id=number, has_side_effects=True, vmem_limit_bytes=63 * 2**20
        ),
    )(*[array for _, array in ins])


def spread_shape(shard, axis, sizes):
    shape = list(shard.shape)
    shape[axis] *= sizes[0]
    return struct(tuple(shape), shard.dtype)


def swap_shape(whole, axis, sizes):
    shape = list(whole.shape)
    shape[axis] //= sizes[0]
    return struct((3 if sizes[0] == 4 else sizes[0],) + tuple(shape), whole.dtype)


def anywhere(items):
    return [("any", item) for item in items]


def held_like(arrays):
    return [VMEM(a.shape, a.dtype) for a in arrays]


def pick(rows, whole):
    return whole.at[rows].get(mode="promise_in_bounds")


def shards(
    tokens,
    cotangent,
    lengths,
    dealing,
    w_query,
    w_key,
    w_value,
    w_swish,
    w_out,
    w_gate,
    w_up,
    w_down,
    gain_attn,
    gain_mlp,
):
    group = lax.axis_index("dp")
    place = lax.axis_index(("heads", "tensor"))
    rows_dev = tokens.shape[0]
    slice_width = tokens.shape[1]
    seq_count = lengths.shape[0]
    ident = jnp.arange(seq_count, dtype=jnp.int32)
    starts = jnp.sum(jnp.where(ident[:, None] > ident[None, :], lengths[None, :], 0), 1)
    picked = lax.dynamic_slice_in_dim(dealing, group * SEQ_DEV, SEQ_DEV)
    match = picked[:, None] == ident[None, :]
    dealt_len = jnp.sum(jnp.where(match, lengths[None, :], 0), 1)
    home_start = jnp.sum(jnp.where(match, starts[None, :], 0), 1)
    slots = jnp.arange(SEQ_DEV, dtype=jnp.int32)
    dealt_start = jnp.sum(jnp.where(slots[:, None] > slots[None, :], dealt_len[None, :], 0), 1)
    rows = jnp.arange(rows_dev, dtype=jnp.int32)
    seq_ids = jnp.sum((rows[:, None] >= dealt_start[None, :]).astype(jnp.int32), 1) - 1
    sizes = (lax.axis_size("dp"), lax.axis_size("heads"))
    ranks = sizes[1] * lax.axis_size("tensor")
    chunk = ranks * PIECE
    count = rows_dev // chunk
    width = slice_width * ranks
    own = rows_dev // ranks
    qk_dim, v_dim, ff_dim = w_query.shape[1], w_value.shape[1], w_gate.shape[1]
    f32 = jnp.float32
    masters = (w_query, w_key, w_value, w_swish, w_out, w_gate, w_up, w_down)
    axes = (0, 0, 0, 0, 1, 0, 0, 1)
    gain_rows = struct((8, gain_attn.shape[0]), f32)
    shifts = home_start - dealt_start
    firsts = jnp.arange(2 * count, dtype=jnp.int32) * (chunk // 2)
    begins = jnp.clip(firsts[:, None] + shifts[None, :], 0, sizes[0] * rows_dev - chunk) // 16
    bf16 = jnp.bfloat16
    rounded = [struct(w.shape) for w in masters]
    full_w = [spread_shape(w, a, sizes) for w, a in zip(rounded, axes)]
    by_runs = struct((rows_dev // 16, 16, slice_width))
    every = spread_shape(by_runs, 0, sizes)
    gains_all = struct((sizes[0] * 8, gain_rows.shape[1]), f32)
    (
        normed_in,
        query,
        keys,
        values,
        swish_in,
        dy_part,
        query_w,
        key_w,
        value_w,
        swish_w,
        *low,
        wide_one,
        wide_two,
        x_rows,
        unit_share,
        scale_one,
    ) = kernel_call(
        functools.partial(front_kernel, sizes),
        0,
        [("smem", dealt_start), ("smem", shifts), ("smem", begins.reshape(-1))]
        + anywhere((tokens.reshape(by_runs.shape), cotangent.reshape(by_runs.shape)))
        + [("vmem", gain_attn.reshape(1, -1)), ("vmem", gain_mlp.reshape(1, -1))]
        + anywhere(masters),
        anywhere(
            [
                struct((rows_dev, width)),
                struct((rows_dev, qk_dim)),
                struct((rows_dev, qk_dim)),
                struct((rows_dev, v_dim)),
                struct((rows_dev, v_dim), f32),
                struct((count, chunk, slice_width)),
            ]
            + full_w[:4]
            + rounded[4:]
        )
        + [
            ("vmem", struct((1, width), f32)),
            ("vmem", struct((1, width), f32)),
            ("vmem", struct((own, width))),
            ("vmem", struct((rows_dev, slice_width), f32)),
            ("vmem", struct((rows_dev, 128), f32)),
        ],
        Gather.scratch(count, sizes, (chunk, slice_width))
        + Spread.scratch(12, sizes)
        + Spread.scratch(1, sizes)
        + held_like(masters)
        + held_like(rounded)
        + held_like(full_w[:4])
        + held_like((by_runs, by_runs, gain_rows, every, every, gains_all))
        + [
            VMEM((count, chunk, slice_width), bf16),
            VMEM((rows_dev, width), bf16),
            VMEM((rows_dev, qk_dim), bf16),
            VMEM((rows_dev, qk_dim), bf16),
            VMEM((rows_dev, v_dim), bf16),
            VMEM((rows_dev, v_dim), f32),
            DMA((10,)),
            DMA((4,)),
            DMA((9,)),
            DMA((count,)),
        ],
    )
    rate = jnp.log1p(-jnp.exp2(-5.0 - place.astype(f32))).reshape(1)
    by_rows = (PIECE, width)
    pieces = (count, sizes[1], 2) + by_rows
    blocks = (sizes[1], 2, slice_width)
    late_w = [struct(shape) for shape in ((width, v_dim), (v_dim, width), (width, v_dim), (qk_dim, width))]
    late_w.append(late_w[3])
    late_axes = (0, 1, 0, 1, 1)
    core_outs = kernel_call(
        functools.partial(core_kernel, sizes),
        1,
        [("smem", dealt_start), ("smem", rate), ("vmem", wide_two), ("vmem", wide_one)]
        + anywhere((query, keys, values, x_rows, dy_part, swish_in))
        + anywhere((normed_in.reshape(pieces), unit_share, scale_one))
        + anywhere([w.reshape(blocks + w.shape[1:]) for w in (query_w, key_w, value_w, swish_w)])
        + anywhere(low),
        anywhere([struct((rows_dev, v_dim)), struct((rows_dev, v_dim), f32)])
        + [("vmem", struct((8, gain_attn.shape[0]), f32))]
        + anywhere(
            [
                struct((sizes[0] * rows_dev, 2 * slice_width)),
                swap_shape(full_w[7], 1, sizes),
                swap_shape(full_w[5], 0, sizes),
                swap_shape(full_w[6], 0, sizes),
            ]
            + [swap_shape(w, a, sizes) for w, a in zip(late_w, late_axes)]
        ),
        held_like((query, keys, values, x_rows))
        + held_like(full_w[4:])
        + Scatter.rooms(count, sizes, by_rows)
        + Scatter.rooms(count, sizes, by_rows)[:1]
        + Scatter.sems(count, sizes) * 4
        + Gather.scratch(count, sizes, by_rows)
        + Gather.scratch(count, sizes, (chunk, slice_width))
        + Gather.scratch(count, sizes, by_rows)
        + Spread.scratch(4, sizes)
        + Spread.scratch(count, sizes)
        + Swap.scratch(3, sizes)
        + Swap.scratch(5, sizes)
        + Swap.scratch(1, sizes)
        + Spread.scratch(count, sizes)
        + [
            VMEM((rows_dev, ff_dim), bf16),
            VMEM((rows_dev, ff_dim), bf16),
            VMEM((rows_dev, ff_dim), bf16),
            VMEM((own, width), f32),
            VMEM((2, chunk, v_dim), f32),
            VMEM((2, chunk, v_dim), f32),
            VMEM((2, chunk, v_dim), bf16),
            VMEM((rows_dev, qk_dim), f32),
            VMEM((rows_dev, v_dim), f32),
            VMEM((chunk, qk_dim), f32),
            VMEM((chunk, v_dim), bf16),
            VMEM((ff_dim, width), bf16),
            VMEM((rows_dev, slice_width), bf16),
            VMEM((8, width), f32),
            VMEM((ranks, count, 8, chunk), f32),
            VMEM((8, slice_width), f32),
            VMEM((ranks, 1, width + slice_width), f32),
            VMEM((8, width), f32),
            VMEM((sizes[0], 8, gain_attn.shape[0]), f32),
            DMA((5,)),
            DMA((5, count)),
            DMA((8,)),
            DMA((2, count)),
            pltpu.SemaphoreType.REGULAR((2, 3)),
            DMA((ranks - 1, count)),
            DMA((ranks - 1, count)),
            DMA((ranks - 1,)),
            DMA((ranks - 1,)),
        ]
        + half_blocks([(full_w[7], 1), (full_w[5], 0), (full_w[6], 0)], sizes)
        + half_blocks(list(zip(late_w, late_axes))[3:], sizes),
    )
    _, _, gains, homes, *parts = core_outs
    slot_match = dealing[:, None] == ident[None, :]
    slot_len = jnp.sum(jnp.where(slot_match, lengths[None, :], 0), 1)
    slot_home = jnp.sum(jnp.where(slot_match, starts[None, :], 0), 1)
    per_group = slot_len.reshape(-1, SEQ_DEV)
    slot_start = (jnp.cumsum(per_group, 1) - per_group).reshape(-1)
    slot_base = ident // SEQ_DEV * rows_dev + slot_start - slot_home
    owner_base = jnp.sum(jnp.where(dealing[None, :] == ident[:, None], slot_base[None, :], 0), 1)
    blocks_at = group * rows_dev + jnp.arange(rows_dev // 128, dtype=jnp.int32) * 128
    first_seq = jnp.sum((blocks_at[:, None] >= starts[None, :]).astype(jnp.int32), 1) - 1
    last_seq = jnp.sum((blocks_at[:, None] + 127 >= starts[None, :]).astype(jnp.int32), 1) - 1
    total_rows = sizes[0] * rows_dev
    home_begins = jnp.clip(blocks_at[:, None] + owner_base[None, :], 0, total_rows - 144) // 16
    all_starts = jnp.concatenate([starts, jnp.full((1,), total_rows, jnp.int32)])
    homes = homes.reshape(total_rows // 16, 16, 2 * slice_width)
    order = [parts[n] for n in (6, 7, 5, 3, 4, 1, 2, 0)]
    owners = (w_query, w_key, w_value, w_swish, w_out, w_gate, w_up, w_down)
    finals = [struct(w.shape, f32) for w in owners]
    picks = struct((2, rows_dev, slice_width))
    one_place = {"smem": pl.BlockSpec(memory_space=pltpu.SMEM), "any": pl.BlockSpec(memory_space=pl.ANY)}
    one_place["vmem"] = pl.BlockSpec(memory_space=pltpu.VMEM)
    mixed_rows, grad_rows, *grads, gain_one, gain_two = pl.pallas_call(
        finish_kernel,
        out_shape=[struct((rows_dev, slice_width))] * 2 + finals + [struct((1, gain_attn.shape[0]), f32)] * 2,
        in_specs=[one_place["smem"]] * 6 + [one_place["vmem"]] + [one_place["any"]] * 9,
        out_specs=[one_place["any"]] * 10 + [one_place["vmem"]] * 2,
        scratch_shapes=held_like([homes] + order + finals + [picks]) + [DMA((9,)), DMA((10,))],
        compiler_params=pltpu.CompilerParams(vmem_limit_bytes=60 * 2**20),
    )(first_seq, last_seq, all_starts, owner_base, home_begins, blocks_at[:1], gains, homes, *order)
    return (
        mixed_rows,
        grad_rows,
        grads[0],
        grads[1],
        grads[2],
        grads[3],
        grads[4],
        grads[5],
        grads[6],
        grads[7],
        gain_one.reshape(-1),
        gain_two.reshape(-1),
    )


def solution(mesh):
    in_specs = (
        P("dp", ("heads", "tensor")),
        P("dp", ("heads", "tensor")),
        P(),
        P(),
        P("dp", ("heads", "tensor")),
        P("dp", ("heads", "tensor")),
        P("dp", ("heads", "tensor")),
        P("dp", ("heads", "tensor")),
        P(("heads", "tensor"), "dp"),
        P("dp", ("heads", "tensor")),
        P("dp", ("heads", "tensor")),
        P(("heads", "tensor"), "dp"),
        P("dp"),
        P("dp"),
    )
    out_specs = (
        P("dp", ("heads", "tensor")),
        P("dp", ("heads", "tensor")),
        P("dp", ("heads", "tensor")),
        P("dp", ("heads", "tensor")),
        P("dp", ("heads", "tensor")),
        P("dp", ("heads", "tensor")),
        P(("heads", "tensor"), "dp"),
        P("dp", ("heads", "tensor")),
        P("dp", ("heads", "tensor")),
        P(("heads", "tensor"), "dp"),
        P("dp"),
        P("dp"),
    )
    return jax.shard_map(shards, mesh=mesh, in_specs=in_specs, out_specs=out_specs, check_vma=False)
```
